32 devices in a mesh: tok: 2 (over core), row: 4 (over y, x), col: 4 (over z).
Axes of the slice: x: 2, y: 2, z: 4, core: 2. Of those that a mesh axis runs over, the one named last changes fastest.
Arguments:
- layer_in: bfloat16 [9216, 2048], P(('tok', 'row'), 'col'), may hold values from -6 to 6
- cotangent: bfloat16 [9216, 2048], P(('tok', 'row'), 'col'), may hold values from -6 to 6
- qkv_weight: bfloat16 [3, 2048, 2048], P(None, 'col', 'row'), may hold values from -0.125 to 0.125
- out_weight: bfloat16 [2048, 2048], P('row', 'col'), may hold values from -0.125 to 0.125
- ffn_weight: bfloat16 [2, 2048, 8192], P(None, 'col', 'row'), may hold values from -0.125 to 0.125
- down_weight: bfloat16 [8192, 2048], P('row', 'col'), may hold values from -0.0625 to 0.0625
- qk_gain: bfloat16 [2, 2048], P(None, 'row'), may hold values from 0.5 to 1.5
- post_gain: bfloat16 [2, 2048], P(None, 'col'), may hold values from 0.5 to 1.5
- qkv_lower: bfloat16 [3, 8, 2048, 16], P(None, None, 'col'), may hold values from -0.125 to 0.125
- qkv_raise: bfloat16 [3, 8, 16, 2048], P(None, None, None, 'row'), may hold values from -0.25 to 0.25
- out_lower: bfloat16 [8, 2048, 16], P(None, 'row'), may hold values from -0.125 to 0.125
- out_raise: bfloat16 [8, 16, 2048], P(None, None, 'col'), may hold values from -0.25 to 0.25
- ffn_lower: bfloat16 [2, 8, 2048, 16], P(None, None, 'col'), may hold values from -0.125 to 0.125
- ffn_raise: bfloat16 [2, 8, 16, 8192], P(None, None, None, 'row'), may hold values from -0.25 to 0.25
- down_lower: bfloat16 [8, 8192, 16], P(None, 'row'), may hold values from -0.0625 to 0.0625
- down_raise: bfloat16 [8, 16, 2048], P(None, None, 'col'), may hold values from -0.25 to 0.25
- adapter_ids: int32 [8, 7], replicated, may hold values from 0 to 7
- prompt_len: int32 [8], replicated, may hold values from 256 to 1024, as said below
Outputs:
- layer_out: float32 [9216, 2048], P(('tok', 'row'), 'col')
- grad_in: float32 [9216, 2048], P(('tok', 'row'), 'col')
- qkv_lower_grad: float32 [3, 8, 2048, 16], P(None, None, 'col')
- qkv_raise_grad: float32 [3, 8, 16, 2048], P(None, None, None, 'row')
- out_lower_grad: float32 [8, 2048, 16], P(None, 'row')
- out_raise_grad: float32 [8, 16, 2048], P(None, None, 'col')
- ffn_lower_grad: float32 [2, 8, 2048, 16], P(None, None, 'col')
- ffn_raise_grad: float32 [2, 8, 16, 8192], P(None, None, None, 'row')
- down_lower_grad: float32 [8, 8192, 16], P(None, 'row')
- down_raise_grad: float32 [8, 16, 2048], P(None, None, 'col')
The draws below stay inside these ranges and needn't reach their ends.
Inputs may be any that keep to these rules, and one draw needn't show every extreme that they name: Group g's prompt holds prompt_len[g] real tokens at its start, the other slots of its 1024 are padding; in every draw some group's prompt is full. adapter_ids[g, p] is the adapter of projection p (q, k, v, out, gate, up, down) for group g.
All inputs are finite; a program needn't handle non-finite values.
Results may differ from the reference program's by a relative error of at most 0.018.
Values may be sent and summed in bfloat16 or wider, within the bound.
A program may use at most 320 MiB of HBM per device.

```python
import math
import jax
import jax.numpy as jnp
from jax import lax

D = 2048
HEADS = 16
FF = 8192
HEAD_DIM = 128
RANK = 16
ADAPTERS = 8
PROMPT = 1024
CONT_LEN = 128
SLAB = 1152
GROUPS = 8
TOKENS = 9216


def draw_prompt_len(key, part):
    first_key, second_key = jax.random.split(jax.random.fold_in(key, 11))
    lengths = jax.random.randint(first_key, (GROUPS,), PROMPT // 4, PROMPT + 1)
    full_group = jax.random.randint(second_key, (), 0, GROUPS)
    return jnp.where(jnp.arange(GROUPS) == full_group, PROMPT, lengths).astype(jnp.int32)


def place_ends(result, key, low, largest):
    spot = [jax.random.randint(jax.random.fold_in(key, axis), (), 0, length) for axis, length in enumerate(result.shape)]
    longest = result.shape.index(max(result.shape))
    neighbour = spot[:longest] + [(spot[longest] + 1) % result.shape[longest]] + spot[longest + 1:]
    return result.at[tuple(spot)].set(low).at[tuple(neighbour)].set(largest)


def shard_levels(rng, dims, cuts, least, largest):
    level, own = 1.0, jax.random.fold_in(rng, 6)
    for dim, shards_of in cuts:
        heights = jnp.exp(jax.random.uniform(jax.random.fold_in(own, dim), (shards_of,), jnp.float32, least / len(cuts), largest / len(cuts)))
        level = level * jnp.repeat(heights, dims[dim] // shards_of).reshape([-1 if axis == dim else 1 for axis in range(len(dims))])
    return level


def centred(rng, extent, scale, reach, shards=(), held_as=jnp.bfloat16):
    factor_of = shard_levels(rng, extent, shards, -0.22, 0.18) if shards else 1.0
    values = jax.random.normal(rng, extent, jnp.float32) * scale * factor_of
    return jnp.minimum(jnp.maximum(values, -reach), reach).astype(held_as)


def setup_inputs(seed: int = 0) -> dict:
    key_of = jax.random.split(jax.random.key(seed), 19)
    layer_in = centred(key_of[0], (TOKENS, D), 1.0, 6.0, ((0, 8), (1, 4)))
    cotangent = centred(key_of[1], (TOKENS, D), 1.0, 6.0, ((0, 8), (1, 4)))
    qkv_weight = centred(key_of[2], (3, D, D), D ** -0.5, 0.125, ((1, 4), (2, 4)))
    out_weight = centred(key_of[3], (D, D), D ** -0.5, 0.125, ((0, 4), (1, 4)))
    ffn_weight = centred(key_of[4], (2, D, FF), D ** -0.5, 0.125, ((1, 4), (2, 4)))
    down_weight = centred(key_of[5], (FF, D), FF ** -0.5, 0.0625, ((0, 4), (1, 4)))
    qk_gain = jnp.clip(1.0 + 0.1 * jax.random.normal(key_of[6], (2, D), jnp.float32), 0.5, 1.5).astype(jnp.bfloat16)
    post_gain = jnp.clip(1.0 + 0.1 * jax.random.normal(key_of[7], (2, D), jnp.float32), 0.5, 1.5).astype(jnp.bfloat16)
    qkv_lower = centred(key_of[8], (3, ADAPTERS, D, RANK), D ** -0.5, 0.125, ((2, 4),))
    qkv_raise = centred(key_of[9], (3, ADAPTERS, RANK, D), (2 * RANK * RANK) ** -0.5, 0.25, ((3, 4),))
    out_lower = centred(key_of[10], (ADAPTERS, D, RANK), D ** -0.5, 0.125, ((1, 4),))
    out_raise = centred(key_of[11], (ADAPTERS, RANK, D), (2 * RANK * RANK) ** -0.5, 0.25, ((2, 4),))
    ffn_lower = centred(key_of[12], (2, ADAPTERS, D, RANK), D ** -0.5, 0.125, ((2, 4),))
    ffn_raise = centred(key_of[13], (2, ADAPTERS, RANK, FF), (2 * RANK * RANK) ** -0.5, 0.25, ((3, 4),))
    down_lower = centred(key_of[14], (ADAPTERS, FF, RANK), FF ** -0.5, 0.0625, ((1, 4),))
    down_raise = centred(key_of[15], (ADAPTERS, RANK, D), (2 * RANK * RANK) ** -0.5, 0.25, ((2, 4),))
    adapter_ids = place_ends(jax.random.randint(key_of[16], (GROUPS, 7), 0, ADAPTERS), jax.random.fold_in(key_of[16], 1), 0, ADAPTERS - 1).astype(jnp.int32)
    prompt_len = draw_prompt_len(jax.random.fold_in(key_of[18], 71), 0)
    return dict(layer_in=layer_in, cotangent=cotangent, qkv_weight=qkv_weight, out_weight=out_weight, ffn_weight=ffn_weight, down_weight=down_weight, qk_gain=qk_gain, post_gain=post_gain, qkv_lower=qkv_lower, qkv_raise=qkv_raise, out_lower=out_lower, out_raise=out_raise, ffn_lower=ffn_lower, ffn_raise=ffn_raise, down_lower=down_lower, down_raise=down_raise, adapter_ids=adapter_ids, prompt_len=prompt_len)


@jax.custom_vjp
def low(v):
    return lax.optimization_barrier(v.astype(jnp.bfloat16)).astype(jnp.float32)

@jax.custom_vjp
def low_back(v):
    return v

def low_keep(v):
    return (low(v), None)

def low_pass(kept, grad):
    return (grad,)

def back_keep(v):
    return (v, None)

def back_low(kept, grad):
    return (low(grad),)
low.defvjp(low_keep, low_pass)
low_back.defvjp(back_keep, back_low)
adapter_scale = 2.0
norm_eps = 1e-06
rope_base = 500000.0
very_low = -1e+30
full_precision = lax.Precision.HIGHEST

def matrix_product(left, right):
    return jnp.dot(left, right, precision=full_precision)

def project(input_rows, dense_weight, down_factor, up_factor):
    return matrix_product(input_rows, dense_weight) + adapter_scale * matrix_product(matrix_product(input_rows, down_factor), up_factor)

def rms_norm(values, gain):
    return values * lax.rsqrt(lax.optimization_barrier(jnp.mean(values * values, axis=-1, keepdims=True)) + norm_eps) * gain

def token_places(length):
    slot_ids = jnp.arange(SLAB, dtype=jnp.int32)
    return jnp.where(slot_ids < PROMPT, slot_ids, length + (slot_ids - PROMPT) % CONT_LEN)

def rotation(places, head_size):
    half_dim = head_size // 2
    frequency = jnp.exp(-(2.0 * jnp.arange(half_dim, dtype=jnp.float32) / head_size) * math.log(rope_base))
    angles = places.astype(jnp.float32)[:, None] * frequency[None, :]
    return (jnp.cos(angles)[:, None, :], jnp.sin(angles)[:, None, :])

def rotate(values, cosine, sine, direction):
    half_dim = values.shape[-1] // 2
    front_half = values[..., :half_dim]
    back_half = values[..., half_dim:]
    return jnp.concatenate([front_half * cosine - direction * back_half * sine, back_half * cosine + direction * front_half * sine], axis=-1)

def key_mask(query_ids, key_ids, length):
    cont_start = jnp.where(query_ids >= PROMPT, PROMPT + (query_ids - PROMPT) // CONT_LEN * CONT_LEN, SLAB)
    causal = key_ids[None, :] <= query_ids[:, None]
    return causal & ((key_ids[None, :] < length) | (key_ids[None, :] >= cont_start[:, None]))

def group_layer(input_rows, chosen, length, adapters, frozen):
    qkv_weight, out_weight, ffn_weight, down_weight, qk_gain, post_gain = frozen
    qkv_lower, qkv_raise, out_lower, out_raise, ffn_lower, ffn_raise, down_lower, down_raise = adapters
    q_lin = low_back(project(input_rows, qkv_weight[0], qkv_lower[0, chosen[0]], qkv_raise[0, chosen[0]]))
    k_lin = low_back(project(input_rows, qkv_weight[1], qkv_lower[1, chosen[1]], qkv_raise[1, chosen[1]]))
    v_lin = low_back(project(input_rows, qkv_weight[2], qkv_lower[2, chosen[2]], qkv_raise[2, chosen[2]]))
    cosine, sine = rotation(token_places(length), HEAD_DIM)
    q_low = low(rotate(rms_norm(q_lin, qk_gain[0]).reshape(SLAB, HEADS, HEAD_DIM), cosine, sine, 1.0))
    k_low = low(rotate(rms_norm(k_lin, qk_gain[1]).reshape(SLAB, HEADS, HEAD_DIM), cosine, sine, 1.0))
    v_low = low(v_lin).reshape(SLAB, HEADS, HEAD_DIM)
    slot_ids = jnp.arange(SLAB, dtype=jnp.int32)
    allowed = key_mask(slot_ids, slot_ids, length)
    score_scale = 1.0 / math.sqrt(HEAD_DIM)

    def one_head(pieces):
        q_head, k_head, v_head = pieces
        scores = low_back(matrix_product(q_head, k_head.T) * score_scale)
        scores = jnp.where(allowed, scores, very_low)
        row_top = lax.optimization_barrier(jnp.max(scores, axis=1, keepdims=True))
        shifted = jnp.exp(scores - row_top)
        attn_probs = shifted / lax.optimization_barrier(jnp.sum(shifted, axis=1, keepdims=True))
        return matrix_product(low(attn_probs), v_head)
    attended = lax.map(jax.checkpoint(one_head), (q_low.transpose(1, 0, 2), k_low.transpose(1, 0, 2), v_low.transpose(1, 0, 2)))
    attn_low = low(low_back(attended.transpose(1, 0, 2).reshape(SLAB, D)))
    attn_lin = low_back(project(attn_low, out_weight, out_lower[chosen[3]], out_raise[chosen[3]]))
    hidden = input_rows + rms_norm(attn_lin, post_gain[0])
    hidden_low = low(hidden)
    gate_lin = low_back(project(hidden_low, ffn_weight[0], ffn_lower[0, chosen[4]], ffn_raise[0, chosen[4]]))
    up_lin = low_back(project(hidden_low, ffn_weight[1], ffn_lower[1, chosen[5]], ffn_raise[1, chosen[5]]))
    act_low = low(gate_lin * jax.nn.sigmoid(gate_lin) * up_lin)
    mlp_lin = low_back(project(act_low, down_weight, down_lower[chosen[6]], down_raise[chosen[6]]))
    return hidden + rms_norm(mlp_lin, post_gain[1])

def reference(layer_in, cotangent, qkv_weight, out_weight, ffn_weight, down_weight, qk_gain, post_gain, qkv_lower, qkv_raise, out_lower, out_raise, ffn_lower, ffn_raise, down_lower, down_raise, adapter_ids, prompt_len):
    frozen = (qkv_weight.astype(jnp.float32), out_weight.astype(jnp.float32), ffn_weight.astype(jnp.float32), down_weight.astype(jnp.float32), qk_gain.astype(jnp.float32), post_gain.astype(jnp.float32))
    adapters = (qkv_lower.astype(jnp.float32), qkv_raise.astype(jnp.float32), out_lower.astype(jnp.float32), out_raise.astype(jnp.float32), ffn_lower.astype(jnp.float32), ffn_raise.astype(jnp.float32), down_lower.astype(jnp.float32), down_raise.astype(jnp.float32))
    input_rows = layer_in.astype(jnp.float32).reshape(GROUPS, SLAB, D)

    def forward(inputs_all, adapters_all):

        def one_group(pieces):
            return group_layer(pieces[0], pieces[1], pieces[2], adapters_all, frozen)
        return lax.map(jax.checkpoint(one_group), (inputs_all, adapter_ids, prompt_len))
    output, pullback = jax.vjp(forward, input_rows, adapters)
    grad_inputs, grad_adapters = pullback(cotangent.astype(jnp.float32).reshape(GROUPS, SLAB, D))
    return (output.reshape(TOKENS, D), grad_inputs.reshape(TOKENS, D), grad_adapters[0], grad_adapters[1], grad_adapters[2], grad_adapters[3], grad_adapters[4], grad_adapters[5], grad_adapters[6], grad_adapters[7])
```

```python
import math

import jax
import jax.numpy as jnp
from jax import lax
from jax.sharding import PartitionSpec as P

D = 2048
HEAD_DIM = 128
RANK = 16
ADAPTERS = 8
PROMPT = 1024
CONT_LEN = 128
SLAB = 1152

adapter_scale = 2.0
norm_eps = 1e-06
rope_base = 500000.0
very_low = -1e30
bf16 = jnp.bfloat16
f32 = jnp.float32


def dot(left, right):
    return jnp.dot(left, right, preferred_element_type=f32)


def dot_nt(left, right):
    return lax.dot_general(left, right, (((1,), (1,)), ((), ())), preferred_element_type=f32)


def dot_tn(left, right):
    return lax.dot_general(left, right, (((0,), (0,)), ((), ())), preferred_element_type=f32)


def gather_weight(local):
    half = local.shape[0] // lax.axis_size("tok")
    part = lax.dynamic_slice_in_dim(local, lax.axis_index("tok") * half, half, 0)
    return lax.all_gather(part, ("col", "tok"), axis=0, tiled=True)


def to_tokens(values):
    rows, cols = lax.axis_size("row"), lax.axis_size("col")
    width = values.shape[1]
    mixed = lax.all_to_all(values, "row", 0, 0, tiled=True)
    mixed = lax.all_to_all(mixed, "col", 0, 0, tiled=True)
    return mixed.reshape(cols, SLAB // rows, width).transpose(1, 0, 2).reshape(SLAB // rows, -1)


def from_tokens(values):
    rows, cols = lax.axis_size("row"), lax.axis_size("col")
    count = values.shape[0]
    mixed = values.reshape(count, cols, -1).transpose(1, 0, 2).reshape(cols * count, -1)
    mixed = lax.all_to_all(mixed, "col", 0, 0, tiled=True)
    return lax.all_to_all(mixed, "row", 0, 0, tiled=True)


def reorder(values, outer, inner):
    if outer == 1 or inner == 1:
        return values
    rest = values.shape[0] // (outer * inner)
    shape = (outer, inner, rest) + values.shape[1:]
    return values.reshape(shape).swapaxes(0, 1).reshape(values.shape)


def gather_tokens(values):
    rows, per_slab = lax.axis_size("row"), lax.axis_size("row") // lax.axis_size("col")
    return reorder(lax.all_gather(values, "row", axis=0, tiled=True), rows, per_slab)


def scatter_tokens(values):
    rows, per_slab = lax.axis_size("row"), lax.axis_size("row") // lax.axis_size("col")
    values = reorder(values.astype(bf16), per_slab, rows)
    return lax.psum_scatter(values, "row", scatter_dimension=0, tiled=True).astype(f32)


def token_places(length):
    slot_ids = jnp.arange(SLAB, dtype=jnp.int32)
    return jnp.where(slot_ids < PROMPT, slot_ids, length + (slot_ids - PROMPT) % CONT_LEN)


def rotation(places, head_size):
    half_dim = head_size // 2
    frequency = jnp.exp(
        -(2.0 * jnp.arange(half_dim, dtype=f32) / head_size) * math.log(rope_base)
    )
    angles = places.astype(f32)[:, None] * frequency[None, :]
    return (jnp.cos(angles)[:, None, :], jnp.sin(angles)[:, None, :])


def rotate(values, cosine, sine, direction):
    half_dim = values.shape[-1] // 2
    front_half = values[..., :half_dim]
    back_half = values[..., half_dim:]
    return jnp.concatenate(
        [
            front_half * cosine - direction * back_half * sine,
            back_half * cosine + direction * front_half * sine,
        ],
        axis=-1,
    )


def key_mask(query_ids, key_ids, length):
    cont_start = jnp.where(
        query_ids >= PROMPT, PROMPT + (query_ids - PROMPT) // CONT_LEN * CONT_LEN, SLAB
    )
    causal = key_ids[None, :] <= query_ids[:, None]
    return causal & ((key_ids[None, :] < length) | (key_ids[None, :] >= cont_start[:, None]))


def norm_forward(values, gain):
    inverse = lax.rsqrt(jnp.mean(values * values, axis=1, keepdims=True) + norm_eps)
    return (values * inverse * gain.astype(f32), inverse)


def norm_backward(values, inverse, gain, grad_out):
    weighted = grad_out * gain.astype(f32)
    inner = jnp.mean(values * weighted, axis=1, keepdims=True)
    return inverse * weighted - values * (inverse**3 * inner)


def attend_forward(queries, keys_low, values_low, length, block_len):
    slab_len = queries.shape[0]
    score_scale = 1.0 / math.sqrt(queries.shape[2])
    key_ids = jnp.arange(slab_len, dtype=jnp.int32)

    def one_block(block_start):
        q_block = lax.dynamic_slice_in_dim(queries, block_start, block_len, 0)
        query_ids = block_start + jnp.arange(block_len, dtype=jnp.int32)
        scores = (
            jnp.einsum("qhd,khd->hqk", q_block, keys_low, preferred_element_type=f32)
            * score_scale
        )
        scores = jnp.where(key_mask(query_ids, key_ids, length)[None], scores, very_low)
        row_top = jnp.max(scores, axis=2, keepdims=True)
        shifted = jnp.exp(scores - row_top)
        row_sum = jnp.sum(shifted, axis=2, keepdims=True)
        attn_probs = (shifted / row_sum).astype(bf16)
        attended = jnp.einsum("hqk,khd->qhd", attn_probs, values_low, preferred_element_type=f32)
        return (attended, (row_top + jnp.log(row_sum))[:, :, 0])

    block_starts = jnp.arange(slab_len // block_len, dtype=jnp.int32) * block_len
    attended, log_sums = lax.map(one_block, block_starts)
    return (attended.reshape(queries.shape), log_sums)


def attend_backward(queries, keys_low, values_low, grad_out, log_sums, length, block_len):
    slab_len = queries.shape[0]
    score_scale = 1.0 / math.sqrt(queries.shape[2])
    key_ids = jnp.arange(slab_len, dtype=jnp.int32)

    def one_block(carry, input_rows):
        grad_keys, grad_values = carry
        block_start, block_sums = input_rows
        q_block = lax.dynamic_slice_in_dim(queries, block_start, block_len, 0)
        g_block = lax.dynamic_slice_in_dim(grad_out, block_start, block_len, 0)
        query_ids = block_start + jnp.arange(block_len, dtype=jnp.int32)
        scores = (
            jnp.einsum("qhd,khd->hqk", q_block, keys_low, preferred_element_type=f32)
            * score_scale
        )
        scores = jnp.where(key_mask(query_ids, key_ids, length)[None], scores, very_low)
        attn_probs = jnp.exp(scores - block_sums[:, :, None])
        probs_low = attn_probs.astype(bf16)
        grad_values = grad_values + jnp.einsum(
            "hqk,qhd->khd", probs_low, g_block, preferred_element_type=f32
        )
        grad_probs = jnp.einsum("qhd,khd->hqk", g_block, values_low, preferred_element_type=f32)
        row_inner = jnp.sum(attn_probs * grad_probs, axis=2, keepdims=True)
        grad_scores = (attn_probs * (grad_probs - row_inner)).astype(bf16)
        grad_query = (
            jnp.einsum("hqk,khd->qhd", grad_scores, keys_low, preferred_element_type=f32)
            * score_scale
        )
        grad_keys = (
            grad_keys
            + jnp.einsum("hqk,qhd->khd", grad_scores, q_block, preferred_element_type=f32)
            * score_scale
        )
        return ((grad_keys, grad_values), grad_query)

    block_starts = jnp.arange(slab_len // block_len, dtype=jnp.int32) * block_len
    zeros_init = jnp.zeros(queries.shape, f32)
    (grad_keys, grad_values), grad_queries = lax.scan(
        one_block, (zeros_init, zeros_init), (block_starts, log_sums)
    )
    return (grad_queries.reshape(queries.shape), grad_keys, grad_values)


def pick(adapters, ids):
    onehot = (ids[:, None] == jnp.arange(adapters.shape[0], dtype=jnp.int32)).astype(adapters.dtype)
    return jnp.tensordot(onehot, adapters, axes=1)


def place(ids, gradients):
    onehot = (jnp.arange(ADAPTERS, dtype=jnp.int32)[:, None] == ids[None, :]).astype(f32)
    total = 0.0
    for index in range(gradients.shape[0]):
        weight = onehot[:, index].reshape((ADAPTERS,) + (1,) * (gradients.ndim - 1))
        total = total + weight * gradients[index][None].astype(f32)
    return total


def block_diagonal(factors):
    count = len(factors)
    lines = []
    for index, factor in enumerate(factors):
        blank = jnp.zeros_like(factor)
        lines.append(
            jnp.concatenate([factor if k == index else blank for k in range(count)], axis=1)
        )
    return jnp.concatenate(lines, axis=0)


def on_device(
    layer_in,
    cotangent,
    qkv_weight,
    out_weight,
    ffn_weight,
    down_weight,
    qk_gain,
    post_gain,
    qkv_lower,
    qkv_raise,
    out_lower,
    out_raise,
    ffn_lower,
    ffn_raise,
    down_lower,
    down_raise,
    adapter_ids,
    prompt_len,
):
    col_count = lax.axis_size("col")
    group_base = lax.axis_index("tok") * col_count
    group = group_base + lax.axis_index("col")
    slab_ids = lax.dynamic_slice_in_dim(adapter_ids, group_base, col_count, 0)
    own_ids = lax.dynamic_index_in_dim(adapter_ids, group, 0, keepdims=False)
    length = lax.dynamic_index_in_dim(prompt_len, group, 0, keepdims=False)
    block_len = math.gcd(SLAB, 512)
    width = layer_in.shape[1]
    head_width = qkv_weight.shape[2]
    ff_width = ffn_weight.shape[2]

    x_own = to_tokens(layer_in)
    qkv_full = gather_weight(qkv_weight.transpose(1, 0, 2).reshape(width, -1))
    out_full = gather_weight(out_weight.T)
    ffn_full = gather_weight(ffn_weight.transpose(1, 0, 2).reshape(width, -1))
    down_full = gather_weight(down_weight.T)

    pieces = jnp.stack(
        [pick(qkv_lower[p].swapaxes(1, 2), slab_ids[:, p]) for p in range(3)]
        + [pick(out_raise, slab_ids[:, 3])]
        + [pick(ffn_lower[p].swapaxes(1, 2), slab_ids[:, 4 + p]) for p in range(2)]
        + [pick(down_raise, slab_ids[:, 6])],
        axis=1,
    )
    factors = lax.all_to_all(pieces, "col", 0, 0, tiled=True)
    factors = factors.transpose(1, 2, 0, 3).reshape(7, RANK, D)
    qkv_a, out_b, ffn_a, down_b = (
        factors[0:3].reshape(3 * RANK, D),
        factors[3],
        factors[4:6].reshape(2 * RANK, D),
        factors[6],
    )
    qkv_b = block_diagonal([pick(qkv_raise[p], own_ids[p : p + 1])[0] for p in range(3)])
    out_a = pick(out_lower, own_ids[3:4])[0]
    ffn_b = block_diagonal([pick(ffn_raise[p], own_ids[4 + p : 5 + p])[0] for p in range(2)])
    down_a = pick(down_lower, own_ids[6:7])[0]

    gains = post_gain.astype(bf16)
    gains = lax.all_gather(gains, "col", axis=1, tiled=True)

    x_all = gather_tokens(x_own)
    qkv_low = (adapter_scale * dot_nt(x_all, qkv_a)).astype(bf16)
    qkv_lin = dot(x_all, qkv_full) + dot(qkv_low, qkv_b)
    q_lin = qkv_lin[:, :head_width]
    k_lin = qkv_lin[:, head_width : 2 * head_width]
    v_lin = qkv_lin[:, 2 * head_width :]
    sums = lax.psum(
        jnp.stack([jnp.sum(q_lin * q_lin, axis=1), jnp.sum(k_lin * k_lin, axis=1)]), "row"
    )
    inverses = lax.rsqrt(sums / D + norm_eps)
    q_inverse, k_inverse = inverses[0], inverses[1]
    head_gain = qk_gain.astype(f32)
    local_heads = head_width // HEAD_DIM
    cosine, sine = rotation(token_places(length), HEAD_DIM)
    heads = (SLAB, local_heads, HEAD_DIM)
    q_low = rotate(
        (q_lin * q_inverse[:, None] * head_gain[0]).reshape(heads), cosine, sine, 1.0
    ).astype(bf16)
    k_low = rotate(
        (k_lin * k_inverse[:, None] * head_gain[1]).reshape(heads), cosine, sine, 1.0
    ).astype(bf16)
    v_low = v_lin.reshape(heads).astype(bf16)
    attended, log_sums = attend_forward(q_low, k_low, v_low, length, block_len)
    attn_low = attended.reshape(SLAB, -1).astype(bf16)

    out_low = (adapter_scale * dot(attn_low, out_a)).astype(bf16)
    attn_lin = scatter_tokens(dot_nt(attn_low, out_full) + dot(out_low, out_b))
    attn_norm, attn_inverse = norm_forward(attn_lin, gains[0])
    hidden = x_own.astype(f32) + attn_norm
    h_all = gather_tokens(hidden.astype(bf16))

    ffn_low = (adapter_scale * dot_nt(h_all, ffn_a)).astype(bf16)
    ffn_lin = dot(h_all, ffn_full) + dot(ffn_low, ffn_b)
    gate_lin = ffn_lin[:, :ff_width]
    up_lin = ffn_lin[:, ff_width:]
    gate_sig = jax.nn.sigmoid(gate_lin)
    gate_act = gate_lin * gate_sig
    act_low = (gate_act * up_lin).astype(bf16)
    down_low = (adapter_scale * dot(act_low, down_a)).astype(bf16)
    mlp_lin = scatter_tokens(dot_nt(act_low, down_full) + dot(down_low, down_b))
    mlp_norm, mlp_inverse = norm_forward(mlp_lin, gains[1])
    layer_out = from_tokens((hidden + mlp_norm).astype(bf16)).astype(f32)

    grad_out = to_tokens(cotangent).astype(f32)
    dm_all = gather_tokens(norm_backward(mlp_lin, mlp_inverse, gains[1], grad_out).astype(bf16))
    down_raise_part = dot_tn(down_low, dm_all)
    down_dlow = (adapter_scale * dot_nt(dm_all, down_b)).astype(bf16)
    grad_act = dot(dm_all, down_full) + dot_nt(down_dlow, down_a)
    down_lower_part = dot_tn(act_low, down_dlow)
    grad_gate = (grad_act * up_lin * gate_sig * (1.0 + gate_lin * (1.0 - gate_sig))).astype(bf16)
    grad_up = (grad_act * gate_act).astype(bf16)
    grad_ffn = jnp.concatenate([grad_gate, grad_up], axis=1)
    ffn_dlow = (adapter_scale * dot_nt(grad_ffn, ffn_b)).astype(bf16)
    ffn_raise_part = dot_tn(ffn_low, grad_ffn)
    ffn_lower_part = dot_tn(ffn_dlow, h_all)
    grad_hidden = grad_out + scatter_tokens(dot_nt(grad_ffn, ffn_full) + dot(ffn_dlow, ffn_a))

    da_all = gather_tokens(
        norm_backward(attn_lin, attn_inverse, gains[0], grad_hidden).astype(bf16)
    )
    out_raise_part = dot_tn(out_low, da_all)
    out_dlow = (adapter_scale * dot_nt(da_all, out_b)).astype(bf16)
    grad_heads = (dot(da_all, out_full) + dot_nt(out_dlow, out_a)).astype(bf16)
    out_lower_part = dot_tn(attn_low, out_dlow)
    grad_q_rot, grad_k_rot, grad_v_all = attend_backward(
        q_low, k_low, v_low, grad_heads.reshape(heads), log_sums, length, block_len
    )
    weighted_q = rotate(grad_q_rot, cosine, sine, -1.0).reshape(SLAB, -1) * head_gain[0]
    weighted_k = rotate(grad_k_rot, cosine, sine, -1.0).reshape(SLAB, -1) * head_gain[1]
    inner = lax.psum(
        jnp.stack([jnp.sum(q_lin * weighted_q, axis=1), jnp.sum(k_lin * weighted_k, axis=1)]),
        "row",
    )
    factor = inverses**3 * inner / D
    grad_qkv = jnp.concatenate(
        [
            (q_inverse[:, None] * weighted_q - q_lin * factor[0][:, None]).astype(bf16),
            (k_inverse[:, None] * weighted_k - k_lin * factor[1][:, None]).astype(bf16),
            grad_v_all.reshape(SLAB, -1).astype(bf16),
        ],
        axis=1,
    )
    qkv_dlow = (adapter_scale * dot_nt(grad_qkv, qkv_b)).astype(bf16)
    qkv_raise_part = dot_tn(qkv_low, grad_qkv)
    qkv_lower_part = dot_tn(qkv_dlow, x_all)
    grad_x = grad_hidden + scatter_tokens(dot_nt(grad_qkv, qkv_full) + dot(qkv_dlow, qkv_a))
    grad_in = from_tokens(grad_x.astype(bf16)).astype(f32)

    parts = jnp.concatenate(
        [
            qkv_lower_part.reshape(3, RANK, D),
            out_raise_part[None],
            ffn_lower_part.reshape(2, RANK, D),
            down_raise_part[None],
        ]
    )
    parts = parts.astype(bf16).reshape(7, RANK, col_count, width).transpose(2, 0, 1, 3)
    parts = lax.all_to_all(parts, "col", 0, 0, tiled=True)
    placed = [place(slab_ids[:, p], parts[:, p]) for p in range(7)]
    col_split = lax.psum(jnp.stack(placed).astype(bf16), ("tok", "row")).astype(f32)
    own = jnp.concatenate(
        [
            qkv_raise_part[p * RANK : (p + 1) * RANK, p * head_width : (p + 1) * head_width]
            for p in range(3)
        ]
        + [out_lower_part.T]
        + [
            ffn_raise_part[p * RANK : (p + 1) * RANK, p * ff_width : (p + 1) * ff_width]
            for p in range(2)
        ]
        + [down_lower_part.T],
        axis=1,
    ).astype(bf16)
    every = lax.all_gather(own, ("tok", "col"), axis=0)
    starts = [0, 1, 2, 3, 4]
    starts = [s * head_width for s in starts] + [
        4 * head_width + (k + 1) * ff_width for k in range(3)
    ]
    row_split = [
        place(adapter_ids[:, p], every[:, :, starts[p] : starts[p + 1]]) for p in range(7)
    ]
    return (
        layer_out,
        grad_in,
        col_split[0:3].swapaxes(2, 3),
        jnp.stack(row_split[0:3]),
        row_split[3].swapaxes(1, 2),
        col_split[3],
        col_split[4:6].swapaxes(2, 3),
        jnp.stack(row_split[4:6]),
        row_split[6].swapaxes(1, 2),
        col_split[6],
    )


def solution(mesh):
    return jax.shard_map(
        on_device,
        mesh=mesh,
        in_specs=(
            P(("tok", "row"), "col"),
            P(("tok", "row"), "col"),
            P(None, "col", "row"),
            P("row", "col"),
            P(None, "col", "row"),
            P("row", "col"),
            P(None, "row"),
            P(None, "col"),
            P(None, None, "col", None),
            P(None, None, None, "row"),
            P(None, "row", None),
            P(None, None, "col"),
            P(None, None, "col", None),
            P(None, None, None, "row"),
            P(None, "row", None),
            P(None, None, "col"),
            P(),
            P(),
        ),
        out_specs=(
            P(("tok", "row"), "col"),
            P(("tok", "row"), "col"),
            P(None, None, "col", None),
            P(None, None, None, "row"),
            P(None, "row", None),
            P(None, None, "col"),
            P(None, None, "col", None),
            P(None, None, None, "row"),
            P(None, "row", None),
            P(None, None, "col"),
        ),
        check_vma=False,
    )
```

```python
import functools
import math

import jax
import jax.numpy as jnp
from jax import lax
from jax.experimental import pallas as pl
from jax.experimental.pallas import tpu as pltpu
from jax.sharding import PartitionSpec as P

D = 2048
HEAD_DIM = 128
RANK = 16
ADAPTERS = 8
PROMPT = 1024
CONT_LEN = 128
SLAB = 1152

adapter_scale = 2.0
norm_eps = 1e-06
rope_base = 500000.0
very_low = -1e30
bf16 = jnp.bfloat16
f32 = jnp.float32
log2_scale = math.log2(math.e) / math.sqrt(HEAD_DIM)
score_scale = 1.0 / math.sqrt(HEAD_DIM)
BLOCK = 384
TILE = 512
MESH = pl.DeviceIdType.MESH


def mm(left, right):
    return jnp.dot(left, right, preferred_element_type=f32)

def mm_nt(left, right):
    return lax.dot_general(left, right, (((1,), (1,)), ((), ())), preferred_element_type=f32)

def greet(near):
    barrier = pltpu.get_barrier_semaphore()
    for other in near:
        pl.semaphore_signal(barrier, inc=1, device_id={"row": other}, device_id_type=MESH)
    pl.semaphore_wait(barrier, len(near))

def send(source, target, sems, index, other):
    copy = pltpu.make_async_remote_copy(
        src_ref=source, dst_ref=target, send_sem=sems[0].at[index], recv_sem=sems[1].at[index],
        device_id={"row": other}, device_id_type=MESH)
    return copy

def gather_matmul_kernel(finish, start, x_ref, w_hbm, f1_ref, f2_ref, *refs, extra_in, extra_out):
    ins = refs[:extra_in]
    all_ref, low_ref = refs[extra_in], refs[extra_in + 1]
    outs = refs[extra_in + 2 : extra_in + 2 + extra_out]
    w_ref, w_sem, send_sem, recv_sem = refs[extra_in + 2 + extra_out :]
    me = lax.axis_index("row")
    xn, yn, dg = me ^ 1, me ^ 2, me ^ 3
    count = x_ref.shape[0]
    half = count // 2
    n = w_ref.shape[1]
    load = pltpu.make_async_copy(w_hbm.at[:, pl.ds(start, w_ref.shape[1])], w_ref, w_sem)
    load.start()
    greet((xn, yn))
    sems = (send_sem, recv_sem)
    top, low = pl.ds(0, half), pl.ds(half, half)
    sends = [
        send(x_ref.at[top], all_ref.at[me, top], sems, 0, xn),
        send(x_ref.at[low], all_ref.at[me, low], sems, 1, yn),
        send(x_ref.at[low], all_ref.at[me, low], sems, 2, xn),
        send(x_ref.at[top], all_ref.at[me, top], sems, 3, yn),
    ]
    for copy in sends:
        copy.start()
    def arrive(owner, part, index):
        send(all_ref.at[owner, part], all_ref.at[owner, part], sems, index, xn).wait_recv()
    all_ref[me] = x_ref[...]
    load.wait()

    def work(owner):
        rows = all_ref[owner]
        lowered = (adapter_scale * mm_nt(rows, f1_ref[...])).astype(bf16)
        low_ref[owner] = lowered
        finish(all_ref, lowered, w_ref, f2_ref, owner, ins, outs)
    arrive(xn, top, 0)
    pass_y = send(all_ref.at[xn, top], all_ref.at[xn, top], sems, 4, yn)
    pass_y.start()
    arrive(yn, low, 1)
    pass_x = send(all_ref.at[yn, low], all_ref.at[yn, low], sems, 5, xn)
    pass_x.start()
    work(me)
    arrive(xn, low, 2)
    work(xn)
    arrive(yn, top, 3)
    work(yn)
    arrive(dg, top, 4)
    arrive(dg, low, 5)
    work(dg)
    for copy in sends + [pass_y, pass_x]:
        copy.wait_send()

def each_tile(width, step, body):
    @pl.loop(0, width // step)
    def _(tile):
        body(pl.ds(pl.multiple_of(tile * step, step), step), tile)


def tile_product(all_ref, lowered, w_ref, f2_ref, owner, cols):
    return mm(all_ref[owner], w_ref[:, cols]) + mm(lowered, f2_ref[:, cols])


def finish_qkv(all_ref, lowered, w_ref, f2_ref, owner, ins, outs):
    width = w_ref.shape[1] // 3
    for index in range(3):
        cols = slice(index * width, (index + 1) * width)
        value = tile_product(all_ref, lowered, w_ref, f2_ref, owner, cols)
        outs[0][owner, :, cols] = value
        if index < 2:
            outs[1][owner, :, index : index + 1] = jnp.sum(value * value, axis=1, keepdims=True)


def finish_plain(all_ref, lowered, w_ref, f2_ref, owner, ins, outs):
    def body(cols, _):
        value = tile_product(all_ref, lowered, w_ref, f2_ref, owner, cols)
        outs[0][owner, :, cols] = value.astype(bf16)

    each_tile(w_ref.shape[1], TILE, body)


def gated(gate, up):
    return gate * jax.nn.sigmoid(gate) * up


def gated_back(grad, gate, up):
    sig = jax.nn.sigmoid(gate)
    act = gate * sig
    return (grad * up * (sig + act * (1.0 - sig)), grad * act)


def finish_ffn(all_ref, lowered, w_ref, f2_ref, owner, ins, outs):
    width = w_ref.shape[1] // 2

    def body(cols, tile):
        shifted = pl.ds(pl.multiple_of(width + tile * TILE, TILE), TILE)
        gate = tile_product(all_ref, lowered, w_ref, f2_ref, owner, cols)
        up = tile_product(all_ref, lowered, w_ref, f2_ref, owner, shifted)
        outs[0][owner, :, cols] = gate.astype(bf16)
        outs[1][owner, :, cols] = up.astype(bf16)
        outs[2][owner, :, cols] = gated(gate, up).astype(bf16)

    each_tile(width, TILE, body)


def finish_gated_back(all_ref, lowered, w_ref, f2_ref, owner, ins, outs):
    width = w_ref.shape[1]

    def body(cols, tile):
        shifted = pl.ds(pl.multiple_of(width + tile * TILE, TILE), TILE)
        grad = tile_product(all_ref, lowered, w_ref, f2_ref, owner, cols)
        gate, up = ins[0][owner, :, cols].astype(f32), ins[1][owner, :, cols].astype(f32)
        grad_gate, grad_up = gated_back(grad, gate, up)
        outs[0][owner, :, cols] = grad_gate.astype(bf16)
        outs[0][owner, :, shifted] = grad_up.astype(bf16)

    each_tile(width, TILE, body)


def gather_matmul(x, w, start, f1, f2, finish, extra, out_shapes, collective_id, name):
    count, depth = x.shape
    n = f2.shape[1]
    vmem = pl.BlockSpec(memory_space=pltpu.VMEM)
    outs = [jax.ShapeDtypeStruct((4, count, depth), bf16), jax.ShapeDtypeStruct((4, count, f1.shape[0]), bf16)] + out_shapes
    return pl.pallas_call(
        functools.partial(gather_matmul_kernel, finish, start, extra_in=len(extra), extra_out=len(out_shapes)),
        in_specs=[vmem, pl.BlockSpec(memory_space=pl.ANY)] + [vmem] * (2 + len(extra)),
        out_specs=[vmem] * len(outs), out_shape=outs,
        scratch_shapes=[pltpu.VMEM((depth, n), bf16), pltpu.SemaphoreType.DMA, pltpu.SemaphoreType.DMA((6,)), pltpu.SemaphoreType.DMA((6,))],
        compiler_params=pltpu.CompilerParams(collective_id=collective_id, has_side_effects=True, vmem_limit_bytes=60 << 20),
        cost_estimate=pl.CostEstimate(flops=8*count*depth*n, bytes_accessed=2*depth*n, transcendentals=0),
        name=name,
    )(x, w, f1, f2, *extra)

def matmul_scatter_kernel(start, y_ref, w_hbm, f1_ref, f2_ref, o_ref, low_ref, w_ref, out_buf, relay_buf, final_buf, w_sem, send_sem, recv_sem):
    me = lax.axis_index("row")
    xn, yn, dg = me ^ 1, me ^ 2, me ^ 3
    count = y_ref.shape[1]
    half = count // 2
    load = pltpu.make_async_copy(w_hbm.at[:, pl.ds(start, w_ref.shape[1])], w_ref, w_sem)
    load.start()
    greet((xn, yn))
    sems = (send_sem, recv_sem)
    top, low = slice(0, half), slice(half, count)
    tiles = w_ref.shape[0] // TILE
    load.wait()
    def partial(owner, store):
        lowered = (adapter_scale * mm_nt(y_ref[owner], f1_ref[...])).astype(bf16)
        low_ref[owner] = lowered
        @pl.loop(0, tiles)
        def _(tile):
            cols = pl.ds(pl.multiple_of(tile * TILE, TILE), TILE)
            store(cols, mm_nt(y_ref[owner], w_ref[cols, :]) + mm(lowered, f2_ref[:, cols]))
    def keep(slot):
        def store(cols, value):
            out_buf[slot, :, cols] = value.astype(bf16)
        return store
    partial(dg, keep(0))
    first = [
        send(out_buf.at[0, top], relay_buf.at[0], sems, 0, xn),
        send(out_buf.at[0, low], relay_buf.at[1], sems, 1, yn),
    ]
    for copy in first:
        copy.start()
    partial(xn, keep(1))
    x_top = send(out_buf.at[1, top], final_buf.at[0, top], sems, 2, xn)
    x_top.start()
    partial(yn, keep(2))
    y_low = send(out_buf.at[2, low], final_buf.at[1, low], sems, 3, yn)
    y_low.start()
    first[0].wait_recv()
    out_buf[2, top] = (out_buf[2, top].astype(f32) + relay_buf[0].astype(f32)).astype(bf16)
    y_top = send(out_buf.at[2, top], final_buf.at[1, top], sems, 4, yn)
    y_top.start()
    first[1].wait_recv()
    out_buf[1, low] = (out_buf[1, low].astype(f32) + relay_buf[1].astype(f32)).astype(bf16)
    x_low = send(out_buf.at[1, low], final_buf.at[0, low], sems, 5, xn)
    x_low.start()
    def own(cols, value):
        o_ref[:, cols] = value
    partial(me, own)
    for copy in (x_top, y_low, y_top, x_low):
        copy.wait_recv()
    o_ref[...] += final_buf[0].astype(f32) + final_buf[1].astype(f32)
    for copy in first + [x_top, y_low, y_top, x_low]:
        copy.wait_send()

def matmul_scatter(y, w, start, f1, f2, collective_id, name):
    _, count, depth = y.shape
    n = w.shape[0]
    vmem = pl.BlockSpec(memory_space=pltpu.VMEM)
    return pl.pallas_call(
        functools.partial(matmul_scatter_kernel, start),
        in_specs=[vmem, pl.BlockSpec(memory_space=pl.ANY), vmem, vmem],
        out_specs=[vmem, vmem],
        out_shape=[jax.ShapeDtypeStruct((count, n), f32), jax.ShapeDtypeStruct((4, count, f1.shape[0]), bf16)],
        scratch_shapes=[pltpu.VMEM((n, depth), bf16), pltpu.VMEM((3, count, n), bf16), pltpu.VMEM((2, count // 2, n), bf16), pltpu.VMEM((2, count, n), bf16),
                        pltpu.SemaphoreType.DMA, pltpu.SemaphoreType.DMA((6,)), pltpu.SemaphoreType.DMA((6,))],
        compiler_params=pltpu.CompilerParams(collective_id=collective_id, has_side_effects=True, vmem_limit_bytes=60 << 20),
        cost_estimate=pl.CostEstimate(flops=8*count*depth*n, bytes_accessed=2*depth*n, transcendentals=0),
        name=name,
    )(y, w, f1, f2)


def score_blocks(k_ref, q_block, bias_ref, start, stop):
    parts = []
    if start:
        parts.append(mm_nt(k_ref[0:start], q_block) + bias_ref[0:start])
    own = mm_nt(k_ref[start:stop], q_block) + bias_ref[start:stop]
    keys = lax.broadcasted_iota(jnp.int32, own.shape, 0)
    queries = lax.broadcasted_iota(jnp.int32, own.shape, 1)
    parts.append(jnp.where(keys <= queries, own, very_low))
    return parts

def attend_kernel(q_ref, k_ref, v_ref, inv_ref, gain_ref, cos_ref, sin_ref, bias_ref,
                  ql_ref, kl_ref, vl_ref, o_ref, lse_ref):
    for source, target, index in ((q_ref, ql_ref, 0), (k_ref, kl_ref, 1)):
        normed = source[...] * inv_ref[:, index:index+1] * gain_ref[index:index+1, :]
        target[...] = (normed * cos_ref[...] + pltpu.roll(normed, HEAD_DIM // 2, 1) * sin_ref[...]).astype(bf16)
    values = v_ref[...].astype(bf16)
    vl_ref[...] = values
    values_t = v_ref[...].T.astype(bf16)
    for start in range(0, SLAB, BLOCK):
        stop = start + BLOCK
        parts = score_blocks(kl_ref, ql_ref[start:stop], bias_ref, start, stop)
        top = functools.reduce(jnp.maximum, [jnp.max(p, axis=0, keepdims=True) for p in parts]) * log2_scale
        total, out, at = 0.0, 0.0, 0
        for part in parts:
            shifted = jnp.exp2(part * log2_scale - top)
            total = total + jnp.sum(shifted, axis=0, keepdims=True)
            out = out + mm(values_t[:, at:at+part.shape[0]], shifted.astype(bf16))
            at += part.shape[0]
        o_ref[start:stop] = (out / total).T.astype(bf16)
        lse_ref[0, :, start:stop] = top + jnp.log2(total)

def attend_back_kernel(ql_ref, kl_ref, vl_ref, o_ref, do_ref, lse_ref, q_ref, k_ref, gain_ref, cos_ref, sin_ref, bias_ref,
                       wq_ref, wk_ref, dv_ref, sum_ref, dk_sum, dv_sum):
    keys_t = kl_ref[...].astype(f32).T.astype(bf16)
    delta_all = jnp.sum((do_ref[...].astype(f32) * o_ref[...].astype(f32)).T, axis=0, keepdims=True)
    dk_sum[...] = jnp.zeros_like(dk_sum)
    dv_sum[...] = jnp.zeros_like(dv_sum)
    def unrotate(values):
        return values * cos_ref[...] - pltpu.roll(values, HEAD_DIM // 2, 1) * sin_ref[...]
    dq_parts = []
    for start in range(0, SLAB, BLOCK):
        stop = start + BLOCK
        queries, grads = ql_ref[start:stop], do_ref[start:stop]
        parts = score_blocks(kl_ref, queries, bias_ref, start, stop)
        lse, delta = lse_ref[0, :, start:stop], delta_all[:, start:stop]
        at, dq = 0, 0.0
        for part in parts:
            span = slice(at, at + part.shape[0])
            probs = jnp.exp2(part * log2_scale - lse)
            dv_sum[span] += mm(probs.astype(bf16), grads)
            dscore = (probs * (mm_nt(vl_ref[span], grads) - delta)).astype(bf16)
            dk_sum[span] += mm(dscore, queries)
            dq = dq + mm(keys_t[:, span], dscore)
            at += part.shape[0]
        dq_parts.append(dq.T)
    dq_all = jnp.concatenate(dq_parts, axis=0) * score_scale
    dv_ref[...] = dv_sum[...].astype(bf16)
    lanes = lax.broadcasted_iota(jnp.int32, (1, 2), 1)
    wq = unrotate(dq_all) * gain_ref[0:1, :]
    wk = unrotate(dk_sum[...] * score_scale) * gain_ref[1:2, :]
    wq_ref[...] = wq.astype(wq_ref.dtype)
    wk_ref[...] = wk.astype(wk_ref.dtype)
    sq = jnp.sum(wq * q_ref[...], axis=1, keepdims=True)
    sk = jnp.sum(wk * k_ref[...], axis=1, keepdims=True)
    both = jnp.where(lanes == 0, sq, sk)
    @pl.when(pl.program_id(0) == 0)
    def _():
        sum_ref[...] = both
    @pl.when(pl.program_id(0) != 0)
    def _():
        sum_ref[...] += both

def attend_specs(heads):
    col = lambda base: pl.BlockSpec((SLAB, HEAD_DIM), lambda h: (0, base * heads + h))
    whole = lambda shape: pl.BlockSpec(shape, lambda h: (0,) * len(shape))
    return col, whole

def attend(qkv_lin, inverses, gains, cosine, sine, bias):
    heads = qkv_lin.shape[1] // (3 * HEAD_DIM)
    col, whole = attend_specs(heads)
    low = jax.ShapeDtypeStruct((SLAB, heads * HEAD_DIM), bf16)
    return pl.pallas_call(
        attend_kernel, grid=(heads,),
        in_specs=[col(0), col(1), col(2), whole((SLAB, 2)), pl.BlockSpec((2, HEAD_DIM), lambda h: (0, h)),
                  whole((SLAB, HEAD_DIM)), whole((SLAB, HEAD_DIM)), whole((SLAB, 1))],
        out_specs=[col(0)] * 4 + [pl.BlockSpec((1, 1, SLAB), lambda h: (h, 0, 0))],
        out_shape=[low] * 4 + [jax.ShapeDtypeStruct((heads, 1, SLAB), f32)],
        compiler_params=pltpu.CompilerParams(vmem_limit_bytes=48 << 20),
        cost_estimate=pl.CostEstimate(flops=heads*4*SLAB*SLAB*HEAD_DIM, bytes_accessed=heads*SLAB*HEAD_DIM*20, transcendentals=heads*SLAB*SLAB),
        name="attend",
    )(qkv_lin, qkv_lin, qkv_lin, inverses, gains, cosine, sine, bias)

def attend_back(ql, kl, vl, o, do, lse, qkv_lin, gains, cosine, sine, bias):
    heads = ql.shape[1] // HEAD_DIM
    col, whole = attend_specs(heads)
    wide = jax.ShapeDtypeStruct(ql.shape, f32)
    return pl.pallas_call(
        attend_back_kernel, grid=(heads,),
        in_specs=[col(0)] * 5 + [pl.BlockSpec((1, 1, SLAB), lambda h: (h, 0, 0)), col(0), col(1), pl.BlockSpec((2, HEAD_DIM), lambda h: (0, h)),
                  whole((SLAB, HEAD_DIM)), whole((SLAB, HEAD_DIM)), whole((SLAB, 1))],
        out_specs=[col(0)] * 3 + [whole((SLAB, 2))],
        out_shape=[wide, wide, jax.ShapeDtypeStruct(ql.shape, bf16), jax.ShapeDtypeStruct((SLAB, 2), f32)],
        scratch_shapes=[pltpu.VMEM((SLAB, HEAD_DIM), f32)] * 2,
        compiler_params=pltpu.CompilerParams(vmem_limit_bytes=48 << 20),
        cost_estimate=pl.CostEstimate(flops=heads*10*SLAB*SLAB*HEAD_DIM, bytes_accessed=heads*SLAB*HEAD_DIM*30, transcendentals=heads*SLAB*SLAB),
        name="attend_back",
    )(ql, kl, vl, o, do, lse, qkv_lin, qkv_lin, gains, cosine, sine, bias)


def dot(left, right):
    return jnp.dot(left, right, preferred_element_type=f32)


def dot_nt(left, right):
    return lax.dot_general(left, right, (((1,), (1,)), ((), ())), preferred_element_type=f32)


def dot_tn(left, right):
    return lax.dot_general(left, right, (((0,), (0,)), ((), ())), preferred_element_type=f32)


def gather_weight(local):
    half = local.shape[0] // lax.axis_size("tok")
    part = lax.dynamic_slice_in_dim(local, lax.axis_index("tok") * half, half, 0)
    return lax.all_gather(part, ("col", "tok"), axis=0, tiled=True)


def to_tokens(values):
    rows, cols = lax.axis_size("row"), lax.axis_size("col")
    width = values.shape[1]
    mixed = lax.all_to_all(values, "row", 0, 0, tiled=True)
    mixed = lax.all_to_all(mixed, "col", 0, 0, tiled=True)
    return mixed.reshape(cols, SLAB // rows, width).transpose(1, 0, 2).reshape(SLAB // rows, -1)


def from_tokens(values):
    rows, cols = lax.axis_size("row"), lax.axis_size("col")
    count = values.shape[0]
    mixed = values.reshape(count, cols, -1).transpose(1, 0, 2).reshape(cols * count, -1)
    mixed = lax.all_to_all(mixed, "col", 0, 0, tiled=True)
    return lax.all_to_all(mixed, "row", 0, 0, tiled=True)


def reorder(values, outer, inner):
    if outer == 1 or inner == 1:
        return values
    rest = values.shape[0] // (outer * inner)
    shape = (outer, inner, rest) + values.shape[1:]
    return values.reshape(shape).swapaxes(0, 1).reshape(values.shape)


def gather_tokens(values):
    rows, per_slab = lax.axis_size("row"), lax.axis_size("row") // lax.axis_size("col")
    return reorder(lax.all_gather(values, "row", axis=0, tiled=True), rows, per_slab)


def scatter_tokens(values):
    rows, per_slab = lax.axis_size("row"), lax.axis_size("row") // lax.axis_size("col")
    values = reorder(values.astype(bf16), per_slab, rows)
    return lax.psum_scatter(values, "row", scatter_dimension=0, tiled=True).astype(f32)


def token_places(length):
    slot_ids = jnp.arange(SLAB, dtype=jnp.int32)
    return jnp.where(slot_ids < PROMPT, slot_ids, length + (slot_ids - PROMPT) % CONT_LEN)


def rotation(places, head_size):
    half_dim = head_size // 2
    frequency = jnp.exp(
        -(2.0 * jnp.arange(half_dim, dtype=f32) / head_size) * math.log(rope_base)
    )
    angles = places.astype(f32)[:, None] * frequency[None, :]
    return (jnp.cos(angles), jnp.sin(angles))


def norm_forward(values, gain):
    inverse = lax.rsqrt(jnp.mean(values * values, axis=1, keepdims=True) + norm_eps)
    return (values * inverse * gain.astype(f32), inverse)


def norm_backward(values, inverse, gain, grad_out):
    weighted = grad_out * gain.astype(f32)
    inner = jnp.mean(values * weighted, axis=1, keepdims=True)
    return inverse * weighted - values * (inverse**3 * inner)


def pick(adapters, ids):
    onehot = (ids[:, None] == jnp.arange(adapters.shape[0], dtype=jnp.int32)).astype(adapters.dtype)
    return jnp.tensordot(onehot, adapters, axes=1)


def place(ids, gradients):
    onehot = (jnp.arange(ADAPTERS, dtype=jnp.int32)[:, None] == ids[None, :]).astype(f32)
    total = 0.0
    for index in range(gradients.shape[0]):
        weight = onehot[:, index].reshape((ADAPTERS,) + (1,) * (gradients.ndim - 1))
        total = total + weight * gradients[index][None].astype(f32)
    return total


def block_diagonal(factors):
    count = len(factors)
    lines = []
    for index, factor in enumerate(factors):
        blank = jnp.zeros_like(factor)
        lines.append(
            jnp.concatenate([factor if k == index else blank for k in range(count)], axis=1)
        )
    return jnp.concatenate(lines, axis=0)


def fast():
    return lax.axis_size("row") == 4


def flat(values):
    return values.reshape((SLAB,) + values.shape[2:])


def enter(x, w, start, f1, f2, finish, extra, outs, collective_id, name):
    if fast():
        shapes = [jax.ShapeDtypeStruct((4, x.shape[0]) + shape, kind) for shape, kind in outs]
        extra = [value.reshape((4, -1) + value.shape[1:]) for value in extra]
        results = gather_matmul(
            x, w, start, f1, f2, finish, extra, shapes, collective_id, name
        )
        return [flat(value) for value in results]
    everything = gather_tokens(x)
    lowered = (adapter_scale * dot_nt(everything, f1)).astype(bf16)
    value = dot(everything, w[:, start : start + f2.shape[1]]) + dot(lowered, f2)
    width = outs[0][0][0]
    if finish is finish_qkv:
        width = width // 3
        parts = [value[:, k * width : (k + 1) * width] for k in range(2)]
        results = [value, jnp.stack([jnp.sum(part * part, axis=1) for part in parts], axis=1)]
    elif finish is finish_ffn:
        gate, up = value[:, :width], value[:, width:]
        results = [gate, up, gated(gate, up)]
    elif finish is finish_gated_back:
        gate, up = extra[0].astype(f32), extra[1].astype(f32)
        results = [jnp.concatenate(gated_back(value, gate, up), axis=1)]
    else:
        results = [value]
    return [everything, lowered] + [r.astype(kind) for r, (_, kind) in zip(results, outs)]


def leave(y, w, start, f1, f2, collective_id, name):
    if fast():
        total, lowered = matmul_scatter(
            y.reshape(4, -1, y.shape[1]), w, start, f1, f2, collective_id, name
        )
        return total, flat(lowered)
    lowered = (adapter_scale * dot_nt(y, f1)).astype(bf16)
    value = dot_nt(y, w[:, start : start + y.shape[1]]) + dot(lowered, f2)
    return scatter_tokens(value), lowered


def on_device(
    layer_in,
    cotangent,
    qkv_weight,
    out_weight,
    ffn_weight,
    down_weight,
    qk_gain,
    post_gain,
    qkv_lower,
    qkv_raise,
    out_lower,
    out_raise,
    ffn_lower,
    ffn_raise,
    down_lower,
    down_raise,
    adapter_ids,
    prompt_len,
):
    col_count = lax.axis_size("col")
    group_base = lax.axis_index("tok") * col_count
    group = group_base + lax.axis_index("col")
    slab_ids = lax.dynamic_slice_in_dim(adapter_ids, group_base, col_count, 0)
    own_ids = lax.dynamic_index_in_dim(adapter_ids, group, 0, keepdims=False)
    length = lax.dynamic_index_in_dim(prompt_len, group, 0, keepdims=False)
    width = layer_in.shape[1]
    head_width = qkv_weight.shape[2]
    ff_width = ffn_weight.shape[2]

    local = jnp.concatenate([qkv_weight.transpose(1, 0, 2).reshape(width, -1), out_weight.T], axis=1)
    attn_full = gather_weight(local)
    ffn_full = gather_weight(ffn_weight.transpose(1, 0, 2).reshape(width, -1))
    down_full = gather_weight(down_weight.T)
    x_own = to_tokens(layer_in)

    pieces = jnp.stack(
        [pick(qkv_lower[p].swapaxes(1, 2), slab_ids[:, p]) for p in range(3)]
        + [pick(out_raise, slab_ids[:, 3])]
        + [pick(ffn_lower[p].swapaxes(1, 2), slab_ids[:, 4 + p]) for p in range(2)]
        + [pick(down_raise, slab_ids[:, 6])],
        axis=1,
    )
    factors = lax.all_to_all(pieces, "col", 0, 0, tiled=True)
    factors = factors.transpose(1, 2, 0, 3).reshape(7, RANK, D)
    qkv_a, out_b, ffn_a, down_b = (
        factors[0:3].reshape(3 * RANK, D),
        factors[3],
        factors[4:6].reshape(2 * RANK, D),
        factors[6],
    )
    qkv_b = block_diagonal([pick(qkv_raise[p], own_ids[p : p + 1])[0] for p in range(3)])
    out_a = pick(out_lower, own_ids[3:4])[0].T
    ffn_b = block_diagonal([pick(ffn_raise[p], own_ids[4 + p : 5 + p])[0] for p in range(2)])
    down_a = pick(down_lower, own_ids[6:7])[0].T
    gains = lax.all_gather(post_gain, "col", axis=1, tiled=True)
    qkv_width = 3 * head_width

    cosine, sine = rotation(token_places(length), HEAD_DIM)
    cosine = jnp.concatenate([cosine, cosine], axis=1)
    sine = jnp.concatenate([-sine, sine], axis=1)
    slots = jnp.arange(SLAB, dtype=jnp.int32)
    bias = jnp.where((slots < length) | (slots >= PROMPT), 0.0, very_low)[:, None].astype(f32)
    head_gain = qk_gain.astype(f32)

    x_all, qkv_low, qkv_lin, squares = enter(
        x_own, attn_full, 0, qkv_a, qkv_b, finish_qkv, [],
        [((qkv_width,), f32), ((2,), f32)], 1, "enter_qkv",
    )
    inverses = lax.rsqrt(lax.psum(squares, "row") / D + norm_eps)
    q_low, k_low, v_low, attn_low, log_sums = attend(
        qkv_lin, inverses, head_gain, cosine, sine, bias
    )
    attn_lin, out_low = leave(attn_low, attn_full, qkv_width, out_a, out_b, 2, "leave_out")
    attn_norm, attn_inverse = norm_forward(attn_lin, gains[0])
    hidden = x_own.astype(f32) + attn_norm
    h_all, ffn_low, gate_lin, up_lin, act_low = enter(
        hidden.astype(bf16), ffn_full, 0, ffn_a, ffn_b, finish_ffn, [],
        [((ff_width,), bf16)] * 3, 3, "enter_ffn",
    )
    mlp_lin, down_low = leave(act_low, down_full, 0, down_a, down_b, 4, "leave_down")
    mlp_norm, mlp_inverse = norm_forward(mlp_lin, gains[1])
    layer_out = from_tokens((hidden + mlp_norm).astype(bf16)).astype(f32)

    grad_out = to_tokens(cotangent).astype(f32)
    grad_mlp = norm_backward(mlp_lin, mlp_inverse, gains[1], grad_out).astype(bf16)
    dm_all, down_dlow, grad_ffn = enter(
        grad_mlp, down_full, 0, down_b, down_a, finish_gated_back, [gate_lin, up_lin],
        [((2 * ff_width,), bf16)], 5, "back_down",
    )
    grad_ffn_in, ffn_dlow = leave(grad_ffn, ffn_full, 0, ffn_b, ffn_a, 6, "back_ffn")
    grad_hidden = grad_out + grad_ffn_in
    grad_attn = norm_backward(attn_lin, attn_inverse, gains[0], grad_hidden).astype(bf16)
    da_all, out_dlow, grad_heads = enter(
        grad_attn, attn_full, qkv_width, out_b, out_a, finish_plain, [],
        [((head_width,), bf16)], 7, "back_out",
    )
    weighted_q, weighted_k, grad_v, inner = attend_back(
        q_low, k_low, v_low, attn_low, grad_heads, log_sums, qkv_lin, head_gain, cosine, sine, bias
    )
    factor = inverses**3 * lax.psum(inner, "row") / D
    q_lin, k_lin = qkv_lin[:, :head_width], qkv_lin[:, head_width : 2 * head_width]
    grad_qkv = jnp.concatenate(
        [
            (inverses[:, 0:1] * weighted_q - q_lin * factor[:, 0:1]).astype(bf16),
            (inverses[:, 1:2] * weighted_k - k_lin * factor[:, 1:2]).astype(bf16),
            grad_v,
        ],
        axis=1,
    )
    grad_qkv_in, qkv_dlow = leave(grad_qkv, attn_full, 0, qkv_b, qkv_a, 8, "back_qkv")
    grad_in = from_tokens((grad_hidden + grad_qkv_in).astype(bf16)).astype(f32)

    down_raise_part = dot_tn(down_low, dm_all)
    down_lower_part = dot_tn(act_low, down_dlow)
    ffn_raise_part = dot_tn(ffn_low, grad_ffn)
    ffn_lower_part = dot_tn(ffn_dlow, h_all)
    out_raise_part = dot_tn(out_low, da_all)
    out_lower_part = dot_tn(attn_low, out_dlow)
    qkv_raise_part = dot_tn(qkv_low, grad_qkv)
    qkv_lower_part = dot_tn(qkv_dlow, x_all)

    parts = jnp.concatenate(
        [
            qkv_lower_part.reshape(3, RANK, D),
            out_raise_part[None],
            ffn_lower_part.reshape(2, RANK, D),
            down_raise_part[None],
        ]
    )
    parts = parts.astype(bf16).reshape(7, RANK, col_count, width).transpose(2, 0, 1, 3)
    parts = lax.all_to_all(parts, "col", 0, 0, tiled=True)
    placed = [place(slab_ids[:, p], parts[:, p]) for p in range(7)]
    col_split = lax.psum(jnp.stack(placed).astype(bf16), ("tok", "row")).astype(f32)
    own = jnp.concatenate(
        [
            qkv_raise_part[p * RANK : (p + 1) * RANK, p * head_width : (p + 1) * head_width]
            for p in range(3)
        ]
        + [out_lower_part.T]
        + [
            ffn_raise_part[p * RANK : (p + 1) * RANK, p * ff_width : (p + 1) * ff_width]
            for p in range(2)
        ]
        + [down_lower_part.T],
        axis=1,
    ).astype(bf16)
    every = lax.all_gather(own, ("tok", "col"), axis=0)
    starts = [0, 1, 2, 3, 4]
    starts = [s * head_width for s in starts] + [
        4 * head_width + (k + 1) * ff_width for k in range(3)
    ]
    row_split = [
        place(adapter_ids[:, p], every[:, :, starts[p] : starts[p + 1]]) for p in range(7)
    ]
    return (
        layer_out,
        grad_in,
        col_split[0:3].swapaxes(2, 3),
        jnp.stack(row_split[0:3]),
        row_split[3].swapaxes(1, 2),
        col_split[3],
        col_split[4:6].swapaxes(2, 3),
        jnp.stack(row_split[4:6]),
        row_split[6].swapaxes(1, 2),
        col_split[6],
    )


def solution(mesh):
    return jax.shard_map(
        on_device,
        mesh=mesh,
        in_specs=(
            P(("tok", "row"), "col"),
            P(("tok", "row"), "col"),
            P(None, "col", "row"),
            P("row", "col"),
            P(None, "col", "row"),
            P("row", "col"),
            P(None, "row"),
            P(None, "col"),
            P(None, None, "col", None),
            P(None, None, None, "row"),
            P(None, "row", None),
            P(None, None, "col"),
            P(None, None, "col", None),
            P(None, None, None, "row"),
            P(None, "row", None),
            P(None, None, "col"),
            P(),
            P(),
        ),
        out_specs=(
            P(("tok", "row"), "col"),
            P(("tok", "row"), "col"),
            P(None, None, "col", None),
            P(None, None, None, "row"),
            P(None, "row", None),
            P(None, None, "col"),
            P(None, None, "col", None),
            P(None, None, None, "row"),
            P(None, "row", None),
            P(None, None, "col"),
        ),
        check_vma=False,
    )
```

```python
import functools
import math

import jax
import jax.numpy as jnp
from jax import lax
from jax.experimental import pallas as pl
from jax.experimental.pallas import tpu as pltpu
from jax.sharding import PartitionSpec as P

D = 2048
HEAD_DIM = 128
RANK = 16
ADAPTERS = 8
PROMPT = 1024
CONT_LEN = 128
SLAB = 1152

adapter_scale = 2.0
norm_eps = 1e-06
rope_base = 500000.0
very_low = -1e30
bf16 = jnp.bfloat16
f32 = jnp.float32
log2_scale = math.log2(math.e) / math.sqrt(HEAD_DIM)
score_scale = 1.0 / math.sqrt(HEAD_DIM)
BLOCK = 384
TILE = 512
MESH = pl.DeviceIdType.MESH


def mm(left, right):
    return jnp.dot(left, right, preferred_element_type=f32)


def mm_nt(left, right):
    return lax.dot_general(left, right, (((1,), (1,)), ((), ())), preferred_element_type=f32)


class Links:
    def __init__(self, send_sem, recv_sem, local_sem):
        self.row, self.col = lax.axis_index("row"), lax.axis_index("col")
        self.xn, self.yn, self.dg = self.row ^ 1, self.row ^ 2, self.row ^ 3
        self.send_sem, self.recv_sem, self.local_sem = send_sem, recv_sem, local_sem
        self.used, self.local_used = 0, 0

    def take(self, count):
        self.used += count
        return self.used - count

    def copy(self, source, target, index, recv_index, row, col=None):
        return pltpu.make_async_remote_copy(
            src_ref=source,
            dst_ref=target,
            send_sem=self.send_sem.at[index],
            recv_sem=self.recv_sem.at[recv_index],
            device_id={"row": row, "col": self.col if col is None else col},
            device_id_type=MESH,
        )

    def local(self, source, target):
        self.local_used += 1
        return pltpu.make_async_copy(source, target, self.local_sem.at[self.local_used - 1])

    def greet(self, rows=2, columns=False):
        barrier = pltpu.get_barrier_semaphore()
        places = [(self.row ^ step, self.col) for step in range(1, rows + 1)]
        if columns:
            places += [(self.row, self.col ^ step) for step in range(1, 4)]
        for row, col in places:
            pl.semaphore_signal(
                barrier, inc=1, device_id={"row": row, "col": col}, device_id_type=MESH
            )
        pl.semaphore_wait(barrier, len(places))


class Exchange:
    def __init__(self, links, axis, piece_at, slot_at):
        self.links, self.axis = links, axis
        self.me = links.row if axis == "row" else links.col
        self.piece_at, self.slot_at = piece_at, slot_at
        self.base = links.take(3)
        self.own = links.local(piece_at(self.me), slot_at(self.me))

    def copy(self, source, target, step):
        links, other, index = self.links, self.me ^ step, self.base + step - 1
        row, col = (other, links.col) if self.axis == "row" else (links.row, other)
        return links.copy(source, target, index, index, row, col)

    def start(self):
        for step in range(1, 4):
            self.copy(self.piece_at(self.me ^ step), self.slot_at(self.me), step).start()
        self.own.start()

    def arrived(self):
        for step in range(1, 4):
            landed = self.slot_at(self.me ^ step)
            self.copy(landed, landed, step).wait_recv()
        self.own.wait()

    def sent(self):
        for step in range(1, 4):
            self.copy(self.piece_at(self.me ^ step), self.slot_at(self.me), step).wait_send()


class Turn:
    def __init__(self, links, inward, source_ref, middle_ref, target_ref, parts=1):
        size, width = middle_ref.shape[1], middle_ref.shape[2]
        self.hops = []
        for part in range(parts):
            start, count = part * (size // parts), size // parts
            rows = pl.ds(start, count)

            def features(ref, col, rows=rows):
                return ref.at[rows, pl.ds(pl.multiple_of(col * width, width), width)]

            def middle(key, rows=rows):
                return middle_ref.at[key, rows]

            if inward:
                first = Exchange(
                    links, "row", lambda key, rows=rows: source_ref.at[key, rows], middle
                )
                second = Exchange(
                    links, "col", middle, lambda key, features=features: features(target_ref, key)
                )
            else:
                first = Exchange(
                    links, "col", lambda key, features=features: features(source_ref, key), middle
                )
                second = Exchange(
                    links,
                    "row",
                    middle,
                    lambda key, start=start, count=count: target_ref.at[
                        pl.ds(pl.multiple_of(key * size + start, 16), count)
                    ],
                )
            self.hops.append((first, second))

    def start(self):
        for first, _ in self.hops:
            first.start()

    def relay(self):
        for first, second in self.hops:
            first.arrived()
            second.start()

    def finish(self):
        for _, second in self.hops:
            second.arrived()
        for first, second in self.hops:
            first.sent()
            second.sent()


def gather(links, all_ref, work, before=None, after=None):
    me, xn, yn, dg = links.row, links.xn, links.yn, links.dg
    half = all_ref.shape[1] // 2
    top, low = pl.ds(0, half), pl.ds(half, half)
    base = links.take(6)

    def move(owner, part, index, other):
        place = all_ref.at[owner, part]
        return links.copy(place, place, base + index, base + index, other)

    sends = [move(me, top, 0, xn), move(me, low, 1, yn), move(me, low, 2, xn), move(me, top, 3, yn)]
    for copy in sends:
        copy.start()
    if before:
        before()
    if work:
        work(me)
    move(xn, top, 0, xn).wait_recv()
    sends.append(move(xn, top, 4, yn))
    sends[-1].start()
    move(yn, low, 1, yn).wait_recv()
    sends.append(move(yn, low, 5, xn))
    sends[-1].start()
    if after:
        after()
    move(xn, low, 2, xn).wait_recv()
    if work:
        work(xn)
    move(yn, top, 3, yn).wait_recv()
    if work:
        work(yn)
    move(dg, top, 4, yn).wait_recv()
    move(dg, low, 5, xn).wait_recv()
    if work:
        work(dg)
    for copy in sends:
        copy.wait_send()


def scatter(links, product, o_ref, out_buf, relay_buf, final_buf, after=None):
    me, xn, yn, dg = links.row, links.xn, links.yn, links.dg
    count = o_ref.shape[0]
    half = count // 2
    top, low = slice(0, half), slice(half, count)
    base = links.take(6)

    def move(source, target, index, other):
        return links.copy(source, target, base + index, base + index, other)

    def keep(slot):
        def store(cols, value):
            out_buf[slot, :, cols] = value.astype(bf16)

        return store

    def own(cols, value):
        o_ref[:, cols] = value

    def add(slot, rows, relay):
        out_buf[slot, rows] = (
            out_buf[slot, rows].astype(f32) + relay_buf[relay].astype(f32)
        ).astype(bf16)

    product(dg, keep(0))
    copies = [
        move(out_buf.at[0, top], relay_buf.at[0], 0, xn),
        move(out_buf.at[0, low], relay_buf.at[1], 1, yn),
        move(out_buf.at[1, top], final_buf.at[0, top], 2, xn),
        move(out_buf.at[2, low], final_buf.at[1, low], 3, yn),
        move(out_buf.at[2, top], final_buf.at[1, top], 4, yn),
        move(out_buf.at[1, low], final_buf.at[0, low], 5, xn),
    ]
    copies[0].start()
    copies[1].start()
    product(xn, keep(1))
    copies[2].start()
    if after:
        after()
    product(yn, keep(2))
    copies[3].start()
    copies[0].wait_recv()
    add(2, top, 0)
    copies[4].start()
    copies[1].wait_recv()
    add(1, low, 1)
    copies[5].start()
    product(me, own)
    for copy in copies[2:]:
        copy.wait_recv()
    for copy in copies:
        copy.wait_send()


def each_tile(width, step, body):
    @pl.loop(0, width // step)
    def _(tile):
        body(pl.multiple_of(tile * step, step))


def lower(rows, factor):
    return (adapter_scale * mm_nt(rows, factor)).astype(bf16)


def leave_product(y_ref, w_ref, f1, f2_ref, f2_rows, low_ref):
    def product(owner, store):
        lowered = lower(y_ref[owner], f1)
        low_ref[owner] = lowered

        def body(at):
            cols = pl.ds(at, TILE)
            store(cols, mm_nt(y_ref[owner], w_ref[cols, :]) + mm(lowered, f2_ref[f2_rows, cols]))

        each_tile(w_ref.shape[0], TILE, body)

    return product


def inverse_of(values):
    return lax.rsqrt(jnp.mean(values * values, axis=1, keepdims=True) + norm_eps)


def norm_back(values, weighted):
    inverse = inverse_of(values)
    inner = jnp.mean(values * weighted, axis=1, keepdims=True)
    return inverse * weighted - values * (inverse**3 * inner)


def gated(gate, up):
    return gate * jax.nn.sigmoid(gate) * up


def gated_back(grad, gate, up):
    sig = jax.nn.sigmoid(gate)
    act = gate * sig
    return (grad * up * (sig + act * (1.0 - sig)), grad * act)


QKV_A, OUT_B, FFN_A, DOWN_B = slice(0, 48), slice(48, 64), slice(64, 96), slice(96, 112)
GAIN0, GAIN1 = slice(112, 113), slice(113, 114)


def share_stats(links, stat_ref, first, second):
    blank = jnp.zeros((6, first.shape[0]), f32)
    sums = [jnp.sum(value.T, axis=0, keepdims=True) for value in (first, second)]
    stat_ref[links.row] = jnp.concatenate(sums + [blank], axis=0)
    base = links.take(3)
    mine = stat_ref.at[links.row]
    copies = []
    for index, other in enumerate((links.xn, links.yn, links.dg)):
        copies.append(links.copy(mine, mine, base + index, base + index, other))
        copies[-1].start()
    for index, other in enumerate((links.xn, links.yn, links.dg)):
        theirs = stat_ref.at[other]
        links.copy(theirs, theirs, base + index, base + index, other).wait_recv()
    for copy in copies:
        copy.wait_send()
    return stat_ref[0] + stat_ref[1] + stat_ref[2] + stat_ref[3]


def lane_sums(values):
    return functools.reduce(
        jnp.add, [values[:, at : at + 128] for at in range(0, values.shape[1], 128)]
    )


def intake_kernel(
    x_ref, pieces_ref,
    own_ref, factors_ref,
    middle_ref, send_sem, recv_sem, local_sem,
):
    links = Links(send_sem, recv_sem, local_sem)
    links.greet(rows=3, columns=True)
    width = pieces_ref.shape[2]
    turn = Turn(links, True, x_ref, middle_ref, own_ref, 2)
    spread = Exchange(
        links,
        "col",
        lambda key: pieces_ref.at[key],
        lambda key: factors_ref.at[:, pl.ds(pl.multiple_of(key * width, width), width)],
    )
    turn.start()
    spread.start()
    turn.relay()
    spread.arrived()
    turn.finish()
    spread.sent()


def enter_qkv_kernel(
    x_ref, w_hbm, factors_ref, f2_ref,
    all_ref, low_ref, lin_ref, inv_ref,
    w_ref, sq_ref, stat_ref, send_sem, recv_sem, local_sem,
):
    links = Links(send_sem, recv_sem, local_sem)
    width = w_ref.shape[1]
    load = links.local(w_hbm.at[:, pl.ds(0, width)], w_ref)
    load.start()
    links.greet(rows=3)
    count = x_ref.shape[0]
    all_ref[links.row] = x_ref[...]

    def work(owner):
        lowered = lower(all_ref[owner], factors_ref[QKV_A])
        low_ref[owner] = lowered
        rows = all_ref[owner]
        third = width // 3
        for index in range(3):
            cols = slice(index * third, (index + 1) * third)
            value = mm(rows, w_ref[:, cols]) + mm(lowered, f2_ref[:, cols])
            lin_ref[owner, :, cols] = value
            if index < 2:
                place = pl.ds(pl.multiple_of(owner * count, 8), count)
                sq_ref[index, place] = lane_sums(value * value)

    gather(links, all_ref, work, load.wait)
    total = share_stats(links, stat_ref, sq_ref[0], sq_ref[1])
    inv_ref[...] = lax.rsqrt(total / D + norm_eps).T


def leave_out_kernel(
    y_ref, w_hbm, f1_ref, factors_ref, x_ref,
    lin_ref, low_ref, hidden_ref, all_ref,
    w_ref, out_buf, relay_buf, final_buf, send_sem, recv_sem, local_sem,
):
    links = Links(send_sem, recv_sem, local_sem)
    width = w_ref.shape[1]
    load = links.local(w_hbm.at[:, pl.ds(w_hbm.shape[1] - width, width)], w_ref)
    load.start()
    links.greet()
    load.wait()
    product = leave_product(y_ref, w_ref, f1_ref[...], factors_ref, OUT_B, low_ref)
    scatter(links, product, lin_ref, out_buf, relay_buf, final_buf)
    gain = factors_ref[GAIN0].astype(f32)

    @pl.loop(0, lin_ref.shape[0] // 16)
    def _(tile):
        rows = pl.ds(pl.multiple_of(tile * 16, 16), 16)
        value = lin_ref[rows] + final_buf[0, rows].astype(f32) + final_buf[1, rows].astype(f32)
        lin_ref[rows] = value
        hidden = x_ref[rows].astype(f32) + value * inverse_of(value) * gain
        hidden_ref[rows] = hidden
        all_ref[links.row, rows] = hidden.astype(bf16)

    gather(links, all_ref, None)


def ffn_kernel(h_ref, wg_ref, wu_ref, factors_ref, fg_ref, fu_ref, low_ref, gate_ref, up_ref, act_ref):
    @pl.when(pl.program_id(0) == 0)
    def _():
        low_ref[...] = lower(h_ref[...], factors_ref[FFN_A])

    lowered = low_ref[...]
    rank = lowered.shape[1] // 2
    for at in range(0, SLAB, BLOCK):
        rows = slice(at, at + BLOCK)
        gate = mm(h_ref[rows], wg_ref[...]) + mm(lowered[rows], fg_ref[...])
        up = mm(h_ref[rows], wu_ref[...]) + mm(lowered[rows], fu_ref[...])
        gate_ref[rows] = gate.astype(bf16)
        up_ref[rows] = up.astype(bf16)
        act_ref[rows] = gated(gate, up).astype(bf16)


def ffn(h_all, w, factors, f2):
    width = f2.shape[1] // 2
    step = 256
    tiles = width // step
    low = jax.ShapeDtypeStruct((SLAB, f2.shape[0]), bf16)
    wide = jax.ShapeDtypeStruct((SLAB, width), bf16)
    whole = lambda value: pl.BlockSpec(value.shape, lambda t: (0, 0))
    cols = lambda rows, base: pl.BlockSpec((rows, step), lambda t: (0, base * tiles + t))
    return pl.pallas_call(
        ffn_kernel,
        grid=(tiles,),
        in_specs=[whole(h_all), cols(D, 0), cols(D, 1), whole(factors)]
        + [cols(f2.shape[0], 0), cols(f2.shape[0], 1)],
        out_specs=[whole(low)] + [cols(SLAB, 0)] * 3,
        out_shape=[low, wide, wide, wide],
        compiler_params=pltpu.CompilerParams(vmem_limit_bytes=48 << 20),
        cost_estimate=pl.CostEstimate(
            flops=4 * SLAB * D * width, bytes_accessed=4 * D * width + 10 * SLAB * width,
            transcendentals=SLAB * width,
        ),
        name="ffn",
    )(h_all, w, w, factors, f2, f2)


def leave_down_kernel(
    y_ref, w_hbm, f1_ref, factors_ref, hidden_ref, cot_ref,
    low_ref, out_ref, dm_ref, own_cot_ref,
    w_ref, lin_ref, middle_ref, out_buf, relay_buf, final_buf, send_sem, recv_sem, local_sem,
):
    links = Links(send_sem, recv_sem, local_sem)
    load = links.local(w_hbm, w_ref)
    load.start()
    links.greet(rows=3, columns=True)
    turn = Turn(links, True, cot_ref, middle_ref, own_cot_ref)
    turn.start()
    load.wait()
    product = leave_product(y_ref, w_ref, f1_ref[...], factors_ref, DOWN_B, low_ref)
    scatter(links, product, lin_ref, out_buf, relay_buf, final_buf, turn.relay)
    turn.finish()
    gain = factors_ref[GAIN1].astype(f32)

    @pl.loop(0, lin_ref.shape[0] // 16)
    def _(tile):
        rows = pl.ds(pl.multiple_of(tile * 16, 16), 16)
        value = lin_ref[rows] + final_buf[0, rows].astype(f32) + final_buf[1, rows].astype(f32)
        out_ref[rows] = (hidden_ref[rows] + value * inverse_of(value) * gain).astype(bf16)
        dm_ref[rows] = norm_back(value, own_cot_ref[rows].astype(f32) * gain).astype(bf16)


def widen(source_ref, target_ref):
    @pl.loop(0, source_ref.shape[0] // 64)
    def _(tile):
        rows = pl.ds(pl.multiple_of(tile * 64, 64), 64)
        target_ref[rows] = source_ref[rows].astype(f32)


def back_down_kernel(
    dm_ref, w_hbm, factors_ref, f2_ref, gate_ref, up_ref, out_ref,
    all_ref, low_ref, grad_ref, final_ref,
    w_ref, middle_ref, out_buf, send_sem, recv_sem, local_sem,
):
    links = Links(send_sem, recv_sem, local_sem)
    load = links.local(w_hbm, w_ref)
    load.start()
    links.greet(rows=3, columns=True)
    width = w_ref.shape[1]
    all_ref[links.row] = dm_ref[...]
    turn = Turn(links, False, out_ref, middle_ref, out_buf)

    def before():
        turn.start()
        load.wait()

    def work(owner):
        lowered = lower(all_ref[owner], factors_ref[DOWN_B])
        low_ref[owner] = lowered

        def body(at):
            cols, far = pl.ds(at, TILE), pl.ds(pl.multiple_of(width + at, TILE), TILE)
            grad = mm(all_ref[owner], w_ref[:, cols]) + mm(lowered, f2_ref[:, cols])
            gate, up = gate_ref[owner, :, cols].astype(f32), up_ref[owner, :, cols].astype(f32)
            grad_gate, grad_up = gated_back(grad, gate, up)
            grad_ref[owner, :, cols] = grad_gate.astype(bf16)
            grad_ref[owner, :, far] = grad_up.astype(bf16)

        each_tile(width, TILE, body)

    waited = []

    def work_and_relay(owner):
        work(owner)
        waited.append(True)
        if len(waited) == 3:
            turn.relay()

    gather(links, all_ref, work_and_relay, before)
    turn.finish()
    widen(out_buf, final_ref)


def back_ffn_kernel(
    y_ref, w_hbm, f1_ref, factors_ref, cot_ref, attn_ref,
    low_ref, hidden_ref, da_ref,
    w_ref, lin_ref, out_buf, relay_buf, final_buf, send_sem, recv_sem, local_sem,
):
    links = Links(send_sem, recv_sem, local_sem)
    load = links.local(w_hbm, w_ref)
    load.start()
    links.greet()
    load.wait()
    product = leave_product(y_ref, w_ref, f1_ref[...], factors_ref, FFN_A, low_ref)
    scatter(links, product, lin_ref, out_buf, relay_buf, final_buf)
    gain = factors_ref[GAIN0].astype(f32)

    @pl.loop(0, lin_ref.shape[0] // 16)
    def _(tile):
        rows = pl.ds(pl.multiple_of(tile * 16, 16), 16)
        value = lin_ref[rows] + final_buf[0, rows].astype(f32) + final_buf[1, rows].astype(f32)
        value = value + cot_ref[rows].astype(f32)
        hidden_ref[rows] = value
        da_ref[rows] = norm_back(attn_ref[rows], value * gain).astype(bf16)


def mm_tn(left, right):
    return lax.dot_general(left, right, (((0,), (0,)), ((), ())), preferred_element_type=f32)


def back_out_kernel(
    da_ref, w_hbm, factors_ref, f2_ref, out_low_ref, attn_ref, down_low_ref, down_dlow_ref,
    ffn_low_ref, ffn_dlow_ref, dm_hbm, act_hbm, grad_hbm, h_hbm,
    all_ref, low_ref, heads_ref, down_raise_ref, down_lower_ref, ffn_raise_ref, ffn_lower_ref,
    out_raise_ref, out_lower_ref,
    w_ref, dm_ref, act_ref, grad_ref, h_ref, send_sem, recv_sem, local_sem,
):
    links = Links(send_sem, recv_sem, local_sem)
    width = w_ref.shape[1]
    load = links.local(w_hbm.at[:, pl.ds(w_hbm.shape[1] - width, width)], w_ref)
    loads = [
        links.local(source, target)
        for source, target in (
            (dm_hbm, dm_ref), (act_hbm, act_ref), (grad_hbm, grad_ref), (h_hbm, h_ref)
        )
    ]
    load.start()
    all_ref[links.row] = da_ref[...]
    links.greet()

    def before():
        for copy in loads:
            copy.start()
        load.wait()

    def after():
        for copy in loads:
            copy.wait()
        rank, half = down_low_ref.shape[1], grad_ref.shape[1] // 2
        down_raise_ref[...] = mm_tn(down_low_ref[...], dm_ref[...])
        down_lower_ref[...] = mm_tn(down_dlow_ref[...], act_ref[...])
        ffn_lower_ref[...] = mm_tn(ffn_dlow_ref[...], h_ref[...])
        both = mm_tn(ffn_low_ref[...], grad_ref[...])
        ffn_raise_ref[:, :half] = both[:rank, :half]
        ffn_raise_ref[:, half:] = both[rank:, half:]

    def work(owner):
        lowered = lower(all_ref[owner], factors_ref[OUT_B])
        low_ref[owner] = lowered
        heads_ref[owner] = (mm(all_ref[owner], w_ref[...]) + mm(lowered, f2_ref[...])).astype(bf16)

    gather(links, all_ref, work, before, after)
    raised, lowered = 0.0, 0.0
    for owner in range(4):
        raised = raised + mm_tn(out_low_ref[owner], all_ref[owner])
        lowered = lowered + mm_tn(low_ref[owner], attn_ref[owner])
    out_raise_ref[...] = raised
    out_lower_ref[...] = lowered


def prepare_kernel(
    wq_ref, wk_ref, dv_ref, lin_ref, inv_ref, inner_ref, f1_ref, low_ref, x_hbm,
    grad_ref, dlow_ref, raise_ref, lower_ref,
    x_ref, total_ref, stat_ref, send_sem, recv_sem, local_sem,
):
    links = Links(send_sem, recv_sem, local_sem)
    load = links.local(x_hbm, x_ref)
    load.start()
    third = wq_ref.shape[1]
    links.greet(rows=3)
    total = share_stats(links, stat_ref, inner_ref[0], inner_ref[1])
    total_ref[...] = total.T / D

    @pl.loop(0, SLAB // 32)
    def _(tile):
        rows = pl.ds(pl.multiple_of(tile * 32, 32), 32)
        inverse = inv_ref[rows]
        factor = inverse**3 * total_ref[rows]
        for index, source in enumerate((wq_ref, wk_ref)):
            cols = slice(index * third, (index + 1) * third)
            one = slice(index, index + 1)
            value = inverse[:, one] * source[rows] - lin_ref[rows, cols] * factor[:, one]
            grad_ref[rows, cols] = value.astype(bf16)
        grad_ref[rows, 2 * third :] = dv_ref[rows]

    dlow_ref[...] = lower(grad_ref[...], f1_ref[...])
    raised = mm_tn(low_ref[...], grad_ref[...])
    for index in range(3):
        cols = slice(index * third, (index + 1) * third)
        raise_ref[:, cols] = raised[index * RANK : (index + 1) * RANK, cols]
    load.wait()
    lower_ref[...] = mm_tn(dlow_ref[...], x_ref[...])


def back_qkv_kernel(
    grad_ref, dlow_ref, w_hbm, factors_ref, hidden_ref,
    final_ref,
    w_ref, sum_ref, own_ref, middle_ref, turn_buf, out_buf, relay_buf, final_buf,
    send_sem, recv_sem, local_sem,
):
    links = Links(send_sem, recv_sem, local_sem)
    load = links.local(w_hbm.at[:, pl.ds(0, w_ref.shape[1])], w_ref)
    load.start()
    links.greet(rows=3, columns=True)
    count = grad_ref.shape[1]

    def product(owner, store):
        def body(at):
            cols = pl.ds(at, TILE)
            value = mm_nt(grad_ref[owner], w_ref[cols, :])
            store(cols, value + mm(dlow_ref[owner], factors_ref[QKV_A, cols]))

        each_tile(w_ref.shape[0], TILE, body)

    load.wait()
    scatter(links, product, sum_ref, out_buf, relay_buf, final_buf)

    @pl.loop(0, count // 16)
    def _(tile):
        rows = pl.ds(pl.multiple_of(tile * 16, 16), 16)
        value = sum_ref[rows] + final_buf[0, rows].astype(f32) + final_buf[1, rows].astype(f32)
        own_ref[rows] = (value + hidden_ref[rows]).astype(bf16)

    turn = Turn(links, False, own_ref, middle_ref, turn_buf, 2)
    turn.start()
    turn.relay()
    turn.finish()
    widen(turn_buf, final_ref)


VMEM = pl.BlockSpec(memory_space=pltpu.VMEM)
ANY = pl.BlockSpec(memory_space=pl.ANY)


def linked(kernel, number, operands, outs, scratch, flops):
    specs = [ANY if isinstance(value, tuple) else VMEM for value in operands]
    values = [value[0] if isinstance(value, tuple) else value for value in operands]
    return pl.pallas_call(
        kernel,
        in_specs=specs,
        out_specs=[VMEM] * len(outs),
        out_shape=[jax.ShapeDtypeStruct(shape, kind) for shape, kind in outs],
        scratch_shapes=[pltpu.VMEM(shape, kind) for shape, kind in scratch]
        + [
            pltpu.SemaphoreType.DMA((32,)),
            pltpu.SemaphoreType.DMA((32,)),
            pltpu.SemaphoreType.DMA((8,)),
        ],
        compiler_params=pltpu.CompilerParams(
            collective_id=number, has_side_effects=True, vmem_limit_bytes=60 << 20
        ),
        cost_estimate=pl.CostEstimate(
            flops=flops, bytes_accessed=flops // 400, transcendentals=0
        ),
        name=kernel.__name__,
    )(*values)


def scatter_buffers(count):
    return [((3, count, D), bf16), ((2, count // 2, D), bf16), ((2, count, D), bf16)]


def score_blocks(k_ref, q_block, bias_ref, start, stop):
    parts = []
    if start:
        parts.append(mm_nt(k_ref[0:start], q_block) + bias_ref[0:start])
    own = mm_nt(k_ref[start:stop], q_block) + bias_ref[start:stop]
    keys = lax.broadcasted_iota(jnp.int32, own.shape, 0)
    queries = lax.broadcasted_iota(jnp.int32, own.shape, 1)
    parts.append(jnp.where(keys <= queries, own, very_low))
    return parts

def attend_kernel(q_ref, k_ref, v_ref, inv_ref, gain_ref, cos_ref, sin_ref, bias_ref,
                  ql_ref, kl_ref, vl_ref, o_ref, lse_ref):
    for source, target, index in ((q_ref, ql_ref, 0), (k_ref, kl_ref, 1)):
        normed = source[...] * inv_ref[:, index:index+1] * gain_ref[index:index+1, :]
        target[...] = (normed * cos_ref[...] + pltpu.roll(normed, HEAD_DIM // 2, 1) * sin_ref[...]).astype(bf16)
    values = v_ref[...].astype(bf16)
    vl_ref[...] = values
    values_t = v_ref[...].T.astype(bf16)
    for start in range(0, SLAB, BLOCK):
        stop = start + BLOCK
        parts = score_blocks(kl_ref, ql_ref[start:stop], bias_ref, start, stop)
        top = functools.reduce(jnp.maximum, [jnp.max(p, axis=0, keepdims=True) for p in parts]) * log2_scale
        total, out, at = 0.0, 0.0, 0
        for part in parts:
            shifted = jnp.exp2(part * log2_scale - top)
            total = total + jnp.sum(shifted, axis=0, keepdims=True)
            out = out + mm(values_t[:, at:at+part.shape[0]], shifted.astype(bf16))
            at += part.shape[0]
        o_ref[start:stop] = (out / total).T.astype(bf16)
        lse_ref[0, :, start:stop] = top + jnp.log2(total)

def attend_back_kernel(ql_ref, kl_ref, vl_ref, o_ref, do_ref, lse_ref, q_ref, k_ref, gain_ref, cos_ref, sin_ref, bias_ref,
                       wq_ref, wk_ref, dv_ref, sum_ref, dk_sum, dv_sum):
    keys_t = kl_ref[...].astype(f32).T.astype(bf16)
    delta_all = jnp.sum((do_ref[...].astype(f32) * o_ref[...].astype(f32)).T, axis=0, keepdims=True)
    dk_sum[...] = jnp.zeros_like(dk_sum)
    dv_sum[...] = jnp.zeros_like(dv_sum)
    def unrotate(values):
        return values * cos_ref[...] - pltpu.roll(values, HEAD_DIM // 2, 1) * sin_ref[...]
    dq_parts = []
    for start in range(0, SLAB, BLOCK):
        stop = start + BLOCK
        queries, grads = ql_ref[start:stop], do_ref[start:stop]
        parts = score_blocks(kl_ref, queries, bias_ref, start, stop)
        lse, delta = lse_ref[0, :, start:stop], delta_all[:, start:stop]
        at, dq = 0, 0.0
        for part in parts:
            span = slice(at, at + part.shape[0])
            probs = jnp.exp2(part * log2_scale - lse)
            dv_sum[span] += mm(probs.astype(bf16), grads)
            dscore = (probs * (mm_nt(vl_ref[span], grads) - delta)).astype(bf16)
            dk_sum[span] += mm(dscore, queries)
            dq = dq + mm(keys_t[:, span], dscore)
            at += part.shape[0]
        dq_parts.append(dq.T)
    dq_all = jnp.concatenate(dq_parts, axis=0) * score_scale
    dv_ref[...] = dv_sum[...].astype(bf16)
    wq = unrotate(dq_all) * gain_ref[0:1, :]
    wk = unrotate(dk_sum[...] * score_scale) * gain_ref[1:2, :]
    wq_ref[...] = wq.astype(wq_ref.dtype)
    wk_ref[...] = wk.astype(wk_ref.dtype)
    first = pl.program_id(0) == 0
    for index, (weighted, source) in enumerate(((wq, q_ref), (wk, k_ref))):
        product = weighted * source[...]

        @pl.when(first)
        def _():
            sum_ref[index] = product

        @pl.when(jnp.logical_not(first))
        def _():
            sum_ref[index] += product


def attend_specs(heads):
    col = lambda base: pl.BlockSpec((SLAB, HEAD_DIM), lambda h: (0, base * heads + h))
    whole = lambda shape: pl.BlockSpec(shape, lambda h: (0,) * len(shape))
    return col, whole

def attend(qkv_lin, inverses, gains, cosine, sine, bias):
    heads = qkv_lin.shape[1] // (3 * HEAD_DIM)
    col, whole = attend_specs(heads)
    low = jax.ShapeDtypeStruct((SLAB, heads * HEAD_DIM), bf16)
    return pl.pallas_call(
        attend_kernel, grid=(heads,),
        in_specs=[col(0), col(1), col(2), whole((SLAB, 8)), pl.BlockSpec((2, HEAD_DIM), lambda h: (0, h)),
                  whole((SLAB, HEAD_DIM)), whole((SLAB, HEAD_DIM)), whole((SLAB, 1))],
        out_specs=[col(0)] * 4 + [pl.BlockSpec((1, 1, SLAB), lambda h: (h, 0, 0))],
        out_shape=[low] * 4 + [jax.ShapeDtypeStruct((heads, 1, SLAB), f32)],
        compiler_params=pltpu.CompilerParams(vmem_limit_bytes=48 << 20),
        cost_estimate=pl.CostEstimate(flops=heads*4*SLAB*SLAB*HEAD_DIM, bytes_accessed=heads*SLAB*HEAD_DIM*20, transcendentals=heads*SLAB*SLAB),
        name="attend",
    )(qkv_lin, qkv_lin, qkv_lin, inverses, gains, cosine, sine, bias)

def attend_back(ql, kl, vl, o, do, lse, qkv_lin, gains, cosine, sine, bias):
    heads = ql.shape[1] // HEAD_DIM
    col, whole = attend_specs(heads)
    wide = jax.ShapeDtypeStruct(ql.shape, f32)
    return pl.pallas_call(
        attend_back_kernel, grid=(heads,),
        in_specs=[col(0)] * 5 + [pl.BlockSpec((1, 1, SLAB), lambda h: (h, 0, 0)), col(0), col(1), pl.BlockSpec((2, HEAD_DIM), lambda h: (0, h)),
                  whole((SLAB, HEAD_DIM)), whole((SLAB, HEAD_DIM)), whole((SLAB, 1))],
        out_specs=[col(0)] * 3 + [whole((2, SLAB, HEAD_DIM))],
        out_shape=[wide, wide, jax.ShapeDtypeStruct(ql.shape, bf16), jax.ShapeDtypeStruct((2, SLAB, HEAD_DIM), f32)],
        scratch_shapes=[pltpu.VMEM((SLAB, HEAD_DIM), f32)] * 2,
        compiler_params=pltpu.CompilerParams(vmem_limit_bytes=48 << 20),
        cost_estimate=pl.CostEstimate(flops=heads*10*SLAB*SLAB*HEAD_DIM, bytes_accessed=heads*SLAB*HEAD_DIM*30, transcendentals=heads*SLAB*SLAB),
        name="attend_back",
    )(ql, kl, vl, o, do, lse, qkv_lin, qkv_lin, gains, cosine, sine, bias)


def dot(left, right):
    return jnp.dot(left, right, preferred_element_type=f32)


def dot_nt(left, right):
    return lax.dot_general(left, right, (((1,), (1,)), ((), ())), preferred_element_type=f32)


def dot_tn(left, right):
    return lax.dot_general(left, right, (((0,), (0,)), ((), ())), preferred_element_type=f32)


def gather_weight(local):
    half = local.shape[0] // lax.axis_size("tok")
    part = lax.dynamic_slice_in_dim(local, lax.axis_index("tok") * half, half, 0)
    return lax.all_gather(part, ("col", "tok"), axis=0, tiled=True)


def to_tokens(values):
    rows, cols = lax.axis_size("row"), lax.axis_size("col")
    width = values.shape[1]
    mixed = lax.all_to_all(values, "row", 0, 0, tiled=True)
    mixed = lax.all_to_all(mixed, "col", 0, 0, tiled=True)
    return mixed.reshape(cols, SLAB // rows, width).transpose(1, 0, 2).reshape(SLAB // rows, -1)


def from_tokens(values):
    rows, cols = lax.axis_size("row"), lax.axis_size("col")
    count = values.shape[0]
    mixed = values.reshape(count, cols, -1).transpose(1, 0, 2).reshape(cols * count, -1)
    mixed = lax.all_to_all(mixed, "col", 0, 0, tiled=True)
    return lax.all_to_all(mixed, "row", 0, 0, tiled=True)


def reorder(values, outer, inner):
    if outer == 1 or inner == 1:
        return values
    rest = values.shape[0] // (outer * inner)
    shape = (outer, inner, rest) + values.shape[1:]
    return values.reshape(shape).swapaxes(0, 1).reshape(values.shape)


def gather_tokens(values):
    rows, per_slab = lax.axis_size("row"), lax.axis_size("row") // lax.axis_size("col")
    return reorder(lax.all_gather(values, "row", axis=0, tiled=True), rows, per_slab)


def scatter_tokens(values):
    rows, per_slab = lax.axis_size("row"), lax.axis_size("row") // lax.axis_size("col")
    values = reorder(values.astype(bf16), per_slab, rows)
    return lax.psum_scatter(values, "row", scatter_dimension=0, tiled=True).astype(f32)


def token_places(length):
    slot_ids = jnp.arange(SLAB, dtype=jnp.int32)
    return jnp.where(slot_ids < PROMPT, slot_ids, length + (slot_ids - PROMPT) % CONT_LEN)


def rotation(places, head_size):
    half_dim = head_size // 2
    frequency = jnp.exp(
        -(2.0 * jnp.arange(half_dim, dtype=f32) / head_size) * math.log(rope_base)
    )
    angles = places.astype(f32)[:, None] * frequency[None, :]
    return (jnp.cos(angles), jnp.sin(angles))


def pick(adapters, ids):
    onehot = (ids[:, None] == jnp.arange(adapters.shape[0], dtype=jnp.int32)).astype(adapters.dtype)
    return jnp.tensordot(onehot, adapters, axes=1)


def place(ids, gradients):
    onehot = (jnp.arange(ADAPTERS, dtype=jnp.int32)[:, None] == ids[None, :]).astype(f32)
    total = 0.0
    for index in range(gradients.shape[0]):
        weight = onehot[:, index].reshape((ADAPTERS,) + (1,) * (gradients.ndim - 1))
        total = total + weight * gradients[index][None].astype(f32)
    return total


def block_diagonal(factors):
    count = len(factors)
    lines = []
    for index, factor in enumerate(factors):
        blank = jnp.zeros_like(factor)
        lines.append(
            jnp.concatenate([factor if k == index else blank for k in range(count)], axis=1)
        )
    return jnp.concatenate(lines, axis=0)


def enter(x, w, f1, f2):
    everything = gather_tokens(x)
    lowered = (adapter_scale * dot_nt(everything, f1)).astype(bf16)
    return everything, lowered, dot(everything, w) + dot(lowered, f2)


def leave(y, w, f1, f2):
    lowered = (adapter_scale * dot_nt(y, f1)).astype(bf16)
    return scatter_tokens(dot_nt(y, w) + dot(lowered, f2)), lowered


def split_layer(
    layer_in, cotangent, attn_full, ffn_full, down_full, pieces, head_gain, qkv_b, out_a, ffn_b,
    down_a, tables,
):
    factors = lax.all_to_all(pieces, "col", 0, 0, tiled=True)
    factors = factors.transpose(1, 0, 2).reshape(-1, D)
    qkv_a, out_b, ffn_a, down_b = (factors[part] for part in (QKV_A, OUT_B, FFN_A, DOWN_B))
    gains = factors[GAIN0.start : GAIN1.stop].astype(f32)
    width = qkv_b.shape[1]
    head_width, ff_width = width // 3, ffn_b.shape[1] // 2
    x_own = to_tokens(layer_in)
    x_all, qkv_low, qkv_lin = enter(x_own, attn_full[:, :width], qkv_a, qkv_b)
    q_lin, k_lin = qkv_lin[:, :head_width], qkv_lin[:, head_width : 2 * head_width]
    squares = jnp.stack([jnp.sum(q_lin * q_lin, axis=1), jnp.sum(k_lin * k_lin, axis=1)], axis=1)
    inverses = lax.rsqrt(lax.psum(squares, "row") / D + norm_eps)
    inverses = jnp.concatenate([inverses] * 4, axis=1)
    q_low, k_low, v_low, attn_low, log_sums = attend(qkv_lin, inverses, head_gain, *tables)
    attn_lin, out_low = leave(attn_low, attn_full[:, width:], out_a, out_b)
    hidden = x_own.astype(f32) + attn_lin * inverse_of(attn_lin) * gains[0]
    h_all, ffn_low, ffn_lin = enter(hidden.astype(bf16), ffn_full, ffn_a, ffn_b)
    gate_lin, up_lin = ffn_lin[:, :ff_width], ffn_lin[:, ff_width:]
    act_low = gated(gate_lin, up_lin).astype(bf16)
    mlp_lin, down_low = leave(act_low, down_full, down_a, down_b)
    layer_out = hidden + mlp_lin * inverse_of(mlp_lin) * gains[1]
    layer_out = from_tokens(layer_out.astype(bf16)).astype(f32)
    grad_out = to_tokens(cotangent).astype(f32)
    grad_mlp = norm_back(mlp_lin, grad_out * gains[1]).astype(bf16)
    dm_all, down_dlow, grad_act = enter(grad_mlp, down_full, down_b, down_a)
    grad_ffn = jnp.concatenate(gated_back(grad_act, gate_lin, up_lin), axis=1).astype(bf16)
    grad_ffn_in, ffn_dlow = leave(grad_ffn, ffn_full, ffn_b, ffn_a)
    grad_hidden = grad_out + grad_ffn_in
    grad_attn = norm_back(attn_lin, grad_hidden * gains[0]).astype(bf16)
    da_all, out_dlow, grad_heads = enter(grad_attn, attn_full[:, width:], out_b, out_a)
    weighted_q, weighted_k, grad_v, inner = attend_back(
        q_low, k_low, v_low, attn_low, grad_heads.astype(bf16), log_sums, qkv_lin, head_gain, *tables
    )
    inner = lax.psum(jnp.sum(inner, axis=2).T, "row")
    factor = inverses[:, :2] ** 3 * inner / D
    grad_qkv = jnp.concatenate(
        [
            (inverses[:, 0:1] * weighted_q - q_lin * factor[:, 0:1]).astype(bf16),
            (inverses[:, 1:2] * weighted_k - k_lin * factor[:, 1:2]).astype(bf16),
            grad_v,
        ],
        axis=1,
    )
    grad_qkv_in, qkv_dlow = leave(grad_qkv, attn_full[:, :width], qkv_b, qkv_a)
    grad_in = from_tokens((grad_hidden + grad_qkv_in).astype(bf16)).astype(f32)
    return (
        layer_out, grad_in,
        dot_tn(down_low, dm_all), dot_tn(down_dlow, act_low),
        diagonal(dot_tn(ffn_low, grad_ffn), 2), dot_tn(ffn_dlow, h_all),
        dot_tn(out_low, da_all), dot_tn(out_dlow, attn_low),
        diagonal(dot_tn(qkv_low, grad_qkv), 3), dot_tn(qkv_dlow, x_all),
    )


def flat(values):
    return values.reshape((SLAB,) + values.shape[2:])


def cube(values):
    return values.reshape((4, SLAB // 4) + values.shape[1:])


def linked_layer(
    layer_in, cotangent, attn_full, ffn_full, down_full, pieces, head_gain, qkv_b, out_a, ffn_b,
    down_a, tables,
):
    count = SLAB // 4
    width = qkv_b.shape[1]
    head_width, ff_width = width // 3, ffn_b.shape[1] // 2
    buffers = scatter_buffers(count)
    per = 2 * SLAB * D
    tokens = ((4, count, D), bf16)

    def low_rows(size):
        return ((4, count, size), bf16)

    piece = (4, count, layer_in.shape[1])
    x_own, factors = linked(
        intake_kernel, 1,
        [cube(layer_in), pieces],
        [((count, D), bf16), ((128, D), bf16)],
        [(piece, bf16)],
        per * 128,
    )
    x_all, qkv_low, qkv_lin, inverses = linked(
        enter_qkv_kernel, 2,
        [x_own, (attn_full,), factors, qkv_b],
        [tokens, low_rows(48), ((4, count, width), f32), ((SLAB, 8), f32)],
        [((D, width), bf16), ((2, SLAB, 128), f32), ((4, 8, SLAB), f32)],
        per * width,
    )
    qkv_lin = flat(qkv_lin)
    q_low, k_low, v_low, attn_low, log_sums = attend(qkv_lin, inverses, head_gain, *tables)
    attn_lin, out_low, hidden, h_all = linked(
        leave_out_kernel, 3,
        [cube(attn_low), (attn_full,), out_a, factors, x_own],
        [((count, D), f32), low_rows(16), ((count, D), f32), tokens],
        [((D, head_width), bf16)] + buffers,
        per * head_width,
    )
    h_all = flat(h_all)
    ffn_low, gate_lin, up_lin, act_low = ffn(h_all, ffn_full, factors, ffn_b)
    down_low, own_out, grad_mlp, own_cot = linked(
        leave_down_kernel, 4,
        [cube(act_low), (down_full,), down_a, factors, hidden, cube(cotangent)],
        [low_rows(16)] + [((count, D), bf16)] * 3,
        [((D, ff_width), bf16), ((count, D), f32), (piece, bf16)] + buffers,
        per * ff_width,
    )
    dm_all, down_dlow, grad_ffn, layer_out = linked(
        back_down_kernel, 5,
        [grad_mlp, (down_full,), factors, down_a, cube(gate_lin), cube(up_lin), own_out],
        [tokens, low_rows(16), ((4, count, 2 * ff_width), bf16), (layer_in.shape, f32)],
        [((D, ff_width), bf16), (piece, bf16), (layer_in.shape, bf16)],
        per * ff_width,
    )
    ffn_dlow, grad_hidden, grad_attn = linked(
        back_ffn_kernel, 6,
        [grad_ffn, (ffn_full,), ffn_b, factors, own_cot, attn_lin],
        [low_rows(32), ((count, D), f32), ((count, D), bf16)],
        [((D, 2 * ff_width), bf16), ((count, D), f32)] + buffers,
        per * 2 * ff_width,
    )
    da_all, out_dlow, grad_heads, *early = linked(
        back_out_kernel, 7,
        [grad_attn, (attn_full,), factors, out_a, out_low, cube(attn_low), flat(down_low)]
        + [flat(down_dlow), ffn_low, flat(ffn_dlow), (flat(dm_all),), (act_low,)]
        + [(flat(grad_ffn),), (h_all,)],
        [tokens, low_rows(16), ((4, count, head_width), bf16), ((16, D), f32)]
        + [((16, ff_width), f32), ((16, 2 * ff_width), f32), ((32, D), f32)]
        + [((16, D), f32), ((16, head_width), f32)],
        [((D, head_width), bf16), ((SLAB, D), bf16), ((SLAB, ff_width), bf16)]
        + [((SLAB, 2 * ff_width), bf16), ((SLAB, D), bf16)],
        per * head_width,
    )
    weighted_q, weighted_k, grad_v, inner = attend_back(
        q_low, k_low, v_low, attn_low, flat(grad_heads), log_sums, qkv_lin, head_gain, *tables
    )
    grad_qkv, qkv_dlow, *late = linked(
        prepare_kernel, 8,
        [weighted_q, weighted_k, grad_v, qkv_lin, inverses, inner, qkv_b, flat(qkv_low)]
        + [(flat(x_all),)],
        [((SLAB, width), bf16), ((SLAB, 48), bf16), ((16, width), f32), ((48, D), f32)],
        [((SLAB, D), bf16), ((SLAB, 8), f32), ((4, 8, SLAB), f32)],
        per * 128,
    )
    (grad_in,) = linked(
        back_qkv_kernel, 9,
        [cube(grad_qkv), cube(qkv_dlow), (attn_full,), factors, grad_hidden],
        [(layer_in.shape, f32)],
        [((D, width), bf16), ((count, D), f32), ((count, D), bf16), (piece, bf16)]
        + [(layer_in.shape, bf16)]
        + buffers,
        per * width,
    )
    return (layer_out, grad_in, *early, *late)


def diagonal(values, count):
    width = values.shape[1] // count
    return jnp.concatenate(
        [
            values[k * RANK : (k + 1) * RANK, k * width : (k + 1) * width]
            for k in range(count)
        ],
        axis=1,
    )


def on_device(
    layer_in,
    cotangent,
    qkv_weight,
    out_weight,
    ffn_weight,
    down_weight,
    qk_gain,
    post_gain,
    qkv_lower,
    qkv_raise,
    out_lower,
    out_raise,
    ffn_lower,
    ffn_raise,
    down_lower,
    down_raise,
    adapter_ids,
    prompt_len,
):
    col_count = lax.axis_size("col")
    group_base = lax.axis_index("tok") * col_count
    group = group_base + lax.axis_index("col")
    slab_ids = lax.dynamic_slice_in_dim(adapter_ids, group_base, col_count, 0)
    own_ids = lax.dynamic_index_in_dim(adapter_ids, group, 0, keepdims=False)
    length = lax.dynamic_index_in_dim(prompt_len, group, 0, keepdims=False)
    width = layer_in.shape[1]
    head_width = qkv_weight.shape[2]
    ff_width = ffn_weight.shape[2]

    local = jnp.concatenate([qkv_weight.transpose(1, 0, 2).reshape(width, -1), out_weight.T], axis=1)
    attn_full = gather_weight(local)
    ffn_full = gather_weight(ffn_weight.transpose(1, 0, 2).reshape(width, -1))
    down_full = gather_weight(down_weight.T)

    pieces = jnp.concatenate(
        [pick(qkv_lower[p].swapaxes(1, 2), slab_ids[:, p]) for p in range(3)]
        + [pick(out_raise, slab_ids[:, 3])]
        + [pick(ffn_lower[p].swapaxes(1, 2), slab_ids[:, 4 + p]) for p in range(2)]
        + [pick(down_raise, slab_ids[:, 6])]
        + [jnp.broadcast_to(jnp.pad(post_gain, ((0, 14), (0, 0))), (col_count, RANK, width))],
        axis=1,
    )
    qkv_b = block_diagonal([pick(qkv_raise[p], own_ids[p : p + 1])[0] for p in range(3)])
    out_a = pick(out_lower, own_ids[3:4])[0].T
    ffn_b = block_diagonal([pick(ffn_raise[p], own_ids[4 + p : 5 + p])[0] for p in range(2)])
    down_a = pick(down_lower, own_ids[6:7])[0].T

    cosine, sine = rotation(token_places(length), HEAD_DIM)
    cosine = jnp.concatenate([cosine, cosine], axis=1)
    sine = jnp.concatenate([-sine, sine], axis=1)
    slots = jnp.arange(SLAB, dtype=jnp.int32)
    bias = jnp.where((slots < length) | (slots >= PROMPT), 0.0, very_low)[:, None].astype(f32)

    layer = linked_layer if (lax.axis_size("row"), col_count) == (4, 4) else split_layer
    (
        layer_out, grad_in, down_raise_part, down_lower_part, ffn_raise_part, ffn_lower_part,
        out_raise_part, out_lower_part, qkv_raise_part, qkv_lower_part,
    ) = layer(
        layer_in, cotangent, attn_full, ffn_full, down_full, pieces, qk_gain.astype(f32), qkv_b,
        out_a, ffn_b, down_a, (cosine, sine, bias),
    )

    def col_sums(parts, numbers):
        count = len(numbers)
        parts = jnp.concatenate(parts).astype(bf16).reshape(count, RANK, col_count, width)
        parts = lax.all_to_all(parts.transpose(2, 0, 1, 3), "col", 0, 0, tiled=True)
        placed = [place(slab_ids[:, p], parts[:, k]) for k, p in enumerate(numbers)]
        return lax.psum(jnp.stack(placed).astype(bf16), ("tok", "row")).astype(f32)

    def row_sums(parts, numbers):
        own = jnp.concatenate(parts, axis=1).astype(bf16)
        every = lax.all_gather(own, ("tok", "col"), axis=0)
        sums, at = [], 0
        for p in numbers:
            size = ff_width if p > 3 else head_width
            sums.append(place(adapter_ids[:, p], every[:, :, at : at + size]))
            at += size
        return sums

    early_cols = col_sums([out_raise_part, ffn_lower_part, down_raise_part], [3, 4, 5, 6])
    early_rows = row_sums([out_lower_part, ffn_raise_part, down_lower_part], [3, 4, 5, 6])
    late_cols = col_sums([qkv_lower_part], [0, 1, 2])
    late_rows = row_sums([qkv_raise_part], [0, 1, 2])
    return (
        layer_out,
        grad_in,
        late_cols.swapaxes(2, 3),
        jnp.stack(late_rows),
        early_rows[0].swapaxes(1, 2),
        early_cols[0],
        early_cols[1:3].swapaxes(2, 3),
        jnp.stack(early_rows[1:3]),
        early_rows[3].swapaxes(1, 2),
        early_cols[3],
    )


def solution(mesh):
    return jax.shard_map(
        on_device,
        mesh=mesh,
        in_specs=(
            P(("tok", "row"), "col"),
            P(("tok", "row"), "col"),
            P(None, "col", "row"),
            P("row", "col"),
            P(None, "col", "row"),
            P("row", "col"),
            P(None, "row"),
            P(None, "col"),
            P(None, None, "col", None),
            P(None, None, None, "row"),
            P(None, "row", None),
            P(None, None, "col"),
            P(None, None, "col", None),
            P(None, None, None, "row"),
            P(None, "row", None),
            P(None, None, "col"),
            P(),
            P(),
        ),
        out_specs=(
            P(("tok", "row"), "col"),
            P(("tok", "row"), "col"),
            P(None, None, "col", None),
            P(None, None, None, "row"),
            P(None, "row", None),
            P(None, None, "col"),
            P(None, None, "col", None),
            P(None, None, None, "row"),
            P(None, "row", None),
            P(None, None, "col"),
        ),
        check_vma=False,
    )
```

```python
import functools
import math

import jax
import jax.numpy as jnp
from jax import lax
from jax.experimental import pallas as pl
from jax.experimental.pallas import tpu as pltpu
from jax.sharding import PartitionSpec as P

D = 2048
HEAD_DIM = 128
RANK = 16
ADAPTERS = 8
PROMPT = 1024
CONT_LEN = 128
SLAB = 1152

adapter_scale = 2.0
norm_eps = 1e-06
rope_base = 500000.0
very_low = -1e30
bf16 = jnp.bfloat16
f32 = jnp.float32
log2_scale = math.log2(math.e) / math.sqrt(HEAD_DIM)
score_scale = 1.0 / math.sqrt(HEAD_DIM)
BLOCK = 384
TILE = 512
MESH = pl.DeviceIdType.MESH


def mm(left, right):
    return jnp.dot(left, right, preferred_element_type=f32)


def mm_nt(left, right):
    return lax.dot_general(left, right, (((1,), (1,)), ((), ())), preferred_element_type=f32)


class Links:
    def __init__(self, send_sem, recv_sem, local_sem):
        self.tok = lax.axis_index("tok")
        self.row, self.col = lax.axis_index("row"), lax.axis_index("col")
        self.xn, self.yn, self.dg = self.row ^ 1, self.row ^ 2, self.row ^ 3
        self.send_sem, self.recv_sem, self.local_sem = send_sem, recv_sem, local_sem
        self.used, self.local_used = 0, 0

    def take(self, count):
        self.used += count
        return self.used - count

    def copy(self, source, target, index, recv_index, row, col=None, tok=None):
        return pltpu.make_async_remote_copy(
            src_ref=source,
            dst_ref=target,
            send_sem=self.send_sem.at[index],
            recv_sem=self.recv_sem.at[recv_index],
            device_id={
                "tok": self.tok if tok is None else tok,
                "row": row,
                "col": self.col if col is None else col,
            },
            device_id_type=MESH,
        )

    def local(self, source, target):
        self.local_used += 1
        return pltpu.make_async_copy(source, target, self.local_sem.at[self.local_used - 1])

    def plan(self, *pairs):
        return [self.local(source, target) for source, target in pairs]

    def fetch(self, *pairs):
        return start_all(self.plan(*pairs))

    def greet(self, rows=2, columns=False, twin=False):
        barrier = pltpu.get_barrier_semaphore()
        places = [(self.tok, self.row ^ step, self.col) for step in range(1, rows + 1)]
        if columns:
            places += [(self.tok, self.row, self.col ^ step) for step in range(1, 4)]
        if twin:
            places += [(self.tok ^ 1, self.row, self.col)]
        for tok, row, col in places:
            pl.semaphore_signal(
                barrier,
                inc=1,
                device_id={"tok": tok, "row": row, "col": col},
                device_id_type=MESH,
            )
        pl.semaphore_wait(barrier, len(places))


def start_all(copies):
    for copy in copies:
        copy.start()
    return copies


def wait_all(copies):
    for copy in copies:
        copy.wait()


class Exchange:
    def __init__(self, links, axis, piece_at, slot_at):
        self.links, self.axis = links, axis
        self.me = links.row if axis == "row" else links.col
        self.piece_at, self.slot_at = piece_at, slot_at
        self.base = links.take(3)
        self.own = links.local(piece_at(self.me), slot_at(self.me))

    def copy(self, source, target, step):
        links, other, index = self.links, self.me ^ step, self.base + step - 1
        row, col = (other, links.col) if self.axis == "row" else (links.row, other)
        return links.copy(source, target, index, index, row, col)

    def start(self):
        for step in range(1, 4):
            self.copy(self.piece_at(self.me ^ step), self.slot_at(self.me), step).start()
        self.own.start()

    def arrived(self):
        for step in range(1, 4):
            landed = self.slot_at(self.me ^ step)
            self.copy(landed, landed, step).wait_recv()
        self.own.wait()

    def sent(self):
        for step in range(1, 4):
            self.copy(self.piece_at(self.me ^ step), self.slot_at(self.me), step).wait_send()


def features(ref, width):
    return lambda col: ref.at[:, pl.ds(pl.multiple_of(col * width, width), width)]


def slot(ref):
    return lambda key: ref.at[key]


def token_rows(ref, count):
    return lambda row: ref.at[pl.ds(pl.multiple_of(row * count, 16), count)]


def gather(links, all_ref, work, before=None, after=None):
    me, xn, yn, dg = links.row, links.xn, links.yn, links.dg
    half = all_ref.shape[1] // 2
    top, low = pl.ds(0, half), pl.ds(half, half)
    base = links.take(6)

    def move(owner, part, index, other):
        place = all_ref.at[owner, part]
        return links.copy(place, place, base + index, base + index, other)

    sends = [move(me, top, 0, xn), move(me, low, 1, yn), move(me, low, 2, xn), move(me, top, 3, yn)]
    for copy in sends:
        copy.start()
    if before:
        before()
    if work:
        work(me)
    move(xn, top, 0, xn).wait_recv()
    sends.append(move(xn, top, 4, yn))
    sends[-1].start()
    move(yn, low, 1, yn).wait_recv()
    sends.append(move(yn, low, 5, xn))
    sends[-1].start()
    if after:
        after()
    move(xn, low, 2, xn).wait_recv()
    if work:
        work(xn)
    move(yn, top, 3, yn).wait_recv()
    if work:
        work(yn)
    move(dg, top, 4, yn).wait_recv()
    move(dg, low, 5, xn).wait_recv()
    if work:
        work(dg)
    for copy in sends:
        copy.wait_send()


SLICES = 4


def scatter(links, product, o_ref, out_buf, relay_buf, final_buf, block=None, ready=None, hooks=None):
    me, xn, yn, dg = links.row, links.xn, links.yn, links.dg
    count, width = o_ref.shape[0], o_ref.shape[1] // SLICES
    half = count // 2
    top, low = pl.ds(0, half), pl.ds(half, half)
    base = links.take(6 * SLICES)
    all_copies = []

    def columns(k):
        at = block(k) * width if block else k * width
        return pl.ds(pl.multiple_of(at, width), width)

    def add(place, k, rows, relay):
        out_buf[place, k, rows] = (
            out_buf[place, k, rows].astype(f32) + relay_buf[relay, k].astype(f32)
        ).astype(bf16)

    def relay(k):
        copies = all_copies[k]
        copies[0].wait_recv()
        add(2, k, top, 0)
        copies[4].start()
        copies[1].wait_recv()
        add(1, k, low, 1)
        copies[5].start()

    def finish(k):
        for copy in all_copies[k][2:]:
            copy.wait_recv()

    for k in range(SLICES):
        cols = columns(k)

        def move(source, target, index, other, k=k):
            at = base + 6 * k + index
            return links.copy(source, target, at, at, other)

        copies = [
            move(out_buf.at[0, k, top], relay_buf.at[0, k], 0, xn),
            move(out_buf.at[0, k, low], relay_buf.at[1, k], 1, yn),
            move(out_buf.at[1, k, top], final_buf.at[0, k, top], 2, xn),
            move(out_buf.at[2, k, low], final_buf.at[1, k, low], 3, yn),
            move(out_buf.at[2, k, top], final_buf.at[1, k, top], 4, yn),
            move(out_buf.at[1, k, low], final_buf.at[0, k, low], 5, xn),
        ]
        all_copies.append(copies)
        if ready:
            ready(k)
        for place, (owner, first) in enumerate(((dg, (0, 1)), (xn, (2,)), (yn, (3,)))):
            out_buf[place, k] = product(owner, k, cols).astype(bf16)
            for index in first:
                copies[index].start()
        if k:
            relay(k - 1)
        o_ref[:, cols] = product(me, k, cols)
        if hooks:
            hooks[k](columns, finish)
    relay(SLICES - 1)

    def sent():
        for copies in all_copies:
            for copy in copies:
                copy.wait_send()

    return columns, finish, sent


def finish_all(result):
    _, finish, sent = result
    for k in range(SLICES):
        finish(k)
    sent()


def each_tile(width, step, body):
    @pl.loop(0, width // step)
    def _(tile):
        body(pl.multiple_of(tile * step, step))


def lower(rows, factor):
    return (adapter_scale * mm_nt(rows, factor)).astype(bf16)


def leave_product(y_ref, weight, f1, f2_ref, f2_rows, low_ref, loads):
    lowered = {}

    def product(owner, k, cols):
        place = len(lowered) % 4 if k == 0 else None
        if k == 0:
            loads[place].wait()
            low_ref[owner] = lower(y_ref[owner], f1)
            lowered[place] = True
        return weight(y_ref[owner], cols) + mm(low_ref[owner], f2_ref[f2_rows, cols])

    return product


class Streams:
    def __init__(self, links, rows, blocks, late=()):
        order = (links.dg, links.xn, links.yn, links.row)
        self.rows = links.plan(*[(rows[0].at[k], rows[1].at[k]) for k in order]) if rows else []
        self.blocks = blocks
        self.late = links.plan(*late)
        start_all(self.rows[:1])
        start_all(blocks[0])

    def ready(self, k):
        wait_all(self.blocks[k])
        if k == 0:
            start_all(self.rows[1:])
        if k < SLICES - 1:
            start_all(self.blocks[k + 1])
        if k == 1:
            start_all(self.late)


def load_qkv(links, w_hbm, w_ref, blocks):
    half, width = w_hbm.shape[1] // 4, w_hbm.shape[2]
    return [
        links.plan(
            *[
                (
                    w_hbm.at[2 * c + t, pl.ds(p * half, half)],
                    w_ref.at[
                        pl.ds(pl.multiple_of((2 * c + t) * half, half), half),
                        pl.ds(p * width, width),
                    ],
                )
                for t in range(2)
                for p in range(3)
            ]
        )
        for c in blocks
    ]


def load_out(links, w_hbm, w_ref):
    half, width = w_hbm.shape[1] // 4, w_hbm.shape[2]
    return [
        links.plan(
            *[
                (
                    w_hbm.at[2 * c + t, pl.ds(3 * half, half)],
                    w_ref.at[pl.ds(t * half, half), pl.ds(c * width, width)],
                )
                for t in range(2)
            ]
        )
        for c in range(4)
    ]


def load_down(links, w_hbm, w_ref):
    half, width = w_hbm.shape[1:]
    return [
        links.plan(
            *[
                (
                    w_hbm.at[2 * c + t],
                    w_ref.at[pl.ds(t * half, half), pl.ds(c * width, width)],
                )
                for t in range(2)
            ]
        )
        for c in range(4)
    ]


def load_ffn(links, w_hbm, w_ref):
    half, width = w_hbm.shape[2:]
    return [
        links.plan(
            *[
                (
                    w_hbm.at[2 * c + t, g],
                    w_ref.at[pl.ds((2 * c + t) * half, half), pl.ds(g * width, width)],
                )
                for t in range(2)
                for g in range(2)
            ]
        )
        for c in range(4)
    ]


def inverse_of(values):
    return lax.rsqrt(jnp.mean(values * values, axis=1, keepdims=True) + norm_eps)


def norm_back(values, weighted):
    inverse = inverse_of(values)
    inner = jnp.mean(values * weighted, axis=1, keepdims=True)
    return inverse * weighted - values * (inverse**3 * inner)


def gated(gate, up):
    return gate * jax.nn.sigmoid(gate) * up


def gated_back(grad, gate, up):
    sig = jax.nn.sigmoid(gate)
    act = gate * sig
    return (grad * up * (sig + act * (1.0 - sig)), grad * act)


QKV_A, OUT_B, FFN_A, DOWN_B = slice(0, 48), slice(48, 64), slice(64, 96), slice(96, 112)
GAIN0, GAIN1 = slice(112, 113), slice(113, 114)


def share_stats(links, stat_ref, first, second):
    blank = jnp.zeros((6, first.shape[0]), f32)
    sums = [jnp.sum(value.T, axis=0, keepdims=True) for value in (first, second)]
    stat_ref[links.row] = jnp.concatenate(sums + [blank], axis=0)
    base = links.take(3)
    mine = stat_ref.at[links.row]
    copies = []
    for index, other in enumerate((links.xn, links.yn, links.dg)):
        copies.append(links.copy(mine, mine, base + index, base + index, other))
        copies[-1].start()
    for index, other in enumerate((links.xn, links.yn, links.dg)):
        theirs = stat_ref.at[other]
        links.copy(theirs, theirs, base + index, base + index, other).wait_recv()
    for copy in copies:
        copy.wait_send()
    return stat_ref[0] + stat_ref[1] + stat_ref[2] + stat_ref[3]


def lane_sums(values):
    return functools.reduce(
        jnp.add, [values[:, at : at + 128] for at in range(0, values.shape[1], 128)]
    )


def intake_kernel(
    x_hbm, cot_hbm, ids_ref, gain_ref, qkv_lower_ref, out_raise_ref, ffn_lower_ref, down_raise_ref,
    qkv_raise_ref, out_lower_ref, ffn_raise_ref, down_lower_ref,
    own_ref, cot_ref, factors_ref, qkv_b_ref, out_a_ref, ffn_b_ref, down_a_ref,
    middle_ref, pieces_ref, send_sem, recv_sem, local_sem,
):
    links = Links(send_sem, recv_sem, local_sem)
    links.greet(rows=3, columns=True)
    width = pieces_ref.shape[2]
    first = Exchange(links, "row", slot(x_hbm), slot(middle_ref))
    second = Exchange(links, "col", slot(middle_ref), features(own_ref, width))
    turned = Exchange(links, "row", slot(cot_hbm), slot(cot_ref))
    spread = Exchange(links, "col", slot(pieces_ref), features(factors_ref, width))
    first.start()
    base = 4 * links.tok
    for place in range(4):
        for p in range(7):
            chosen = ids_ref[base + place, p]
            if p < 3:
                value = qkv_lower_ref[p, chosen]
            elif p == 3:
                value = out_raise_ref[chosen]
            elif p < 6:
                value = ffn_lower_ref[p - 4, chosen]
            else:
                value = down_raise_ref[chosen]
            pieces_ref[place, p * RANK : (p + 1) * RANK] = value
        pieces_ref[place, 7 * RANK :] = gain_ref[...]
    spread.start()
    first.arrived()
    second.start()
    turned.start()
    own = base + links.col
    qkv_b_ref[...] = jnp.zeros_like(qkv_b_ref)
    ffn_b_ref[...] = jnp.zeros_like(ffn_b_ref)
    for p in range(3):
        cols = slice(p * qkv_raise_ref.shape[3], (p + 1) * qkv_raise_ref.shape[3])
        qkv_b_ref[p * RANK : (p + 1) * RANK, cols] = qkv_raise_ref[p, ids_ref[own, p]]
    for p in range(2):
        cols = slice(p * ffn_raise_ref.shape[3], (p + 1) * ffn_raise_ref.shape[3])
        ffn_b_ref[p * RANK : (p + 1) * RANK, cols] = ffn_raise_ref[p, ids_ref[own, 4 + p]]
    out_a_ref[...] = out_lower_ref[ids_ref[own, 3]]
    down_a_ref[...] = down_lower_ref[ids_ref[own, 6]]
    for exchange in (spread, second, turned):
        exchange.arrived()
    for exchange in (first, spread, second, turned):
        exchange.sent()


def enter_qkv_kernel(
    x_ref, w_hbm, factors_ref, f2_ref,
    all_hbm, low_ref, lin_hbm, inv_ref,
    all_ref, lin_ref, w_ref, sq_ref, stat_ref, send_sem, recv_sem, local_sem,
):
    links = Links(send_sem, recv_sem, local_sem)
    width = w_ref.shape[1]
    loads = start_all(sum(load_qkv(links, w_hbm, w_ref, range(4)), []))
    all_ref[links.row] = x_ref[...]
    links.greet(rows=3)
    count = x_ref.shape[0]
    stores = []

    def work(owner):
        lowered = lower(all_ref[owner], factors_ref[QKV_A])
        low_ref[owner] = lowered
        rows = all_ref[owner]
        third = width // 3
        for index in range(3):
            cols = slice(index * third, (index + 1) * third)
            value = mm(rows, w_ref[:, cols]) + mm(lowered, f2_ref[:, cols])
            lin_ref[owner, :, cols] = value
            if index < 2:
                place = pl.ds(pl.multiple_of(owner * count, 8), count)
                sq_ref[index, place] = lane_sums(value * value)
        stores.extend(
            links.fetch(
                (lin_ref.at[owner], lin_hbm.at[owner]), (all_ref.at[owner], all_hbm.at[owner])
            )
        )

    gather(links, all_ref, work, lambda: wait_all(loads))
    total = share_stats(links, stat_ref, sq_ref[0], sq_ref[1])
    inv_ref[...] = lax.rsqrt(total / D + norm_eps).T
    wait_all(stores)


def summed(o_ref, final_buf, rows):
    return o_ref[rows] + jnp.concatenate(
        [
            final_buf[0, k, rows].astype(f32) + final_buf[1, k, rows].astype(f32)
            for k in range(SLICES)
        ],
        axis=1,
    )


def leave_out_kernel(
    y_ref, w_hbm, f1_ref, factors_ref, x_ref,
    lin_ref, low_ref, hidden_ref, all_ref,
    w_ref, out_buf, relay_buf, final_buf, send_sem, recv_sem, local_sem,
):
    links = Links(send_sem, recv_sem, local_sem)
    streams = Streams(links, None, load_out(links, w_hbm, w_ref))
    links.greet()

    def product(owner, k, cols):
        if k == 0:
            low_ref[owner] = lower(y_ref[owner], f1_ref[...])
        return mm(y_ref[owner], w_ref[:, cols]) + mm(low_ref[owner], factors_ref[OUT_B, cols])

    finish_all(
        scatter(
            links, product, lin_ref, out_buf, relay_buf, final_buf,
            ready=streams.ready,
        )
    )
    gain = factors_ref[GAIN0].astype(f32)

    @pl.loop(0, lin_ref.shape[0] // 16)
    def _(tile):
        rows = pl.ds(pl.multiple_of(tile * 16, 16), 16)
        value = summed(lin_ref, final_buf, rows)
        lin_ref[rows] = value
        hidden = x_ref[rows].astype(f32) + value * inverse_of(value) * gain
        hidden_ref[rows] = hidden
        all_ref[links.row, rows] = hidden.astype(bf16)

    gather(links, all_ref, None)


def flat_weight(ref):
    return ref[...].reshape(D, ref.shape[3])


def ffn_kernel(h_ref, wg_ref, wu_ref, factors_ref, fg_ref, fu_ref, low_ref, gate_ref, up_ref, act_ref):
    @pl.when(pl.program_id(0) == 0)
    def _():
        low_ref[...] = lower(h_ref[...], factors_ref[FFN_A])

    lowered = low_ref[...]
    rank = lowered.shape[1] // 2
    for at in range(0, SLAB, BLOCK):
        rows = slice(at, at + BLOCK)
        gate = mm(h_ref[rows], flat_weight(wg_ref)) + mm(lowered[rows], fg_ref[...])
        up = mm(h_ref[rows], flat_weight(wu_ref)) + mm(lowered[rows], fu_ref[...])
        gate_ref[rows] = gate.astype(bf16)
        up_ref[rows] = up.astype(bf16)
        act_ref[rows] = gated(gate, up).astype(bf16)


def ffn(h_all, w, factors, f2):
    width = f2.shape[1] // 2
    step = 256
    tiles = width // step
    low = jax.ShapeDtypeStruct((SLAB, f2.shape[0]), bf16)
    wide = jax.ShapeDtypeStruct((SLAB, width), bf16)
    whole = lambda value: pl.BlockSpec(value.shape, lambda t: (0, 0))
    cols = lambda rows, base: pl.BlockSpec((rows, step), lambda t: (0, base * tiles + t))
    block = (w.shape[0], 1, w.shape[2], step)
    part = lambda which: pl.BlockSpec(block, lambda t: (0, which, 0, t))
    return pl.pallas_call(
        ffn_kernel,
        grid=(tiles,),
        in_specs=[whole(h_all), part(0), part(1), whole(factors)]
        + [cols(f2.shape[0], 0), cols(f2.shape[0], 1)],
        out_specs=[whole(low)] + [cols(SLAB, 0)] * 3,
        out_shape=[low, wide, wide, wide],
        compiler_params=pltpu.CompilerParams(vmem_limit_bytes=48 << 20),
        cost_estimate=pl.CostEstimate(
            flops=4 * SLAB * D * width, bytes_accessed=4 * D * width + 10 * SLAB * width,
            transcendentals=SLAB * width,
        ),
        name="ffn",
    )(h_all, w, w, factors, f2, f2)


def leave_down_kernel(
    y_hbm, w_hbm, f1_ref, factors_ref, hidden_hbm, cot_ref,
    low_ref, out_ref, dm_ref, own_cot_ref,
    y_ref, w_ref, hidden_ref, lin_ref, out_buf, relay_buf, final_buf,
    send_sem, recv_sem, local_sem,
):
    links = Links(send_sem, recv_sem, local_sem)
    streams = Streams(
        links, (y_hbm, y_ref), load_down(links, w_hbm, w_ref), [(hidden_hbm, hidden_ref)]
    )
    links.greet(columns=True)
    turned = Exchange(links, "col", slot(cot_ref), features(own_cot_ref, cot_ref.shape[2]))
    turned.start()
    product = leave_product(
        y_ref, lambda rows, cols: mm(rows, w_ref[:, cols]), f1_ref[...], factors_ref, DOWN_B,
        low_ref, streams.rows,
    )
    finish_all(
        scatter(
            links, product, lin_ref, out_buf, relay_buf, final_buf,
            ready=streams.ready,
        )
    )
    turned.arrived()
    wait_all(streams.late)
    gain = factors_ref[GAIN1].astype(f32)

    @pl.loop(0, lin_ref.shape[0] // 16)
    def _(tile):
        rows = pl.ds(pl.multiple_of(tile * 16, 16), 16)
        value = summed(lin_ref, final_buf, rows)
        out_ref[rows] = (hidden_ref[rows] + value * inverse_of(value) * gain).astype(bf16)
        dm_ref[rows] = norm_back(value, own_cot_ref[rows].astype(f32) * gain).astype(bf16)

    turned.sent()


def widen(source_ref, target_ref):
    @pl.loop(0, source_ref.shape[0] // 64)
    def _(tile):
        rows = pl.ds(pl.multiple_of(tile * 64, 64), 64)
        target_ref[rows] = source_ref[rows].astype(f32)


def back_down_kernel(
    dm_ref, w_hbm, factors_ref, f2_ref, gate_hbm, up_hbm, out_ref,
    all_hbm, low_ref, grad_hbm, out_mid_ref,
    all_ref, w_ref, gate_ref, up_ref, grad_ref, send_sem, recv_sem, local_sem,
):
    links = Links(send_sem, recv_sem, local_sem)
    loads = start_all(sum(load_down(links, w_hbm, w_ref), []))
    order = (links.row, links.xn, links.yn, links.dg)
    gates = [
        links.plan((gate_hbm.at[k], gate_ref.at[k]), (up_hbm.at[k], up_ref.at[k])) for k in order
    ]
    start_all(gates[0])
    all_ref[links.row] = dm_ref[...]
    links.greet(columns=True)
    width = w_ref.shape[0]
    turned = Exchange(links, "col", features(out_ref, out_mid_ref.shape[2]), slot(out_mid_ref))
    stores = []

    def before():
        turned.start()
        wait_all(loads)
        for gate in gates[1:]:
            start_all(gate)

    def work(owner):
        wait_all(gates[len(stores) // 2])
        lowered = lower(all_ref[owner], factors_ref[DOWN_B])
        low_ref[owner] = lowered

        def body(at):
            cols, far = pl.ds(at, TILE), pl.ds(pl.multiple_of(width + at, TILE), TILE)
            grad = mm_nt(all_ref[owner], w_ref[cols, :]) + mm(lowered, f2_ref[:, cols])
            gate, up = gate_ref[owner, :, cols].astype(f32), up_ref[owner, :, cols].astype(f32)
            grad_gate, grad_up = gated_back(grad, gate, up)
            grad_ref[owner, :, cols] = grad_gate.astype(bf16)
            grad_ref[owner, :, far] = grad_up.astype(bf16)

        each_tile(width, TILE, body)
        stores.extend(
            links.fetch(
                (grad_ref.at[owner], grad_hbm.at[owner]), (all_ref.at[owner], all_hbm.at[owner])
            )
        )

    gather(links, all_ref, work, before)
    turned.arrived()
    turned.sent()
    wait_all(stores)


def back_ffn_kernel(
    y_hbm, w_hbm, f1_ref, factors_ref, cot_hbm, attn_hbm,
    low_ref, hidden_ref, da_ref,
    y_ref, w_ref, cot_ref, attn_ref, lin_ref, out_buf, relay_buf, final_buf,
    send_sem, recv_sem, local_sem,
):
    links = Links(send_sem, recv_sem, local_sem)
    streams = Streams(
        links,
        (y_hbm, y_ref),
        load_ffn(links, w_hbm, w_ref),
        [(cot_hbm, cot_ref), (attn_hbm, attn_ref)],
    )
    links.greet()
    product = leave_product(
        y_ref, lambda rows, cols: mm_nt(rows, w_ref[cols, :]), f1_ref[...], factors_ref, FFN_A,
        low_ref, streams.rows,
    )
    finish_all(
        scatter(
            links, product, lin_ref, out_buf, relay_buf, final_buf,
            ready=streams.ready,
        )
    )
    wait_all(streams.late)
    gain = factors_ref[GAIN0].astype(f32)

    @pl.loop(0, lin_ref.shape[0] // 16)
    def _(tile):
        rows = pl.ds(pl.multiple_of(tile * 16, 16), 16)
        value = summed(lin_ref, final_buf, rows) + cot_ref[rows].astype(f32)
        hidden_ref[rows] = value
        da_ref[rows] = norm_back(attn_ref[rows], value * gain).astype(bf16)


def mm_tn(left, right):
    return lax.dot_general(left, right, (((0,), (0,)), ((), ())), preferred_element_type=f32)


def back_out_kernel(
    da_ref, w_hbm, factors_ref, f2_ref, out_low_ref, attn_ref, down_low_ref, down_dlow_ref,
    ffn_low_ref, ffn_dlow_ref, dm_hbm, act_hbm, grad_hbm, h_hbm,
    heads_ref, cols_ref, rows_ref,
    all_ref, low_ref, w_ref, dm_ref, act_ref, grad_ref, h_ref, raise_ref, lower_ref, send_sem, recv_sem, local_sem,
):
    links = Links(send_sem, recv_sem, local_sem)
    load = start_all(sum(load_out(links, w_hbm, w_ref), []))
    all_ref[links.row] = da_ref[...]
    links.greet()
    loads = []

    def before():
        loads.extend(
            links.fetch((dm_hbm, dm_ref), (act_hbm, act_ref), (grad_hbm, grad_ref), (h_hbm, h_ref))
        )
        wait_all(load)

    heads, half = heads_ref.shape[2], grad_ref.shape[1] // 2

    def after():
        wait_all(loads)
        down_raise = mm_tn(down_low_ref[...], dm_ref[...])
        cols_ref[3 * RANK : 4 * RANK] = down_raise.astype(bf16)
        cols_ref[RANK : 3 * RANK] = mm_tn(ffn_dlow_ref[...], h_ref[...]).astype(bf16)
        both = mm_tn(ffn_low_ref[...], grad_ref[...]).astype(bf16)
        rows_ref[:, heads : heads + half] = both[:RANK, :half]
        rows_ref[:, heads + half : heads + 2 * half] = both[RANK:, half:]
        rows_ref[:, heads + 2 * half :] = mm_tn(down_dlow_ref[...], act_ref[...]).astype(bf16)

    def work(owner):
        lowered = lower(all_ref[owner], factors_ref[OUT_B])
        low_ref[owner] = lowered
        value = mm_nt(all_ref[owner], w_ref[...]) + mm(lowered, f2_ref[...])
        heads_ref[owner] = value.astype(bf16)
        raise_ref[...] += mm_tn(out_low_ref[owner], all_ref[owner])
        lower_ref[...] += mm_tn(low_ref[owner], attn_ref[owner])

    raise_ref[...] = jnp.zeros_like(raise_ref)
    lower_ref[...] = jnp.zeros_like(lower_ref)
    gather(links, all_ref, work, before, after)
    cols_ref[0:RANK] = raise_ref[...].astype(bf16)
    rows_ref[:, :heads] = lower_ref[...].astype(bf16)


def prepare_kernel(
    wq_hbm, wk_hbm, dv_ref, lin_hbm, inv_ref, inner_ref, f1_ref, low_ref, early_ref,
    grad_ref, dlow_ref, rows_ref,
    wq_ref, wk_ref, lin_ref, total_ref, stat_ref, send_sem, recv_sem, local_sem,
):
    links = Links(send_sem, recv_sem, local_sem)
    third = wq_ref.shape[1]
    loads = links.fetch(
        (wq_hbm, wq_ref),
        (wk_hbm, wk_ref),
        (lin_hbm.at[:, pl.ds(0, 2 * third)], lin_ref),
    )
    links.greet(rows=3)
    total = share_stats(links, stat_ref, inner_ref[0], inner_ref[1])
    total_ref[...] = total.T / D
    wait_all(loads)

    @pl.loop(0, SLAB // 96)
    def _(tile):
        rows = pl.ds(pl.multiple_of(tile * 96, 96), 96)
        inverse = inv_ref[rows]
        factor = inverse**3 * total_ref[rows]
        for index, source in enumerate((wq_ref, wk_ref)):
            cols = slice(index * third, (index + 1) * third)
            one = slice(index, index + 1)
            value = inverse[:, one] * source[rows] - lin_ref[rows, cols] * factor[:, one]
            grad_ref[rows, cols] = value.astype(bf16)
        grad_ref[rows, 2 * third :] = dv_ref[rows]

    dlow_ref[...] = lower(grad_ref[...], f1_ref[...])
    for index in range(3):
        cols = slice(index * third, (index + 1) * third)
        low = low_ref[:, index * RANK : (index + 1) * RANK]
        rows_ref[:, cols] = mm_tn(low, grad_ref[:, cols]).astype(bf16)
    rows_ref[:, 3 * third :] = early_ref[...]


def back_qkv_kernel(
    grad_ref, dlow_ref, w_hbm, factors_ref, hidden_hbm, x_hbm, early_ref, chosen_ref,
    final_ref, sums_ref,
    w_ref, hidden_ref, x_ref, sum_ref, own_ref, middle_ref, turn_buf, parts_ref, got_ref, total_ref, groups_ref,
    placed_ref, out_buf, relay_buf, final_buf, send_sem, recv_sem, local_sem,
):
    links = Links(send_sem, recv_sem, local_sem)
    steps = (2, 3, 1, 0)
    streams = Streams(
        links,
        None,
        load_qkv(links, w_hbm, w_ref, [links.col ^ step for step in steps]),
        [(hidden_hbm, hidden_ref)],
    )
    x_load = links.fetch((x_hbm, x_ref))
    links.greet(rows=3, columns=True, twin=True)
    width = own_ref.shape[2]
    count = grad_ref.shape[1]
    by_row = Exchange(links, "row", slot(parts_ref), slot(got_ref))
    base = 4 * links.tok
    by_col = Exchange(
        links, "col", slot(total_ref), lambda key: groups_ref.at[base + key]
    )
    index = links.take(1)
    mine, theirs = groups_ref.at[pl.ds(base, 4)], groups_ref.at[pl.ds(4 - base, 4)]
    to_twin = links.copy(mine, mine, index, index, links.row, tok=links.tok ^ 1)
    from_twin = links.copy(theirs, theirs, index, index, links.row, tok=links.tok ^ 1)
    spread = Exchange(links, "row", lambda key: placed_ref, slot(sums_ref))

    def lower_grad():
        wait_all(x_load)
        late = 0.0
        for owner in range(4):
            late = late + mm_tn(dlow_ref[owner], x_ref[owner])
        late = late.astype(bf16)
        parts_ref[0] = late[0 : 2 * RANK]
        parts_ref[1, :RANK] = late[2 * RANK :]
        parts_ref[1, RANK:] = early_ref[:RANK]
        parts_ref[2] = early_ref[RANK : 3 * RANK]
        parts_ref[3, :RANK] = early_ref[3 * RANK :]
        parts_ref[3, RANK:] = jnp.zeros((RANK, D), bf16)
        by_row.start()

    def add_rows():
        by_row.arrived()
        for f in range(4):
            cols = slice(f * width, (f + 1) * width)
            value = got_ref[0, :, cols].astype(f32)
            for q in range(1, 4):
                value = value + got_ref[q, :, cols].astype(f32)
            total_ref[f] = value.astype(bf16)
        by_col.start()

    def share():
        by_col.arrived()
        to_twin.start()

    def place_groups():
        from_twin.wait_recv()
        for half in range(2):
            rows = slice(half * RANK, (half + 1) * RANK)
            values = [groups_ref[g, rows].astype(f32) for g in range(8)]
            for adapter in range(ADAPTERS):
                value = 0.0
                for g in range(8):
                    value = value + chosen_ref[2 * links.row + half, adapter * 8 + g] * values[g]
                placed_ref[adapter, rows] = value.astype(bf16)
        spread.start()

    def product(owner, k, cols):
        value = mm_nt(grad_ref[owner], w_ref[cols, :])
        return value + mm(dlow_ref[owner], factors_ref[QKV_A, cols])

    z_base, row_base = links.take(3), links.take(4)
    near = links.local(middle_ref.at[links.row], token_rows(turn_buf, count)(links.row))
    z_copies = []

    def leave_col(k, columns, finish):
        finish(k)
        cols, step = columns(k), steps[k]
        value = (
            sum_ref[:, cols]
            + final_buf[0, k].astype(f32)
            + final_buf[1, k].astype(f32)
            + hidden_ref[:, cols]
        ).astype(bf16)
        if step == 0:
            middle_ref[links.col] = value
            return
        own_ref[k] = value
        at = z_base + k
        copy = links.copy(
            own_ref.at[k], middle_ref.at[links.col], at, at, links.row, links.col ^ step
        )
        copy.start()
        z_copies.append(copy)

    def to_row(step):
        other = links.row ^ step
        return links.copy(
            middle_ref.at[other],
            token_rows(turn_buf, count)(links.row),
            row_base + step,
            row_base + step,
            other,
        )

    def leave_row(k):
        source = links.col ^ steps[k]
        if steps[k]:
            at = z_base + k
            landed = middle_ref.at[source]
            links.copy(landed, landed, at, at, links.row, source).wait_recv()
        step = links.row ^ source

        @pl.when(step == 0)
        def _():
            near.start()

        @pl.when(step != 0)
        def _():
            to_row(step).start()

    def second(columns, finish):
        add_rows()

    def third(columns, finish):
        share()
        wait_all(streams.late)
        leave_col(0, columns, finish)

    def fourth(columns, finish):
        place_groups()
        leave_col(1, columns, finish)

    columns, finish, sent = scatter(
        links, product, sum_ref, out_buf, relay_buf, final_buf,
        block=lambda k: links.col ^ steps[k],
        ready=streams.ready,
        hooks=[lambda columns, finish: lower_grad(), second, third, fourth],
    )
    leave_row(0)
    leave_col(2, columns, finish)
    leave_row(1)
    leave_col(3, columns, finish)
    leave_row(3)
    leave_row(2)
    near.wait()
    for step in range(1, 4):
        landed = token_rows(turn_buf, count)(links.row ^ step)
        at = row_base + step
        links.copy(landed, landed, at, at, links.row ^ step).wait_recv()
    widen(turn_buf, final_ref)
    spread.arrived()
    for step in range(1, 4):
        to_row(step).wait_send()
    for copy in z_copies:
        copy.wait_send()
    to_twin.wait_send()
    for exchange in (by_row, by_col, spread):
        exchange.sent()
    sent()


VMEM = pl.BlockSpec(memory_space=pltpu.VMEM)
ANY = pl.BlockSpec(memory_space=pl.ANY)
SMEM = pl.BlockSpec(memory_space=pltpu.SMEM)


def linked(kernel, number, operands, outs, scratch, flops):
    specs = [ANY if isinstance(value, tuple) else VMEM for value in operands]
    values = [value[0] if isinstance(value, tuple) else value for value in operands]
    specs = [
        SMEM if value.ndim == 2 and value.shape[0] == 8 and value.dtype != bf16 else spec
        for spec, value in zip(specs, values)
    ]
    return pl.pallas_call(
        kernel,
        in_specs=specs,
        out_specs=[ANY if len(out) == 3 else VMEM for out in outs],
        out_shape=[jax.ShapeDtypeStruct(out[0], out[1]) for out in outs],
        scratch_shapes=[pltpu.VMEM(shape, kind) for shape, kind in scratch]
        + [
            pltpu.SemaphoreType.DMA((48,)),
            pltpu.SemaphoreType.DMA((48,)),
            pltpu.SemaphoreType.DMA((48,)),
        ],
        compiler_params=pltpu.CompilerParams(
            collective_id=number, has_side_effects=True, vmem_limit_bytes=60 << 20
        ),
        cost_estimate=pl.CostEstimate(
            flops=flops, bytes_accessed=flops // 400, transcendentals=0
        ),
        name=kernel.__name__,
    )(*values)


def scatter_buffers(count):
    part = D // SLICES
    return [
        ((3, SLICES, count, part), bf16),
        ((2, SLICES, count // 2, part), bf16),
        ((2, SLICES, count, part), bf16),
    ]


def score_blocks(k_ref, q_block, bias_ref, start, stop):
    parts = []
    if start:
        parts.append(mm_nt(k_ref[0:start], q_block) + bias_ref[0:start])
    own = mm_nt(k_ref[start:stop], q_block) + bias_ref[start:stop]
    keys = lax.broadcasted_iota(jnp.int32, own.shape, 0)
    queries = lax.broadcasted_iota(jnp.int32, own.shape, 1)
    parts.append(jnp.where(keys <= queries, own, very_low))
    return parts

def attend_kernel(q_ref, k_ref, v_ref, inv_ref, gain_ref, cos_ref, sin_ref, bias_ref,
                  ql_ref, kl_ref, vl_ref, o_ref, lse_ref):
    for source, target, index in ((q_ref, ql_ref, 0), (k_ref, kl_ref, 1)):
        normed = source[...] * inv_ref[:, index:index+1] * gain_ref[index:index+1, :]
        target[...] = (normed * cos_ref[...] + pltpu.roll(normed, HEAD_DIM // 2, 1) * sin_ref[...]).astype(bf16)
    values = v_ref[...].astype(bf16)
    vl_ref[...] = values
    values_t = v_ref[...].T.astype(bf16)
    for start in range(0, SLAB, BLOCK):
        stop = start + BLOCK
        parts = score_blocks(kl_ref, ql_ref[start:stop], bias_ref, start, stop)
        top = functools.reduce(jnp.maximum, [jnp.max(p, axis=0, keepdims=True) for p in parts]) * log2_scale
        total, out, at = 0.0, 0.0, 0
        for part in parts:
            shifted = jnp.exp2(part * log2_scale - top)
            total = total + jnp.sum(shifted, axis=0, keepdims=True)
            out = out + mm(values_t[:, at:at+part.shape[0]], shifted.astype(bf16))
            at += part.shape[0]
        o_ref[start:stop] = (out / total).T.astype(bf16)
        lse_ref[0, :, start:stop] = top + jnp.log2(total)

def attend_back_kernel(ql_ref, kl_ref, vl_ref, o_ref, do_ref, lse_ref, q_ref, k_ref, gain_ref, cos_ref, sin_ref, bias_ref, *refs):
    mid_ref, wq_ref, wk_ref, dv_ref, sum_ref, turn_ref, dk_sum, dv_sum, *sems = refs if len(refs) > 8 else (None, *refs[:4], None, *refs[4:])
    if sems:
        links = Links(*sems)
        turned = Exchange(links, "row", slot(mid_ref), token_rows(turn_ref, mid_ref.shape[1]))

        @pl.when(pl.program_id(0) == 0)
        def _():
            links.greet(rows=3)
            turned.start()

    keys_t = kl_ref[...].astype(f32).T.astype(bf16)
    delta_all = jnp.sum((do_ref[...].astype(f32) * o_ref[...].astype(f32)).T, axis=0, keepdims=True)
    dk_sum[...] = jnp.zeros_like(dk_sum)
    dv_sum[...] = jnp.zeros_like(dv_sum)
    def unrotate(values):
        return values * cos_ref[...] - pltpu.roll(values, HEAD_DIM // 2, 1) * sin_ref[...]
    dq_parts = []
    for start in range(0, SLAB, BLOCK):
        stop = start + BLOCK
        queries, grads = ql_ref[start:stop], do_ref[start:stop]
        parts = score_blocks(kl_ref, queries, bias_ref, start, stop)
        lse, delta = lse_ref[0, :, start:stop], delta_all[:, start:stop]
        at, dq = 0, 0.0
        for part in parts:
            span = slice(at, at + part.shape[0])
            probs = jnp.exp2(part * log2_scale - lse)
            dv_sum[span] += mm(probs.astype(bf16), grads)
            dscore = (probs * (mm_nt(vl_ref[span], grads) - delta)).astype(bf16)
            dk_sum[span] += mm(dscore, queries)
            dq = dq + mm(keys_t[:, span], dscore)
            at += part.shape[0]
        dq_parts.append(dq.T)
    dq_all = jnp.concatenate(dq_parts, axis=0) * score_scale
    dv_ref[...] = dv_sum[...].astype(bf16)
    wq = unrotate(dq_all) * gain_ref[0:1, :]
    wk = unrotate(dk_sum[...] * score_scale) * gain_ref[1:2, :]
    wq_ref[...] = wq.astype(wq_ref.dtype)
    wk_ref[...] = wk.astype(wk_ref.dtype)
    first = pl.program_id(0) == 0
    for index, (weighted, source) in enumerate(((wq, q_ref), (wk, k_ref))):
        product = weighted * source[...]

        @pl.when(first)
        def _():
            sum_ref[index] = product

        @pl.when(jnp.logical_not(first))
        def _():
            sum_ref[index] += product

    if sems:

        @pl.when(pl.program_id(0) == pl.num_programs(0) - 1)
        def _():
            turned.arrived()
            turned.sent()


def attend_specs(heads):
    col = lambda base: pl.BlockSpec((SLAB, HEAD_DIM), lambda h: (0, base * heads + h))
    whole = lambda shape: pl.BlockSpec(shape, lambda h: (0,) * len(shape))
    return col, whole

def attend(qkv_lin, inverses, gains, cosine, sine, bias):
    heads = qkv_lin.shape[1] // (3 * HEAD_DIM)
    col, whole = attend_specs(heads)
    low = jax.ShapeDtypeStruct((SLAB, heads * HEAD_DIM), bf16)
    return pl.pallas_call(
        attend_kernel, grid=(heads,),
        in_specs=[col(0), col(1), col(2), whole((SLAB, 8)), pl.BlockSpec((2, HEAD_DIM), lambda h: (0, h)),
                  whole((SLAB, HEAD_DIM)), whole((SLAB, HEAD_DIM)), whole((SLAB, 1))],
        out_specs=[col(0)] * 4 + [pl.BlockSpec((1, 1, SLAB), lambda h: (h, 0, 0))],
        out_shape=[low] * 4 + [jax.ShapeDtypeStruct((heads, 1, SLAB), f32)],
        compiler_params=pltpu.CompilerParams(vmem_limit_bytes=48 << 20),
        cost_estimate=pl.CostEstimate(flops=heads*4*SLAB*SLAB*HEAD_DIM, bytes_accessed=heads*SLAB*HEAD_DIM*20, transcendentals=heads*SLAB*SLAB),
        name="attend",
    )(qkv_lin, qkv_lin, qkv_lin, inverses, gains, cosine, sine, bias)

def attend_back(ql, kl, vl, o, do, lse, qkv_lin, gains, cosine, sine, bias, middle=None):
    heads = ql.shape[1] // HEAD_DIM
    col, whole = attend_specs(heads)
    wide = jax.ShapeDtypeStruct(ql.shape, f32)
    outs = [wide, wide, jax.ShapeDtypeStruct(ql.shape, bf16)]
    outs.append(jax.ShapeDtypeStruct((2, SLAB, HEAD_DIM), f32))
    moved, turned, params, sems = [], [], dict(vmem_limit_bytes=48 << 20), []
    if middle is not None:
        moved, turned = [middle], [jax.ShapeDtypeStruct((SLAB, middle.shape[2]), bf16)]
        params.update(collective_id=10, has_side_effects=True)
        sems = [pltpu.SemaphoreType.DMA((4,))] * 3
    hbm = pl.BlockSpec(memory_space=pl.ANY)
    return pl.pallas_call(
        attend_back_kernel,
        grid=(heads,),
        in_specs=[col(0)] * 5
        + [pl.BlockSpec((1, 1, SLAB), lambda h: (h, 0, 0)), col(0), col(1)]
        + [pl.BlockSpec((2, HEAD_DIM), lambda h: (0, h))]
        + [whole((SLAB, HEAD_DIM)), whole((SLAB, HEAD_DIM)), whole((SLAB, 1))]
        + [hbm] * len(moved),
        out_specs=[col(0)] * 3 + [whole((2, SLAB, HEAD_DIM))] + [hbm] * len(turned),
        out_shape=outs + turned,
        scratch_shapes=[pltpu.VMEM((SLAB, HEAD_DIM), f32)] * 2 + sems,
        compiler_params=pltpu.CompilerParams(**params),
        cost_estimate=pl.CostEstimate(
            flops=heads * 10 * SLAB * SLAB * HEAD_DIM,
            bytes_accessed=heads * SLAB * HEAD_DIM * 30,
            transcendentals=heads * SLAB * SLAB,
        ),
        name="attend_back",
    )(ql, kl, vl, o, do, lse, qkv_lin, qkv_lin, gains, cosine, sine, bias, *moved)


def dot(left, right):
    return jnp.dot(left, right, preferred_element_type=f32)


def dot_nt(left, right):
    return lax.dot_general(left, right, (((1,), (1,)), ((), ())), preferred_element_type=f32)


def dot_tn(left, right):
    return lax.dot_general(left, right, (((0,), (0,)), ((), ())), preferred_element_type=f32)


def gather_weight(local):
    half = local.shape[0] // lax.axis_size("tok")
    part = lax.dynamic_slice_in_dim(local, lax.axis_index("tok") * half, half, 0)
    return lax.all_gather(part, ("col", "tok"), axis=0, tiled=True)


def to_tokens(values):
    rows, cols = lax.axis_size("row"), lax.axis_size("col")
    width = values.shape[1]
    mixed = lax.all_to_all(values, "row", 0, 0, tiled=True)
    mixed = lax.all_to_all(mixed, "col", 0, 0, tiled=True)
    return mixed.reshape(cols, SLAB // rows, width).transpose(1, 0, 2).reshape(SLAB // rows, -1)


def from_tokens(values):
    rows, cols = lax.axis_size("row"), lax.axis_size("col")
    count = values.shape[0]
    mixed = values.reshape(count, cols, -1).transpose(1, 0, 2).reshape(cols * count, -1)
    mixed = lax.all_to_all(mixed, "col", 0, 0, tiled=True)
    return lax.all_to_all(mixed, "row", 0, 0, tiled=True)


def reorder(values, outer, inner):
    if outer == 1 or inner == 1:
        return values
    rest = values.shape[0] // (outer * inner)
    shape = (outer, inner, rest) + values.shape[1:]
    return values.reshape(shape).swapaxes(0, 1).reshape(values.shape)


def gather_tokens(values):
    rows, per_slab = lax.axis_size("row"), lax.axis_size("row") // lax.axis_size("col")
    return reorder(lax.all_gather(values, "row", axis=0, tiled=True), rows, per_slab)


def scatter_tokens(values):
    rows, per_slab = lax.axis_size("row"), lax.axis_size("row") // lax.axis_size("col")
    values = reorder(values.astype(bf16), per_slab, rows)
    return lax.psum_scatter(values, "row", scatter_dimension=0, tiled=True).astype(f32)


def token_places(length):
    slot_ids = jnp.arange(SLAB, dtype=jnp.int32)
    return jnp.where(slot_ids < PROMPT, slot_ids, length + (slot_ids - PROMPT) % CONT_LEN)


def rotation(places, head_size):
    half_dim = head_size // 2
    frequency = jnp.exp(
        -(2.0 * jnp.arange(half_dim, dtype=f32) / head_size) * math.log(rope_base)
    )
    angles = places.astype(f32)[:, None] * frequency[None, :]
    return (jnp.cos(angles), jnp.sin(angles))


def pick(adapters, ids):
    onehot = (ids[:, None] == jnp.arange(adapters.shape[0], dtype=jnp.int32)).astype(adapters.dtype)
    return jnp.tensordot(onehot, adapters, axes=1)


def place(ids, gradients):
    onehot = (jnp.arange(ADAPTERS, dtype=jnp.int32)[:, None] == ids[None, :]).astype(f32)
    total = 0.0
    for index in range(gradients.shape[0]):
        weight = onehot[:, index].reshape((ADAPTERS,) + (1,) * (gradients.ndim - 1))
        total = total + weight * gradients[index][None].astype(f32)
    return total


def block_diagonal(factors):
    count = len(factors)
    lines = []
    for index, factor in enumerate(factors):
        blank = jnp.zeros_like(factor)
        lines.append(
            jnp.concatenate([factor if k == index else blank for k in range(count)], axis=1)
        )
    return jnp.concatenate(lines, axis=0)


def enter(x, w, f1, f2):
    everything = gather_tokens(x)
    lowered = (adapter_scale * dot_nt(everything, f1)).astype(bf16)
    return everything, lowered, dot(everything, w) + dot(lowered, f2)


def leave(y, w, f1, f2):
    lowered = (adapter_scale * dot_nt(y, f1)).astype(bf16)
    return scatter_tokens(dot_nt(y, w) + dot(lowered, f2)), lowered


def split_layer(
    layer_in, cotangent, qkv_weight, out_weight, ffn_weight, down_weight, head_gain, post_gain,
    adapters, adapter_ids, tables,
):
    qkv_lower, out_raise, ffn_lower, down_raise, qkv_raise, out_lower, ffn_raise, down_lower = (
        adapters
    )
    col_count = lax.axis_size("col")
    group_base = lax.axis_index("tok") * col_count
    group = group_base + lax.axis_index("col")
    slab_ids = lax.dynamic_slice_in_dim(adapter_ids, group_base, col_count, 0)
    own_ids = lax.dynamic_index_in_dim(adapter_ids, group, 0, keepdims=False)
    size = layer_in.shape[1]
    local = jnp.concatenate([qkv_weight.transpose(1, 0, 2).reshape(size, -1), out_weight.T], axis=1)
    attn_full = gather_weight(local)
    ffn_full = gather_weight(ffn_weight.transpose(1, 0, 2).reshape(size, -1))
    down_full = gather_weight(down_weight.T)
    pieces = jnp.concatenate(
        [pick(qkv_lower[p], slab_ids[:, p]) for p in range(3)]
        + [pick(out_raise, slab_ids[:, 3])]
        + [pick(ffn_lower[p], slab_ids[:, 4 + p]) for p in range(2)]
        + [pick(down_raise, slab_ids[:, 6])]
        + [jnp.broadcast_to(jnp.pad(post_gain, ((0, 14), (0, 0))), (col_count, RANK, size))],
        axis=1,
    )
    qkv_b = block_diagonal([pick(qkv_raise[p], own_ids[p : p + 1])[0] for p in range(3)])
    out_a = pick(out_lower, own_ids[3:4])[0]
    ffn_b = block_diagonal([pick(ffn_raise[p], own_ids[4 + p : 5 + p])[0] for p in range(2)])
    down_a = pick(down_lower, own_ids[6:7])[0]
    factors = lax.all_to_all(pieces, "col", 0, 0, tiled=True)
    factors = factors.transpose(1, 0, 2).reshape(-1, D)
    qkv_a, out_b, ffn_a, down_b = (factors[part] for part in (QKV_A, OUT_B, FFN_A, DOWN_B))
    gains = factors[GAIN0.start : GAIN1.stop].astype(f32)
    width = qkv_b.shape[1]
    head_width, ff_width = width // 3, ffn_b.shape[1] // 2
    x_own = to_tokens(layer_in)
    x_all, qkv_low, qkv_lin = enter(x_own, attn_full[:, :width], qkv_a, qkv_b)
    q_lin, k_lin = qkv_lin[:, :head_width], qkv_lin[:, head_width : 2 * head_width]
    squares = jnp.stack([jnp.sum(q_lin * q_lin, axis=1), jnp.sum(k_lin * k_lin, axis=1)], axis=1)
    inverses = lax.rsqrt(lax.psum(squares, "row") / D + norm_eps)
    inverses = jnp.concatenate([inverses] * 4, axis=1)
    q_low, k_low, v_low, attn_low, log_sums = attend(qkv_lin, inverses, head_gain, *tables)
    attn_lin, out_low = leave(attn_low, attn_full[:, width:], out_a, out_b)
    hidden = x_own.astype(f32) + attn_lin * inverse_of(attn_lin) * gains[0]
    h_all, ffn_low, ffn_lin = enter(hidden.astype(bf16), ffn_full, ffn_a, ffn_b)
    gate_lin, up_lin = ffn_lin[:, :ff_width], ffn_lin[:, ff_width:]
    act_low = gated(gate_lin, up_lin).astype(bf16)
    mlp_lin, down_low = leave(act_low, down_full, down_a, down_b)
    layer_out = hidden + mlp_lin * inverse_of(mlp_lin) * gains[1]
    layer_out = from_tokens(layer_out.astype(bf16)).astype(f32)
    grad_out = to_tokens(cotangent).astype(f32)
    grad_mlp = norm_back(mlp_lin, grad_out * gains[1]).astype(bf16)
    dm_all, down_dlow, grad_act = enter(grad_mlp, down_full, down_b, down_a)
    grad_ffn = jnp.concatenate(gated_back(grad_act, gate_lin, up_lin), axis=1).astype(bf16)
    grad_ffn_in, ffn_dlow = leave(grad_ffn, ffn_full, ffn_b, ffn_a)
    grad_hidden = grad_out + grad_ffn_in
    grad_attn = norm_back(attn_lin, grad_hidden * gains[0]).astype(bf16)
    da_all, out_dlow, grad_heads = enter(grad_attn, attn_full[:, width:], out_b, out_a)
    weighted_q, weighted_k, grad_v, inner = attend_back(
        q_low, k_low, v_low, attn_low, grad_heads.astype(bf16), log_sums, qkv_lin, head_gain, *tables
    )
    inner = lax.psum(jnp.sum(inner, axis=2).T, "row")
    factor = inverses[:, :2] ** 3 * inner / D
    grad_qkv = jnp.concatenate(
        [
            (inverses[:, 0:1] * weighted_q - q_lin * factor[:, 0:1]).astype(bf16),
            (inverses[:, 1:2] * weighted_k - k_lin * factor[:, 1:2]).astype(bf16),
            grad_v,
        ],
        axis=1,
    )
    grad_qkv_in, qkv_dlow = leave(grad_qkv, attn_full[:, :width], qkv_b, qkv_a)
    grad_in = from_tokens((grad_hidden + grad_qkv_in).astype(bf16)).astype(f32)
    parts = jnp.concatenate(
        [dot_tn(qkv_dlow, x_all), dot_tn(out_low, da_all), dot_tn(ffn_dlow, h_all)]
        + [dot_tn(down_low, dm_all)]
    )
    parts = parts.astype(bf16).reshape(7, RANK, col_count, size).transpose(2, 0, 1, 3)
    parts = lax.all_to_all(parts, "col", 0, 0, tiled=True)
    placed = [place(slab_ids[:, p], parts[:, p]) for p in range(7)]
    col_grads = list(lax.psum(jnp.stack(placed).astype(bf16), ("tok", "row")).astype(f32))
    own_rows = jnp.concatenate(
        [diagonal(dot_tn(qkv_low, grad_qkv), 3), dot_tn(out_dlow, attn_low)]
        + [diagonal(dot_tn(ffn_low, grad_ffn), 2), dot_tn(down_dlow, act_low)],
        axis=1,
    )
    every = lax.all_gather(own_rows.astype(bf16), ("tok", "col"), axis=0)
    row_grads, at = [], 0
    for p in range(7):
        part = ff_width if p > 3 else head_width
        row_grads.append(place(adapter_ids[:, p], every[:, :, at : at + part]))
        at += part
    return layer_out, grad_in, col_grads, row_grads


def flat(values):
    return values.reshape((SLAB,) + values.shape[2:])


def cube(values):
    return values.reshape((4, SLAB // 4) + values.shape[1:])


def linked_layer(
    layer_in, cotangent, qkv_weight, out_weight, ffn_weight, down_weight, head_gain, post_gain,
    adapters, adapter_ids, tables,
):
    count = SLAB // 4
    piece = (4, count, layer_in.shape[1])
    head_width, ff_width = qkv_weight.shape[2], ffn_weight.shape[2]
    width = 3 * head_width
    buffers = scatter_buffers(count)
    per = 2 * SLAB * D
    tokens = ((4, count, D), bf16)
    own = ((count, D), bf16)
    wide = ((count, D), f32)

    def low_rows(size):
        return ((4, count, size), bf16)

    def gather_halves(local, axis):
        half = local.shape[axis] // 2
        return lax.dynamic_slice_in_dim(local, lax.axis_index("tok") * half, half, axis)

    def gathered(local):
        return lax.all_gather(local, ("col", "tok"), axis=0)

    attn_full = gathered(
        jnp.concatenate(
            [gather_halves(qkv_weight, 1).reshape(-1, head_width), gather_halves(out_weight, 0)]
        )
    )
    ffn_full = gathered(gather_halves(ffn_weight, 1))
    down_full = gathered(gather_halves(down_weight, 0))

    x_own, cot_mid, factors, qkv_b, out_a, ffn_b, down_a = linked(
        intake_kernel, 1,
        [(cube(layer_in),), (cube(cotangent),), adapter_ids]
        + [jnp.pad(post_gain, ((0, RANK - 2), (0, 0)))]
        + adapters,
        [own, (piece, bf16), ((128, D), bf16), ((48, width), bf16), ((16, head_width), bf16)]
        + [((32, 2 * ff_width), bf16), ((16, ff_width), bf16)],
        [(piece, bf16), ((4, 128, piece[2]), bf16)],
        per * 128,
    )
    x_all, qkv_low, qkv_lin, inverses = linked(
        enter_qkv_kernel, 2,
        [x_own, (attn_full,), factors, qkv_b],
        [tokens + (ANY,), low_rows(48), ((4, count, width), f32, ANY), ((SLAB, 8), f32)],
        [tokens, ((4, count, width), f32), ((D, width), bf16), ((2, SLAB, 128), f32)]
        + [((4, 8, SLAB), f32)],
        per * width,
    )
    qkv_lin = flat(qkv_lin)
    q_low, k_low, v_low, attn_low, log_sums = attend(qkv_lin, inverses, head_gain, *tables)
    attn_lin, out_low, hidden, h_all = linked(
        leave_out_kernel, 3,
        [cube(attn_low), (attn_full,), out_a, factors, x_own],
        [wide, low_rows(16), wide, tokens],
        [((head_width, D), bf16)] + buffers,
        per * head_width,
    )
    h_all = flat(h_all)
    ffn_low, gate_lin, up_lin, act_low = ffn(h_all, ffn_full, factors, ffn_b)
    down_low, own_out, grad_mlp, own_cot = linked(
        leave_down_kernel, 4,
        [(cube(act_low),), (down_full,), down_a, factors, (hidden,), cot_mid],
        [low_rows(16), own, own, own],
        [((4, count, ff_width), bf16), ((ff_width, D), bf16), wide, wide] + buffers,
        per * ff_width,
    )
    dm_all, down_dlow, grad_ffn, out_mid = linked(
        back_down_kernel, 5,
        [grad_mlp, (down_full,), factors, down_a, (cube(gate_lin),), (cube(up_lin),), own_out],
        [tokens + (ANY,), low_rows(16), ((4, count, 2 * ff_width), bf16, ANY), (piece, bf16)],
        [tokens, ((ff_width, D), bf16)]
        + [((4, count, ff_width), bf16)] * 2
        + [((4, count, 2 * ff_width), bf16)],
        per * ff_width,
    )
    ffn_dlow, grad_hidden, grad_attn = linked(
        back_ffn_kernel, 6,
        [(grad_ffn,), (ffn_full,), ffn_b, factors, (own_cot,), (attn_lin,)],
        [low_rows(32), wide, own],
        [((4, count, 2 * ff_width), bf16), ((D, 2 * ff_width), bf16), own, wide, wide] + buffers,
        per * 2 * ff_width,
    )
    grad_heads, early_cols, early_rows = linked(
        back_out_kernel, 7,
        [grad_attn, (attn_full,), factors, out_a, out_low, cube(attn_low), flat(down_low)]
        + [flat(down_dlow), ffn_low, flat(ffn_dlow), (flat(dm_all),), (act_low,)]
        + [(flat(grad_ffn),), (h_all,)],
        [((4, count, head_width), bf16), ((64, D), bf16)]
        + [((16, head_width + 3 * ff_width), bf16)],
        [tokens, low_rows(16), ((head_width, D), bf16), ((SLAB, D), bf16)]
        + [((SLAB, ff_width), bf16), ((SLAB, 2 * ff_width), bf16), ((SLAB, D), bf16)]
        + [((16, D), f32), ((16, head_width), f32)],
        per * head_width,
    )
    weighted_q, weighted_k, grad_v, inner, layer_out = attend_back(
        q_low, k_low, v_low, attn_low, flat(grad_heads), log_sums, qkv_lin, head_gain, *tables,
        out_mid,
    )
    grad_qkv, qkv_dlow, own_rows = linked(
        prepare_kernel, 8,
        [(weighted_q,), (weighted_k,), grad_v, (qkv_lin,), inverses, inner, qkv_b, flat(qkv_low)]
        + [early_rows],
        [((SLAB, width), bf16), ((SLAB, 48), bf16)]
        + [((16, width + head_width + 3 * ff_width), bf16)],
        [((SLAB, head_width), f32)] * 2
        + [((SLAB, 2 * head_width), f32), ((SLAB, 8), f32), ((4, 8, SLAB), f32)],
        per * 128,
    )
    every = lax.all_gather(own_rows, ("tok", "col"), axis=0)
    numbers = jnp.arange(ADAPTERS, dtype=jnp.int32)
    chosen = (adapter_ids.T[:, None, :] == numbers[None, :, None]).astype(f32).reshape(7, -1)
    chosen = jnp.pad(chosen, ((0, 1), (0, 0)))
    grad_in, col_parts = linked(
        back_qkv_kernel, 9,
        [cube(grad_qkv), cube(qkv_dlow), (attn_full,), factors, (grad_hidden,), (x_all,)]
        + [early_cols, chosen],
        [(layer_in.shape, f32), ((4, ADAPTERS, 32, piece[2]), bf16)],
        [((D, width), bf16), wide, tokens, wide, (piece, bf16), (piece, bf16)]
        + [(layer_in.shape, bf16)]
        + [((4, 32, D), bf16)] * 2
        + [((4, 32, piece[2]), bf16), ((8, 32, piece[2]), bf16)]
        + [((ADAPTERS, 32, piece[2]), bf16)]
        + buffers,
        per * width,
    )
    col_grads = []
    for p in range(7):
        rows = slice(p % 2 * RANK, (p % 2 + 1) * RANK)
        col_grads.append(col_parts[p // 2, :, rows].astype(f32))
    row_grads, at = [], 0
    for p in range(7):
        size = ff_width if p > 3 else head_width
        row_grads.append(place(adapter_ids[:, p], every[:, :, at : at + size]))
        at += size
    return layer_out.astype(f32), grad_in, col_grads, row_grads


def diagonal(values, count):
    width = values.shape[1] // count
    return jnp.concatenate(
        [
            values[k * RANK : (k + 1) * RANK, k * width : (k + 1) * width]
            for k in range(count)
        ],
        axis=1,
    )


def on_device(
    layer_in,
    cotangent,
    qkv_weight,
    out_weight,
    ffn_weight,
    down_weight,
    qk_gain,
    post_gain,
    qkv_lower,
    qkv_raise,
    out_lower,
    out_raise,
    ffn_lower,
    ffn_raise,
    down_lower,
    down_raise,
    adapter_ids,
    prompt_len,
):
    group = lax.axis_index("tok") * lax.axis_size("col") + lax.axis_index("col")
    length = lax.dynamic_index_in_dim(prompt_len, group, 0, keepdims=False)
    cosine, sine = rotation(token_places(length), HEAD_DIM)
    cosine = jnp.concatenate([cosine, cosine], axis=1)
    sine = jnp.concatenate([-sine, sine], axis=1)
    slots = jnp.arange(SLAB, dtype=jnp.int32)
    bias = jnp.where((slots < length) | (slots >= PROMPT), 0.0, very_low)[:, None].astype(f32)

    plane = (lax.axis_size("tok"), lax.axis_size("row"), lax.axis_size("col"))
    layer = linked_layer if plane == (2, 4, 4) else split_layer
    adapters = [
        qkv_lower.swapaxes(2, 3), out_raise, ffn_lower.swapaxes(2, 3), down_raise,
        qkv_raise, out_lower.swapaxes(1, 2), ffn_raise, down_lower.swapaxes(1, 2),
    ]
    layer_out, grad_in, col_grads, row_grads = layer(
        layer_in, cotangent, qkv_weight, out_weight, ffn_weight, down_weight, qk_gain.astype(f32),
        post_gain, adapters, adapter_ids, (cosine, sine, bias),
    )
    return (
        layer_out,
        grad_in,
        jnp.stack(col_grads[0:3]).swapaxes(2, 3),
        jnp.stack(row_grads[0:3]),
        row_grads[3].swapaxes(1, 2),
        col_grads[3],
        jnp.stack(col_grads[4:6]).swapaxes(2, 3),
        jnp.stack(row_grads[4:6]),
        row_grads[6].swapaxes(1, 2),
        col_grads[6],
    )


def solution(mesh):
    return jax.shard_map(
        on_device,
        mesh=mesh,
        in_specs=(
            P(("tok", "row"), "col"),
            P(("tok", "row"), "col"),
            P(None, "col", "row"),
            P("row", "col"),
            P(None, "col", "row"),
            P("row", "col"),
            P(None, "row"),
            P(None, "col"),
            P(None, None, "col", None),
            P(None, None, None, "row"),
            P(None, "row", None),
            P(None, None, "col"),
            P(None, None, "col", None),
            P(None, None, None, "row"),
            P(None, "row", None),
            P(None, None, "col"),
            P(),
            P(),
        ),
        out_specs=(
            P(("tok", "row"), "col"),
            P(("tok", "row"), "col"),
            P(None, None, "col", None),
            P(None, None, None, "row"),
            P(None, "row", None),
            P(None, None, "col"),
            P(None, None, "col", None),
            P(None, None, None, "row"),
            P(None, "row", None),
            P(None, None, "col"),
        ),
        check_vma=False,
    )
```

```python
import functools
import math

import jax
import jax.numpy as jnp
from jax import lax
from jax.experimental import pallas as pl
from jax.experimental.pallas import tpu as pltpu
from jax.sharding import PartitionSpec as P

D = 2048
HEAD_DIM = 128
RANK = 16
ADAPTERS = 8
PROMPT = 1024
CONT_LEN = 128
SLAB = 1152

adapter_scale = 2.0
norm_eps = 1e-06
rope_base = 500000.0
very_low = -1e30
bf16 = jnp.bfloat16
f32 = jnp.float32
log2_scale = math.log2(math.e) / math.sqrt(HEAD_DIM)
score_scale = 1.0 / math.sqrt(HEAD_DIM)
BLOCK = 384
TILE = 512
MESH = pl.DeviceIdType.MESH


def mm(left, right):
    return jnp.dot(left, right, preferred_element_type=f32)


def mm_nt(left, right):
    return lax.dot_general(left, right, (((1,), (1,)), ((), ())), preferred_element_type=f32)


class Links:
    def __init__(self, send_sem, recv_sem, local_sem):
        self.tok = lax.axis_index("tok")
        self.row, self.col = lax.axis_index("row"), lax.axis_index("col")
        self.xn, self.yn, self.dg = self.row ^ 1, self.row ^ 2, self.row ^ 3
        self.send_sem, self.recv_sem, self.local_sem = send_sem, recv_sem, local_sem
        self.used, self.local_used = 0, 0

    def take(self, count):
        self.used += count
        return self.used - count

    def copy(self, source, target, index, recv_index, row, col=None, tok=None):
        return pltpu.make_async_remote_copy(
            src_ref=source,
            dst_ref=target,
            send_sem=self.send_sem.at[index],
            recv_sem=self.recv_sem.at[recv_index],
            device_id={
                "tok": self.tok if tok is None else tok,
                "row": row,
                "col": self.col if col is None else col,
            },
            device_id_type=MESH,
        )

    def local(self, source, target):
        self.local_used += 1
        return pltpu.make_async_copy(source, target, self.local_sem.at[self.local_used - 1])

    def plan(self, *pairs):
        return [self.local(source, target) for source, target in pairs]

    def fetch(self, *pairs):
        return start_all(self.plan(*pairs))

    def greet(self, rows=2, columns=False, twin=False):
        barrier = pltpu.get_barrier_semaphore()
        places = [(self.tok, self.row ^ step, self.col) for step in range(1, rows + 1)]
        if columns:
            places += [(self.tok, self.row, self.col ^ step) for step in range(1, 4)]
        if twin:
            places += [(self.tok ^ 1, self.row, self.col)]
        for tok, row, col in places:
            pl.semaphore_signal(
                barrier,
                inc=1,
                device_id={"tok": tok, "row": row, "col": col},
                device_id_type=MESH,
            )
        pl.semaphore_wait(barrier, len(places))


def start_all(copies):
    for copy in copies:
        copy.start()
    return copies


def wait_all(copies):
    for copy in copies:
        copy.wait()


class Exchange:
    def __init__(self, links, axis, piece_at, slot_at):
        self.links, self.axis = links, axis
        self.me = links.row if axis == "row" else links.col
        self.piece_at, self.slot_at = piece_at, slot_at
        self.base = links.take(3)
        self.own = links.local(piece_at(self.me), slot_at(self.me))

    def copy(self, source, target, step):
        links, other, index = self.links, self.me ^ step, self.base + step - 1
        row, col = (other, links.col) if self.axis == "row" else (links.row, other)
        return links.copy(source, target, index, index, row, col)

    def start(self):
        for step in range(1, 4):
            self.copy(self.piece_at(self.me ^ step), self.slot_at(self.me), step).start()
        self.own.start()

    def arrived(self):
        for step in range(1, 4):
            landed = self.slot_at(self.me ^ step)
            self.copy(landed, landed, step).wait_recv()
        self.own.wait()

    def sent(self):
        for step in range(1, 4):
            self.copy(self.piece_at(self.me ^ step), self.slot_at(self.me), step).wait_send()


def features(ref, width):
    return lambda col: ref.at[:, pl.ds(pl.multiple_of(col * width, width), width)]


def slot(ref):
    return lambda key: ref.at[key]


def token_rows(ref, count):
    return lambda row: ref.at[pl.ds(pl.multiple_of(row * count, 16), count)]


def gather(links, all_ref, work, before=None, after=None):
    me, xn, yn, dg = links.row, links.xn, links.yn, links.dg
    half = all_ref.shape[1] // 2
    top, low = pl.ds(0, half), pl.ds(half, half)
    base = links.take(6)

    def move(owner, part, index, other):
        place = all_ref.at[owner, part, pl.ds(0, D)]
        return links.copy(place, place, base + index, base + index, other)

    sends = [move(me, top, 0, xn), move(me, low, 1, yn), move(me, low, 2, xn), move(me, top, 3, yn)]
    for copy in sends:
        copy.start()
    if before:
        before()
    if work:
        work(me)
    move(xn, top, 0, xn).wait_recv()
    sends.append(move(xn, top, 4, yn))
    sends[-1].start()
    move(yn, low, 1, yn).wait_recv()
    sends.append(move(yn, low, 5, xn))
    sends[-1].start()
    if after:
        after()
    move(xn, low, 2, xn).wait_recv()
    if work:
        work(xn)
    move(yn, top, 3, yn).wait_recv()
    if work:
        work(yn)
    move(dg, top, 4, yn).wait_recv()
    move(dg, low, 5, xn).wait_recv()
    if work:
        work(dg)
    for copy in sends:
        copy.wait_send()


SLICES = 4


def scatter(links, product, o_ref, out_buf, relay_buf, final_buf, block=None, ready=None, hooks=None):
    me, xn, yn, dg = links.row, links.xn, links.yn, links.dg
    count, width = o_ref.shape[0], o_ref.shape[1] // SLICES
    half = count // 2
    top, low = pl.ds(0, half), pl.ds(half, half)
    base = links.take(6 * SLICES)
    all_copies = []

    def columns(k):
        at = block(k) * width if block else k * width
        return pl.ds(pl.multiple_of(at, width), width)

    def add(place, k, rows, relay):
        out_buf[place, k, rows] = (
            out_buf[place, k, rows].astype(f32) + relay_buf[relay, k].astype(f32)
        ).astype(bf16)

    def relay(k):
        copies = all_copies[k]
        copies[0].wait_recv()
        add(2, k, top, 0)
        copies[4].start()
        copies[1].wait_recv()
        add(1, k, low, 1)
        copies[5].start()

    def finish(k):
        for copy in all_copies[k][2:]:
            copy.wait_recv()

    for k in range(SLICES):
        cols = columns(k)

        def move(source, target, index, other, k=k):
            at = base + 6 * k + index
            return links.copy(source, target, at, at, other)

        copies = [
            move(out_buf.at[0, k, top], relay_buf.at[0, k], 0, xn),
            move(out_buf.at[0, k, low], relay_buf.at[1, k], 1, yn),
            move(out_buf.at[1, k, top], final_buf.at[0, k, top], 2, xn),
            move(out_buf.at[2, k, low], final_buf.at[1, k, low], 3, yn),
            move(out_buf.at[2, k, top], final_buf.at[1, k, top], 4, yn),
            move(out_buf.at[1, k, low], final_buf.at[0, k, low], 5, xn),
        ]
        all_copies.append(copies)
        if ready:
            ready(k)
        for place, (owner, first) in enumerate(((dg, (0, 1)), (xn, (2,)), (yn, (3,)))):
            out_buf[place, k] = product(owner, k, cols).astype(bf16)
            for index in first:
                copies[index].start()
        if k:
            relay(k - 1)
        if hooks:
            o_ref[:, cols] = product(me, k, cols)
            hooks[k](columns, finish)
    for k in range(SLICES):
        if k == (0 if hooks else SLICES // 2):
            relay(SLICES - 1)
        if not hooks:
            o_ref[:, columns(k)] = product(me, k, columns(k))

    def sent():
        for copies in all_copies:
            for copy in copies:
                copy.wait_send()

    return columns, finish, sent


def finish_all(result):
    _, finish, sent = result
    for k in range(SLICES):
        finish(k)
    sent()


def each_tile(width, step, body):
    @pl.loop(0, width // step)
    def _(tile):
        body(pl.multiple_of(tile * step, step))


def lower(rows, factor):
    step = rows.shape[1] // 4
    parts = [
        mm_nt(rows[:, at : at + step], factor[:, at : at + step])
        for at in range(0, rows.shape[1], step)
    ]
    return (adapter_scale * functools.reduce(jnp.add, parts)).astype(bf16)


def leave_product(y_ref, weight, f1_ref, low_ref, loads):
    depth = f1_ref.shape[1]
    used = []

    def product(owner, k, cols):
        if k == 0:
            if loads:
                loads[len(used)].wait()
            used.append(True)
            lowered = lower(y_ref[owner, :, :depth], f1_ref[...])
            low_ref[owner] = lowered
            y_ref[owner, :, depth:] = lowered
        return weight(y_ref[owner], cols)

    return product


class Streams:
    def __init__(self, links, rows, blocks, late=()):
        order = (links.dg, links.xn, links.yn, links.row)
        self.rows = []
        if rows:
            cols = pl.ds(0, rows[0].shape[2])
            self.rows = links.plan(*[(rows[0].at[k], rows[1].at[k, :, cols]) for k in order])
        self.blocks = blocks
        self.late = links.plan(*late)
        start_all(self.rows[:1])
        start_all(blocks[0])

    def ready(self, k):
        wait_all(self.blocks[k])
        if k == 0:
            start_all(self.rows[1:])
        if k < SLICES - 1:
            start_all(self.blocks[k + 1])
        if k == 1:
            start_all(self.late)


def load_qkv(links, w_hbm, w_ref, blocks):
    half, width = w_hbm.shape[1] // 4, w_hbm.shape[2]
    return [
        links.plan(
            *[
                (
                    w_hbm.at[2 * c + t, pl.ds(p * half, half)],
                    w_ref.at[
                        pl.ds(pl.multiple_of((2 * c + t) * half, half), half),
                        pl.ds(p * width, width),
                    ],
                )
                for t in range(2)
                for p in range(3)
            ]
        )
        for c in blocks
    ]


def load_out(links, w_hbm, w_ref):
    half, width = w_hbm.shape[1] // 4, w_hbm.shape[2]
    return [
        links.plan(
            *[
                (
                    w_hbm.at[2 * c + t, pl.ds(3 * half, half)],
                    w_ref.at[pl.ds(t * half, half), pl.ds(c * width, width)],
                )
                for t in range(2)
            ]
        )
        for c in range(4)
    ]


def load_down(links, w_hbm, w_ref):
    half, width = w_hbm.shape[1:]
    return [
        links.plan(
            *[
                (
                    w_hbm.at[2 * c + t],
                    w_ref.at[pl.ds(t * half, half), pl.ds(c * width, width)],
                )
                for t in range(2)
            ]
        )
        for c in range(4)
    ]


def load_ffn(links, w_hbm, w_ref):
    half, width = w_hbm.shape[2:]
    return [
        links.plan(
            *[
                (
                    w_hbm.at[2 * c + t, g],
                    w_ref.at[pl.ds((2 * c + t) * half, half), pl.ds(g * width, width)],
                )
                for t in range(2)
                for g in range(2)
            ]
        )
        for c in range(4)
    ]


def inverse_of(values):
    return lax.rsqrt(jnp.mean(values * values, axis=1, keepdims=True) + norm_eps)


def norm_back(values, weighted):
    inverse = inverse_of(values)
    inner = jnp.mean(values * weighted, axis=1, keepdims=True)
    return inverse * weighted - values * (inverse**3 * inner)


def gated(gate, up):
    return gate * jax.nn.sigmoid(gate) * up


def gated_back(grad, gate, up):
    sig = jax.nn.sigmoid(gate)
    act = gate * sig
    return (grad * up * (sig + act * (1.0 - sig)), grad * act)


QKV_A, OUT_B, FFN_A, DOWN_B = slice(0, 48), slice(48, 64), slice(64, 96), slice(96, 112)
GAIN0, GAIN1 = slice(112, 113), slice(113, 114)


def share_stats(links, stat_ref, first, second):
    blank = jnp.zeros((6, first.shape[0]), f32)
    sums = [jnp.sum(value.T, axis=0, keepdims=True) for value in (first, second)]
    stat_ref[links.row] = jnp.concatenate(sums + [blank], axis=0)
    base = links.take(3)
    mine = stat_ref.at[links.row]
    copies = []
    for index, other in enumerate((links.xn, links.yn, links.dg)):
        copies.append(links.copy(mine, mine, base + index, base + index, other))
        copies[-1].start()
    for index, other in enumerate((links.xn, links.yn, links.dg)):
        theirs = stat_ref.at[other]
        links.copy(theirs, theirs, base + index, base + index, other).wait_recv()
    for copy in copies:
        copy.wait_send()
    return stat_ref[0] + stat_ref[1] + stat_ref[2] + stat_ref[3]


def lane_sums(values):
    return functools.reduce(
        jnp.add, [values[:, at : at + 128] for at in range(0, values.shape[1], 128)]
    )


def intake_kernel(
    x_hbm, cot_hbm, ids_ref, gain_ref, qkv_lower_ref, out_raise_ref, ffn_lower_ref, down_raise_ref,
    qkv_raise_ref, out_lower_ref, ffn_raise_ref, down_lower_ref,
    own_ref, cot_ref, factors_ref, factors_t_ref, qkv_b_ref, out_a_ref, out_at_ref, ffn_b_ref,
    down_a_ref, down_at_ref,
    middle_ref, pieces_ref, send_sem, recv_sem, local_sem,
):
    links = Links(send_sem, recv_sem, local_sem)
    links.greet(rows=3, columns=True)
    width = pieces_ref.shape[2]
    first = Exchange(links, "row", slot(x_hbm), slot(middle_ref))
    second = Exchange(links, "col", slot(middle_ref), features(own_ref, width))
    turned = Exchange(links, "row", slot(cot_hbm), slot(cot_ref))
    spread = Exchange(links, "col", slot(pieces_ref), features(factors_ref, width))
    first.start()
    base = 4 * links.tok
    for place in range(4):
        for p in range(7):
            chosen = ids_ref[base + place, p]
            if p < 3:
                value = qkv_lower_ref[p, chosen]
            elif p == 3:
                value = out_raise_ref[chosen]
            elif p < 6:
                value = ffn_lower_ref[p - 4, chosen]
            else:
                value = down_raise_ref[chosen]
            pieces_ref[place, p * RANK : (p + 1) * RANK] = value
        pieces_ref[place, 7 * RANK :] = gain_ref[...]
    spread.start()
    first.arrived()
    second.start()
    turned.start()
    own = base + links.col
    for ref in (qkv_b_ref, out_a_ref, ffn_b_ref, down_a_ref):
        ref[...] = jnp.zeros_like(ref)
    for p in range(3):
        cols = slice(p * qkv_raise_ref.shape[3], (p + 1) * qkv_raise_ref.shape[3])
        qkv_b_ref[p * RANK : (p + 1) * RANK, cols] = qkv_raise_ref[p, ids_ref[own, p]]
    for p in range(2):
        cols = slice(p * ffn_raise_ref.shape[3], (p + 1) * ffn_raise_ref.shape[3])
        rows = slice((4 + p) * RANK, (5 + p) * RANK)
        ffn_b_ref[rows, cols] = ffn_raise_ref[p, ids_ref[own, 4 + p]]
    out_a_ref[OUT_B] = out_lower_ref[ids_ref[own, 3]]
    down_a_ref[DOWN_B] = down_lower_ref[ids_ref[own, 6]]
    spread.arrived()
    for source, target in (
        (out_a_ref, out_at_ref), (down_a_ref, down_at_ref), (factors_ref, factors_t_ref)
    ):
        target[...] = source[...].astype(f32).T.astype(bf16)
    for exchange in (second, turned):
        exchange.arrived()
    for exchange in (first, spread, second, turned):
        exchange.sent()


def enter_qkv_kernel(
    x_ref, w_hbm, factors_ref, f2_ref,
    all_hbm, low_ref, lin_hbm, inv_ref,
    all_ref, lin_ref, w_ref, sq_ref, stat_ref, send_sem, recv_sem, local_sem,
):
    links = Links(send_sem, recv_sem, local_sem)
    width = w_ref.shape[1]
    loads = start_all(sum(load_qkv(links, w_hbm, w_ref, range(4)), []))
    loads += links.fetch((f2_ref, w_ref.at[pl.ds(D, 128)]))
    all_ref[links.row, :, :D] = x_ref[...]
    links.greet(rows=3)
    count = x_ref.shape[0]
    stores = []

    def work(owner):
        lowered = lower(all_ref[owner, :, :D], factors_ref[...])
        low_ref[owner] = lowered
        all_ref[owner, :, D:] = lowered
        rows = all_ref[owner]
        third = width // 3
        for index in range(3):
            cols = slice(index * third, (index + 1) * third)
            value = mm(rows, w_ref[:, cols])
            lin_ref[owner, :, cols] = value
            if index < 2:
                place = pl.ds(pl.multiple_of(owner * count, 8), count)
                sq_ref[index, place] = lane_sums(value * value)
        stores.extend(
            links.fetch(
                (lin_ref.at[owner], lin_hbm.at[owner]),
                (all_ref.at[owner, :, pl.ds(0, D)], all_hbm.at[owner]),
            )
        )

    gather(links, all_ref, work, lambda: wait_all(loads))
    total = share_stats(links, stat_ref, sq_ref[0], sq_ref[1])
    inv_ref[...] = lax.rsqrt(total / D + norm_eps).T
    wait_all(stores)


def summed(o_ref, final_buf, rows):
    return o_ref[rows] + jnp.concatenate(
        [
            final_buf[0, k, rows].astype(f32) + final_buf[1, k, rows].astype(f32)
            for k in range(SLICES)
        ],
        axis=1,
    )


def leave_out_kernel(
    y_hbm, w_hbm, f1_ref, factors_ref, x_ref,
    lin_ref, low_ref, hidden_ref, all_ref,
    y_ref, w_ref, out_buf, relay_buf, final_buf, send_sem, recv_sem, local_sem,
):
    links = Links(send_sem, recv_sem, local_sem)
    streams = Streams(links, (y_hbm, y_ref), load_out(links, w_hbm, w_ref))
    w_ref[f1_ref.shape[1] :] = factors_ref[...]
    links.greet()
    product = leave_product(
        y_ref, lambda rows, cols: mm(rows, w_ref[:, cols]), f1_ref, low_ref, streams.rows
    )
    finish_all(
        scatter(links, product, lin_ref, out_buf, relay_buf, final_buf, ready=streams.ready)
    )
    gain = factors_ref[GAIN0].astype(f32)

    @pl.loop(0, lin_ref.shape[0] // 16)
    def _(tile):
        rows = pl.ds(pl.multiple_of(tile * 16, 16), 16)
        value = summed(lin_ref, final_buf, rows)
        lin_ref[rows] = value
        hidden = x_ref[rows].astype(f32) + value * inverse_of(value) * gain
        hidden_ref[rows] = hidden
        all_ref[links.row, rows] = hidden.astype(bf16)

    gather(links, all_ref, None)


def flat_weight(ref):
    return ref[...].reshape(D, ref.shape[3])


def ffn_kernel(h_ref, wg_ref, wu_ref, factors_ref, fg_ref, fu_ref, low_ref, gate_ref, up_ref, act_ref):
    @pl.when(pl.program_id(0) == 0)
    def _():
        low_ref[...] = lower(h_ref[...], factors_ref[...])

    lowered = low_ref[...]
    rank = lowered.shape[1] // 2
    for at in range(0, SLAB, BLOCK):
        rows = slice(at, at + BLOCK)
        gate = mm(h_ref[rows], flat_weight(wg_ref)) + mm(lowered[rows], fg_ref[...])
        up = mm(h_ref[rows], flat_weight(wu_ref)) + mm(lowered[rows], fu_ref[...])
        gate_ref[rows] = gate.astype(bf16)
        up_ref[rows] = up.astype(bf16)
        act_ref[rows] = gated(gate, up).astype(bf16)


def ffn(h_all, w, factors, f2):
    width = f2.shape[1] // 2
    step = 256
    tiles = width // step
    low = jax.ShapeDtypeStruct((SLAB, f2.shape[0]), bf16)
    wide = jax.ShapeDtypeStruct((SLAB, width), bf16)
    whole = lambda value: pl.BlockSpec(value.shape, lambda t: (0, 0))
    cols = lambda rows, base: pl.BlockSpec((rows, step), lambda t: (0, base * tiles + t))
    block = (w.shape[0], 1, w.shape[2], step)
    part = lambda which: pl.BlockSpec(block, lambda t: (0, which, 0, t))
    return pl.pallas_call(
        ffn_kernel,
        grid=(tiles,),
        in_specs=[whole(h_all), part(0), part(1), whole(factors)]
        + [cols(f2.shape[0], 0), cols(f2.shape[0], 1)],
        out_specs=[whole(low)] + [cols(SLAB, 0)] * 3,
        out_shape=[low, wide, wide, wide],
        compiler_params=pltpu.CompilerParams(vmem_limit_bytes=48 << 20),
        cost_estimate=pl.CostEstimate(
            flops=4 * SLAB * D * width, bytes_accessed=4 * D * width + 10 * SLAB * width,
            transcendentals=SLAB * width,
        ),
        name="ffn",
    )(h_all, w, w, factors, f2, f2)


def leave_down_kernel(
    y_hbm, w_hbm, f1_ref, factors_ref, hidden_hbm, cot_ref,
    low_ref, out_ref, dm_ref, own_cot_ref,
    y_ref, w_ref, hidden_ref, lin_ref, out_buf, relay_buf, final_buf,
    send_sem, recv_sem, local_sem,
):
    links = Links(send_sem, recv_sem, local_sem)
    streams = Streams(
        links, (y_hbm, y_ref), load_down(links, w_hbm, w_ref), [(hidden_hbm, hidden_ref)]
    )
    links.greet(columns=True)
    turned = Exchange(links, "col", slot(cot_ref), features(own_cot_ref, cot_ref.shape[2]))
    turned.start()
    w_ref[f1_ref.shape[1] :] = factors_ref[...]
    product = leave_product(
        y_ref, lambda rows, cols: mm(rows, w_ref[:, cols]), f1_ref, low_ref, streams.rows
    )
    finish_all(
        scatter(
            links, product, lin_ref, out_buf, relay_buf, final_buf,
            ready=streams.ready,
        )
    )
    turned.arrived()
    wait_all(streams.late)
    gain = factors_ref[GAIN1].astype(f32)

    @pl.loop(0, lin_ref.shape[0] // 16)
    def _(tile):
        rows = pl.ds(pl.multiple_of(tile * 16, 16), 16)
        value = summed(lin_ref, final_buf, rows)
        out_ref[rows] = (hidden_ref[rows] + value * inverse_of(value) * gain).astype(bf16)
        dm_ref[rows] = norm_back(value, own_cot_ref[rows].astype(f32) * gain).astype(bf16)

    turned.sent()


def widen(source_ref, target_ref):
    @pl.loop(0, source_ref.shape[0] // 64)
    def _(tile):
        rows = pl.ds(pl.multiple_of(tile * 64, 64), 64)
        target_ref[rows] = source_ref[rows].astype(f32)


def finish_kernel(
    chosen_ref, out_ref, grad_ref, parts_ref, every_ref,
    out32_ref, grad32_ref, qkv_lower_ref, out_raise_ref, ffn_lower_ref, down_raise_ref,
    qkv_raise_ref, out_lower_ref, ffn_raise_ref, down_lower_ref,
):
    widen(out_ref, out32_ref)
    widen(grad_ref, grad32_ref)
    targets = [qkv_lower_ref.at[p] for p in range(3)]
    targets += [out_raise_ref, ffn_lower_ref.at[0], ffn_lower_ref.at[1], down_raise_ref]
    for p, target in enumerate(targets):
        rows = slice(p % 2 * RANK, (p % 2 + 1) * RANK)
        for adapter in range(ADAPTERS):
            target[adapter] = parts_ref[p // 2, adapter, rows].astype(f32)
    targets = [qkv_raise_ref.at[p] for p in range(3)]
    targets += [out_lower_ref, ffn_raise_ref.at[0], ffn_raise_ref.at[1], down_lower_ref]
    base = 0
    for p, target in enumerate(targets):
        step = 256
        weights = [chosen_ref[p, at] for at in range(64)]

        @pl.loop(0, target.shape[2] // step)
        def _(tile, p=p, target=target, base=base, weights=weights):
            cols = pl.ds(pl.multiple_of(base + tile * step, step), step)
            here = pl.ds(pl.multiple_of(tile * step, step), step)
            values = [every_ref[g, :, cols].astype(f32) for g in range(8)]
            for adapter in range(ADAPTERS):
                terms = [weights[adapter * 8 + g] * values[g] for g in range(8)]
                target[adapter, :, here] = functools.reduce(jnp.add, terms)

        base += target.shape[2]


def finish(chosen, layer_out, grad_in, col_parts, every, head_width, ff_width):
    piece = col_parts.shape[3]

    def out(*shape):
        return jax.ShapeDtypeStruct(shape, f32)

    return pl.pallas_call(
        finish_kernel,
        in_specs=[SMEM] + [VMEM] * 4,
        out_specs=[VMEM] * 10,
        out_shape=[
            out(*layer_out.shape), out(*grad_in.shape),
            out(3, ADAPTERS, RANK, piece), out(ADAPTERS, RANK, piece),
            out(2, ADAPTERS, RANK, piece), out(ADAPTERS, RANK, piece),
            out(3, ADAPTERS, RANK, head_width), out(ADAPTERS, RANK, head_width),
            out(2, ADAPTERS, RANK, ff_width), out(ADAPTERS, RANK, ff_width),
        ],
        compiler_params=pltpu.CompilerParams(vmem_limit_bytes=48 << 20),
        cost_estimate=pl.CostEstimate(flops=10**8, bytes_accessed=16 << 20, transcendentals=0),
        name="finish",
    )(chosen, layer_out, grad_in, col_parts, every)


def back_down_kernel(
    dm_ref, w_hbm, factors_ref, f2_ref, gate_hbm, up_hbm, out_ref,
    all_hbm, low_ref, grad_hbm, out_mid_ref,
    all_ref, w_ref, gate_ref, up_ref, grad_ref, send_sem, recv_sem, local_sem,
):
    links = Links(send_sem, recv_sem, local_sem)
    loads = start_all(sum(load_down(links, w_hbm, w_ref), []))
    order = (links.row, links.xn, links.yn, links.dg)
    gates = [
        links.plan((gate_hbm.at[k], gate_ref.at[k]), (up_hbm.at[k], up_ref.at[k])) for k in order
    ]
    start_all(gates[0])
    all_ref[links.row, :, :D] = dm_ref[...]
    w_ref[:, D:] = f2_ref[...]
    links.greet(columns=True)
    width = w_ref.shape[0]
    turned = Exchange(links, "col", features(out_ref, out_mid_ref.shape[2]), slot(out_mid_ref))
    stores = []

    def before():
        turned.start()
        wait_all(loads)
        for gate in gates[1:]:
            start_all(gate)

    def work(owner):
        wait_all(gates[len(stores) // 2])
        lowered = lower(all_ref[owner, :, :D], factors_ref[...])
        low_ref[owner] = lowered
        all_ref[owner, :, D:] = lowered

        def body(at):
            cols, far = pl.ds(at, TILE), pl.ds(pl.multiple_of(width + at, TILE), TILE)
            grad = mm_nt(all_ref[owner], w_ref[cols, :])
            gate, up = gate_ref[owner, :, cols].astype(f32), up_ref[owner, :, cols].astype(f32)
            grad_gate, grad_up = gated_back(grad, gate, up)
            grad_ref[owner, :, cols] = grad_gate.astype(bf16)
            grad_ref[owner, :, far] = grad_up.astype(bf16)

        each_tile(width, TILE, body)
        stores.extend(
            links.fetch(
                (grad_ref.at[owner], grad_hbm.at[owner]),
                (all_ref.at[owner, :, pl.ds(0, D)], all_hbm.at[owner]),
            )
        )

    gather(links, all_ref, work, before)
    turned.arrived()
    turned.sent()
    wait_all(stores)


def back_ffn_kernel(
    y_hbm, w_hbm, f1_ref, factors_ref, factors_t_ref, cot_hbm, attn_hbm,
    low_ref, hidden_ref, da_ref,
    y_ref, w_ref, cot_ref, attn_ref, lin_ref, out_buf, relay_buf, final_buf,
    send_sem, recv_sem, local_sem,
):
    links = Links(send_sem, recv_sem, local_sem)
    streams = Streams(
        links,
        (y_hbm, y_ref),
        load_ffn(links, w_hbm, w_ref),
        [(cot_hbm, cot_ref), (attn_hbm, attn_ref)],
    )
    links.greet()
    w_ref[:, f1_ref.shape[1] :] = factors_t_ref[...]
    product = leave_product(
        y_ref, lambda rows, cols: mm_nt(rows, w_ref[cols, :]), f1_ref, low_ref, streams.rows
    )
    finish_all(
        scatter(
            links, product, lin_ref, out_buf, relay_buf, final_buf,
            ready=streams.ready,
        )
    )
    wait_all(streams.late)
    gain = factors_ref[GAIN0].astype(f32)

    @pl.loop(0, lin_ref.shape[0] // 16)
    def _(tile):
        rows = pl.ds(pl.multiple_of(tile * 16, 16), 16)
        value = summed(lin_ref, final_buf, rows) + cot_ref[rows].astype(f32)
        hidden_ref[rows] = value
        da_ref[rows] = norm_back(attn_ref[rows], value * gain).astype(bf16)


def mm_tn(left, right):
    return lax.dot_general(left, right, (((0,), (0,)), ((), ())), preferred_element_type=f32)


def back_out_kernel(
    da_ref, w_hbm, factors_ref, f2_ref, out_low_ref, attn_ref, down_low_ref, down_dlow_ref,
    ffn_low_ref, ffn_dlow_ref, dm_hbm, act_hbm, grad_hbm, h_hbm,
    heads_ref, cols_ref, rows_ref,
    all_ref, w_ref, dm_ref, act_ref, grad_ref, h_ref, raise_ref, lower_ref, send_sem, recv_sem, local_sem,
):
    links = Links(send_sem, recv_sem, local_sem)
    load = start_all(sum(load_out(links, w_hbm, w_ref), []))
    all_ref[links.row, :, :D] = da_ref[...]
    w_ref[:, D:] = f2_ref[...]
    links.greet()
    loads = []

    def before():
        loads.extend(
            links.fetch((dm_hbm, dm_ref), (act_hbm, act_ref), (grad_hbm, grad_ref), (h_hbm, h_ref))
        )
        wait_all(load)

    heads, half = heads_ref.shape[2], grad_ref.shape[1] // 2

    def after():
        wait_all(loads)
        down_raise = mm_tn(down_low_ref[:, DOWN_B], dm_ref[...])
        cols_ref[3 * RANK : 4 * RANK] = down_raise.astype(bf16)
        cols_ref[RANK : 3 * RANK] = mm_tn(ffn_dlow_ref[:, FFN_A], h_ref[...]).astype(bf16)
        for p in range(2):
            low = ffn_low_ref[:, (4 + p) * RANK : (5 + p) * RANK]
            raised = mm_tn(low, grad_ref[:, p * half : (p + 1) * half])
            rows_ref[:, heads + p * half : heads + (p + 1) * half] = raised.astype(bf16)
        rows_ref[:, heads + 2 * half :] = mm_tn(down_dlow_ref[:, DOWN_B], act_ref[...]).astype(bf16)

    def work(owner):
        lowered = lower(all_ref[owner, :, :D], factors_ref[...])
        all_ref[owner, :, D:] = lowered
        heads_ref[owner] = mm_nt(all_ref[owner], w_ref[...]).astype(bf16)
        raise_ref[...] += mm_tn(out_low_ref[owner, :, OUT_B], all_ref[owner, :, :D])
        lower_ref[...] += mm_tn(lowered[:, OUT_B], attn_ref[owner])

    raise_ref[...] = jnp.zeros_like(raise_ref)
    lower_ref[...] = jnp.zeros_like(lower_ref)
    gather(links, all_ref, work, before, after)
    cols_ref[0:RANK] = raise_ref[...].astype(bf16)
    rows_ref[:, :heads] = lower_ref[...].astype(bf16)


def prepare_kernel(
    wq_hbm, wk_hbm, dv_ref, lin_hbm, inv_ref, inner_ref, f1_ref, low_ref, early_ref,
    grad_ref, rows_ref,
    wq_ref, wk_ref, lin_ref, total_ref, stat_ref, send_sem, recv_sem, local_sem,
):
    links = Links(send_sem, recv_sem, local_sem)
    third = wq_ref.shape[1]
    loads = links.fetch(
        (wq_hbm, wq_ref),
        (wk_hbm, wk_ref),
        (lin_hbm.at[:, pl.ds(0, 2 * third)], lin_ref),
    )
    links.greet(rows=3)
    total = share_stats(links, stat_ref, inner_ref[0], inner_ref[1])
    total_ref[...] = total.T / D
    wait_all(loads)

    @pl.loop(0, SLAB // 96)
    def _(tile):
        rows = pl.ds(pl.multiple_of(tile * 96, 96), 96)
        inverse = inv_ref[rows]
        factor = inverse**3 * total_ref[rows]
        for index, source in enumerate((wq_ref, wk_ref)):
            cols = slice(index * third, (index + 1) * third)
            one = slice(index, index + 1)
            value = inverse[:, one] * source[rows] - lin_ref[rows, cols] * factor[:, one]
            grad_ref[rows, cols] = value.astype(bf16)
        grad_ref[rows, 2 * third : 3 * third] = dv_ref[rows]

    grad_ref[:, 3 * third :] = lower(grad_ref[:, : 3 * third], f1_ref[...])
    for index in range(3):
        cols = slice(index * third, (index + 1) * third)
        low = low_ref[:, index * RANK : (index + 1) * RANK]
        rows_ref[:, cols] = mm_tn(low, grad_ref[:, cols]).astype(bf16)
    rows_ref[:, 3 * third :] = early_ref[...]


def back_qkv_kernel(
    grad_ref, w_hbm, factors_t_ref, hidden_hbm, x_hbm, early_ref, chosen_ref,
    turn_buf, sums_ref,
    w_ref, hidden_ref, x_ref, sum_ref, own_ref, middle_ref, parts_ref, got_ref, total_ref, groups_ref,
    placed_ref, out_buf, relay_buf, final_buf, send_sem, recv_sem, local_sem,
):
    links = Links(send_sem, recv_sem, local_sem)
    steps = (2, 3, 1, 0)
    streams = Streams(
        links,
        None,
        load_qkv(links, w_hbm, w_ref, [links.col ^ step for step in steps]),
        [(hidden_hbm, hidden_ref)],
    )
    x_load = links.plan((x_hbm, x_ref))
    depth = w_ref.shape[1] - 128
    w_ref[:, depth:] = factors_t_ref[...]
    links.greet(rows=3, columns=True, twin=True)
    width = own_ref.shape[2]
    count = grad_ref.shape[1]
    by_row = Exchange(links, "row", slot(parts_ref), slot(got_ref))
    base = 4 * links.tok
    by_col = Exchange(
        links, "col", slot(total_ref), lambda key: groups_ref.at[base + key]
    )
    index = links.take(1)
    mine, theirs = groups_ref.at[pl.ds(base, 4)], groups_ref.at[pl.ds(4 - base, 4)]
    to_twin = links.copy(mine, mine, index, index, links.row, tok=links.tok ^ 1)
    from_twin = links.copy(theirs, theirs, index, index, links.row, tok=links.tok ^ 1)
    spread = Exchange(links, "row", lambda key: placed_ref, slot(sums_ref))

    def lower_grad():
        wait_all(x_load)
        late = 0.0
        for owner in range(4):
            late = late + mm_tn(grad_ref[owner, :, depth : depth + 3 * RANK], x_ref[owner])
        late = late.astype(bf16)
        parts_ref[0] = late[0 : 2 * RANK]
        parts_ref[1, :RANK] = late[2 * RANK :]
        parts_ref[1, RANK:] = early_ref[:RANK]
        parts_ref[2] = early_ref[RANK : 3 * RANK]
        parts_ref[3, :RANK] = early_ref[3 * RANK :]
        parts_ref[3, RANK:] = jnp.zeros((RANK, D), bf16)
        by_row.start()

    def add_rows():
        by_row.arrived()
        for f in range(4):
            cols = slice(f * width, (f + 1) * width)
            value = got_ref[0, :, cols].astype(f32)
            for q in range(1, 4):
                value = value + got_ref[q, :, cols].astype(f32)
            total_ref[f] = value.astype(bf16)
        by_col.start()

    def share():
        by_col.arrived()
        to_twin.start()

    def place_groups():
        from_twin.wait_recv()
        for half in range(2):
            rows = slice(half * RANK, (half + 1) * RANK)
            values = [groups_ref[g, rows].astype(f32) for g in range(8)]
            for adapter in range(ADAPTERS):
                value = 0.0
                for g in range(8):
                    value = value + chosen_ref[2 * links.row + half, adapter * 8 + g] * values[g]
                placed_ref[adapter, rows] = value.astype(bf16)
        spread.start()

    def product(owner, k, cols):
        return mm_nt(grad_ref[owner], w_ref[cols, :])

    z_base, row_base = links.take(3), links.take(4)
    near = links.local(middle_ref.at[links.row], token_rows(turn_buf, count)(links.row))
    z_copies = []

    def leave_col(k, columns, finish):
        finish(k)
        cols, step = columns(k), steps[k]
        value = (
            sum_ref[:, cols]
            + final_buf[0, k].astype(f32)
            + final_buf[1, k].astype(f32)
            + hidden_ref[:, cols]
        ).astype(bf16)
        if step == 0:
            middle_ref[links.col] = value
            return
        own_ref[k] = value
        at = z_base + k
        copy = links.copy(
            own_ref.at[k], middle_ref.at[links.col], at, at, links.row, links.col ^ step
        )
        copy.start()
        z_copies.append(copy)

    def to_row(step):
        other = links.row ^ step
        return links.copy(
            middle_ref.at[other],
            token_rows(turn_buf, count)(links.row),
            row_base + step,
            row_base + step,
            other,
        )

    def leave_row(k):
        source = links.col ^ steps[k]
        if steps[k]:
            at = z_base + k
            landed = middle_ref.at[source]
            links.copy(landed, landed, at, at, links.row, source).wait_recv()
        step = links.row ^ source

        @pl.when(step == 0)
        def _():
            near.start()

        @pl.when(step != 0)
        def _():
            to_row(step).start()

    def first(columns, finish):
        start_all(x_load)

    def second(columns, finish):
        lower_grad()

    def third(columns, finish):
        add_rows()
        wait_all(streams.late)
        leave_col(0, columns, finish)

    def fourth(columns, finish):
        share()
        leave_col(1, columns, finish)

    columns, finish, sent = scatter(
        links, product, sum_ref, out_buf, relay_buf, final_buf,
        block=lambda k: links.col ^ steps[k],
        ready=streams.ready,
        hooks=[first, second, third, fourth],
    )
    leave_row(0)
    place_groups()
    leave_col(2, columns, finish)
    leave_col(3, columns, finish)
    leave_row(3)
    leave_row(2)
    leave_row(1)
    near.wait()
    for step in range(1, 4):
        landed = token_rows(turn_buf, count)(links.row ^ step)
        at = row_base + step
        links.copy(landed, landed, at, at, links.row ^ step).wait_recv()
    spread.arrived()
    for step in range(1, 4):
        to_row(step).wait_send()
    for copy in z_copies:
        copy.wait_send()
    to_twin.wait_send()
    for exchange in (by_row, by_col, spread):
        exchange.sent()
    sent()


VMEM = pl.BlockSpec(memory_space=pltpu.VMEM)
ANY = pl.BlockSpec(memory_space=pl.ANY)
SMEM = pl.BlockSpec(memory_space=pltpu.SMEM)


def linked(kernel, number, operands, outs, scratch, flops):
    specs = [ANY if isinstance(value, tuple) else VMEM for value in operands]
    values = [value[0] if isinstance(value, tuple) else value for value in operands]
    specs = [
        SMEM if value.ndim == 2 and value.shape[0] == 8 and value.dtype != bf16 else spec
        for spec, value in zip(specs, values)
    ]
    return pl.pallas_call(
        kernel,
        in_specs=specs,
        out_specs=[ANY if len(out) == 3 else VMEM for out in outs],
        out_shape=[jax.ShapeDtypeStruct(out[0], out[1]) for out in outs],
        scratch_shapes=[pltpu.VMEM(shape, kind) for shape, kind in scratch]
        + [
            pltpu.SemaphoreType.DMA((48,)),
            pltpu.SemaphoreType.DMA((48,)),
            pltpu.SemaphoreType.DMA((48,)),
        ],
        compiler_params=pltpu.CompilerParams(
            collective_id=number, has_side_effects=True, vmem_limit_bytes=60 << 20
        ),
        cost_estimate=pl.CostEstimate(
            flops=flops, bytes_accessed=flops // 400, transcendentals=0
        ),
        name=kernel.__name__,
    )(*values)


def scatter_buffers(count):
    part = D // SLICES
    return [
        ((3, SLICES, count, part), bf16),
        ((2, SLICES, count // 2, part), bf16),
        ((2, SLICES, count, part), bf16),
    ]


def score_blocks(k_ref, q_block, bias_ref, start, stop):
    parts = []
    if start:
        parts.append(mm_nt(k_ref[0:start], q_block) + bias_ref[0:start])
    own = mm_nt(k_ref[start:stop], q_block) + bias_ref[start:stop]
    keys = lax.broadcasted_iota(jnp.int32, own.shape, 0)
    queries = lax.broadcasted_iota(jnp.int32, own.shape, 1)
    parts.append(jnp.where(keys <= queries, own, very_low))
    return parts

def attend_kernel(q_ref, k_ref, v_ref, inv_ref, gain_ref, cos_ref, sin_ref, bias_ref,
                  ql_ref, kl_ref, vl_ref, o_ref, lse_ref):
    for source, target, index in ((q_ref, ql_ref, 0), (k_ref, kl_ref, 1)):
        normed = source[...] * inv_ref[:, index:index+1] * gain_ref[index:index+1, :]
        target[...] = (normed * cos_ref[...] + pltpu.roll(normed, HEAD_DIM // 2, 1) * sin_ref[...]).astype(bf16)
    values = v_ref[...].astype(bf16)
    vl_ref[...] = values
    values_t = v_ref[...].T.astype(bf16)
    for start in range(0, SLAB, BLOCK):
        stop = start + BLOCK
        parts = score_blocks(kl_ref, ql_ref[start:stop], bias_ref, start, stop)
        top = functools.reduce(jnp.maximum, [jnp.max(p, axis=0, keepdims=True) for p in parts]) * log2_scale
        total, out, at = 0.0, 0.0, 0
        for part in parts:
            shifted = jnp.exp2(part * log2_scale - top)
            total = total + jnp.sum(shifted, axis=0, keepdims=True)
            out = out + mm(values_t[:, at:at+part.shape[0]], shifted.astype(bf16))
            at += part.shape[0]
        o_ref[start:stop] = (out / total).T.astype(bf16)
        lse_ref[0, :, start:stop] = top + jnp.log2(total)

def attend_back_kernel(ql_ref, kl_ref, vl_ref, o_ref, do_ref, lse_ref, q_ref, k_ref, gain_ref, cos_ref, sin_ref, bias_ref, *refs):
    mid_ref, wq_ref, wk_ref, dv_ref, sum_ref, turn_ref, dk_sum, dv_sum, *sems = refs if len(refs) > 8 else (None, *refs[:4], None, *refs[4:])
    if sems:
        links = Links(*sems)
        turned = Exchange(links, "row", slot(mid_ref), token_rows(turn_ref, mid_ref.shape[1]))

        @pl.when(pl.program_id(0) == 0)
        def _():
            links.greet(rows=3)
            turned.start()

    keys_t = kl_ref[...].astype(f32).T.astype(bf16)
    delta_all = jnp.sum((do_ref[...].astype(f32) * o_ref[...].astype(f32)).T, axis=0, keepdims=True)
    dk_sum[...] = jnp.zeros_like(dk_sum)
    dv_sum[...] = jnp.zeros_like(dv_sum)
    def unrotate(values):
        return values * cos_ref[...] - pltpu.roll(values, HEAD_DIM // 2, 1) * sin_ref[...]
    dq_parts = []
    for start in range(0, SLAB, BLOCK):
        stop = start + BLOCK
        queries, grads = ql_ref[start:stop], do_ref[start:stop]
        parts = score_blocks(kl_ref, queries, bias_ref, start, stop)
        lse, delta = lse_ref[0, :, start:stop], delta_all[:, start:stop]
        at, dq = 0, 0.0
        for part in parts:
            span = slice(at, at + part.shape[0])
            probs = jnp.exp2(part * log2_scale - lse)
            dv_sum[span] += mm(probs.astype(bf16), grads)
            dscore = (probs * (mm_nt(vl_ref[span], grads) - delta)).astype(bf16)
            dk_sum[span] += mm(dscore, queries)
            dq = dq + mm(keys_t[:, span], dscore)
            at += part.shape[0]
        dq_parts.append(dq.T)
    dq_all = jnp.concatenate(dq_parts, axis=0) * score_scale
    dv_ref[...] = dv_sum[...].astype(bf16)
    wq = unrotate(dq_all) * gain_ref[0:1, :]
    wk = unrotate(dk_sum[...] * score_scale) * gain_ref[1:2, :]
    wq_ref[...] = wq.astype(wq_ref.dtype)
    wk_ref[...] = wk.astype(wk_ref.dtype)
    first = pl.program_id(0) == 0
    for index, (weighted, source) in enumerate(((wq, q_ref), (wk, k_ref))):
        product = weighted * source[...]

        @pl.when(first)
        def _():
            sum_ref[index] = product

        @pl.when(jnp.logical_not(first))
        def _():
            sum_ref[index] += product

    if sems:

        @pl.when(pl.program_id(0) == pl.num_programs(0) - 1)
        def _():
            turned.arrived()
            turned.sent()


def attend_specs(heads):
    col = lambda base: pl.BlockSpec((SLAB, HEAD_DIM), lambda h: (0, base * heads + h))
    whole = lambda shape: pl.BlockSpec(shape, lambda h: (0,) * len(shape))
    return col, whole

def attend(qkv_lin, inverses, gains, cosine, sine, bias):
    heads = qkv_lin.shape[1] // (3 * HEAD_DIM)
    col, whole = attend_specs(heads)
    low = jax.ShapeDtypeStruct((SLAB, heads * HEAD_DIM), bf16)
    return pl.pallas_call(
        attend_kernel, grid=(heads,),
        in_specs=[col(0), col(1), col(2), whole((SLAB, 8)), pl.BlockSpec((2, HEAD_DIM), lambda h: (0, h)),
                  whole((SLAB, HEAD_DIM)), whole((SLAB, HEAD_DIM)), whole((SLAB, 1))],
        out_specs=[col(0)] * 4 + [pl.BlockSpec((1, 1, SLAB), lambda h: (h, 0, 0))],
        out_shape=[low] * 4 + [jax.ShapeDtypeStruct((heads, 1, SLAB), f32)],
        compiler_params=pltpu.CompilerParams(vmem_limit_bytes=48 << 20),
        cost_estimate=pl.CostEstimate(flops=heads*4*SLAB*SLAB*HEAD_DIM, bytes_accessed=heads*SLAB*HEAD_DIM*20, transcendentals=heads*SLAB*SLAB),
        name="attend",
    )(qkv_lin, qkv_lin, qkv_lin, inverses, gains, cosine, sine, bias)

def attend_back(ql, kl, vl, o, do, lse, qkv_lin, gains, cosine, sine, bias, middle=None):
    heads = ql.shape[1] // HEAD_DIM
    col, whole = attend_specs(heads)
    wide = jax.ShapeDtypeStruct(ql.shape, f32)
    outs = [wide, wide, jax.ShapeDtypeStruct(ql.shape, bf16)]
    outs.append(jax.ShapeDtypeStruct((2, SLAB, HEAD_DIM), f32))
    moved, turned, params, sems = [], [], dict(vmem_limit_bytes=48 << 20), []
    if middle is not None:
        moved, turned = [middle], [jax.ShapeDtypeStruct((SLAB, middle.shape[2]), bf16)]
        params.update(collective_id=10, has_side_effects=True)
        sems = [pltpu.SemaphoreType.DMA((4,))] * 3
    hbm = pl.BlockSpec(memory_space=pl.ANY)
    return pl.pallas_call(
        attend_back_kernel,
        grid=(heads,),
        in_specs=[col(0)] * 5
        + [pl.BlockSpec((1, 1, SLAB), lambda h: (h, 0, 0)), col(0), col(1)]
        + [pl.BlockSpec((2, HEAD_DIM), lambda h: (0, h))]
        + [whole((SLAB, HEAD_DIM)), whole((SLAB, HEAD_DIM)), whole((SLAB, 1))]
        + [hbm] * len(moved),
        out_specs=[col(0)] * 3 + [whole((2, SLAB, HEAD_DIM))] + [hbm] * len(turned),
        out_shape=outs + turned,
        scratch_shapes=[pltpu.VMEM((SLAB, HEAD_DIM), f32)] * 2 + sems,
        compiler_params=pltpu.CompilerParams(**params),
        cost_estimate=pl.CostEstimate(
            flops=heads * 10 * SLAB * SLAB * HEAD_DIM,
            bytes_accessed=heads * SLAB * HEAD_DIM * 30,
            transcendentals=heads * SLAB * SLAB,
        ),
        name="attend_back",
    )(ql, kl, vl, o, do, lse, qkv_lin, qkv_lin, gains, cosine, sine, bias, *moved)


def dot(left, right):
    return jnp.dot(left, right, preferred_element_type=f32)


def dot_nt(left, right):
    return lax.dot_general(left, right, (((1,), (1,)), ((), ())), preferred_element_type=f32)


def dot_tn(left, right):
    return lax.dot_general(left, right, (((0,), (0,)), ((), ())), preferred_element_type=f32)


def gather_weight(local):
    half = local.shape[0] // lax.axis_size("tok")
    part = lax.dynamic_slice_in_dim(local, lax.axis_index("tok") * half, half, 0)
    return lax.all_gather(part, ("col", "tok"), axis=0, tiled=True)


def to_tokens(values):
    rows, cols = lax.axis_size("row"), lax.axis_size("col")
    width = values.shape[1]
    mixed = lax.all_to_all(values, "row", 0, 0, tiled=True)
    mixed = lax.all_to_all(mixed, "col", 0, 0, tiled=True)
    return mixed.reshape(cols, SLAB // rows, width).transpose(1, 0, 2).reshape(SLAB // rows, -1)


def from_tokens(values):
    rows, cols = lax.axis_size("row"), lax.axis_size("col")
    count = values.shape[0]
    mixed = values.reshape(count, cols, -1).transpose(1, 0, 2).reshape(cols * count, -1)
    mixed = lax.all_to_all(mixed, "col", 0, 0, tiled=True)
    return lax.all_to_all(mixed, "row", 0, 0, tiled=True)


def reorder(values, outer, inner):
    if outer == 1 or inner == 1:
        return values
    rest = values.shape[0] // (outer * inner)
    shape = (outer, inner, rest) + values.shape[1:]
    return values.reshape(shape).swapaxes(0, 1).reshape(values.shape)


def gather_tokens(values):
    rows, per_slab = lax.axis_size("row"), lax.axis_size("row") // lax.axis_size("col")
    return reorder(lax.all_gather(values, "row", axis=0, tiled=True), rows, per_slab)


def scatter_tokens(values):
    rows, per_slab = lax.axis_size("row"), lax.axis_size("row") // lax.axis_size("col")
    values = reorder(values.astype(bf16), per_slab, rows)
    return lax.psum_scatter(values, "row", scatter_dimension=0, tiled=True).astype(f32)


def token_places(length):
    slot_ids = jnp.arange(SLAB, dtype=jnp.int32)
    return jnp.where(slot_ids < PROMPT, slot_ids, length + (slot_ids - PROMPT) % CONT_LEN)


def rotation(places, head_size):
    half_dim = head_size // 2
    frequency = jnp.exp(
        -(2.0 * jnp.arange(half_dim, dtype=f32) / head_size) * math.log(rope_base)
    )
    angles = places.astype(f32)[:, None] * frequency[None, :]
    return (jnp.cos(angles), jnp.sin(angles))


def pick(adapters, ids):
    onehot = (ids[:, None] == jnp.arange(adapters.shape[0], dtype=jnp.int32)).astype(adapters.dtype)
    return jnp.tensordot(onehot, adapters, axes=1)


def place(ids, gradients):
    onehot = (jnp.arange(ADAPTERS, dtype=jnp.int32)[:, None] == ids[None, :]).astype(f32)
    total = 0.0
    for index in range(gradients.shape[0]):
        weight = onehot[:, index].reshape((ADAPTERS,) + (1,) * (gradients.ndim - 1))
        total = total + weight * gradients[index][None].astype(f32)
    return total


def block_diagonal(factors):
    count = len(factors)
    lines = []
    for index, factor in enumerate(factors):
        blank = jnp.zeros_like(factor)
        lines.append(
            jnp.concatenate([factor if k == index else blank for k in range(count)], axis=1)
        )
    return jnp.concatenate(lines, axis=0)


def enter(x, w, f1, f2):
    everything = gather_tokens(x)
    lowered = (adapter_scale * dot_nt(everything, f1)).astype(bf16)
    return everything, lowered, dot(everything, w) + dot(lowered, f2)


def leave(y, w, f1, f2):
    lowered = (adapter_scale * dot_nt(y, f1)).astype(bf16)
    return scatter_tokens(dot_nt(y, w) + dot(lowered, f2)), lowered


def split_layer(
    layer_in, cotangent, qkv_weight, out_weight, ffn_weight, down_weight, head_gain, post_gain,
    adapters, adapter_ids, tables,
):
    qkv_lower, out_raise, ffn_lower, down_raise, qkv_raise, out_lower, ffn_raise, down_lower = (
        adapters
    )
    col_count = lax.axis_size("col")
    group_base = lax.axis_index("tok") * col_count
    group = group_base + lax.axis_index("col")
    slab_ids = lax.dynamic_slice_in_dim(adapter_ids, group_base, col_count, 0)
    own_ids = lax.dynamic_index_in_dim(adapter_ids, group, 0, keepdims=False)
    size = layer_in.shape[1]
    local = jnp.concatenate([qkv_weight.transpose(1, 0, 2).reshape(size, -1), out_weight.T], axis=1)
    attn_full = gather_weight(local)
    ffn_full = gather_weight(ffn_weight.transpose(1, 0, 2).reshape(size, -1))
    down_full = gather_weight(down_weight.T)
    pieces = jnp.concatenate(
        [pick(qkv_lower[p], slab_ids[:, p]) for p in range(3)]
        + [pick(out_raise, slab_ids[:, 3])]
        + [pick(ffn_lower[p], slab_ids[:, 4 + p]) for p in range(2)]
        + [pick(down_raise, slab_ids[:, 6])]
        + [jnp.broadcast_to(jnp.pad(post_gain, ((0, 14), (0, 0))), (col_count, RANK, size))],
        axis=1,
    )
    qkv_b = block_diagonal([pick(qkv_raise[p], own_ids[p : p + 1])[0] for p in range(3)])
    out_a = pick(out_lower, own_ids[3:4])[0]
    ffn_b = block_diagonal([pick(ffn_raise[p], own_ids[4 + p : 5 + p])[0] for p in range(2)])
    down_a = pick(down_lower, own_ids[6:7])[0]
    factors = lax.all_to_all(pieces, "col", 0, 0, tiled=True)
    factors = factors.transpose(1, 0, 2).reshape(-1, D)
    qkv_a, out_b, ffn_a, down_b = (factors[part] for part in (QKV_A, OUT_B, FFN_A, DOWN_B))
    gains = factors[GAIN0.start : GAIN1.stop].astype(f32)
    width = qkv_b.shape[1]
    head_width, ff_width = width // 3, ffn_b.shape[1] // 2
    x_own = to_tokens(layer_in)
    x_all, qkv_low, qkv_lin = enter(x_own, attn_full[:, :width], qkv_a, qkv_b)
    q_lin, k_lin = qkv_lin[:, :head_width], qkv_lin[:, head_width : 2 * head_width]
    squares = jnp.stack([jnp.sum(q_lin * q_lin, axis=1), jnp.sum(k_lin * k_lin, axis=1)], axis=1)
    inverses = lax.rsqrt(lax.psum(squares, "row") / D + norm_eps)
    inverses = jnp.concatenate([inverses] * 4, axis=1)
    q_low, k_low, v_low, attn_low, log_sums = attend(qkv_lin, inverses, head_gain, *tables)
    attn_lin, out_low = leave(attn_low, attn_full[:, width:], out_a, out_b)
    hidden = x_own.astype(f32) + attn_lin * inverse_of(attn_lin) * gains[0]
    h_all, ffn_low, ffn_lin = enter(hidden.astype(bf16), ffn_full, ffn_a, ffn_b)
    gate_lin, up_lin = ffn_lin[:, :ff_width], ffn_lin[:, ff_width:]
    act_low = gated(gate_lin, up_lin).astype(bf16)
    mlp_lin, down_low = leave(act_low, down_full, down_a, down_b)
    layer_out = hidden + mlp_lin * inverse_of(mlp_lin) * gains[1]
    layer_out = from_tokens(layer_out.astype(bf16)).astype(f32)
    grad_out = to_tokens(cotangent).astype(f32)
    grad_mlp = norm_back(mlp_lin, grad_out * gains[1]).astype(bf16)
    dm_all, down_dlow, grad_act = enter(grad_mlp, down_full, down_b, down_a)
    grad_ffn = jnp.concatenate(gated_back(grad_act, gate_lin, up_lin), axis=1).astype(bf16)
    grad_ffn_in, ffn_dlow = leave(grad_ffn, ffn_full, ffn_b, ffn_a)
    grad_hidden = grad_out + grad_ffn_in
    grad_attn = norm_back(attn_lin, grad_hidden * gains[0]).astype(bf16)
    da_all, out_dlow, grad_heads = enter(grad_attn, attn_full[:, width:], out_b, out_a)
    weighted_q, weighted_k, grad_v, inner = attend_back(
        q_low, k_low, v_low, attn_low, grad_heads.astype(bf16), log_sums, qkv_lin, head_gain, *tables
    )
    inner = lax.psum(jnp.sum(inner, axis=2).T, "row")
    factor = inverses[:, :2] ** 3 * inner / D
    grad_qkv = jnp.concatenate(
        [
            (inverses[:, 0:1] * weighted_q - q_lin * factor[:, 0:1]).astype(bf16),
            (inverses[:, 1:2] * weighted_k - k_lin * factor[:, 1:2]).astype(bf16),
            grad_v,
        ],
        axis=1,
    )
    grad_qkv_in, qkv_dlow = leave(grad_qkv, attn_full[:, :width], qkv_b, qkv_a)
    grad_in = from_tokens((grad_hidden + grad_qkv_in).astype(bf16)).astype(f32)
    parts = jnp.concatenate(
        [dot_tn(qkv_dlow, x_all), dot_tn(out_low, da_all), dot_tn(ffn_dlow, h_all)]
        + [dot_tn(down_low, dm_all)]
    )
    parts = parts.astype(bf16).reshape(7, RANK, col_count, size).transpose(2, 0, 1, 3)
    parts = lax.all_to_all(parts, "col", 0, 0, tiled=True)
    placed = [place(slab_ids[:, p], parts[:, p]) for p in range(7)]
    col_grads = list(lax.psum(jnp.stack(placed).astype(bf16), ("tok", "row")).astype(f32))
    own_rows = jnp.concatenate(
        [diagonal(dot_tn(qkv_low, grad_qkv), 3), dot_tn(out_dlow, attn_low)]
        + [diagonal(dot_tn(ffn_low, grad_ffn), 2), dot_tn(down_dlow, act_low)],
        axis=1,
    )
    every = lax.all_gather(own_rows.astype(bf16), ("tok", "col"), axis=0)
    row_grads, at = [], 0
    for p in range(7):
        part = ff_width if p > 3 else head_width
        row_grads.append(place(adapter_ids[:, p], every[:, :, at : at + part]))
        at += part
    return (
        layer_out, grad_in,
        jnp.stack(col_grads[0:3]), col_grads[3], jnp.stack(col_grads[4:6]), col_grads[6],
        jnp.stack(row_grads[0:3]), row_grads[3], jnp.stack(row_grads[4:6]), row_grads[6],
    )


def flat(values):
    return values.reshape((SLAB,) + values.shape[2:])


def cube(values):
    return values.reshape((4, SLAB // 4) + values.shape[1:])


def linked_layer(
    layer_in, cotangent, qkv_weight, out_weight, ffn_weight, down_weight, head_gain, post_gain,
    adapters, adapter_ids, tables,
):
    count = SLAB // 4
    piece = (4, count, layer_in.shape[1])
    head_width, ff_width = qkv_weight.shape[2], ffn_weight.shape[2]
    width = 3 * head_width
    buffers = scatter_buffers(count)
    per = 2 * SLAB * D
    tokens = ((4, count, D), bf16)
    own = ((count, D), bf16)
    wide = ((count, D), f32)

    def gather_halves(local, axis):
        half = local.shape[axis] // 2
        return lax.dynamic_slice_in_dim(local, lax.axis_index("tok") * half, half, axis)

    def gathered(local):
        return lax.all_gather(local, ("col", "tok"), axis=0)

    attn_full = gathered(
        jnp.concatenate(
            [gather_halves(qkv_weight, 1).reshape(-1, head_width), gather_halves(out_weight, 0)]
        )
    )
    ffn_full = gathered(gather_halves(ffn_weight, 1))
    down_full = gathered(gather_halves(down_weight, 0))

    (
        x_own, cot_mid, factors, factors_t, qkv_b, out_a, out_at, ffn_b, down_a, down_at
    ) = linked(
        intake_kernel, 1,
        [(cube(layer_in),), (cube(cotangent),), adapter_ids]
        + [jnp.pad(post_gain, ((0, RANK - 2), (0, 0)))]
        + adapters,
        [own, (piece, bf16), ((128, D), bf16), ((D, 128), bf16), ((128, width), bf16)]
        + [((128, head_width), bf16), ((head_width, 128), bf16), ((128, 2 * ff_width), bf16)]
        + [((128, ff_width), bf16), ((ff_width, 128), bf16)],
        [(piece, bf16), ((4, 128, piece[2]), bf16)],
        per * 128,
    )
    low = ((4, count, 128), bf16)
    tall = ((4, count, D + 128), bf16)
    x_all, qkv_low, qkv_lin, inverses = linked(
        enter_qkv_kernel, 2,
        [x_own, (attn_full,), factors, (qkv_b,)],
        [tokens + (ANY,), low, ((4, count, width), f32, ANY), ((SLAB, 8), f32)],
        [tall, ((4, count, width), f32), ((D + 128, width), bf16), ((2, SLAB, 128), f32)]
        + [((4, 8, SLAB), f32)],
        per * width,
    )
    qkv_lin = flat(qkv_lin)
    q_low, k_low, v_low, attn_low, log_sums = attend(qkv_lin, inverses, head_gain, *tables)
    attn_lin, out_low, hidden, h_all = linked(
        leave_out_kernel, 3,
        [(cube(attn_low),), (attn_full,), out_a, factors, x_own],
        [wide, low, wide, tokens],
        [((4, count, head_width + 128), bf16), ((head_width + 128, D), bf16)] + buffers,
        per * head_width,
    )
    h_all = flat(h_all)
    ffn_low, gate_lin, up_lin, act_low = ffn(h_all, ffn_full, factors, ffn_b)
    down_low, own_out, grad_mlp, own_cot = linked(
        leave_down_kernel, 4,
        [(cube(act_low),), (down_full,), down_a, factors, (hidden,), cot_mid],
        [low, own, own, own],
        [((4, count, ff_width + 128), bf16), ((ff_width + 128, D), bf16), wide, wide] + buffers,
        per * ff_width,
    )
    dm_all, down_dlow, grad_ffn, out_mid = linked(
        back_down_kernel, 5,
        [grad_mlp, (down_full,), factors, down_at, (cube(gate_lin),), (cube(up_lin),), own_out],
        [tokens + (ANY,), low, ((4, count, 2 * ff_width), bf16, ANY), (piece, bf16)],
        [tall, ((ff_width, D + 128), bf16)]
        + [((4, count, ff_width), bf16)] * 2
        + [((4, count, 2 * ff_width), bf16)],
        per * ff_width,
    )
    ffn_dlow, grad_hidden, grad_attn = linked(
        back_ffn_kernel, 6,
        [(grad_ffn,), (ffn_full,), ffn_b, factors, factors_t, (own_cot,), (attn_lin,)],
        [low, wide, own],
        [((4, count, 2 * ff_width + 128), bf16), ((D, 2 * ff_width + 128), bf16), own, wide, wide]
        + buffers,
        per * 2 * ff_width,
    )
    grad_heads, early_cols, early_rows = linked(
        back_out_kernel, 7,
        [grad_attn, (attn_full,), factors, out_at, out_low, cube(attn_low), flat(down_low)]
        + [flat(down_dlow), ffn_low, flat(ffn_dlow), (flat(dm_all),), (act_low,)]
        + [(flat(grad_ffn),), (h_all,)],
        [((4, count, head_width), bf16), ((64, D), bf16)]
        + [((16, head_width + 3 * ff_width), bf16)],
        [tall, ((head_width, D + 128), bf16), ((SLAB, D), bf16)]
        + [((SLAB, ff_width), bf16), ((SLAB, 2 * ff_width), bf16), ((SLAB, D), bf16)]
        + [((16, D), f32), ((16, head_width), f32)],
        per * head_width,
    )
    weighted_q, weighted_k, grad_v, inner, layer_out = attend_back(
        q_low, k_low, v_low, attn_low, flat(grad_heads), log_sums, qkv_lin, head_gain, *tables,
        out_mid,
    )
    grad_qkv, own_rows = linked(
        prepare_kernel, 8,
        [(weighted_q,), (weighted_k,), grad_v, (qkv_lin,), inverses, inner, qkv_b, flat(qkv_low)]
        + [early_rows],
        [((SLAB, width + 128), bf16)]
        + [((16, width + head_width + 3 * ff_width), bf16)],
        [((SLAB, head_width), f32)] * 2
        + [((SLAB, 2 * head_width), f32), ((SLAB, 8), f32), ((4, 8, SLAB), f32)],
        per * 128,
    )
    every = lax.all_gather(own_rows, ("tok", "col"), axis=0)
    numbers = jnp.arange(ADAPTERS, dtype=jnp.int32)
    chosen = (adapter_ids.T[:, None, :] == numbers[None, :, None]).astype(f32).reshape(7, -1)
    chosen = jnp.pad(chosen, ((0, 1), (0, 0)))
    grad_in, col_parts = linked(
        back_qkv_kernel, 9,
        [cube(grad_qkv), (attn_full,), factors_t, (grad_hidden,), (x_all,)]
        + [early_cols, chosen],
        [(layer_in.shape, bf16), ((4, ADAPTERS, 32, piece[2]), bf16)],
        [((D, width + 128), bf16), wide, tokens, wide, (piece, bf16), (piece, bf16)]
        + [((4, 32, D), bf16)] * 2
        + [((4, 32, piece[2]), bf16), ((8, 32, piece[2]), bf16)]
        + [((ADAPTERS, 32, piece[2]), bf16)]
        + buffers,
        per * width,
    )
    return finish(chosen, layer_out, grad_in, col_parts, every, head_width, ff_width)


def diagonal(values, count):
    width = values.shape[1] // count
    return jnp.concatenate(
        [
            values[k * RANK : (k + 1) * RANK, k * width : (k + 1) * width]
            for k in range(count)
        ],
        axis=1,
    )


def on_device(
    layer_in,
    cotangent,
    qkv_weight,
    out_weight,
    ffn_weight,
    down_weight,
    qk_gain,
    post_gain,
    qkv_lower,
    qkv_raise,
    out_lower,
    out_raise,
    ffn_lower,
    ffn_raise,
    down_lower,
    down_raise,
    adapter_ids,
    prompt_len,
):
    group = lax.axis_index("tok") * lax.axis_size("col") + lax.axis_index("col")
    length = lax.dynamic_index_in_dim(prompt_len, group, 0, keepdims=False)
    cosine, sine = rotation(token_places(length), HEAD_DIM)
    cosine = jnp.concatenate([cosine, cosine], axis=1)
    sine = jnp.concatenate([-sine, sine], axis=1)
    slots = jnp.arange(SLAB, dtype=jnp.int32)
    bias = jnp.where((slots < length) | (slots >= PROMPT), 0.0, very_low)[:, None].astype(f32)

    plane = (lax.axis_size("tok"), lax.axis_size("row"), lax.axis_size("col"))
    layer = linked_layer if plane == (2, 4, 4) else split_layer
    adapters = [
        qkv_lower.swapaxes(2, 3), out_raise, ffn_lower.swapaxes(2, 3), down_raise,
        qkv_raise, out_lower.swapaxes(1, 2), ffn_raise, down_lower.swapaxes(1, 2),
    ]
    (
        layer_out, grad_in, qkv_lower_grad, out_raise_grad, ffn_lower_grad, down_raise_grad,
        qkv_raise_grad, out_lower_grad, ffn_raise_grad, down_lower_grad,
    ) = layer(
        layer_in, cotangent, qkv_weight, out_weight, ffn_weight, down_weight, qk_gain.astype(f32),
        post_gain, adapters, adapter_ids, (cosine, sine, bias),
    )
    return (
        layer_out,
        grad_in,
        qkv_lower_grad.swapaxes(2, 3),
        qkv_raise_grad,
        out_lower_grad.swapaxes(1, 2),
        out_raise_grad,
        ffn_lower_grad.swapaxes(2, 3),
        ffn_raise_grad,
        down_lower_grad.swapaxes(1, 2),
        down_raise_grad,
    )


def solution(mesh):
    return jax.shard_map(
        on_device,
        mesh=mesh,
        in_specs=(
            P(("tok", "row"), "col"),
            P(("tok", "row"), "col"),
            P(None, "col", "row"),
            P("row", "col"),
            P(None, "col", "row"),
            P("row", "col"),
            P(None, "row"),
            P(None, "col"),
            P(None, None, "col", None),
            P(None, None, None, "row"),
            P(None, "row", None),
            P(None, None, "col"),
            P(None, None, "col", None),
            P(None, None, None, "row"),
            P(None, "row", None),
            P(None, None, "col"),
            P(),
            P(),
        ),
        out_specs=(
            P(("tok", "row"), "col"),
            P(("tok", "row"), "col"),
            P(None, None, "col", None),
            P(None, None, None, "row"),
            P(None, "row", None),
            P(None, None, "col"),
            P(None, None, "col", None),
            P(None, None, None, "row"),
            P(None, "row", None),
            P(None, None, "col"),
        ),
        check_vma=False,
    )
```

```python
import functools
import math

import jax
import jax.numpy as jnp
from jax import lax
from jax.experimental import pallas as pl
from jax.experimental.pallas import tpu as pltpu
from jax.sharding import PartitionSpec as P

D = 2048
HEAD_DIM = 128
RANK = 16
ADAPTERS = 8
PROMPT = 1024
CONT_LEN = 128
SLAB = 1152

adapter_scale = 2.0
norm_eps = 1e-06
rope_base = 500000.0
very_low = -1e30
bf16 = jnp.bfloat16
f32 = jnp.float32
log2_scale = math.log2(math.e) / math.sqrt(HEAD_DIM)
score_scale = 1.0 / math.sqrt(HEAD_DIM)
BLOCK = 384
TILE = 512
MESH = pl.DeviceIdType.MESH


def mm(left, right):
    return jnp.dot(left, right, preferred_element_type=f32)


def mm_nt(left, right):
    return lax.dot_general(left, right, (((1,), (1,)), ((), ())), preferred_element_type=f32)


class Links:
    def __init__(self, send_sem, recv_sem, local_sem):
        self.tok = lax.axis_index("tok")
        self.row, self.col = lax.axis_index("row"), lax.axis_index("col")
        self.xn, self.yn, self.dg = self.row ^ 1, self.row ^ 2, self.row ^ 3
        self.send_sem, self.recv_sem, self.local_sem = send_sem, recv_sem, local_sem
        self.used, self.local_used = 0, 0

    def take(self, count):
        self.used += count
        return self.used - count

    def copy(self, source, target, index, recv_index, row, col=None, tok=None):
        return pltpu.make_async_remote_copy(
            src_ref=source,
            dst_ref=target,
            send_sem=self.send_sem.at[index],
            recv_sem=self.recv_sem.at[recv_index],
            device_id={
                "tok": self.tok if tok is None else tok,
                "row": row,
                "col": self.col if col is None else col,
            },
            device_id_type=MESH,
        )

    def local(self, source, target):
        self.local_used += 1
        return pltpu.make_async_copy(source, target, self.local_sem.at[self.local_used - 1])

    def plan(self, *pairs):
        return [self.local(source, target) for source, target in pairs]

    def fetch(self, *pairs):
        return start_all(self.plan(*pairs))

    def greet(self, rows=2, columns=False, twin=False):
        barrier = pltpu.get_barrier_semaphore()
        places = [(self.tok, self.row ^ step, self.col) for step in range(1, rows + 1)]
        if columns:
            places += [(self.tok, self.row, self.col ^ step) for step in range(1, 4)]
        if twin:
            places += [(self.tok ^ 1, self.row, self.col)]
        for tok, row, col in places:
            pl.semaphore_signal(
                barrier,
                inc=1,
                device_id={"tok": tok, "row": row, "col": col},
                device_id_type=MESH,
            )
        pl.semaphore_wait(barrier, len(places))


def start_all(copies):
    for copy in copies:
        copy.start()
    return copies


def wait_all(copies):
    for copy in copies:
        copy.wait()


class Exchange:
    def __init__(self, links, axis, piece_at, slot_at):
        self.links, self.axis = links, axis
        self.me = links.row if axis == "row" else links.col
        self.piece_at, self.slot_at = piece_at, slot_at
        self.base = links.take(3)
        self.own = links.local(piece_at(self.me), slot_at(self.me))

    def copy(self, source, target, step):
        links, other, index = self.links, self.me ^ step, self.base + step - 1
        row, col = (other, links.col) if self.axis == "row" else (links.row, other)
        return links.copy(source, target, index, index, row, col)

    def start(self):
        for step in range(1, 4):
            self.copy(self.piece_at(self.me ^ step), self.slot_at(self.me), step).start()
        self.own.start()

    def arrived(self):
        for step in range(1, 4):
            landed = self.slot_at(self.me ^ step)
            self.copy(landed, landed, step).wait_recv()
        self.own.wait()

    def sent(self):
        for step in range(1, 4):
            self.copy(self.piece_at(self.me ^ step), self.slot_at(self.me), step).wait_send()


def features(ref, width):
    return lambda col: ref.at[:, pl.ds(pl.multiple_of(col * width, width), width)]


def slot(ref):
    return lambda key: ref.at[key]


def token_rows(ref, count):
    return lambda row: ref.at[pl.ds(pl.multiple_of(row * count, 16), count)]


def gather(links, all_ref, work, before=None, after=None):
    me, xn, yn, dg = links.row, links.xn, links.yn, links.dg
    half = all_ref.shape[1] // 2
    top, low = pl.ds(0, half), pl.ds(half, half)
    base = links.take(6)

    def move(owner, part, index, other):
        place = all_ref.at[owner, part, pl.ds(0, D)]
        return links.copy(place, place, base + index, base + index, other)

    sends = [move(me, top, 0, xn), move(me, low, 1, yn), move(me, low, 2, xn), move(me, top, 3, yn)]
    for copy in sends:
        copy.start()
    if before:
        before()
    if work:
        work(me)
    move(xn, top, 0, xn).wait_recv()
    sends.append(move(xn, top, 4, yn))
    sends[-1].start()
    move(yn, low, 1, yn).wait_recv()
    sends.append(move(yn, low, 5, xn))
    sends[-1].start()
    if after:
        after()
    move(xn, low, 2, xn).wait_recv()
    if work:
        work(xn)
    move(yn, top, 3, yn).wait_recv()
    if work:
        work(yn)
    move(dg, top, 4, yn).wait_recv()
    move(dg, low, 5, xn).wait_recv()
    if work:
        work(dg)
    for copy in sends:
        copy.wait_send()


SLICES = 4


def scatter(links, product, o_ref, out_buf, relay_buf, final_buf, block=None, ready=None, hooks=None):
    me, xn, yn, dg = links.row, links.xn, links.yn, links.dg
    count, width = o_ref.shape[0], o_ref.shape[1] // SLICES
    half = count // 2
    top, low = pl.ds(0, half), pl.ds(half, half)
    base = links.take(6 * SLICES)
    all_copies = []

    def columns(k):
        at = block(k) * width if block else k * width
        return pl.ds(pl.multiple_of(at, width), width)

    def add(place, k, rows, relay):
        out_buf[place, k, rows] = (
            out_buf[place, k, rows].astype(f32) + relay_buf[relay, k].astype(f32)
        ).astype(bf16)

    def relay(k):
        copies = all_copies[k]
        copies[0].wait_recv()
        add(2, k, top, 0)
        copies[4].start()
        copies[1].wait_recv()
        add(1, k, low, 1)
        copies[5].start()

    def finish(k):
        for copy in all_copies[k][2:]:
            copy.wait_recv()

    for k in range(SLICES):
        cols = columns(k)

        def move(source, target, index, other, k=k):
            at = base + 6 * k + index
            return links.copy(source, target, at, at, other)

        copies = [
            move(out_buf.at[0, k, top], relay_buf.at[0, k], 0, xn),
            move(out_buf.at[0, k, low], relay_buf.at[1, k], 1, yn),
            move(out_buf.at[1, k, top], final_buf.at[0, k, top], 2, xn),
            move(out_buf.at[2, k, low], final_buf.at[1, k, low], 3, yn),
            move(out_buf.at[2, k, top], final_buf.at[1, k, top], 4, yn),
            move(out_buf.at[1, k, low], final_buf.at[0, k, low], 5, xn),
        ]
        all_copies.append(copies)
        if ready:
            ready(k)
        for place, (owner, first) in enumerate(((dg, (0, 1)), (xn, (2,)), (yn, (3,)))):
            out_buf[place, k] = product(owner, k, cols).astype(bf16)
            for index in first:
                copies[index].start()
        if k:
            relay(k - 1)
        if hooks:
            o_ref[:, cols] = product(me, k, cols)
            hooks[k](columns, finish)
    for k in range(SLICES):
        if k == (0 if hooks else SLICES // 2):
            relay(SLICES - 1)
        if not hooks:
            o_ref[:, columns(k)] = product(me, k, columns(k))

    def sent():
        for copies in all_copies:
            for copy in copies:
                copy.wait_send()

    return columns, finish, sent


def finish_all(result):
    _, finish, sent = result
    for k in range(SLICES):
        finish(k)
    sent()


def each_tile(width, step, body):
    @pl.loop(0, width // step)
    def _(tile):
        body(pl.multiple_of(tile * step, step))


def lower(rows, factor):
    step = rows.shape[1] // 4
    parts = [
        mm_nt(rows[:, at : at + step], factor[:, at : at + step])
        for at in range(0, rows.shape[1], step)
    ]
    return (adapter_scale * functools.reduce(jnp.add, parts)).astype(bf16)


def leave_product(y_ref, weight, f1_ref, low_ref, loads):
    depth = f1_ref.shape[1]
    used = []

    def product(owner, k, cols):
        if k == 0:
            if loads:
                loads[len(used)].wait()
            used.append(True)
            lowered = lower(y_ref[owner, :, :depth], f1_ref[...])
            low_ref[owner] = lowered
            y_ref[owner, :, depth:] = lowered
        return weight(y_ref[owner], cols)

    return product


class Streams:
    def __init__(self, links, rows, blocks, late=()):
        order = (links.dg, links.xn, links.yn, links.row)
        self.rows = []
        if rows:
            cols = pl.ds(0, rows[0].shape[2])
            self.rows = links.plan(*[(rows[0].at[k], rows[1].at[k, :, cols]) for k in order])
        self.blocks = blocks
        self.late = links.plan(*late)
        start_all(self.rows[:1])
        start_all(blocks[0])

    def ready(self, k):
        wait_all(self.blocks[k])
        if k == 0:
            start_all(self.rows[1:])
        if k < SLICES - 1:
            start_all(self.blocks[k + 1])
        if k == 1:
            start_all(self.late)


def load_qkv(links, w_hbm, w_ref, blocks):
    half, width = w_hbm.shape[1] // 4, w_hbm.shape[2]
    return [
        links.plan(
            *[
                (
                    w_hbm.at[2 * c + t, pl.ds(p * half, half)],
                    w_ref.at[
                        pl.ds(pl.multiple_of((2 * c + t) * half, half), half),
                        pl.ds(p * width, width),
                    ],
                )
                for t in range(2)
                for p in range(3)
            ]
        )
        for c in blocks
    ]


def load_out(links, w_hbm, w_ref):
    half, width = w_hbm.shape[1] // 4, w_hbm.shape[2]
    return [
        links.plan(
            *[
                (
                    w_hbm.at[2 * c + t, pl.ds(3 * half, half)],
                    w_ref.at[pl.ds(t * half, half), pl.ds(c * width, width)],
                )
                for t in range(2)
            ]
        )
        for c in range(4)
    ]


def load_down(links, w_hbm, w_ref):
    half, width = w_hbm.shape[1:]
    return [
        links.plan(
            *[
                (
                    w_hbm.at[2 * c + t],
                    w_ref.at[pl.ds(t * half, half), pl.ds(c * width, width)],
                )
                for t in range(2)
            ]
        )
        for c in range(4)
    ]


def load_ffn(links, w_hbm, w_ref):
    half, width = w_hbm.shape[2:]
    return [
        links.plan(
            *[
                (
                    w_hbm.at[2 * c + t, g],
                    w_ref.at[pl.ds((2 * c + t) * half, half), pl.ds(g * width, width)],
                )
                for t in range(2)
                for g in range(2)
            ]
        )
        for c in range(4)
    ]


def inverse_of(values):
    return lax.rsqrt(jnp.mean(values * values, axis=1, keepdims=True) + norm_eps)


def norm_back(values, weighted):
    inverse = inverse_of(values)
    inner = jnp.mean(values * weighted, axis=1, keepdims=True)
    return inverse * weighted - values * (inverse**3 * inner)


def gated(gate, up):
    return gate * jax.nn.sigmoid(gate) * up


def gated_back(grad, gate, up):
    sig = jax.nn.sigmoid(gate)
    act = gate * sig
    return (grad * up * (sig + act * (1.0 - sig)), grad * act)


QKV_A, OUT_B, FFN_A, DOWN_B = slice(0, 48), slice(48, 64), slice(64, 96), slice(96, 112)
GAIN0, GAIN1 = slice(112, 113), slice(113, 114)


def share_stats(links, stat_ref, first, second):
    blank = jnp.zeros((6, first.shape[0]), f32)
    sums = [jnp.sum(value.T, axis=0, keepdims=True) for value in (first, second)]
    stat_ref[links.row] = jnp.concatenate(sums + [blank], axis=0)
    base = links.take(3)
    mine = stat_ref.at[links.row]
    copies = []
    for index, other in enumerate((links.xn, links.yn, links.dg)):
        copies.append(links.copy(mine, mine, base + index, base + index, other))
        copies[-1].start()
    for index, other in enumerate((links.xn, links.yn, links.dg)):
        theirs = stat_ref.at[other]
        links.copy(theirs, theirs, base + index, base + index, other).wait_recv()
    for copy in copies:
        copy.wait_send()
    return stat_ref[0] + stat_ref[1] + stat_ref[2] + stat_ref[3]


def lane_sums(values):
    return functools.reduce(
        jnp.add, [values[:, at : at + 128] for at in range(0, values.shape[1], 128)]
    )


def intake_kernel(
    x_hbm, cot_hbm, ids_ref, gain_ref, qkv_lower_ref, out_raise_ref, ffn_lower_ref, down_raise_ref,
    qkv_raise_ref, out_lower_ref, ffn_raise_ref, down_lower_ref,
    own_ref, cot_ref, factors_ref, factors_t_ref, qkv_b_ref, out_a_ref, out_at_ref, ffn_b_ref,
    down_a_ref, down_at_ref,
    middle_ref, pieces_ref, send_sem, recv_sem, local_sem,
):
    links = Links(send_sem, recv_sem, local_sem)
    links.greet(rows=3, columns=True)
    width = pieces_ref.shape[2]
    first = Exchange(links, "row", slot(x_hbm), slot(middle_ref))
    second = Exchange(links, "col", slot(middle_ref), features(own_ref, width))
    turned = Exchange(links, "row", slot(cot_hbm), slot(cot_ref))
    spread = Exchange(links, "col", slot(pieces_ref), features(factors_ref, width))
    first.start()
    base = 4 * links.tok
    for place in range(4):
        for p in range(7):
            chosen = ids_ref[base + place, p]
            if p < 3:
                value = qkv_lower_ref[p, chosen]
            elif p == 3:
                value = out_raise_ref[chosen]
            elif p < 6:
                value = ffn_lower_ref[p - 4, chosen]
            else:
                value = down_raise_ref[chosen]
            pieces_ref[place, p * RANK : (p + 1) * RANK] = value
        pieces_ref[place, 7 * RANK :] = gain_ref[...]
    spread.start()
    first.arrived()
    second.start()
    turned.start()
    own = base + links.col
    for ref in (qkv_b_ref, out_a_ref, ffn_b_ref, down_a_ref):
        ref[...] = jnp.zeros_like(ref)
    for p in range(3):
        cols = slice(p * qkv_raise_ref.shape[3], (p + 1) * qkv_raise_ref.shape[3])
        qkv_b_ref[p * RANK : (p + 1) * RANK, cols] = qkv_raise_ref[p, ids_ref[own, p]]
    for p in range(2):
        cols = slice(p * ffn_raise_ref.shape[3], (p + 1) * ffn_raise_ref.shape[3])
        rows = slice((4 + p) * RANK, (5 + p) * RANK)
        ffn_b_ref[rows, cols] = ffn_raise_ref[p, ids_ref[own, 4 + p]]
    out_a_ref[OUT_B] = out_lower_ref[ids_ref[own, 3]]
    down_a_ref[DOWN_B] = down_lower_ref[ids_ref[own, 6]]
    spread.arrived()
    for source, target in (
        (out_a_ref, out_at_ref), (down_a_ref, down_at_ref), (factors_ref, factors_t_ref)
    ):
        target[...] = source[...].astype(f32).T.astype(bf16)
    for exchange in (second, turned):
        exchange.arrived()
    for exchange in (first, spread, second, turned):
        exchange.sent()


def enter_qkv_kernel(
    x_ref, w_hbm, factors_ref, f2_ref,
    all_hbm, low_ref, lin_hbm, inv_ref,
    all_ref, lin_ref, w_ref, sq_ref, stat_ref, send_sem, recv_sem, local_sem,
):
    links = Links(send_sem, recv_sem, local_sem)
    width = w_ref.shape[1]
    loads = start_all(sum(load_qkv(links, w_hbm, w_ref, range(4)), []))
    loads += links.fetch((f2_ref, w_ref.at[pl.ds(D, 128)]))
    all_ref[links.row, :, :D] = x_ref[...]
    links.greet(rows=3)
    count = x_ref.shape[0]
    stores = []

    def work(owner):
        lowered = lower(all_ref[owner, :, :D], factors_ref[...])
        low_ref[owner] = lowered
        all_ref[owner, :, D:] = lowered
        rows = all_ref[owner]
        third = width // 3
        for index in range(3):
            cols = slice(index * third, (index + 1) * third)
            value = mm(rows, w_ref[:, cols])
            lin_ref[owner, :, cols] = value
            if index < 2:
                place = pl.ds(pl.multiple_of(owner * count, 8), count)
                sq_ref[index, place] = lane_sums(value * value)
        stores.extend(
            links.fetch(
                (lin_ref.at[owner], lin_hbm.at[owner]),
                (all_ref.at[owner, :, pl.ds(0, D)], all_hbm.at[owner]),
            )
        )

    gather(links, all_ref, work, lambda: wait_all(loads))
    total = share_stats(links, stat_ref, sq_ref[0], sq_ref[1])
    inv_ref[...] = lax.rsqrt(total / D + norm_eps).T
    wait_all(stores)


def summed(o_ref, final_buf, rows):
    return o_ref[rows] + jnp.concatenate(
        [
            final_buf[0, k, rows].astype(f32) + final_buf[1, k, rows].astype(f32)
            for k in range(SLICES)
        ],
        axis=1,
    )


def leave_out_kernel(
    y_hbm, w_hbm, f1_ref, factors_ref, x_ref,
    lin_ref, low_ref, hidden_ref, all_ref,
    y_ref, w_ref, out_buf, relay_buf, final_buf, send_sem, recv_sem, local_sem,
):
    links = Links(send_sem, recv_sem, local_sem)
    streams = Streams(links, (y_hbm, y_ref), load_out(links, w_hbm, w_ref))
    w_ref[f1_ref.shape[1] :] = factors_ref[...]
    links.greet()
    product = leave_product(
        y_ref, lambda rows, cols: mm(rows, w_ref[:, cols]), f1_ref, low_ref, streams.rows
    )
    finish_all(
        scatter(links, product, lin_ref, out_buf, relay_buf, final_buf, ready=streams.ready)
    )
    gain = factors_ref[GAIN0].astype(f32)

    @pl.loop(0, lin_ref.shape[0] // 16)
    def _(tile):
        rows = pl.ds(pl.multiple_of(tile * 16, 16), 16)
        value = summed(lin_ref, final_buf, rows)
        lin_ref[rows] = value
        hidden = x_ref[rows].astype(f32) + value * inverse_of(value) * gain
        hidden_ref[rows] = hidden
        all_ref[links.row, rows] = hidden.astype(bf16)

    gather(links, all_ref, None)


def flat_weight(ref):
    return ref[...].reshape(D, ref.shape[3])


def ffn_kernel(h_ref, wg_ref, wu_ref, factors_ref, fg_ref, fu_ref, low_ref, gate_ref, up_ref, act_ref):
    @pl.when(pl.program_id(0) == 0)
    def _():
        low_ref[...] = lower(h_ref[...], factors_ref[...])

    lowered = low_ref[...]
    rank = lowered.shape[1] // 2
    for at in range(0, SLAB, BLOCK):
        rows = slice(at, at + BLOCK)
        gate = mm(h_ref[rows], flat_weight(wg_ref)) + mm(lowered[rows], fg_ref[...])
        up = mm(h_ref[rows], flat_weight(wu_ref)) + mm(lowered[rows], fu_ref[...])
        gate_ref[rows] = gate.astype(bf16)
        up_ref[rows] = up.astype(bf16)
        act_ref[rows] = gated(gate, up).astype(bf16)


def ffn(h_all, w, factors, f2):
    width = f2.shape[1] // 2
    step = 256
    tiles = width // step
    low = jax.ShapeDtypeStruct((SLAB, f2.shape[0]), bf16)
    wide = jax.ShapeDtypeStruct((SLAB, width), bf16)
    whole = lambda value: pl.BlockSpec(value.shape, lambda t: (0, 0))
    cols = lambda rows, base: pl.BlockSpec((rows, step), lambda t: (0, base * tiles + t))
    block = (w.shape[0], 1, w.shape[2], step)
    part = lambda which: pl.BlockSpec(block, lambda t: (0, which, 0, t))
    return pl.pallas_call(
        ffn_kernel,
        grid=(tiles,),
        in_specs=[whole(h_all), part(0), part(1), whole(factors)]
        + [cols(f2.shape[0], 0), cols(f2.shape[0], 1)],
        out_specs=[whole(low)] + [cols(SLAB, 0)] * 3,
        out_shape=[low, wide, wide, wide],
        compiler_params=pltpu.CompilerParams(vmem_limit_bytes=48 << 20),
        cost_estimate=pl.CostEstimate(
            flops=4 * SLAB * D * width, bytes_accessed=4 * D * width + 10 * SLAB * width,
            transcendentals=SLAB * width,
        ),
        name="ffn",
    )(h_all, w, w, factors, f2, f2)


def leave_down_kernel(
    y_hbm, w_hbm, f1_ref, factors_ref, hidden_hbm, cot_ref,
    low_ref, out_ref, dm_ref, own_cot_ref,
    y_ref, w_ref, hidden_ref, lin_ref, out_buf, relay_buf, final_buf,
    send_sem, recv_sem, local_sem,
):
    links = Links(send_sem, recv_sem, local_sem)
    streams = Streams(
        links, (y_hbm, y_ref), load_down(links, w_hbm, w_ref), [(hidden_hbm, hidden_ref)]
    )
    links.greet(columns=True)
    turned = Exchange(links, "col", slot(cot_ref), features(own_cot_ref, cot_ref.shape[2]))
    w_ref[f1_ref.shape[1] :] = factors_ref[...]
    product = leave_product(
        y_ref, lambda rows, cols: mm(rows, w_ref[:, cols]), f1_ref, low_ref, streams.rows
    )
    def ready(k):
        if k == 2:
            turned.start()
        streams.ready(k)

    finish_all(
        scatter(
            links, product, lin_ref, out_buf, relay_buf, final_buf,
            ready=ready,
        )
    )
    turned.arrived()
    wait_all(streams.late)
    gain = factors_ref[GAIN1].astype(f32)

    @pl.loop(0, lin_ref.shape[0] // 16)
    def _(tile):
        rows = pl.ds(pl.multiple_of(tile * 16, 16), 16)
        value = summed(lin_ref, final_buf, rows)
        out_ref[rows] = (hidden_ref[rows] + value * inverse_of(value) * gain).astype(bf16)
        dm_ref[rows] = norm_back(value, own_cot_ref[rows].astype(f32) * gain).astype(bf16)

    turned.sent()


def widen(source_ref, target_ref):
    @pl.loop(0, source_ref.shape[0] // 64)
    def _(tile):
        rows = pl.ds(pl.multiple_of(tile * 64, 64), 64)
        target_ref[rows] = source_ref[rows].astype(f32)


def finish_kernel(
    chosen_ref, out_ref, grad_ref, parts_ref, every_ref,
    out32_ref, grad32_ref, qkv_lower_ref, out_raise_ref, ffn_lower_ref, down_raise_ref,
    qkv_raise_ref, out_lower_ref, ffn_raise_ref, down_lower_ref,
):
    widen(out_ref, out32_ref)
    widen(grad_ref, grad32_ref)
    targets = [qkv_lower_ref.at[p] for p in range(3)]
    targets += [out_raise_ref, ffn_lower_ref.at[0], ffn_lower_ref.at[1], down_raise_ref]
    for p, target in enumerate(targets):
        rows = slice(p % 2 * RANK, (p % 2 + 1) * RANK)
        for adapter in range(ADAPTERS):
            target[adapter] = parts_ref[p // 2, adapter, rows].astype(f32)
    targets = [qkv_raise_ref.at[p] for p in range(3)]
    targets += [out_lower_ref, ffn_raise_ref.at[0], ffn_raise_ref.at[1], down_lower_ref]
    base = 0
    for p, target in enumerate(targets):
        step = 256
        weights = [chosen_ref[p, at] for at in range(64)]

        @pl.loop(0, target.shape[2] // step)
        def _(tile, p=p, target=target, base=base, weights=weights):
            cols = pl.ds(pl.multiple_of(base + tile * step, step), step)
            here = pl.ds(pl.multiple_of(tile * step, step), step)
            values = [every_ref[g, :, cols].astype(f32) for g in range(8)]
            for adapter in range(ADAPTERS):
                terms = [weights[adapter * 8 + g] * values[g] for g in range(8)]
                target[adapter, :, here] = functools.reduce(jnp.add, terms)

        base += target.shape[2]


def finish(chosen, layer_out, grad_in, col_parts, every, head_width, ff_width):
    piece = col_parts.shape[3]

    def out(*shape):
        return jax.ShapeDtypeStruct(shape, f32)

    return pl.pallas_call(
        finish_kernel,
        in_specs=[SMEM] + [VMEM] * 4,
        out_specs=[VMEM] * 10,
        out_shape=[
            out(*layer_out.shape), out(*grad_in.shape),
            out(3, ADAPTERS, RANK, piece), out(ADAPTERS, RANK, piece),
            out(2, ADAPTERS, RANK, piece), out(ADAPTERS, RANK, piece),
            out(3, ADAPTERS, RANK, head_width), out(ADAPTERS, RANK, head_width),
            out(2, ADAPTERS, RANK, ff_width), out(ADAPTERS, RANK, ff_width),
        ],
        compiler_params=pltpu.CompilerParams(vmem_limit_bytes=48 << 20),
        cost_estimate=pl.CostEstimate(flops=10**8, bytes_accessed=16 << 20, transcendentals=0),
        name="finish",
    )(chosen, layer_out, grad_in, col_parts, every)


def back_down_kernel(
    dm_ref, w_hbm, factors_ref, f2_ref, gate_hbm, up_hbm, out_ref,
    all_hbm, low_ref, grad_hbm, out_mid_ref,
    all_ref, w_ref, gate_ref, up_ref, grad_ref, send_sem, recv_sem, local_sem,
):
    links = Links(send_sem, recv_sem, local_sem)
    loads = start_all(sum(load_down(links, w_hbm, w_ref), []))
    order = (links.row, links.xn, links.yn, links.dg)
    gates = [
        links.plan((gate_hbm.at[k], gate_ref.at[k]), (up_hbm.at[k], up_ref.at[k])) for k in order
    ]
    start_all(gates[0])
    all_ref[links.row, :, :D] = dm_ref[...]
    w_ref[:, D:] = f2_ref[...]
    links.greet(columns=True)
    width = w_ref.shape[0]
    turned = Exchange(links, "col", features(out_ref, out_mid_ref.shape[2]), slot(out_mid_ref))
    stores = []

    def before():
        wait_all(loads)
        for gate in gates[1:]:
            start_all(gate)

    def work(owner):
        wait_all(gates[len(stores) // 2])
        lowered = lower(all_ref[owner, :, :D], factors_ref[...])
        low_ref[owner] = lowered
        all_ref[owner, :, D:] = lowered

        def body(at):
            cols, far = pl.ds(at, TILE), pl.ds(pl.multiple_of(width + at, TILE), TILE)
            grad = mm_nt(all_ref[owner], w_ref[cols, :])
            gate, up = gate_ref[owner, :, cols].astype(f32), up_ref[owner, :, cols].astype(f32)
            grad_gate, grad_up = gated_back(grad, gate, up)
            grad_ref[owner, :, cols] = grad_gate.astype(bf16)
            grad_ref[owner, :, far] = grad_up.astype(bf16)

        each_tile(width, TILE, body)
        stores.extend(
            links.fetch(
                (grad_ref.at[owner], grad_hbm.at[owner]),
                (all_ref.at[owner, :, pl.ds(0, D)], all_hbm.at[owner]),
            )
        )

    gather(links, all_ref, work, before, turned.start)
    turned.arrived()
    turned.sent()
    wait_all(stores)


def back_ffn_kernel(
    y_hbm, w_hbm, f1_ref, factors_ref, factors_t_ref, cot_hbm, attn_hbm,
    low_ref, hidden_ref, da_ref,
    y_ref, w_ref, cot_ref, attn_ref, lin_ref, out_buf, relay_buf, final_buf,
    send_sem, recv_sem, local_sem,
):
    links = Links(send_sem, recv_sem, local_sem)
    streams = Streams(
        links,
        (y_hbm, y_ref),
        load_ffn(links, w_hbm, w_ref),
        [(cot_hbm, cot_ref), (attn_hbm, attn_ref)],
    )
    links.greet()
    w_ref[:, f1_ref.shape[1] :] = factors_t_ref[...]
    product = leave_product(
        y_ref, lambda rows, cols: mm_nt(rows, w_ref[cols, :]), f1_ref, low_ref, streams.rows
    )
    finish_all(
        scatter(
            links, product, lin_ref, out_buf, relay_buf, final_buf,
            ready=streams.ready,
        )
    )
    wait_all(streams.late)
    gain = factors_ref[GAIN0].astype(f32)

    @pl.loop(0, lin_ref.shape[0] // 16)
    def _(tile):
        rows = pl.ds(pl.multiple_of(tile * 16, 16), 16)
        value = summed(lin_ref, final_buf, rows) + cot_ref[rows].astype(f32)
        hidden_ref[rows] = value
        da_ref[rows] = norm_back(attn_ref[rows], value * gain).astype(bf16)


def mm_tn(left, right):
    return lax.dot_general(left, right, (((0,), (0,)), ((), ())), preferred_element_type=f32)


def back_out_kernel(
    da_ref, w_hbm, factors_ref, f2_ref, out_low_ref, attn_ref, down_low_ref, down_dlow_ref,
    ffn_low_ref, ffn_dlow_ref, dm_hbm, act_hbm, grad_hbm, h_hbm,
    heads_ref, cols_ref, rows_ref,
    all_ref, w_ref, dm_ref, act_ref, grad_ref, h_ref, raise_ref, lower_ref, send_sem, recv_sem, local_sem,
):
    links = Links(send_sem, recv_sem, local_sem)
    load = start_all(sum(load_out(links, w_hbm, w_ref), []))
    all_ref[links.row, :, :D] = da_ref[...]
    w_ref[:, D:] = f2_ref[...]
    links.greet()
    loads = []

    def before():
        loads.extend(
            links.fetch((dm_hbm, dm_ref), (act_hbm, act_ref), (grad_hbm, grad_ref), (h_hbm, h_ref))
        )
        wait_all(load)

    heads, half = heads_ref.shape[2], grad_ref.shape[1] // 2

    def after():
        wait_all(loads)
        down_raise = mm_tn(down_low_ref[:, DOWN_B], dm_ref[...])
        cols_ref[3 * RANK : 4 * RANK] = down_raise.astype(bf16)
        cols_ref[RANK : 3 * RANK] = mm_tn(ffn_dlow_ref[:, FFN_A], h_ref[...]).astype(bf16)
        for p in range(2):
            low = ffn_low_ref[:, (4 + p) * RANK : (5 + p) * RANK]
            raised = mm_tn(low, grad_ref[:, p * half : (p + 1) * half])
            rows_ref[:, heads + p * half : heads + (p + 1) * half] = raised.astype(bf16)
        rows_ref[:, heads + 2 * half :] = mm_tn(down_dlow_ref[:, DOWN_B], act_ref[...]).astype(bf16)

    def work(owner):
        lowered = lower(all_ref[owner, :, :D], factors_ref[...])
        all_ref[owner, :, D:] = lowered
        heads_ref[owner] = mm_nt(all_ref[owner], w_ref[...]).astype(bf16)
        raise_ref[...] += mm_tn(out_low_ref[owner, :, OUT_B], all_ref[owner, :, :D])
        lower_ref[...] += mm_tn(lowered[:, OUT_B], attn_ref[owner])

    raise_ref[...] = jnp.zeros_like(raise_ref)
    lower_ref[...] = jnp.zeros_like(lower_ref)
    gather(links, all_ref, work, before, after)
    cols_ref[0:RANK] = raise_ref[...].astype(bf16)
    rows_ref[:, :heads] = lower_ref[...].astype(bf16)


def prepare_kernel(
    wq_hbm, wk_hbm, dv_ref, lin_hbm, inv_ref, inner_ref, f1_ref, low_ref, early_ref,
    grad_ref, rows_ref,
    wq_ref, wk_ref, lin_ref, total_ref, stat_ref, send_sem, recv_sem, local_sem,
):
    links = Links(send_sem, recv_sem, local_sem)
    third = wq_ref.shape[1]
    loads = links.fetch(
        (wq_hbm, wq_ref),
        (wk_hbm, wk_ref),
        (lin_hbm.at[:, pl.ds(0, 2 * third)], lin_ref),
    )
    links.greet(rows=3)
    total = share_stats(links, stat_ref, inner_ref[0], inner_ref[1])
    total_ref[...] = total.T / D
    wait_all(loads)

    @pl.loop(0, SLAB // 96)
    def _(tile):
        rows = pl.ds(pl.multiple_of(tile * 96, 96), 96)
        inverse = inv_ref[rows]
        factor = inverse**3 * total_ref[rows]
        for index, source in enumerate((wq_ref, wk_ref)):
            cols = slice(index * third, (index + 1) * third)
            one = slice(index, index + 1)
            value = inverse[:, one] * source[rows] - lin_ref[rows, cols] * factor[:, one]
            grad_ref[rows, cols] = value.astype(bf16)
        grad_ref[rows, 2 * third : 3 * third] = dv_ref[rows]

    grad_ref[:, 3 * third :] = lower(grad_ref[:, : 3 * third], f1_ref[...])
    for index in range(3):
        cols = slice(index * third, (index + 1) * third)
        low = low_ref[:, index * RANK : (index + 1) * RANK]
        rows_ref[:, cols] = mm_tn(low, grad_ref[:, cols]).astype(bf16)
    rows_ref[:, 3 * third :] = early_ref[...]


def back_qkv_kernel(
    grad_ref, w_hbm, factors_t_ref, hidden_hbm, x_hbm, early_ref, chosen_ref,
    turn_buf, sums_ref,
    w_ref, hidden_ref, x_ref, sum_ref, own_ref, middle_ref, parts_ref, got_ref, total_ref, groups_ref,
    placed_ref, out_buf, relay_buf, final_buf, send_sem, recv_sem, local_sem,
):
    links = Links(send_sem, recv_sem, local_sem)
    steps = (2, 3, 1, 0)
    streams = Streams(
        links,
        None,
        load_qkv(links, w_hbm, w_ref, [links.col ^ step for step in steps]),
        [(hidden_hbm, hidden_ref)],
    )
    x_load = links.plan((x_hbm, x_ref))
    depth = w_ref.shape[1] - 128
    w_ref[:, depth:] = factors_t_ref[...]
    links.greet(rows=3, columns=True, twin=True)
    width = own_ref.shape[2]
    count = grad_ref.shape[1]
    by_row = Exchange(links, "row", slot(parts_ref), slot(got_ref))
    base = 4 * links.tok
    by_col = Exchange(
        links, "col", slot(total_ref), lambda key: groups_ref.at[base + key]
    )
    index = links.take(1)
    mine, theirs = groups_ref.at[pl.ds(base, 4)], groups_ref.at[pl.ds(4 - base, 4)]
    to_twin = links.copy(mine, mine, index, index, links.row, tok=links.tok ^ 1)
    from_twin = links.copy(theirs, theirs, index, index, links.row, tok=links.tok ^ 1)
    spread = Exchange(links, "row", lambda key: placed_ref, slot(sums_ref))

    def lower_grad():
        wait_all(x_load)
        late = 0.0
        for owner in range(4):
            late = late + mm_tn(grad_ref[owner, :, depth : depth + 3 * RANK], x_ref[owner])
        late = late.astype(bf16)
        parts_ref[0] = late[0 : 2 * RANK]
        parts_ref[1, :RANK] = late[2 * RANK :]
        parts_ref[1, RANK:] = early_ref[:RANK]
        parts_ref[2] = early_ref[RANK : 3 * RANK]
        parts_ref[3, :RANK] = early_ref[3 * RANK :]
        parts_ref[3, RANK:] = jnp.zeros((RANK, D), bf16)
        by_row.start()

    def add_rows():
        by_row.arrived()
        for f in range(4):
            cols = slice(f * width, (f + 1) * width)
            value = got_ref[0, :, cols].astype(f32)
            for q in range(1, 4):
                value = value + got_ref[q, :, cols].astype(f32)
            total_ref[f] = value.astype(bf16)
        by_col.start()

    def share():
        by_col.arrived()
        to_twin.start()

    def place_groups():
        from_twin.wait_recv()
        for half in range(2):
            rows = slice(half * RANK, (half + 1) * RANK)
            values = [groups_ref[g, rows].astype(f32) for g in range(8)]
            for adapter in range(ADAPTERS):
                value = 0.0
                for g in range(8):
                    value = value + chosen_ref[2 * links.row + half, adapter * 8 + g] * values[g]
                placed_ref[adapter, rows] = value.astype(bf16)
        spread.start()

    def product(owner, k, cols):
        return mm_nt(grad_ref[owner], w_ref[cols, :])

    z_base, row_base = links.take(3), links.take(4)
    near = links.local(middle_ref.at[links.row], token_rows(turn_buf, count)(links.row))
    z_copies = []

    def leave_col(k, columns, finish):
        finish(k)
        cols, step = columns(k), steps[k]
        value = (
            sum_ref[:, cols]
            + final_buf[0, k].astype(f32)
            + final_buf[1, k].astype(f32)
            + hidden_ref[:, cols]
        ).astype(bf16)
        if step == 0:
            middle_ref[links.col] = value
            return
        own_ref[k] = value
        at = z_base + k
        copy = links.copy(
            own_ref.at[k], middle_ref.at[links.col], at, at, links.row, links.col ^ step
        )
        copy.start()
        z_copies.append(copy)

    def to_row(step):
        other = links.row ^ step
        return links.copy(
            middle_ref.at[other],
            token_rows(turn_buf, count)(links.row),
            row_base + step,
            row_base + step,
            other,
        )

    def leave_row(k):
        source = links.col ^ steps[k]
        if steps[k]:
            at = z_base + k
            landed = middle_ref.at[source]
            links.copy(landed, landed, at, at, links.row, source).wait_recv()
        step = links.row ^ source

        @pl.when(step == 0)
        def _():
            near.start()

        @pl.when(step != 0)
        def _():
            to_row(step).start()

    def first(columns, finish):
        start_all(x_load)

    def second(columns, finish):
        lower_grad()

    def third(columns, finish):
        add_rows()
        wait_all(streams.late)
        leave_col(0, columns, finish)

    def fourth(columns, finish):
        share()
        leave_col(1, columns, finish)

    columns, finish, sent = scatter(
        links, product, sum_ref, out_buf, relay_buf, final_buf,
        block=lambda k: links.col ^ steps[k],
        ready=streams.ready,
        hooks=[first, second, third, fourth],
    )
    leave_row(0)
    place_groups()
    leave_col(2, columns, finish)
    leave_col(3, columns, finish)
    leave_row(3)
    leave_row(2)
    leave_row(1)
    near.wait()
    for step in range(1, 4):
        landed = token_rows(turn_buf, count)(links.row ^ step)
        at = row_base + step
        links.copy(landed, landed, at, at, links.row ^ step).wait_recv()
    spread.arrived()
    for step in range(1, 4):
        to_row(step).wait_send()
    for copy in z_copies:
        copy.wait_send()
    to_twin.wait_send()
    for exchange in (by_row, by_col, spread):
        exchange.sent()
    sent()


VMEM = pl.BlockSpec(memory_space=pltpu.VMEM)
ANY = pl.BlockSpec(memory_space=pl.ANY)
SMEM = pl.BlockSpec(memory_space=pltpu.SMEM)


def linked(kernel, number, operands, outs, scratch, flops):
    specs = [ANY if isinstance(value, tuple) else VMEM for value in operands]
    values = [value[0] if isinstance(value, tuple) else value for value in operands]
    specs = [
        SMEM if value.ndim == 2 and value.shape[0] == 8 and value.dtype != bf16 else spec
        for spec, value in zip(specs, values)
    ]
    return pl.pallas_call(
        kernel,
        in_specs=specs,
        out_specs=[ANY if len(out) == 3 else VMEM for out in outs],
        out_shape=[jax.ShapeDtypeStruct(out[0], out[1]) for out in outs],
        scratch_shapes=[pltpu.VMEM(shape, kind) for shape, kind in scratch]
        + [
            pltpu.SemaphoreType.DMA((48,)),
            pltpu.SemaphoreType.DMA((48,)),
            pltpu.SemaphoreType.DMA((48,)),
        ],
        compiler_params=pltpu.CompilerParams(
            collective_id=number, has_side_effects=True, vmem_limit_bytes=60 << 20
        ),
        cost_estimate=pl.CostEstimate(
            flops=flops, bytes_accessed=flops // 400, transcendentals=0
        ),
        name=kernel.__name__,
    )(*values)


def scatter_buffers(count):
    part = D // SLICES
    return [
        ((3, SLICES, count, part), bf16),
        ((2, SLICES, count // 2, part), bf16),
        ((2, SLICES, count, part), bf16),
    ]


def score_blocks(k_ref, q_block, bias_ref, start, stop):
    parts = []
    if start:
        parts.append(mm_nt(k_ref[0:start], q_block) + bias_ref[0:start])
    own = mm_nt(k_ref[start:stop], q_block) + bias_ref[start:stop]
    keys = lax.broadcasted_iota(jnp.int32, own.shape, 0)
    queries = lax.broadcasted_iota(jnp.int32, own.shape, 1)
    parts.append(jnp.where(keys <= queries, own, very_low))
    return parts

def attend_kernel(q_ref, k_ref, v_ref, inv_ref, gain_ref, cos_ref, sin_ref, bias_ref,
                  ql_ref, kl_ref, vl_ref, o_ref, lse_ref):
    for source, target, index in ((q_ref, ql_ref, 0), (k_ref, kl_ref, 1)):
        normed = source[...] * inv_ref[:, index:index+1] * gain_ref[index:index+1, :]
        target[...] = (normed * cos_ref[...] + pltpu.roll(normed, HEAD_DIM // 2, 1) * sin_ref[...]).astype(bf16)
    values = v_ref[...].astype(bf16)
    vl_ref[...] = values
    values_t = v_ref[...].T.astype(bf16)
    for start in range(0, SLAB, BLOCK):
        stop = start + BLOCK
        parts = score_blocks(kl_ref, ql_ref[start:stop], bias_ref, start, stop)
        top = functools.reduce(jnp.maximum, [jnp.max(p, axis=0, keepdims=True) for p in parts]) * log2_scale
        total, out, at = 0.0, 0.0, 0
        for part in parts:
            shifted = jnp.exp2(part * log2_scale - top)
            total = total + jnp.sum(shifted, axis=0, keepdims=True)
            out = out + mm(values_t[:, at:at+part.shape[0]], shifted.astype(bf16))
            at += part.shape[0]
        o_ref[start:stop] = (out / total).T.astype(bf16)
        lse_ref[0, :, start:stop] = top + jnp.log2(total)

def attend_back_kernel(ql_ref, kl_ref, vl_ref, o_ref, do_ref, lse_ref, q_ref, k_ref, gain_ref, cos_ref, sin_ref, bias_ref, *refs):
    mid_ref, wq_ref, wk_ref, dv_ref, sum_ref, turn_ref, dk_sum, dv_sum, *sems = refs if len(refs) > 8 else (None, *refs[:4], None, *refs[4:])
    if sems:
        links = Links(*sems)
        turned = Exchange(links, "row", slot(mid_ref), token_rows(turn_ref, mid_ref.shape[1]))

        @pl.when(pl.program_id(0) == 0)
        def _():
            links.greet(rows=3)
            turned.start()

    keys_t = kl_ref[...].astype(f32).T.astype(bf16)
    delta_all = jnp.sum((do_ref[...].astype(f32) * o_ref[...].astype(f32)).T, axis=0, keepdims=True)
    dk_sum[...] = jnp.zeros_like(dk_sum)
    dv_sum[...] = jnp.zeros_like(dv_sum)
    def unrotate(values):
        return values * cos_ref[...] - pltpu.roll(values, HEAD_DIM // 2, 1) * sin_ref[...]
    dq_parts = []
    for start in range(0, SLAB, BLOCK):
        stop = start + BLOCK
        queries, grads = ql_ref[start:stop], do_ref[start:stop]
        parts = score_blocks(kl_ref, queries, bias_ref, start, stop)
        lse, delta = lse_ref[0, :, start:stop], delta_all[:, start:stop]
        at, dq = 0, 0.0
        for part in parts:
            span = slice(at, at + part.shape[0])
            probs = jnp.exp2(part * log2_scale - lse)
            dv_sum[span] += mm(probs.astype(bf16), grads)
            dscore = (probs * (mm_nt(vl_ref[span], grads) - delta)).astype(bf16)
            dk_sum[span] += mm(dscore, queries)
            dq = dq + mm(keys_t[:, span], dscore)
            at += part.shape[0]
        dq_parts.append(dq.T)
    dq_all = jnp.concatenate(dq_parts, axis=0) * score_scale
    dv_ref[...] = dv_sum[...].astype(bf16)
    wq = unrotate(dq_all) * gain_ref[0:1, :]
    wk = unrotate(dk_sum[...] * score_scale) * gain_ref[1:2, :]
    wq_ref[...] = wq.astype(wq_ref.dtype)
    wk_ref[...] = wk.astype(wk_ref.dtype)
    first = pl.program_id(0) == 0
    for index, (weighted, source) in enumerate(((wq, q_ref), (wk, k_ref))):
        product = weighted * source[...]

        @pl.when(first)
        def _():
            sum_ref[index] = product

        @pl.when(jnp.logical_not(first))
        def _():
            sum_ref[index] += product

    if sems:

        @pl.when(pl.program_id(0) == pl.num_programs(0) - 1)
        def _():
            turned.arrived()
            turned.sent()


def attend_specs(heads):
    col = lambda base: pl.BlockSpec((SLAB, HEAD_DIM), lambda h: (0, base * heads + h))
    whole = lambda shape: pl.BlockSpec(shape, lambda h: (0,) * len(shape))
    return col, whole

def attend(qkv_lin, inverses, gains, cosine, sine, bias):
    heads = qkv_lin.shape[1] // (3 * HEAD_DIM)
    col, whole = attend_specs(heads)
    low = jax.ShapeDtypeStruct((SLAB, heads * HEAD_DIM), bf16)
    return pl.pallas_call(
        attend_kernel, grid=(heads,),
        in_specs=[col(0), col(1), col(2), whole((SLAB, 8)), pl.BlockSpec((2, HEAD_DIM), lambda h: (0, h)),
                  whole((SLAB, HEAD_DIM)), whole((SLAB, HEAD_DIM)), whole((SLAB, 1))],
        out_specs=[col(0)] * 4 + [pl.BlockSpec((1, 1, SLAB), lambda h: (h, 0, 0))],
        out_shape=[low] * 4 + [jax.ShapeDtypeStruct((heads, 1, SLAB), f32)],
        compiler_params=pltpu.CompilerParams(vmem_limit_bytes=48 << 20),
        cost_estimate=pl.CostEstimate(flops=heads*4*SLAB*SLAB*HEAD_DIM, bytes_accessed=heads*SLAB*HEAD_DIM*20, transcendentals=heads*SLAB*SLAB),
        name="attend",
    )(qkv_lin, qkv_lin, qkv_lin, inverses, gains, cosine, sine, bias)

def attend_back(ql, kl, vl, o, do, lse, qkv_lin, gains, cosine, sine, bias, middle=None):
    heads = ql.shape[1] // HEAD_DIM
    col, whole = attend_specs(heads)
    wide = jax.ShapeDtypeStruct(ql.shape, f32)
    outs = [wide, wide, jax.ShapeDtypeStruct(ql.shape, bf16)]
    outs.append(jax.ShapeDtypeStruct((2, SLAB, HEAD_DIM), f32))
    moved, turned, params, sems = [], [], dict(vmem_limit_bytes=48 << 20), []
    if middle is not None:
        moved, turned = [middle], [jax.ShapeDtypeStruct((SLAB, middle.shape[2]), bf16)]
        params.update(collective_id=10, has_side_effects=True)
        sems = [pltpu.SemaphoreType.DMA((4,))] * 3
    hbm = pl.BlockSpec(memory_space=pl.ANY)
    return pl.pallas_call(
        attend_back_kernel,
        grid=(heads,),
        in_specs=[col(0)] * 5
        + [pl.BlockSpec((1, 1, SLAB), lambda h: (h, 0, 0)), col(0), col(1)]
        + [pl.BlockSpec((2, HEAD_DIM), lambda h: (0, h))]
        + [whole((SLAB, HEAD_DIM)), whole((SLAB, HEAD_DIM)), whole((SLAB, 1))]
        + [hbm] * len(moved),
        out_specs=[col(0)] * 3 + [whole((2, SLAB, HEAD_DIM))] + [hbm] * len(turned),
        out_shape=outs + turned,
        scratch_shapes=[pltpu.VMEM((SLAB, HEAD_DIM), f32)] * 2 + sems,
        compiler_params=pltpu.CompilerParams(**params),
        cost_estimate=pl.CostEstimate(
            flops=heads * 10 * SLAB * SLAB * HEAD_DIM,
            bytes_accessed=heads * SLAB * HEAD_DIM * 30,
            transcendentals=heads * SLAB * SLAB,
        ),
        name="attend_back",
    )(ql, kl, vl, o, do, lse, qkv_lin, qkv_lin, gains, cosine, sine, bias, *moved)


def dot(left, right):
    return jnp.dot(left, right, preferred_element_type=f32)


def dot_nt(left, right):
    return lax.dot_general(left, right, (((1,), (1,)), ((), ())), preferred_element_type=f32)


def dot_tn(left, right):
    return lax.dot_general(left, right, (((0,), (0,)), ((), ())), preferred_element_type=f32)


def gather_weight(local):
    half = local.shape[0] // lax.axis_size("tok")
    part = lax.dynamic_slice_in_dim(local, lax.axis_index("tok") * half, half, 0)
    return lax.all_gather(part, ("col", "tok"), axis=0, tiled=True)


def to_tokens(values):
    rows, cols = lax.axis_size("row"), lax.axis_size("col")
    width = values.shape[1]
    mixed = lax.all_to_all(values, "row", 0, 0, tiled=True)
    mixed = lax.all_to_all(mixed, "col", 0, 0, tiled=True)
    return mixed.reshape(cols, SLAB // rows, width).transpose(1, 0, 2).reshape(SLAB // rows, -1)


def from_tokens(values):
    rows, cols = lax.axis_size("row"), lax.axis_size("col")
    count = values.shape[0]
    mixed = values.reshape(count, cols, -1).transpose(1, 0, 2).reshape(cols * count, -1)
    mixed = lax.all_to_all(mixed, "col", 0, 0, tiled=True)
    return lax.all_to_all(mixed, "row", 0, 0, tiled=True)


def reorder(values, outer, inner):
    if outer == 1 or inner == 1:
        return values
    rest = values.shape[0] // (outer * inner)
    shape = (outer, inner, rest) + values.shape[1:]
    return values.reshape(shape).swapaxes(0, 1).reshape(values.shape)


def gather_tokens(values):
    rows, per_slab = lax.axis_size("row"), lax.axis_size("row") // lax.axis_size("col")
    return reorder(lax.all_gather(values, "row", axis=0, tiled=True), rows, per_slab)


def scatter_tokens(values):
    rows, per_slab = lax.axis_size("row"), lax.axis_size("row") // lax.axis_size("col")
    values = reorder(values.astype(bf16), per_slab, rows)
    return lax.psum_scatter(values, "row", scatter_dimension=0, tiled=True).astype(f32)


def token_places(length):
    slot_ids = jnp.arange(SLAB, dtype=jnp.int32)
    return jnp.where(slot_ids < PROMPT, slot_ids, length + (slot_ids - PROMPT) % CONT_LEN)


def rotation(places, head_size):
    half_dim = head_size // 2
    frequency = jnp.exp(
        -(2.0 * jnp.arange(half_dim, dtype=f32) / head_size) * math.log(rope_base)
    )
    angles = places.astype(f32)[:, None] * frequency[None, :]
    return (jnp.cos(angles), jnp.sin(angles))


def pick(adapters, ids):
    onehot = (ids[:, None] == jnp.arange(adapters.shape[0], dtype=jnp.int32)).astype(adapters.dtype)
    return jnp.tensordot(onehot, adapters, axes=1)


def place(ids, gradients):
    onehot = (jnp.arange(ADAPTERS, dtype=jnp.int32)[:, None] == ids[None, :]).astype(f32)
    total = 0.0
    for index in range(gradients.shape[0]):
        weight = onehot[:, index].reshape((ADAPTERS,) + (1,) * (gradients.ndim - 1))
        total = total + weight * gradients[index][None].astype(f32)
    return total


def block_diagonal(factors):
    count = len(factors)
    lines = []
    for index, factor in enumerate(factors):
        blank = jnp.zeros_like(factor)
        lines.append(
            jnp.concatenate([factor if k == index else blank for k in range(count)], axis=1)
        )
    return jnp.concatenate(lines, axis=0)


def enter(x, w, f1, f2):
    everything = gather_tokens(x)
    lowered = (adapter_scale * dot_nt(everything, f1)).astype(bf16)
    return everything, lowered, dot(everything, w) + dot(lowered, f2)


def leave(y, w, f1, f2):
    lowered = (adapter_scale * dot_nt(y, f1)).astype(bf16)
    return scatter_tokens(dot_nt(y, w) + dot(lowered, f2)), lowered


def split_layer(
    layer_in, cotangent, qkv_weight, out_weight, ffn_weight, down_weight, head_gain, post_gain,
    adapters, adapter_ids, tables,
):
    qkv_lower, out_raise, ffn_lower, down_raise, qkv_raise, out_lower, ffn_raise, down_lower = (
        adapters
    )
    col_count = lax.axis_size("col")
    group_base = lax.axis_index("tok") * col_count
    group = group_base + lax.axis_index("col")
    slab_ids = lax.dynamic_slice_in_dim(adapter_ids, group_base, col_count, 0)
    own_ids = lax.dynamic_index_in_dim(adapter_ids, group, 0, keepdims=False)
    size = layer_in.shape[1]
    local = jnp.concatenate([qkv_weight.transpose(1, 0, 2).reshape(size, -1), out_weight.T], axis=1)
    attn_full = gather_weight(local)
    ffn_full = gather_weight(ffn_weight.transpose(1, 0, 2).reshape(size, -1))
    down_full = gather_weight(down_weight.T)
    pieces = jnp.concatenate(
        [pick(qkv_lower[p], slab_ids[:, p]) for p in range(3)]
        + [pick(out_raise, slab_ids[:, 3])]
        + [pick(ffn_lower[p], slab_ids[:, 4 + p]) for p in range(2)]
        + [pick(down_raise, slab_ids[:, 6])]
        + [jnp.broadcast_to(jnp.pad(post_gain, ((0, 14), (0, 0))), (col_count, RANK, size))],
        axis=1,
    )
    qkv_b = block_diagonal([pick(qkv_raise[p], own_ids[p : p + 1])[0] for p in range(3)])
    out_a = pick(out_lower, own_ids[3:4])[0]
    ffn_b = block_diagonal([pick(ffn_raise[p], own_ids[4 + p : 5 + p])[0] for p in range(2)])
    down_a = pick(down_lower, own_ids[6:7])[0]
    factors = lax.all_to_all(pieces, "col", 0, 0, tiled=True)
    factors = factors.transpose(1, 0, 2).reshape(-1, D)
    qkv_a, out_b, ffn_a, down_b = (factors[part] for part in (QKV_A, OUT_B, FFN_A, DOWN_B))
    gains = factors[GAIN0.start : GAIN1.stop].astype(f32)
    width = qkv_b.shape[1]
    head_width, ff_width = width // 3, ffn_b.shape[1] // 2
    x_own = to_tokens(layer_in)
    x_all, qkv_low, qkv_lin = enter(x_own, attn_full[:, :width], qkv_a, qkv_b)
    q_lin, k_lin = qkv_lin[:, :head_width], qkv_lin[:, head_width : 2 * head_width]
    squares = jnp.stack([jnp.sum(q_lin * q_lin, axis=1), jnp.sum(k_lin * k_lin, axis=1)], axis=1)
    inverses = lax.rsqrt(lax.psum(squares, "row") / D + norm_eps)
    inverses = jnp.concatenate([inverses] * 4, axis=1)
    q_low, k_low, v_low, attn_low, log_sums = attend(qkv_lin, inverses, head_gain, *tables)
    attn_lin, out_low = leave(attn_low, attn_full[:, width:], out_a, out_b)
    hidden = x_own.astype(f32) + attn_lin * inverse_of(attn_lin) * gains[0]
    h_all, ffn_low, ffn_lin = enter(hidden.astype(bf16), ffn_full, ffn_a, ffn_b)
    gate_lin, up_lin = ffn_lin[:, :ff_width], ffn_lin[:, ff_width:]
    act_low = gated(gate_lin, up_lin).astype(bf16)
    mlp_lin, down_low = leave(act_low, down_full, down_a, down_b)
    layer_out = hidden + mlp_lin * inverse_of(mlp_lin) * gains[1]
    layer_out = from_tokens(layer_out.astype(bf16)).astype(f32)
    grad_out = to_tokens(cotangent).astype(f32)
    grad_mlp = norm_back(mlp_lin, grad_out * gains[1]).astype(bf16)
    dm_all, down_dlow, grad_act = enter(grad_mlp, down_full, down_b, down_a)
    grad_ffn = jnp.concatenate(gated_back(grad_act, gate_lin, up_lin), axis=1).astype(bf16)
    grad_ffn_in, ffn_dlow = leave(grad_ffn, ffn_full, ffn_b, ffn_a)
    grad_hidden = grad_out + grad_ffn_in
    grad_attn = norm_back(attn_lin, grad_hidden * gains[0]).astype(bf16)
    da_all, out_dlow, grad_heads = enter(grad_attn, attn_full[:, width:], out_b, out_a)
    weighted_q, weighted_k, grad_v, inner = attend_back(
        q_low, k_low, v_low, attn_low, grad_heads.astype(bf16), log_sums, qkv_lin, head_gain, *tables
    )
    inner = lax.psum(jnp.sum(inner, axis=2).T, "row")
    factor = inverses[:, :2] ** 3 * inner / D
    grad_qkv = jnp.concatenate(
        [
            (inverses[:, 0:1] * weighted_q - q_lin * factor[:, 0:1]).astype(bf16),
            (inverses[:, 1:2] * weighted_k - k_lin * factor[:, 1:2]).astype(bf16),
            grad_v,
        ],
        axis=1,
    )
    grad_qkv_in, qkv_dlow = leave(grad_qkv, attn_full[:, :width], qkv_b, qkv_a)
    grad_in = from_tokens((grad_hidden + grad_qkv_in).astype(bf16)).astype(f32)
    parts = jnp.concatenate(
        [dot_tn(qkv_dlow, x_all), dot_tn(out_low, da_all), dot_tn(ffn_dlow, h_all)]
        + [dot_tn(down_low, dm_all)]
    )
    parts = parts.astype(bf16).reshape(7, RANK, col_count, size).transpose(2, 0, 1, 3)
    parts = lax.all_to_all(parts, "col", 0, 0, tiled=True)
    placed = [place(slab_ids[:, p], parts[:, p]) for p in range(7)]
    col_grads = list(lax.psum(jnp.stack(placed).astype(bf16), ("tok", "row")).astype(f32))
    own_rows = jnp.concatenate(
        [diagonal(dot_tn(qkv_low, grad_qkv), 3), dot_tn(out_dlow, attn_low)]
        + [diagonal(dot_tn(ffn_low, grad_ffn), 2), dot_tn(down_dlow, act_low)],
        axis=1,
    )
    every = lax.all_gather(own_rows.astype(bf16), ("tok", "col"), axis=0)
    row_grads, at = [], 0
    for p in range(7):
        part = ff_width if p > 3 else head_width
        row_grads.append(place(adapter_ids[:, p], every[:, :, at : at + part]))
        at += part
    return (
        layer_out, grad_in,
        jnp.stack(col_grads[0:3]), col_grads[3], jnp.stack(col_grads[4:6]), col_grads[6],
        jnp.stack(row_grads[0:3]), row_grads[3], jnp.stack(row_grads[4:6]), row_grads[6],
    )


def flat(values):
    return values.reshape((SLAB,) + values.shape[2:])


def cube(values):
    return values.reshape((4, SLAB // 4) + values.shape[1:])


def linked_layer(
    layer_in, cotangent, qkv_weight, out_weight, ffn_weight, down_weight, head_gain, post_gain,
    adapters, adapter_ids, tables,
):
    count = SLAB // 4
    piece = (4, count, layer_in.shape[1])
    head_width, ff_width = qkv_weight.shape[2], ffn_weight.shape[2]
    width = 3 * head_width
    buffers = scatter_buffers(count)
    per = 2 * SLAB * D
    tokens = ((4, count, D), bf16)
    own = ((count, D), bf16)
    wide = ((count, D), f32)

    def gather_halves(local, axis):
        half = local.shape[axis] // 2
        return lax.dynamic_slice_in_dim(local, lax.axis_index("tok") * half, half, axis)

    def gathered(local):
        return lax.all_gather(local, ("col", "tok"), axis=0)

    attn_full = gathered(
        jnp.concatenate(
            [gather_halves(qkv_weight, 1).reshape(-1, head_width), gather_halves(out_weight, 0)]
        )
    )
    ffn_full = gathered(gather_halves(ffn_weight, 1))
    down_full = gathered(gather_halves(down_weight, 0))

    (
        x_own, cot_mid, factors, factors_t, qkv_b, out_a, out_at, ffn_b, down_a, down_at
    ) = linked(
        intake_kernel, 1,
        [(cube(layer_in),), (cube(cotangent),), adapter_ids]
        + [jnp.pad(post_gain, ((0, RANK - 2), (0, 0)))]
        + adapters,
        [own, (piece, bf16), ((128, D), bf16), ((D, 128), bf16), ((128, width), bf16)]
        + [((128, head_width), bf16), ((head_width, 128), bf16), ((128, 2 * ff_width), bf16)]
        + [((128, ff_width), bf16), ((ff_width, 128), bf16)],
        [(piece, bf16), ((4, 128, piece[2]), bf16)],
        per * 128,
    )
    low = ((4, count, 128), bf16)
    tall = ((4, count, D + 128), bf16)
    x_all, qkv_low, qkv_lin, inverses = linked(
        enter_qkv_kernel, 2,
        [x_own, (attn_full,), factors, (qkv_b,)],
        [tokens + (ANY,), low, ((4, count, width), f32, ANY), ((SLAB, 8), f32)],
        [tall, ((4, count, width), f32), ((D + 128, width), bf16), ((2, SLAB, 128), f32)]
        + [((4, 8, SLAB), f32)],
        per * width,
    )
    qkv_lin = flat(qkv_lin)
    q_low, k_low, v_low, attn_low, log_sums = attend(qkv_lin, inverses, head_gain, *tables)
    attn_lin, out_low, hidden, h_all = linked(
        leave_out_kernel, 3,
        [(cube(attn_low),), (attn_full,), out_a, factors, x_own],
        [wide, low, wide, tokens],
        [((4, count, head_width + 128), bf16), ((head_width + 128, D), bf16)] + buffers,
        per * head_width,
    )
    h_all = flat(h_all)
    ffn_low, gate_lin, up_lin, act_low = ffn(h_all, ffn_full, factors, ffn_b)
    down_low, own_out, grad_mlp, own_cot = linked(
        leave_down_kernel, 4,
        [(cube(act_low),), (down_full,), down_a, factors, (hidden,), cot_mid],
        [low, own, own, own],
        [((4, count, ff_width + 128), bf16), ((ff_width + 128, D), bf16), wide, wide] + buffers,
        per * ff_width,
    )
    dm_all, down_dlow, grad_ffn, out_mid = linked(
        back_down_kernel, 5,
        [grad_mlp, (down_full,), factors, down_at, (cube(gate_lin),), (cube(up_lin),), own_out],
        [tokens + (ANY,), low, ((4, count, 2 * ff_width), bf16, ANY), (piece, bf16)],
        [tall, ((ff_width, D + 128), bf16)]
        + [((4, count, ff_width), bf16)] * 2
        + [((4, count, 2 * ff_width), bf16)],
        per * ff_width,
    )
    ffn_dlow, grad_hidden, grad_attn = linked(
        back_ffn_kernel, 6,
        [(grad_ffn,), (ffn_full,), ffn_b, factors, factors_t, (own_cot,), (attn_lin,)],
        [low, wide, own],
        [((4, count, 2 * ff_width + 128), bf16), ((D, 2 * ff_width + 128), bf16), own, wide, wide]
        + buffers,
        per * 2 * ff_width,
    )
    grad_heads, early_cols, early_rows = linked(
        back_out_kernel, 7,
        [grad_attn, (attn_full,), factors, out_at, out_low, cube(attn_low), flat(down_low)]
        + [flat(down_dlow), ffn_low, flat(ffn_dlow), (flat(dm_all),), (act_low,)]
        + [(flat(grad_ffn),), (h_all,)],
        [((4, count, head_width), bf16), ((64, D), bf16)]
        + [((16, head_width + 3 * ff_width), bf16)],
        [tall, ((head_width, D + 128), bf16), ((SLAB, D), bf16)]
        + [((SLAB, ff_width), bf16), ((SLAB, 2 * ff_width), bf16), ((SLAB, D), bf16)]
        + [((16, D), f32), ((16, head_width), f32)],
        per * head_width,
    )
    weighted_q, weighted_k, grad_v, inner, layer_out = attend_back(
        q_low, k_low, v_low, attn_low, flat(grad_heads), log_sums, qkv_lin, head_gain, *tables,
        out_mid,
    )
    grad_qkv, own_rows = linked(
        prepare_kernel, 8,
        [(weighted_q,), (weighted_k,), grad_v, (qkv_lin,), inverses, inner, qkv_b, flat(qkv_low)]
        + [early_rows],
        [((SLAB, width + 128), bf16)]
        + [((16, width + head_width + 3 * ff_width), bf16)],
        [((SLAB, head_width), f32)] * 2
        + [((SLAB, 2 * head_width), f32), ((SLAB, 8), f32), ((4, 8, SLAB), f32)],
        per * 128,
    )
    every = lax.all_gather(own_rows, ("tok", "col"), axis=0)
    numbers = jnp.arange(ADAPTERS, dtype=jnp.int32)
    chosen = (adapter_ids.T[:, None, :] == numbers[None, :, None]).astype(f32).reshape(7, -1)
    chosen = jnp.pad(chosen, ((0, 1), (0, 0)))
    grad_in, col_parts = linked(
        back_qkv_kernel, 9,
        [cube(grad_qkv), (attn_full,), factors_t, (grad_hidden,), (x_all,)]
        + [early_cols, chosen],
        [(layer_in.shape, bf16), ((4, ADAPTERS, 32, piece[2]), bf16)],
        [((D, width + 128), bf16), wide, tokens, wide, (piece, bf16), (piece, bf16)]
        + [((4, 32, D), bf16)] * 2
        + [((4, 32, piece[2]), bf16), ((8, 32, piece[2]), bf16)]
        + [((ADAPTERS, 32, piece[2]), bf16)]
        + buffers,
        per * width,
    )
    return finish(chosen, layer_out, grad_in, col_parts, every, head_width, ff_width)


def diagonal(values, count):
    width = values.shape[1] // count
    return jnp.concatenate(
        [
            values[k * RANK : (k + 1) * RANK, k * width : (k + 1) * width]
            for k in range(count)
        ],
        axis=1,
    )


def on_device(
    layer_in,
    cotangent,
    qkv_weight,
    out_weight,
    ffn_weight,
    down_weight,
    qk_gain,
    post_gain,
    qkv_lower,
    qkv_raise,
    out_lower,
    out_raise,
    ffn_lower,
    ffn_raise,
    down_lower,
    down_raise,
    adapter_ids,
    prompt_len,
):
    group = lax.axis_index("tok") * lax.axis_size("col") + lax.axis_index("col")
    length = lax.dynamic_index_in_dim(prompt_len, group, 0, keepdims=False)
    cosine, sine = rotation(token_places(length), HEAD_DIM)
    cosine = jnp.concatenate([cosine, cosine], axis=1)
    sine = jnp.concatenate([-sine, sine], axis=1)
    slots = jnp.arange(SLAB, dtype=jnp.int32)
    bias = jnp.where((slots < length) | (slots >= PROMPT), 0.0, very_low)[:, None].astype(f32)

    plane = (lax.axis_size("tok"), lax.axis_size("row"), lax.axis_size("col"))
    layer = linked_layer if plane == (2, 4, 4) else split_layer
    adapters = [
        qkv_lower.swapaxes(2, 3), out_raise, ffn_lower.swapaxes(2, 3), down_raise,
        qkv_raise, out_lower.swapaxes(1, 2), ffn_raise, down_lower.swapaxes(1, 2),
    ]
    (
        layer_out, grad_in, qkv_lower_grad, out_raise_grad, ffn_lower_grad, down_raise_grad,
        qkv_raise_grad, out_lower_grad, ffn_raise_grad, down_lower_grad,
    ) = layer(
        layer_in, cotangent, qkv_weight, out_weight, ffn_weight, down_weight, qk_gain.astype(f32),
        post_gain, adapters, adapter_ids, (cosine, sine, bias),
    )
    return (
        layer_out,
        grad_in,
        qkv_lower_grad.swapaxes(2, 3),
        qkv_raise_grad,
        out_lower_grad.swapaxes(1, 2),
        out_raise_grad,
        ffn_lower_grad.swapaxes(2, 3),
        ffn_raise_grad,
        down_lower_grad.swapaxes(1, 2),
        down_raise_grad,
    )


def solution(mesh):
    return jax.shard_map(
        on_device,
        mesh=mesh,
        in_specs=(
            P(("tok", "row"), "col"),
            P(("tok", "row"), "col"),
            P(None, "col", "row"),
            P("row", "col"),
            P(None, "col", "row"),
            P("row", "col"),
            P(None, "row"),
            P(None, "col"),
            P(None, None, "col", None),
            P(None, None, None, "row"),
            P(None, "row", None),
            P(None, None, "col"),
            P(None, None, "col", None),
            P(None, None, None, "row"),
            P(None, "row", None),
            P(None, None, "col"),
            P(),
            P(),
        ),
        out_specs=(
            P(("tok", "row"), "col"),
            P(("tok", "row"), "col"),
            P(None, None, "col", None),
            P(None, None, None, "row"),
            P(None, "row", None),
            P(None, None, "col"),
            P(None, None, "col", None),
            P(None, None, None, "row"),
            P(None, "row", None),
            P(None, None, "col"),
        ),
        check_vma=False,
    )
```

```python
import functools
import math

import jax
import jax.numpy as jnp
from jax import lax
from jax.experimental import pallas as pl
from jax.experimental.pallas import tpu as pltpu
from jax.sharding import PartitionSpec as P

D = 2048
HEAD_DIM = 128
RANK = 16
ADAPTERS = 8
PROMPT = 1024
CONT_LEN = 128
SLAB = 1152

adapter_scale = 2.0
norm_eps = 1e-06
rope_base = 500000.0
very_low = -1e30
bf16 = jnp.bfloat16
f32 = jnp.float32
log2_scale = math.log2(math.e) / math.sqrt(HEAD_DIM)
score_scale = 1.0 / math.sqrt(HEAD_DIM)
BLOCK = 384
TILE = 512
MESH = pl.DeviceIdType.MESH


def mm(left, right):
    return jnp.dot(left, right, preferred_element_type=f32)


def mm_nt(left, right):
    return lax.dot_general(left, right, (((1,), (1,)), ((), ())), preferred_element_type=f32)


class Links:
    def __init__(self, send_sem, recv_sem, local_sem):
        self.tok = lax.axis_index("tok")
        self.row, self.col = lax.axis_index("row"), lax.axis_index("col")
        self.xn, self.yn, self.dg = self.row ^ 1, self.row ^ 2, self.row ^ 3
        self.send_sem, self.recv_sem, self.local_sem = send_sem, recv_sem, local_sem
        self.used, self.local_used = 0, 0

    def take(self, count):
        self.used += count
        return self.used - count

    def copy(self, source, target, index, recv_index, row, col=None, tok=None):
        return pltpu.make_async_remote_copy(
            src_ref=source,
            dst_ref=target,
            send_sem=self.send_sem.at[index],
            recv_sem=self.recv_sem.at[recv_index],
            device_id={
                "tok": self.tok if tok is None else tok,
                "row": row,
                "col": self.col if col is None else col,
            },
            device_id_type=MESH,
        )

    def local(self, source, target):
        self.local_used += 1
        return pltpu.make_async_copy(source, target, self.local_sem.at[self.local_used - 1])

    def plan(self, *pairs):
        return [self.local(source, target) for source, target in pairs]

    def fetch(self, *pairs):
        return start_all(self.plan(*pairs))

    def greet(self, rows=2, columns=False, twin=False):
        barrier = pltpu.get_barrier_semaphore()
        places = [(self.tok, self.row ^ step, self.col) for step in range(1, rows + 1)]
        if columns:
            places += [(self.tok, self.row, self.col ^ step) for step in range(1, 4)]
        if twin:
            places += [(self.tok ^ 1, self.row, self.col)]
        for tok, row, col in places:
            pl.semaphore_signal(
                barrier,
                inc=1,
                device_id={"tok": tok, "row": row, "col": col},
                device_id_type=MESH,
            )
        pl.semaphore_wait(barrier, len(places))


def start_all(copies):
    for copy in copies:
        copy.start()
    return copies


def wait_all(copies):
    for copy in copies:
        copy.wait()


class Exchange:
    def __init__(self, links, axis, piece_at, slot_at):
        self.links, self.axis = links, axis
        self.me = links.row if axis == "row" else links.col
        self.piece_at, self.slot_at = piece_at, slot_at
        self.base = links.take(3)
        self.own = links.local(piece_at(self.me), slot_at(self.me))

    def copy(self, source, target, step):
        links, other, index = self.links, self.me ^ step, self.base + step - 1
        row, col = (other, links.col) if self.axis == "row" else (links.row, other)
        return links.copy(source, target, index, index, row, col)

    def start(self):
        for step in range(1, 4):
            self.copy(self.piece_at(self.me ^ step), self.slot_at(self.me), step).start()
        self.own.start()

    def arrived(self):
        for step in range(1, 4):
            landed = self.slot_at(self.me ^ step)
            self.copy(landed, landed, step).wait_recv()
        self.own.wait()

    def sent(self):
        for step in range(1, 4):
            self.copy(self.piece_at(self.me ^ step), self.slot_at(self.me), step).wait_send()


def features(ref, width):
    return lambda col: ref.at[:, pl.ds(pl.multiple_of(col * width, width), width)]


def slot(ref):
    return lambda key: ref.at[key]


def token_rows(ref, count):
    return lambda row: ref.at[pl.ds(pl.multiple_of(row * count, 16), count)]


def gather(links, all_ref, work, before=None, after=None):
    me, xn, yn, dg = links.row, links.xn, links.yn, links.dg
    half = all_ref.shape[1] // 2
    top, low = pl.ds(0, half), pl.ds(half, half)
    base = links.take(6)

    def move(owner, part, index, other):
        place = all_ref.at[owner, part, pl.ds(0, D)]
        return links.copy(place, place, base + index, base + index, other)

    sends = [move(me, top, 0, xn), move(me, low, 1, yn), move(me, low, 2, xn), move(me, top, 3, yn)]
    for copy in sends:
        copy.start()
    if before:
        before()
    if work:
        work(me)
    move(xn, top, 0, xn).wait_recv()
    sends.append(move(xn, top, 4, yn))
    sends[-1].start()
    move(yn, low, 1, yn).wait_recv()
    sends.append(move(yn, low, 5, xn))
    sends[-1].start()
    if after:
        after()
    move(xn, low, 2, xn).wait_recv()
    if work:
        work(xn)
    move(yn, top, 3, yn).wait_recv()
    if work:
        work(yn)
    move(dg, top, 4, yn).wait_recv()
    move(dg, low, 5, xn).wait_recv()
    if work:
        work(dg)
    for copy in sends:
        copy.wait_send()


SLICES = 4


def scatter(links, product, o_ref, out_buf, relay_buf, final_buf, block=None, ready=None, hooks=None):
    me, xn, yn, dg = links.row, links.xn, links.yn, links.dg
    count, width = o_ref.shape[0], o_ref.shape[1] // SLICES
    half = count // 2
    top, low = pl.ds(0, half), pl.ds(half, half)
    base = links.take(6 * SLICES)
    all_copies = []

    def columns(k):
        at = block(k) * width if block else k * width
        return pl.ds(pl.multiple_of(at, width), width)

    def add(place, k, rows, relay):
        out_buf[place, k, rows] = (
            out_buf[place, k, rows].astype(f32) + relay_buf[relay, k].astype(f32)
        ).astype(bf16)

    def relay(k):
        copies = all_copies[k]
        copies[0].wait_recv()
        add(2, k, top, 0)
        copies[4].start()
        copies[1].wait_recv()
        add(1, k, low, 1)
        copies[5].start()

    def finish(k):
        for copy in all_copies[k][2:]:
            copy.wait_recv()

    for k in range(SLICES):
        cols = columns(k)

        def move(source, target, index, other, k=k):
            at = base + 6 * k + index
            return links.copy(source, target, at, at, other)

        copies = [
            move(out_buf.at[0, k, top], relay_buf.at[0, k], 0, xn),
            move(out_buf.at[0, k, low], relay_buf.at[1, k], 1, yn),
            move(out_buf.at[1, k, top], final_buf.at[0, k, top], 2, xn),
            move(out_buf.at[2, k, low], final_buf.at[1, k, low], 3, yn),
            move(out_buf.at[2, k, top], final_buf.at[1, k, top], 4, yn),
            move(out_buf.at[1, k, low], final_buf.at[0, k, low], 5, xn),
        ]
        all_copies.append(copies)
        if ready:
            ready(k)
        for place, (owner, first) in enumerate(((dg, (0, 1)), (xn, (2,)), (yn, (3,)))):
            out_buf[place, k] = product(owner, k, cols).astype(bf16)
            for index in first:
                copies[index].start()
        if k:
            relay(k - 1)
        if hooks:
            o_ref[:, cols] = product(me, k, cols)
            hooks[k](columns, finish)
    for k in range(SLICES):
        if k == (0 if hooks else SLICES // 2):
            relay(SLICES - 1)
        if not hooks:
            o_ref[:, columns(k)] = product(me, k, columns(k))

    def sent():
        for copies in all_copies:
            for copy in copies:
                copy.wait_send()

    return columns, finish, sent


def finish_all(result):
    _, finish, sent = result
    for k in range(SLICES):
        finish(k)
    sent()


def each_tile(width, step, body):
    @pl.loop(0, width // step)
    def _(tile):
        body(pl.multiple_of(tile * step, step))


def lower(rows, factor):
    step = rows.shape[1] // 4
    parts = [
        mm_nt(rows[:, at : at + step], factor[:, at : at + step])
        for at in range(0, rows.shape[1], step)
    ]
    return (adapter_scale * functools.reduce(jnp.add, parts)).astype(bf16)


def leave_product(y_ref, weight, f1_ref, low_ref, loads):
    depth = f1_ref.shape[1]
    used = []

    def product(owner, k, cols):
        if k == 0:
            if loads:
                loads[len(used)].wait()
            used.append(True)
            lowered = lower(y_ref[owner, :, :depth], f1_ref[...])
            low_ref[owner] = lowered
            y_ref[owner, :, depth:] = lowered
        return weight(y_ref[owner], cols)

    return product


class Streams:
    def __init__(self, links, rows, blocks, late=()):
        order = (links.dg, links.xn, links.yn, links.row)
        self.rows = []
        if rows:
            cols = pl.ds(0, rows[0].shape[2])
            self.rows = links.plan(*[(rows[0].at[k], rows[1].at[k, :, cols]) for k in order])
        self.blocks = blocks
        self.late = links.plan(*late)
        start_all(self.rows[:1])
        start_all(blocks[0])

    def ready(self, k):
        wait_all(self.blocks[k])
        if k == 0:
            start_all(self.rows[1:])
        if k < SLICES - 1:
            start_all(self.blocks[k + 1])
        if k == 1:
            start_all(self.late)


def load_qkv(links, w_hbm, w_ref, blocks):
    half, width = w_hbm.shape[1] // 4, w_hbm.shape[2]
    return [
        links.plan(
            *[
                (
                    w_hbm.at[2 * c + t, pl.ds(p * half, half)],
                    w_ref.at[
                        pl.ds(pl.multiple_of((2 * c + t) * half, half), half),
                        pl.ds(p * width, width),
                    ],
                )
                for t in range(2)
                for p in range(3)
            ]
        )
        for c in blocks
    ]


def load_out(links, w_hbm, w_ref):
    half, width = w_hbm.shape[1] // 4, w_hbm.shape[2]
    return [
        links.plan(
            *[
                (
                    w_hbm.at[2 * c + t, pl.ds(3 * half, half)],
                    w_ref.at[pl.ds(t * half, half), pl.ds(c * width, width)],
                )
                for t in range(2)
            ]
        )
        for c in range(4)
    ]


def load_down(links, w_hbm, w_ref):
    half, width = w_hbm.shape[1:]
    return [
        links.plan(
            *[
                (
                    w_hbm.at[2 * c + t],
                    w_ref.at[pl.ds(t * half, half), pl.ds(c * width, width)],
                )
                for t in range(2)
            ]
        )
        for c in range(4)
    ]


def load_ffn(links, w_hbm, w_ref):
    half, width = w_hbm.shape[2:]
    return [
        links.plan(
            *[
                (
                    w_hbm.at[2 * c + t, g],
                    w_ref.at[pl.ds((2 * c + t) * half, half), pl.ds(g * width, width)],
                )
                for t in range(2)
                for g in range(2)
            ]
        )
        for c in range(4)
    ]


def inverse_of(values):
    return lax.rsqrt(jnp.mean(values * values, axis=1, keepdims=True) + norm_eps)


def norm_back(values, weighted):
    inverse = inverse_of(values)
    inner = jnp.mean(values * weighted, axis=1, keepdims=True)
    return inverse * weighted - values * (inverse**3 * inner)


def gated(gate, up):
    return gate * jax.nn.sigmoid(gate) * up


def gated_back(grad, gate, up):
    sig = jax.nn.sigmoid(gate)
    act = gate * sig
    return (grad * up * (sig + act * (1.0 - sig)), grad * act)


QKV_A, OUT_B, FFN_A, DOWN_B = slice(0, 48), slice(48, 64), slice(64, 96), slice(96, 112)
GAIN0, GAIN1 = slice(112, 113), slice(113, 114)


def share_stats(links, stat_ref, first, second):
    blank = jnp.zeros((6, first.shape[0]), f32)
    sums = [jnp.sum(value.T, axis=0, keepdims=True) for value in (first, second)]
    stat_ref[links.row] = jnp.concatenate(sums + [blank], axis=0)
    base = links.take(3)
    mine = stat_ref.at[links.row]
    copies = []
    for index, other in enumerate((links.xn, links.yn, links.dg)):
        copies.append(links.copy(mine, mine, base + index, base + index, other))
        copies[-1].start()
    for index, other in enumerate((links.xn, links.yn, links.dg)):
        theirs = stat_ref.at[other]
        links.copy(theirs, theirs, base + index, base + index, other).wait_recv()
    for copy in copies:
        copy.wait_send()
    return stat_ref[0] + stat_ref[1] + stat_ref[2] + stat_ref[3]


def lane_sums(values):
    return functools.reduce(
        jnp.add, [values[:, at : at + 128] for at in range(0, values.shape[1], 128)]
    )


def intake_kernel(
    x_hbm, cot_hbm, ids_ref, gain_ref, qkv_lower_ref, out_raise_ref, ffn_lower_ref, down_raise_ref,
    qkv_raise_ref, out_lower_ref, ffn_raise_ref, down_lower_ref,
    own_ref, cot_ref, factors_ref, factors_t_ref, qkv_b_ref, out_a_ref, out_at_ref, ffn_b_ref,
    down_a_ref, down_at_ref,
    middle_ref, pieces_ref, send_sem, recv_sem, local_sem,
):
    links = Links(send_sem, recv_sem, local_sem)
    links.greet(rows=3, columns=True)
    width = pieces_ref.shape[2]
    first = Exchange(links, "row", slot(x_hbm), slot(middle_ref))
    second = Exchange(links, "col", slot(middle_ref), features(own_ref, width))
    turned = Exchange(links, "row", slot(cot_hbm), slot(cot_ref))
    spread = Exchange(links, "col", slot(pieces_ref), features(factors_ref, width))
    first.start()
    base = 4 * links.tok
    for place in range(4):
        for p in range(7):
            chosen = ids_ref[base + place, p]
            if p < 3:
                value = qkv_lower_ref[p, chosen]
            elif p == 3:
                value = out_raise_ref[chosen]
            elif p < 6:
                value = ffn_lower_ref[p - 4, chosen]
            else:
                value = down_raise_ref[chosen]
            pieces_ref[place, p * RANK : (p + 1) * RANK] = value
        pieces_ref[place, 7 * RANK :] = gain_ref[...]
    spread.start()
    first.arrived()
    second.start()
    turned.start()
    own = base + links.col
    for ref in (qkv_b_ref, out_a_ref, ffn_b_ref, down_a_ref):
        ref[...] = jnp.zeros_like(ref)
    for p in range(3):
        cols = slice(p * qkv_raise_ref.shape[3], (p + 1) * qkv_raise_ref.shape[3])
        qkv_b_ref[p * RANK : (p + 1) * RANK, cols] = qkv_raise_ref[p, ids_ref[own, p]]
    for p in range(2):
        cols = slice(p * ffn_raise_ref.shape[3], (p + 1) * ffn_raise_ref.shape[3])
        rows = slice((4 + p) * RANK, (5 + p) * RANK)
        ffn_b_ref[rows, cols] = ffn_raise_ref[p, ids_ref[own, 4 + p]]
    out_a_ref[OUT_B] = out_lower_ref[ids_ref[own, 3]]
    down_a_ref[DOWN_B] = down_lower_ref[ids_ref[own, 6]]
    spread.arrived()
    for source, target in (
        (out_a_ref, out_at_ref), (down_a_ref, down_at_ref), (factors_ref, factors_t_ref)
    ):
        target[...] = source[...].astype(f32).T.astype(bf16)
    for exchange in (second, turned):
        exchange.arrived()
    for exchange in (first, spread, second, turned):
        exchange.sent()


def enter_qkv_kernel(
    x_ref, w_hbm, factors_ref, f2_ref,
    all_hbm, low_ref, lin_hbm, inv_ref,
    all_ref, lin_ref, w_ref, sq_ref, stat_ref, send_sem, recv_sem, local_sem,
):
    links = Links(send_sem, recv_sem, local_sem)
    width = w_ref.shape[1]
    loads = start_all(sum(load_qkv(links, w_hbm, w_ref, range(4)), []))
    loads += links.fetch((f2_ref, w_ref.at[pl.ds(D, 128)]))
    all_ref[links.row, :, :D] = x_ref[...]
    links.greet(rows=3)
    count = x_ref.shape[0]
    stores = []

    def work(owner):
        lowered = lower(all_ref[owner, :, :D], factors_ref[...])
        low_ref[owner] = lowered
        all_ref[owner, :, D:] = lowered
        rows = all_ref[owner]
        third = width // 3
        for index in range(3):
            cols = slice(index * third, (index + 1) * third)
            value = mm(rows, w_ref[:, cols])
            lin_ref[owner, :, cols] = value
            if index < 2:
                place = pl.ds(pl.multiple_of(owner * count, 8), count)
                sq_ref[index, place] = lane_sums(value * value)
        stores.extend(
            links.fetch(
                (lin_ref.at[owner], lin_hbm.at[owner]),
                (all_ref.at[owner, :, pl.ds(0, D)], all_hbm.at[owner]),
            )
        )

    gather(links, all_ref, work, lambda: wait_all(loads))
    total = share_stats(links, stat_ref, sq_ref[0], sq_ref[1])
    inv_ref[...] = lax.rsqrt(total / D + norm_eps).T
    wait_all(stores)


def summed(o_ref, final_buf, rows):
    return o_ref[rows] + jnp.concatenate(
        [
            final_buf[0, k, rows].astype(f32) + final_buf[1, k, rows].astype(f32)
            for k in range(SLICES)
        ],
        axis=1,
    )


def leave_out_kernel(
    y_hbm, w_hbm, f1_ref, factors_ref, x_ref,
    lin_ref, low_ref, hidden_ref, all_ref,
    y_ref, w_ref, out_buf, relay_buf, final_buf, send_sem, recv_sem, local_sem,
):
    links = Links(send_sem, recv_sem, local_sem)
    streams = Streams(links, (y_hbm, y_ref), load_out(links, w_hbm, w_ref))
    w_ref[f1_ref.shape[1] :] = factors_ref[...]
    links.greet()
    product = leave_product(
        y_ref, lambda rows, cols: mm(rows, w_ref[:, cols]), f1_ref, low_ref, streams.rows
    )
    finish_all(
        scatter(links, product, lin_ref, out_buf, relay_buf, final_buf, ready=streams.ready)
    )
    gain = factors_ref[GAIN0].astype(f32)

    @pl.loop(0, lin_ref.shape[0] // 16)
    def _(tile):
        rows = pl.ds(pl.multiple_of(tile * 16, 16), 16)
        value = summed(lin_ref, final_buf, rows)
        lin_ref[rows] = value
        hidden = x_ref[rows].astype(f32) + value * inverse_of(value) * gain
        hidden_ref[rows] = hidden
        all_ref[links.row, rows] = hidden.astype(bf16)

    gather(links, all_ref, None)


def flat_weight(ref):
    return ref[...].reshape(D, ref.shape[3])


def ffn_kernel(h_ref, wg_ref, wu_ref, factors_ref, fg_ref, fu_ref, low_ref, gate_ref, up_ref, act_ref):
    @pl.when(pl.program_id(0) == 0)
    def _():
        low_ref[...] = lower(h_ref[...], factors_ref[...])

    lowered = low_ref[...]
    rank = lowered.shape[1] // 2
    for at in range(0, SLAB, BLOCK):
        rows = slice(at, at + BLOCK)
        gate = mm(h_ref[rows], flat_weight(wg_ref)) + mm(lowered[rows], fg_ref[...])
        up = mm(h_ref[rows], flat_weight(wu_ref)) + mm(lowered[rows], fu_ref[...])
        gate_ref[rows] = gate.astype(bf16)
        up_ref[rows] = up.astype(bf16)
        act_ref[rows] = gated(gate, up).astype(bf16)


def ffn(h_all, w, factors, f2):
    width = f2.shape[1] // 2
    step = 256
    tiles = width // step
    low = jax.ShapeDtypeStruct((SLAB, f2.shape[0]), bf16)
    wide = jax.ShapeDtypeStruct((SLAB, width), bf16)
    whole = lambda value: pl.BlockSpec(value.shape, lambda t: (0, 0))
    cols = lambda rows, base: pl.BlockSpec((rows, step), lambda t: (0, base * tiles + t))
    block = (w.shape[0], 1, w.shape[2], step)
    part = lambda which: pl.BlockSpec(block, lambda t: (0, which, 0, t))
    return pl.pallas_call(
        ffn_kernel,
        grid=(tiles,),
        in_specs=[whole(h_all), part(0), part(1), whole(factors)]
        + [cols(f2.shape[0], 0), cols(f2.shape[0], 1)],
        out_specs=[whole(low)] + [cols(SLAB, 0)] * 3,
        out_shape=[low, wide, wide, wide],
        compiler_params=pltpu.CompilerParams(vmem_limit_bytes=48 << 20),
        cost_estimate=pl.CostEstimate(
            flops=4 * SLAB * D * width, bytes_accessed=4 * D * width + 10 * SLAB * width,
            transcendentals=SLAB * width,
        ),
        name="ffn",
    )(h_all, w, w, factors, f2, f2)


def leave_down_kernel(
    y_hbm, w_hbm, f1_ref, factors_ref, hidden_hbm, cot_ref,
    low_ref, out_ref, dm_ref, own_cot_ref,
    y_ref, w_ref, hidden_ref, lin_ref, out_buf, relay_buf, final_buf,
    send_sem, recv_sem, local_sem,
):
    links = Links(send_sem, recv_sem, local_sem)
    streams = Streams(
        links, (y_hbm, y_ref), load_down(links, w_hbm, w_ref), [(hidden_hbm, hidden_ref)]
    )
    links.greet(columns=True)
    turned = Exchange(links, "col", slot(cot_ref), features(own_cot_ref, cot_ref.shape[2]))
    w_ref[f1_ref.shape[1] :] = factors_ref[...]
    product = leave_product(
        y_ref, lambda rows, cols: mm(rows, w_ref[:, cols]), f1_ref, low_ref, streams.rows
    )
    def ready(k):
        if k == 2:
            turned.start()
        streams.ready(k)

    finish_all(
        scatter(
            links, product, lin_ref, out_buf, relay_buf, final_buf,
            ready=ready,
        )
    )
    turned.arrived()
    wait_all(streams.late)
    gain = factors_ref[GAIN1].astype(f32)

    @pl.loop(0, lin_ref.shape[0] // 16)
    def _(tile):
        rows = pl.ds(pl.multiple_of(tile * 16, 16), 16)
        value = summed(lin_ref, final_buf, rows)
        out_ref[rows] = (hidden_ref[rows] + value * inverse_of(value) * gain).astype(bf16)
        dm_ref[rows] = norm_back(value, own_cot_ref[rows].astype(f32) * gain).astype(bf16)

    turned.sent()


def widen(source_ref, target_ref):
    @pl.loop(0, source_ref.shape[0] // 64)
    def _(tile):
        rows = pl.ds(pl.multiple_of(tile * 64, 64), 64)
        target_ref[rows] = source_ref[rows].astype(f32)


def finish_kernel(
    chosen_ref, out_ref, grad_ref, parts_ref, every_ref,
    out32_ref, grad32_ref, qkv_lower_ref, out_raise_ref, ffn_lower_ref, down_raise_ref,
    qkv_raise_ref, out_lower_ref, ffn_raise_ref, down_lower_ref,
):
    widen(out_ref, out32_ref)
    widen(grad_ref, grad32_ref)
    targets = [qkv_lower_ref.at[p] for p in range(3)]
    targets += [out_raise_ref, ffn_lower_ref.at[0], ffn_lower_ref.at[1], down_raise_ref]
    for p, target in enumerate(targets):
        rows = slice(p % 2 * RANK, (p % 2 + 1) * RANK)
        for adapter in range(ADAPTERS):
            target[adapter] = parts_ref[p // 2, adapter, rows].astype(f32)
    targets = [qkv_raise_ref.at[p] for p in range(3)]
    targets += [out_lower_ref, ffn_raise_ref.at[0], ffn_raise_ref.at[1], down_lower_ref]
    base = 0
    for p, target in enumerate(targets):
        step = 256
        weights = [chosen_ref[p, at] for at in range(64)]

        @pl.loop(0, target.shape[2] // step)
        def _(tile, p=p, target=target, base=base, weights=weights):
            cols = pl.ds(pl.multiple_of(base + tile * step, step), step)
            here = pl.ds(pl.multiple_of(tile * step, step), step)
            values = [every_ref[g, :, cols].astype(f32) for g in range(8)]
            for adapter in range(ADAPTERS):
                terms = [weights[adapter * 8 + g] * values[g] for g in range(8)]
                target[adapter, :, here] = functools.reduce(jnp.add, terms)

        base += target.shape[2]


def finish(chosen, layer_out, grad_in, col_parts, every, head_width, ff_width):
    piece = col_parts.shape[3]

    def out(*shape):
        return jax.ShapeDtypeStruct(shape, f32)

    return pl.pallas_call(
        finish_kernel,
        in_specs=[SMEM] + [VMEM] * 4,
        out_specs=[VMEM] * 10,
        out_shape=[
            out(*layer_out.shape), out(*grad_in.shape),
            out(3, ADAPTERS, RANK, piece), out(ADAPTERS, RANK, piece),
            out(2, ADAPTERS, RANK, piece), out(ADAPTERS, RANK, piece),
            out(3, ADAPTERS, RANK, head_width), out(ADAPTERS, RANK, head_width),
            out(2, ADAPTERS, RANK, ff_width), out(ADAPTERS, RANK, ff_width),
        ],
        compiler_params=pltpu.CompilerParams(vmem_limit_bytes=48 << 20),
        cost_estimate=pl.CostEstimate(flops=10**8, bytes_accessed=16 << 20, transcendentals=0),
        name="finish",
    )(chosen, layer_out, grad_in, col_parts, every)


def back_down_kernel(
    dm_ref, w_hbm, factors_ref, f2_ref, gate_hbm, up_hbm, out_ref,
    all_hbm, low_ref, grad_hbm, out_mid_ref,
    all_ref, w_ref, gate_ref, up_ref, grad_ref, send_sem, recv_sem, local_sem,
):
    links = Links(send_sem, recv_sem, local_sem)
    loads = start_all(sum(load_down(links, w_hbm, w_ref), []))
    order = (links.row, links.xn, links.yn, links.dg)
    gates = [
        links.plan((gate_hbm.at[k], gate_ref.at[k]), (up_hbm.at[k], up_ref.at[k])) for k in order
    ]
    start_all(gates[0])
    all_ref[links.row, :, :D] = dm_ref[...]
    w_ref[:, D:] = f2_ref[...]
    links.greet(columns=True)
    width = w_ref.shape[0]
    turned = Exchange(links, "col", features(out_ref, out_mid_ref.shape[2]), slot(out_mid_ref))
    stores = []

    def before():
        wait_all(loads)
        for gate in gates[1:]:
            start_all(gate)

    def work(owner):
        wait_all(gates[len(stores) // 2])
        lowered = lower(all_ref[owner, :, :D], factors_ref[...])
        low_ref[owner] = lowered
        all_ref[owner, :, D:] = lowered

        def body(at):
            cols, far = pl.ds(at, TILE), pl.ds(pl.multiple_of(width + at, TILE), TILE)
            grad = mm_nt(all_ref[owner], w_ref[cols, :])
            gate, up = gate_ref[owner, :, cols].astype(f32), up_ref[owner, :, cols].astype(f32)
            grad_gate, grad_up = gated_back(grad, gate, up)
            grad_ref[owner, :, cols] = grad_gate.astype(bf16)
            grad_ref[owner, :, far] = grad_up.astype(bf16)

        each_tile(width, TILE, body)
        stores.extend(
            links.fetch(
                (grad_ref.at[owner], grad_hbm.at[owner]),
                (all_ref.at[owner, :, pl.ds(0, D)], all_hbm.at[owner]),
            )
        )

    gather(links, all_ref, work, before, turned.start)
    turned.arrived()
    turned.sent()
    wait_all(stores)


def back_ffn_kernel(
    y_hbm, w_hbm, f1_ref, factors_ref, factors_t_ref, cot_hbm, attn_hbm,
    low_ref, hidden_ref, da_ref,
    y_ref, w_ref, cot_ref, attn_ref, lin_ref, out_buf, relay_buf, final_buf,
    send_sem, recv_sem, local_sem,
):
    links = Links(send_sem, recv_sem, local_sem)
    streams = Streams(
        links,
        (y_hbm, y_ref),
        load_ffn(links, w_hbm, w_ref),
        [(cot_hbm, cot_ref), (attn_hbm, attn_ref)],
    )
    links.greet()
    w_ref[:, f1_ref.shape[1] :] = factors_t_ref[...]
    product = leave_product(
        y_ref, lambda rows, cols: mm_nt(rows, w_ref[cols, :]), f1_ref, low_ref, streams.rows
    )
    finish_all(
        scatter(
            links, product, lin_ref, out_buf, relay_buf, final_buf,
            ready=streams.ready,
        )
    )
    wait_all(streams.late)
    gain = factors_ref[GAIN0].astype(f32)

    @pl.loop(0, lin_ref.shape[0] // 16)
    def _(tile):
        rows = pl.ds(pl.multiple_of(tile * 16, 16), 16)
        value = summed(lin_ref, final_buf, rows) + cot_ref[rows].astype(f32)
        hidden_ref[rows] = value
        da_ref[rows] = norm_back(attn_ref[rows], value * gain).astype(bf16)


def mm_tn(left, right):
    return lax.dot_general(left, right, (((0,), (0,)), ((), ())), preferred_element_type=f32)


def back_out_kernel(
    da_ref, w_hbm, factors_ref, f2_ref, out_low_ref, attn_ref, down_low_ref, down_dlow_ref,
    ffn_low_ref, ffn_dlow_ref, dm_hbm, act_hbm, grad_hbm, h_hbm,
    heads_ref, cols_ref, rows_ref,
    all_ref, w_ref, dm_ref, act_ref, grad_ref, h_ref, raise_ref, lower_ref, send_sem, recv_sem, local_sem,
):
    links = Links(send_sem, recv_sem, local_sem)
    load = start_all(sum(load_out(links, w_hbm, w_ref), []))
    all_ref[links.row, :, :D] = da_ref[...]
    w_ref[:, D:] = f2_ref[...]
    links.greet()
    loads = []

    def before():
        loads.extend(
            links.fetch((dm_hbm, dm_ref), (act_hbm, act_ref), (grad_hbm, grad_ref), (h_hbm, h_ref))
        )
        wait_all(load)

    heads, half = heads_ref.shape[2], grad_ref.shape[1] // 2

    def after():
        wait_all(loads)
        down_raise = mm_tn(down_low_ref[:, DOWN_B], dm_ref[...])
        cols_ref[3 * RANK : 4 * RANK] = down_raise.astype(bf16)
        cols_ref[RANK : 3 * RANK] = mm_tn(ffn_dlow_ref[:, FFN_A], h_ref[...]).astype(bf16)
        for p in range(2):
            low = ffn_low_ref[:, (4 + p) * RANK : (5 + p) * RANK]
            raised = mm_tn(low, grad_ref[:, p * half : (p + 1) * half])
            rows_ref[:, heads + p * half : heads + (p + 1) * half] = raised.astype(bf16)
        rows_ref[:, heads + 2 * half :] = mm_tn(down_dlow_ref[:, DOWN_B], act_ref[...]).astype(bf16)

    def work(owner):
        lowered = lower(all_ref[owner, :, :D], factors_ref[...])
        all_ref[owner, :, D:] = lowered
        heads_ref[owner] = mm_nt(all_ref[owner], w_ref[...]).astype(bf16)
        raise_ref[...] += mm_tn(out_low_ref[owner, :, OUT_B], all_ref[owner, :, :D])
        lower_ref[...] += mm_tn(lowered[:, OUT_B], attn_ref[owner])

    raise_ref[...] = jnp.zeros_like(raise_ref)
    lower_ref[...] = jnp.zeros_like(lower_ref)
    gather(links, all_ref, work, before, after)
    cols_ref[0:RANK] = raise_ref[...].astype(bf16)
    rows_ref[:, :heads] = lower_ref[...].astype(bf16)


def prepare_kernel(
    wq_hbm, wk_hbm, dv_ref, lin_hbm, inv_ref, inner_ref, f1_ref, low_ref, early_ref,
    grad_ref, rows_ref,
    wq_ref, wk_ref, lin_ref, total_ref, stat_ref, send_sem, recv_sem, local_sem,
):
    links = Links(send_sem, recv_sem, local_sem)
    third = wq_ref.shape[1]
    loads = links.fetch(
        (wq_hbm, wq_ref),
        (wk_hbm, wk_ref),
        (lin_hbm.at[:, pl.ds(0, 2 * third)], lin_ref),
    )
    links.greet(rows=3)
    total = share_stats(links, stat_ref, inner_ref[0], inner_ref[1])
    total_ref[...] = total.T / D
    wait_all(loads)

    @pl.loop(0, SLAB // 96)
    def _(tile):
        rows = pl.ds(pl.multiple_of(tile * 96, 96), 96)
        inverse = inv_ref[rows]
        factor = inverse**3 * total_ref[rows]
        for index, source in enumerate((wq_ref, wk_ref)):
            cols = slice(index * third, (index + 1) * third)
            one = slice(index, index + 1)
            value = inverse[:, one] * source[rows] - lin_ref[rows, cols] * factor[:, one]
            grad_ref[rows, cols] = value.astype(bf16)
        grad_ref[rows, 2 * third : 3 * third] = dv_ref[rows]

    grad_ref[:, 3 * third :] = lower(grad_ref[:, : 3 * third], f1_ref[...])
    for index in range(3):
        cols = slice(index * third, (index + 1) * third)
        low = low_ref[:, index * RANK : (index + 1) * RANK]
        rows_ref[:, cols] = mm_tn(low, grad_ref[:, cols]).astype(bf16)
    rows_ref[:, 3 * third :] = early_ref[...]


def back_qkv_kernel(
    grad_ref, w_hbm, factors_t_ref, hidden_hbm, x_hbm, early_ref, chosen_ref,
    turn_buf, sums_ref,
    w_ref, hidden_ref, x_ref, sum_ref, own_ref, middle_ref, parts_ref, got_ref, total_ref, groups_ref,
    placed_ref, out_buf, relay_buf, final_buf, send_sem, recv_sem, local_sem,
):
    links = Links(send_sem, recv_sem, local_sem)
    steps = (2, 3, 1, 0)
    streams = Streams(
        links,
        None,
        load_qkv(links, w_hbm, w_ref, [links.col ^ step for step in steps]),
        [(hidden_hbm, hidden_ref)],
    )
    x_load = links.plan((x_hbm, x_ref))
    depth = w_ref.shape[1] - 128
    w_ref[:, depth:] = factors_t_ref[...]
    links.greet(rows=3, columns=True, twin=True)
    width = own_ref.shape[2]
    count = grad_ref.shape[1]
    by_row = Exchange(links, "row", slot(parts_ref), slot(got_ref))
    base = 4 * links.tok
    by_col = Exchange(
        links, "col", slot(total_ref), lambda key: groups_ref.at[base + key]
    )
    index = links.take(1)
    mine, theirs = groups_ref.at[pl.ds(base, 4)], groups_ref.at[pl.ds(4 - base, 4)]
    to_twin = links.copy(mine, mine, index, index, links.row, tok=links.tok ^ 1)
    from_twin = links.copy(theirs, theirs, index, index, links.row, tok=links.tok ^ 1)
    mine_half, their_half = (pl.ds(tok * RANK, RANK) for tok in (links.tok, 1 - links.tok))
    spread = Exchange(
        links,
        "row",
        lambda key: placed_ref.at[:, mine_half],
        lambda key: sums_ref.at[key, :, mine_half],
    )
    index = links.take(1)
    sent_half, got_half = sums_ref.at[:, :, mine_half], sums_ref.at[:, :, their_half]
    half_out = links.copy(sent_half, sent_half, index, index, links.row, tok=links.tok ^ 1)
    half_in = links.copy(got_half, got_half, index, index, links.row, tok=links.tok ^ 1)

    def lower_grad():
        wait_all(x_load)
        late = 0.0
        for owner in range(4):
            late = late + mm_tn(grad_ref[owner, :, depth : depth + 3 * RANK], x_ref[owner])
        late = late.astype(bf16)
        parts_ref[0] = late[0 : 2 * RANK]
        parts_ref[1, :RANK] = late[2 * RANK :]
        parts_ref[1, RANK:] = early_ref[:RANK]
        parts_ref[2] = early_ref[RANK : 3 * RANK]
        parts_ref[3, :RANK] = early_ref[3 * RANK :]
        parts_ref[3, RANK:] = jnp.zeros((RANK, D), bf16)
        by_row.start()

    def add_rows():
        by_row.arrived()
        for f in range(4):
            cols = slice(f * width, (f + 1) * width)
            value = got_ref[0, :, cols].astype(f32)
            for q in range(1, 4):
                value = value + got_ref[q, :, cols].astype(f32)
            total_ref[f] = value.astype(bf16)
        by_col.start()

    def share():
        by_col.arrived()
        to_twin.start()

    def place_groups():
        from_twin.wait_recv()
        for half in range(2):
            rows = slice(half * RANK, (half + 1) * RANK)
            values = [groups_ref[g, rows].astype(f32) for g in range(8)]
            for adapter in range(ADAPTERS):
                value = 0.0
                for g in range(8):
                    value = value + chosen_ref[2 * links.row + half, adapter * 8 + g] * values[g]
                placed_ref[adapter, rows] = value.astype(bf16)
        spread.start()

    def product(owner, k, cols):
        return mm_nt(grad_ref[owner], w_ref[cols, :])

    z_base, row_base = links.take(3), links.take(4)
    near = links.local(middle_ref.at[links.row], token_rows(turn_buf, count)(links.row))
    z_copies = []

    def leave_col(k, columns, finish):
        finish(k)
        cols, step = columns(k), steps[k]
        value = (
            sum_ref[:, cols]
            + final_buf[0, k].astype(f32)
            + final_buf[1, k].astype(f32)
            + hidden_ref[:, cols]
        ).astype(bf16)
        if step == 0:
            middle_ref[links.col] = value
            return
        own_ref[k] = value
        at = z_base + k
        copy = links.copy(
            own_ref.at[k], middle_ref.at[links.col], at, at, links.row, links.col ^ step
        )
        copy.start()
        z_copies.append(copy)

    def to_row(step):
        other = links.row ^ step
        return links.copy(
            middle_ref.at[other],
            token_rows(turn_buf, count)(links.row),
            row_base + step,
            row_base + step,
            other,
        )

    def leave_row(k):
        source = links.col ^ steps[k]
        if steps[k]:
            at = z_base + k
            landed = middle_ref.at[source]
            links.copy(landed, landed, at, at, links.row, source).wait_recv()
        step = links.row ^ source

        @pl.when(step == 0)
        def _():
            near.start()

        @pl.when(step != 0)
        def _():
            to_row(step).start()

    def first(columns, finish):
        start_all(x_load)

    def second(columns, finish):
        lower_grad()

    def third(columns, finish):
        wait_all(streams.late)
        leave_col(0, columns, finish)

    def fourth(columns, finish):
        add_rows()
        leave_col(1, columns, finish)

    columns, finish, sent = scatter(
        links, product, sum_ref, out_buf, relay_buf, final_buf,
        block=lambda k: links.col ^ steps[k],
        ready=streams.ready,
        hooks=[first, second, third, fourth],
    )
    leave_row(0)
    share()
    leave_col(2, columns, finish)
    leave_col(3, columns, finish)
    leave_row(3)
    place_groups()
    leave_row(2)
    leave_row(1)
    spread.arrived()
    half_out.start()
    near.wait()
    for step in range(1, 4):
        landed = token_rows(turn_buf, count)(links.row ^ step)
        at = row_base + step
        links.copy(landed, landed, at, at, links.row ^ step).wait_recv()
    half_in.wait_recv()
    for step in range(1, 4):
        to_row(step).wait_send()
    half_out.wait_send()
    for copy in z_copies:
        copy.wait_send()
    to_twin.wait_send()
    for exchange in (by_row, by_col, spread):
        exchange.sent()
    sent()


VMEM = pl.BlockSpec(memory_space=pltpu.VMEM)
ANY = pl.BlockSpec(memory_space=pl.ANY)
SMEM = pl.BlockSpec(memory_space=pltpu.SMEM)


def linked(kernel, number, operands, outs, scratch, flops):
    specs = [ANY if isinstance(value, tuple) else VMEM for value in operands]
    values = [value[0] if isinstance(value, tuple) else value for value in operands]
    specs = [
        SMEM if value.ndim == 2 and value.shape[0] == 8 and value.dtype != bf16 else spec
        for spec, value in zip(specs, values)
    ]
    return pl.pallas_call(
        kernel,
        in_specs=specs,
        out_specs=[ANY if len(out) == 3 else VMEM for out in outs],
        out_shape=[jax.ShapeDtypeStruct(out[0], out[1]) for out in outs],
        scratch_shapes=[pltpu.VMEM(shape, kind) for shape, kind in scratch]
        + [
            pltpu.SemaphoreType.DMA((48,)),
            pltpu.SemaphoreType.DMA((48,)),
            pltpu.SemaphoreType.DMA((48,)),
        ],
        compiler_params=pltpu.CompilerParams(
            collective_id=number, has_side_effects=True, vmem_limit_bytes=60 << 20
        ),
        cost_estimate=pl.CostEstimate(
            flops=flops, bytes_accessed=flops // 400, transcendentals=0
        ),
        name=kernel.__name__,
    )(*values)


def scatter_buffers(count):
    part = D // SLICES
    return [
        ((3, SLICES, count, part), bf16),
        ((2, SLICES, count // 2, part), bf16),
        ((2, SLICES, count, part), bf16),
    ]


def score_blocks(k_ref, q_block, bias_ref, start, stop):
    parts = []
    if start:
        parts.append(mm_nt(k_ref[0:start], q_block) + bias_ref[0:start])
    own = mm_nt(k_ref[start:stop], q_block) + bias_ref[start:stop]
    keys = lax.broadcasted_iota(jnp.int32, own.shape, 0)
    queries = lax.broadcasted_iota(jnp.int32, own.shape, 1)
    parts.append(jnp.where(keys <= queries, own, very_low))
    return parts

def attend_kernel(q_ref, k_ref, v_ref, inv_ref, gain_ref, cos_ref, sin_ref, bias_ref,
                  ql_ref, kl_ref, vl_ref, o_ref, lse_ref):
    for source, target, index in ((q_ref, ql_ref, 0), (k_ref, kl_ref, 1)):
        normed = source[...] * inv_ref[:, index:index+1] * gain_ref[index:index+1, :]
        target[...] = (normed * cos_ref[...] + pltpu.roll(normed, HEAD_DIM // 2, 1) * sin_ref[...]).astype(bf16)
    values = v_ref[...].astype(bf16)
    vl_ref[...] = values
    values_t = v_ref[...].T.astype(bf16)
    for start in range(0, SLAB, BLOCK):
        stop = start + BLOCK
        parts = score_blocks(kl_ref, ql_ref[start:stop], bias_ref, start, stop)
        top = functools.reduce(jnp.maximum, [jnp.max(p, axis=0, keepdims=True) for p in parts]) * log2_scale
        total, out, at = 0.0, 0.0, 0
        for part in parts:
            shifted = jnp.exp2(part * log2_scale - top)
            total = total + jnp.sum(shifted, axis=0, keepdims=True)
            out = out + mm(values_t[:, at:at+part.shape[0]], shifted.astype(bf16))
            at += part.shape[0]
        o_ref[start:stop] = (out / total).T.astype(bf16)
        lse_ref[0, :, start:stop] = top + jnp.log2(total)

def attend_back_kernel(ql_ref, kl_ref, vl_ref, o_ref, do_ref, lse_ref, q_ref, k_ref, gain_ref, cos_ref, sin_ref, bias_ref, *refs):
    mid_ref, wq_ref, wk_ref, dv_ref, sum_ref, turn_ref, dk_sum, dv_sum, *sems = refs if len(refs) > 8 else (None, *refs[:4], None, *refs[4:])
    if sems:
        links = Links(*sems)
        turned = Exchange(links, "row", slot(mid_ref), token_rows(turn_ref, mid_ref.shape[1]))

        @pl.when(pl.program_id(0) == 0)
        def _():
            links.greet(rows=3)
            turned.start()

    keys_t = kl_ref[...].astype(f32).T.astype(bf16)
    delta_all = jnp.sum((do_ref[...].astype(f32) * o_ref[...].astype(f32)).T, axis=0, keepdims=True)
    dk_sum[...] = jnp.zeros_like(dk_sum)
    dv_sum[...] = jnp.zeros_like(dv_sum)
    def unrotate(values):
        return values * cos_ref[...] - pltpu.roll(values, HEAD_DIM // 2, 1) * sin_ref[...]
    dq_parts = []
    for start in range(0, SLAB, BLOCK):
        stop = start + BLOCK
        queries, grads = ql_ref[start:stop], do_ref[start:stop]
        parts = score_blocks(kl_ref, queries, bias_ref, start, stop)
        lse, delta = lse_ref[0, :, start:stop], delta_all[:, start:stop]
        at, dq = 0, 0.0
        for part in parts:
            span = slice(at, at + part.shape[0])
            probs = jnp.exp2(part * log2_scale - lse)
            dv_sum[span] += mm(probs.astype(bf16), grads)
            dscore = (probs * (mm_nt(vl_ref[span], grads) - delta)).astype(bf16)
            dk_sum[span] += mm(dscore, queries)
            dq = dq + mm(keys_t[:, span], dscore)
            at += part.shape[0]
        dq_parts.append(dq.T)
    dq_all = jnp.concatenate(dq_parts, axis=0) * score_scale
    dv_ref[...] = dv_sum[...].astype(bf16)
    wq = unrotate(dq_all) * gain_ref[0:1, :]
    wk = unrotate(dk_sum[...] * score_scale) * gain_ref[1:2, :]
    wq_ref[...] = wq.astype(wq_ref.dtype)
    wk_ref[...] = wk.astype(wk_ref.dtype)
    first = pl.program_id(0) == 0
    for index, (weighted, source) in enumerate(((wq, q_ref), (wk, k_ref))):
        product = weighted * source[...]

        @pl.when(first)
        def _():
            sum_ref[index] = product

        @pl.when(jnp.logical_not(first))
        def _():
            sum_ref[index] += product

    if sems:

        @pl.when(pl.program_id(0) == pl.num_programs(0) - 1)
        def _():
            turned.arrived()
            turned.sent()


def attend_specs(heads):
    col = lambda base: pl.BlockSpec((SLAB, HEAD_DIM), lambda h: (0, base * heads + h))
    whole = lambda shape: pl.BlockSpec(shape, lambda h: (0,) * len(shape))
    return col, whole

def attend(qkv_lin, inverses, gains, cosine, sine, bias):
    heads = qkv_lin.shape[1] // (3 * HEAD_DIM)
    col, whole = attend_specs(heads)
    low = jax.ShapeDtypeStruct((SLAB, heads * HEAD_DIM), bf16)
    return pl.pallas_call(
        attend_kernel, grid=(heads,),
        in_specs=[col(0), col(1), col(2), whole((SLAB, 8)), pl.BlockSpec((2, HEAD_DIM), lambda h: (0, h)),
                  whole((SLAB, HEAD_DIM)), whole((SLAB, HEAD_DIM)), whole((SLAB, 1))],
        out_specs=[col(0)] * 4 + [pl.BlockSpec((1, 1, SLAB), lambda h: (h, 0, 0))],
        out_shape=[low] * 4 + [jax.ShapeDtypeStruct((heads, 1, SLAB), f32)],
        compiler_params=pltpu.CompilerParams(vmem_limit_bytes=48 << 20),
        cost_estimate=pl.CostEstimate(flops=heads*4*SLAB*SLAB*HEAD_DIM, bytes_accessed=heads*SLAB*HEAD_DIM*20, transcendentals=heads*SLAB*SLAB),
        name="attend",
    )(qkv_lin, qkv_lin, qkv_lin, inverses, gains, cosine, sine, bias)

def attend_back(ql, kl, vl, o, do, lse, qkv_lin, gains, cosine, sine, bias, middle=None):
    heads = ql.shape[1] // HEAD_DIM
    col, whole = attend_specs(heads)
    wide = jax.ShapeDtypeStruct(ql.shape, f32)
    outs = [wide, wide, jax.ShapeDtypeStruct(ql.shape, bf16)]
    outs.append(jax.ShapeDtypeStruct((2, SLAB, HEAD_DIM), f32))
    moved, turned, params, sems = [], [], dict(vmem_limit_bytes=48 << 20), []
    if middle is not None:
        moved, turned = [middle], [jax.ShapeDtypeStruct((SLAB, middle.shape[2]), bf16)]
        params.update(collective_id=10, has_side_effects=True)
        sems = [pltpu.SemaphoreType.DMA((4,))] * 3
    hbm = pl.BlockSpec(memory_space=pl.ANY)
    return pl.pallas_call(
        attend_back_kernel,
        grid=(heads,),
        in_specs=[col(0)] * 5
        + [pl.BlockSpec((1, 1, SLAB), lambda h: (h, 0, 0)), col(0), col(1)]
        + [pl.BlockSpec((2, HEAD_DIM), lambda h: (0, h))]
        + [whole((SLAB, HEAD_DIM)), whole((SLAB, HEAD_DIM)), whole((SLAB, 1))]
        + [hbm] * len(moved),
        out_specs=[col(0)] * 3 + [whole((2, SLAB, HEAD_DIM))] + [hbm] * len(turned),
        out_shape=outs + turned,
        scratch_shapes=[pltpu.VMEM((SLAB, HEAD_DIM), f32)] * 2 + sems,
        compiler_params=pltpu.CompilerParams(**params),
        cost_estimate=pl.CostEstimate(
            flops=heads * 10 * SLAB * SLAB * HEAD_DIM,
            bytes_accessed=heads * SLAB * HEAD_DIM * 30,
            transcendentals=heads * SLAB * SLAB,
        ),
        name="attend_back",
    )(ql, kl, vl, o, do, lse, qkv_lin, qkv_lin, gains, cosine, sine, bias, *moved)


def dot(left, right):
    return jnp.dot(left, right, preferred_element_type=f32)


def dot_nt(left, right):
    return lax.dot_general(left, right, (((1,), (1,)), ((), ())), preferred_element_type=f32)


def dot_tn(left, right):
    return lax.dot_general(left, right, (((0,), (0,)), ((), ())), preferred_element_type=f32)


def gather_weight(local):
    half = local.shape[0] // lax.axis_size("tok")
    part = lax.dynamic_slice_in_dim(local, lax.axis_index("tok") * half, half, 0)
    return lax.all_gather(part, ("col", "tok"), axis=0, tiled=True)


def to_tokens(values):
    rows, cols = lax.axis_size("row"), lax.axis_size("col")
    width = values.shape[1]
    mixed = lax.all_to_all(values, "row", 0, 0, tiled=True)
    mixed = lax.all_to_all(mixed, "col", 0, 0, tiled=True)
    return mixed.reshape(cols, SLAB // rows, width).transpose(1, 0, 2).reshape(SLAB // rows, -1)


def from_tokens(values):
    rows, cols = lax.axis_size("row"), lax.axis_size("col")
    count = values.shape[0]
    mixed = values.reshape(count, cols, -1).transpose(1, 0, 2).reshape(cols * count, -1)
    mixed = lax.all_to_all(mixed, "col", 0, 0, tiled=True)
    return lax.all_to_all(mixed, "row", 0, 0, tiled=True)


def reorder(values, outer, inner):
    if outer == 1 or inner == 1:
        return values
    rest = values.shape[0] // (outer * inner)
    shape = (outer, inner, rest) + values.shape[1:]
    return values.reshape(shape).swapaxes(0, 1).reshape(values.shape)


def gather_tokens(values):
    rows, per_slab = lax.axis_size("row"), lax.axis_size("row") // lax.axis_size("col")
    return reorder(lax.all_gather(values, "row", axis=0, tiled=True), rows, per_slab)


def scatter_tokens(values):
    rows, per_slab = lax.axis_size("row"), lax.axis_size("row") // lax.axis_size("col")
    values = reorder(values.astype(bf16), per_slab, rows)
    return lax.psum_scatter(values, "row", scatter_dimension=0, tiled=True).astype(f32)


def token_places(length):
    slot_ids = jnp.arange(SLAB, dtype=jnp.int32)
    return jnp.where(slot_ids < PROMPT, slot_ids, length + (slot_ids - PROMPT) % CONT_LEN)


def rotation(places, head_size):
    half_dim = head_size // 2
    frequency = jnp.exp(
        -(2.0 * jnp.arange(half_dim, dtype=f32) / head_size) * math.log(rope_base)
    )
    angles = places.astype(f32)[:, None] * frequency[None, :]
    return (jnp.cos(angles), jnp.sin(angles))


def pick(adapters, ids):
    onehot = (ids[:, None] == jnp.arange(adapters.shape[0], dtype=jnp.int32)).astype(adapters.dtype)
    return jnp.tensordot(onehot, adapters, axes=1)


def place(ids, gradients):
    onehot = (jnp.arange(ADAPTERS, dtype=jnp.int32)[:, None] == ids[None, :]).astype(f32)
    total = 0.0
    for index in range(gradients.shape[0]):
        weight = onehot[:, index].reshape((ADAPTERS,) + (1,) * (gradients.ndim - 1))
        total = total + weight * gradients[index][None].astype(f32)
    return total


def block_diagonal(factors):
    count = len(factors)
    lines = []
    for index, factor in enumerate(factors):
        blank = jnp.zeros_like(factor)
        lines.append(
            jnp.concatenate([factor if k == index else blank for k in range(count)], axis=1)
        )
    return jnp.concatenate(lines, axis=0)


def enter(x, w, f1, f2):
    everything = gather_tokens(x)
    lowered = (adapter_scale * dot_nt(everything, f1)).astype(bf16)
    return everything, lowered, dot(everything, w) + dot(lowered, f2)


def leave(y, w, f1, f2):
    lowered = (adapter_scale * dot_nt(y, f1)).astype(bf16)
    return scatter_tokens(dot_nt(y, w) + dot(lowered, f2)), lowered


def split_layer(
    layer_in, cotangent, qkv_weight, out_weight, ffn_weight, down_weight, head_gain, post_gain,
    adapters, adapter_ids, tables,
):
    qkv_lower, out_raise, ffn_lower, down_raise, qkv_raise, out_lower, ffn_raise, down_lower = (
        adapters
    )
    col_count = lax.axis_size("col")
    group_base = lax.axis_index("tok") * col_count
    group = group_base + lax.axis_index("col")
    slab_ids = lax.dynamic_slice_in_dim(adapter_ids, group_base, col_count, 0)
    own_ids = lax.dynamic_index_in_dim(adapter_ids, group, 0, keepdims=False)
    size = layer_in.shape[1]
    local = jnp.concatenate([qkv_weight.transpose(1, 0, 2).reshape(size, -1), out_weight.T], axis=1)
    attn_full = gather_weight(local)
    ffn_full = gather_weight(ffn_weight.transpose(1, 0, 2).reshape(size, -1))
    down_full = gather_weight(down_weight.T)
    pieces = jnp.concatenate(
        [pick(qkv_lower[p], slab_ids[:, p]) for p in range(3)]
        + [pick(out_raise, slab_ids[:, 3])]
        + [pick(ffn_lower[p], slab_ids[:, 4 + p]) for p in range(2)]
        + [pick(down_raise, slab_ids[:, 6])]
        + [jnp.broadcast_to(jnp.pad(post_gain, ((0, 14), (0, 0))), (col_count, RANK, size))],
        axis=1,
    )
    qkv_b = block_diagonal([pick(qkv_raise[p], own_ids[p : p + 1])[0] for p in range(3)])
    out_a = pick(out_lower, own_ids[3:4])[0]
    ffn_b = block_diagonal([pick(ffn_raise[p], own_ids[4 + p : 5 + p])[0] for p in range(2)])
    down_a = pick(down_lower, own_ids[6:7])[0]
    factors = lax.all_to_all(pieces, "col", 0, 0, tiled=True)
    factors = factors.transpose(1, 0, 2).reshape(-1, D)
    qkv_a, out_b, ffn_a, down_b = (factors[part] for part in (QKV_A, OUT_B, FFN_A, DOWN_B))
    gains = factors[GAIN0.start : GAIN1.stop].astype(f32)
    width = qkv_b.shape[1]
    head_width, ff_width = width // 3, ffn_b.shape[1] // 2
    x_own = to_tokens(layer_in)
    x_all, qkv_low, qkv_lin = enter(x_own, attn_full[:, :width], qkv_a, qkv_b)
    q_lin, k_lin = qkv_lin[:, :head_width], qkv_lin[:, head_width : 2 * head_width]
    squares = jnp.stack([jnp.sum(q_lin * q_lin, axis=1), jnp.sum(k_lin * k_lin, axis=1)], axis=1)
    inverses = lax.rsqrt(lax.psum(squares, "row") / D + norm_eps)
    inverses = jnp.concatenate([inverses] * 4, axis=1)
    q_low, k_low, v_low, attn_low, log_sums = attend(qkv_lin, inverses, head_gain, *tables)
    attn_lin, out_low = leave(attn_low, attn_full[:, width:], out_a, out_b)
    hidden = x_own.astype(f32) + attn_lin * inverse_of(attn_lin) * gains[0]
    h_all, ffn_low, ffn_lin = enter(hidden.astype(bf16), ffn_full, ffn_a, ffn_b)
    gate_lin, up_lin = ffn_lin[:, :ff_width], ffn_lin[:, ff_width:]
    act_low = gated(gate_lin, up_lin).astype(bf16)
    mlp_lin, down_low = leave(act_low, down_full, down_a, down_b)
    layer_out = hidden + mlp_lin * inverse_of(mlp_lin) * gains[1]
    layer_out = from_tokens(layer_out.astype(bf16)).astype(f32)
    grad_out = to_tokens(cotangent).astype(f32)
    grad_mlp = norm_back(mlp_lin, grad_out * gains[1]).astype(bf16)
    dm_all, down_dlow, grad_act = enter(grad_mlp, down_full, down_b, down_a)
    grad_ffn = jnp.concatenate(gated_back(grad_act, gate_lin, up_lin), axis=1).astype(bf16)
    grad_ffn_in, ffn_dlow = leave(grad_ffn, ffn_full, ffn_b, ffn_a)
    grad_hidden = grad_out + grad_ffn_in
    grad_attn = norm_back(attn_lin, grad_hidden * gains[0]).astype(bf16)
    da_all, out_dlow, grad_heads = enter(grad_attn, attn_full[:, width:], out_b, out_a)
    weighted_q, weighted_k, grad_v, inner = attend_back(
        q_low, k_low, v_low, attn_low, grad_heads.astype(bf16), log_sums, qkv_lin, head_gain, *tables
    )
    inner = lax.psum(jnp.sum(inner, axis=2).T, "row")
    factor = inverses[:, :2] ** 3 * inner / D
    grad_qkv = jnp.concatenate(
        [
            (inverses[:, 0:1] * weighted_q - q_lin * factor[:, 0:1]).astype(bf16),
            (inverses[:, 1:2] * weighted_k - k_lin * factor[:, 1:2]).astype(bf16),
            grad_v,
        ],
        axis=1,
    )
    grad_qkv_in, qkv_dlow = leave(grad_qkv, attn_full[:, :width], qkv_b, qkv_a)
    grad_in = from_tokens((grad_hidden + grad_qkv_in).astype(bf16)).astype(f32)
    parts = jnp.concatenate(
        [dot_tn(qkv_dlow, x_all), dot_tn(out_low, da_all), dot_tn(ffn_dlow, h_all)]
        + [dot_tn(down_low, dm_all)]
    )
    parts = parts.astype(bf16).reshape(7, RANK, col_count, size).transpose(2, 0, 1, 3)
    parts = lax.all_to_all(parts, "col", 0, 0, tiled=True)
    placed = [place(slab_ids[:, p], parts[:, p]) for p in range(7)]
    col_grads = list(lax.psum(jnp.stack(placed).astype(bf16), ("tok", "row")).astype(f32))
    own_rows = jnp.concatenate(
        [diagonal(dot_tn(qkv_low, grad_qkv), 3), dot_tn(out_dlow, attn_low)]
        + [diagonal(dot_tn(ffn_low, grad_ffn), 2), dot_tn(down_dlow, act_low)],
        axis=1,
    )
    every = lax.all_gather(own_rows.astype(bf16), ("tok", "col"), axis=0)
    row_grads, at = [], 0
    for p in range(7):
        part = ff_width if p > 3 else head_width
        row_grads.append(place(adapter_ids[:, p], every[:, :, at : at + part]))
        at += part
    return (
        layer_out, grad_in,
        jnp.stack(col_grads[0:3]), col_grads[3], jnp.stack(col_grads[4:6]), col_grads[6],
        jnp.stack(row_grads[0:3]), row_grads[3], jnp.stack(row_grads[4:6]), row_grads[6],
    )


def flat(values):
    return values.reshape((SLAB,) + values.shape[2:])


def cube(values):
    return values.reshape((4, SLAB // 4) + values.shape[1:])


def linked_layer(
    layer_in, cotangent, qkv_weight, out_weight, ffn_weight, down_weight, head_gain, post_gain,
    adapters, adapter_ids, tables,
):
    count = SLAB // 4
    piece = (4, count, layer_in.shape[1])
    head_width, ff_width = qkv_weight.shape[2], ffn_weight.shape[2]
    width = 3 * head_width
    buffers = scatter_buffers(count)
    per = 2 * SLAB * D
    tokens = ((4, count, D), bf16)
    own = ((count, D), bf16)
    wide = ((count, D), f32)

    def gather_halves(local, axis):
        half = local.shape[axis] // 2
        return lax.dynamic_slice_in_dim(local, lax.axis_index("tok") * half, half, axis)

    def gathered(local):
        return lax.all_gather(local, ("col", "tok"), axis=0)

    attn_full = gathered(
        jnp.concatenate(
            [gather_halves(qkv_weight, 1).reshape(-1, head_width), gather_halves(out_weight, 0)]
        )
    )
    ffn_full = gathered(gather_halves(ffn_weight, 1))
    down_full = gathered(gather_halves(down_weight, 0))

    (
        x_own, cot_mid, factors, factors_t, qkv_b, out_a, out_at, ffn_b, down_a, down_at
    ) = linked(
        intake_kernel, 1,
        [(cube(layer_in),), (cube(cotangent),), adapter_ids]
        + [jnp.pad(post_gain, ((0, RANK - 2), (0, 0)))]
        + adapters,
        [own, (piece, bf16), ((128, D), bf16), ((D, 128), bf16), ((128, width), bf16)]
        + [((128, head_width), bf16), ((head_width, 128), bf16), ((128, 2 * ff_width), bf16)]
        + [((128, ff_width), bf16), ((ff_width, 128), bf16)],
        [(piece, bf16), ((4, 128, piece[2]), bf16)],
        per * 128,
    )
    low = ((4, count, 128), bf16)
    tall = ((4, count, D + 128), bf16)
    x_all, qkv_low, qkv_lin, inverses = linked(
        enter_qkv_kernel, 2,
        [x_own, (attn_full,), factors, (qkv_b,)],
        [tokens + (ANY,), low, ((4, count, width), f32, ANY), ((SLAB, 8), f32)],
        [tall, ((4, count, width), f32), ((D + 128, width), bf16), ((2, SLAB, 128), f32)]
        + [((4, 8, SLAB), f32)],
        per * width,
    )
    qkv_lin = flat(qkv_lin)
    q_low, k_low, v_low, attn_low, log_sums = attend(qkv_lin, inverses, head_gain, *tables)
    attn_lin, out_low, hidden, h_all = linked(
        leave_out_kernel, 3,
        [(cube(attn_low),), (attn_full,), out_a, factors, x_own],
        [wide, low, wide, tokens],
        [((4, count, head_width + 128), bf16), ((head_width + 128, D), bf16)] + buffers,
        per * head_width,
    )
    h_all = flat(h_all)
    ffn_low, gate_lin, up_lin, act_low = ffn(h_all, ffn_full, factors, ffn_b)
    down_low, own_out, grad_mlp, own_cot = linked(
        leave_down_kernel, 4,
        [(cube(act_low),), (down_full,), down_a, factors, (hidden,), cot_mid],
        [low, own, own, own],
        [((4, count, ff_width + 128), bf16), ((ff_width + 128, D), bf16), wide, wide] + buffers,
        per * ff_width,
    )
    dm_all, down_dlow, grad_ffn, out_mid = linked(
        back_down_kernel, 5,
        [grad_mlp, (down_full,), factors, down_at, (cube(gate_lin),), (cube(up_lin),), own_out],
        [tokens + (ANY,), low, ((4, count, 2 * ff_width), bf16, ANY), (piece, bf16)],
        [tall, ((ff_width, D + 128), bf16)]
        + [((4, count, ff_width), bf16)] * 2
        + [((4, count, 2 * ff_width), bf16)],
        per * ff_width,
    )
    ffn_dlow, grad_hidden, grad_attn = linked(
        back_ffn_kernel, 6,
        [(grad_ffn,), (ffn_full,), ffn_b, factors, factors_t, (own_cot,), (attn_lin,)],
        [low, wide, own],
        [((4, count, 2 * ff_width + 128), bf16), ((D, 2 * ff_width + 128), bf16), own, wide, wide]
        + buffers,
        per * 2 * ff_width,
    )
    grad_heads, early_cols, early_rows = linked(
        back_out_kernel, 7,
        [grad_attn, (attn_full,), factors, out_at, out_low, cube(attn_low), flat(down_low)]
        + [flat(down_dlow), ffn_low, flat(ffn_dlow), (flat(dm_all),), (act_low,)]
        + [(flat(grad_ffn),), (h_all,)],
        [((4, count, head_width), bf16), ((64, D), bf16)]
        + [((16, head_width + 3 * ff_width), bf16)],
        [tall, ((head_width, D + 128), bf16), ((SLAB, D), bf16)]
        + [((SLAB, ff_width), bf16), ((SLAB, 2 * ff_width), bf16), ((SLAB, D), bf16)]
        + [((16, D), f32), ((16, head_width), f32)],
        per * head_width,
    )
    weighted_q, weighted_k, grad_v, inner, layer_out = attend_back(
        q_low, k_low, v_low, attn_low, flat(grad_heads), log_sums, qkv_lin, head_gain, *tables,
        out_mid,
    )
    grad_qkv, own_rows = linked(
        prepare_kernel, 8,
        [(weighted_q,), (weighted_k,), grad_v, (qkv_lin,), inverses, inner, qkv_b, flat(qkv_low)]
        + [early_rows],
        [((SLAB, width + 128), bf16)]
        + [((16, width + head_width + 3 * ff_width), bf16)],
        [((SLAB, head_width), f32)] * 2
        + [((SLAB, 2 * head_width), f32), ((SLAB, 8), f32), ((4, 8, SLAB), f32)],
        per * 128,
    )
    every = lax.all_gather(own_rows, ("tok", "col"), axis=0)
    numbers = jnp.arange(ADAPTERS, dtype=jnp.int32)
    chosen = (adapter_ids.T[:, None, :] == numbers[None, :, None]).astype(f32).reshape(7, -1)
    chosen = jnp.pad(chosen, ((0, 1), (0, 0)))
    grad_in, col_parts = linked(
        back_qkv_kernel, 9,
        [cube(grad_qkv), (attn_full,), factors_t, (grad_hidden,), (x_all,)]
        + [early_cols, chosen],
        [(layer_in.shape, bf16), ((4, ADAPTERS, 32, piece[2]), bf16)],
        [((D, width + 128), bf16), wide, tokens, wide, (piece, bf16), (piece, bf16)]
        + [((4, 32, D), bf16)] * 2
        + [((4, 32, piece[2]), bf16), ((8, 32, piece[2]), bf16)]
        + [((ADAPTERS, 32, piece[2]), bf16)]
        + buffers,
        per * width,
    )
    return finish(chosen, layer_out, grad_in, col_parts, every, head_width, ff_width)


def diagonal(values, count):
    width = values.shape[1] // count
    return jnp.concatenate(
        [
            values[k * RANK : (k + 1) * RANK, k * width : (k + 1) * width]
            for k in range(count)
        ],
        axis=1,
    )


def on_device(
    layer_in,
    cotangent,
    qkv_weight,
    out_weight,
    ffn_weight,
    down_weight,
    qk_gain,
    post_gain,
    qkv_lower,
    qkv_raise,
    out_lower,
    out_raise,
    ffn_lower,
    ffn_raise,
    down_lower,
    down_raise,
    adapter_ids,
    prompt_len,
):
    group = lax.axis_index("tok") * lax.axis_size("col") + lax.axis_index("col")
    length = lax.dynamic_index_in_dim(prompt_len, group, 0, keepdims=False)
    cosine, sine = rotation(token_places(length), HEAD_DIM)
    cosine = jnp.concatenate([cosine, cosine], axis=1)
    sine = jnp.concatenate([-sine, sine], axis=1)
    slots = jnp.arange(SLAB, dtype=jnp.int32)
    bias = jnp.where((slots < length) | (slots >= PROMPT), 0.0, very_low)[:, None].astype(f32)

    plane = (lax.axis_size("tok"), lax.axis_size("row"), lax.axis_size("col"))
    layer = linked_layer if plane == (2, 4, 4) else split_layer
    adapters = [
        qkv_lower.swapaxes(2, 3), out_raise, ffn_lower.swapaxes(2, 3), down_raise,
        qkv_raise, out_lower.swapaxes(1, 2), ffn_raise, down_lower.swapaxes(1, 2),
    ]
    (
        layer_out, grad_in, qkv_lower_grad, out_raise_grad, ffn_lower_grad, down_raise_grad,
        qkv_raise_grad, out_lower_grad, ffn_raise_grad, down_lower_grad,
    ) = layer(
        layer_in, cotangent, qkv_weight, out_weight, ffn_weight, down_weight, qk_gain.astype(f32),
        post_gain, adapters, adapter_ids, (cosine, sine, bias),
    )
    return (
        layer_out,
        grad_in,
        qkv_lower_grad.swapaxes(2, 3),
        qkv_raise_grad,
        out_lower_grad.swapaxes(1, 2),
        out_raise_grad,
        ffn_lower_grad.swapaxes(2, 3),
        ffn_raise_grad,
        down_lower_grad.swapaxes(1, 2),
        down_raise_grad,
    )


def solution(mesh):
    return jax.shard_map(
        on_device,
        mesh=mesh,
        in_specs=(
            P(("tok", "row"), "col"),
            P(("tok", "row"), "col"),
            P(None, "col", "row"),
            P("row", "col"),
            P(None, "col", "row"),
            P("row", "col"),
            P(None, "row"),
            P(None, "col"),
            P(None, None, "col", None),
            P(None, None, None, "row"),
            P(None, "row", None),
            P(None, None, "col"),
            P(None, None, "col", None),
            P(None, None, None, "row"),
            P(None, "row", None),
            P(None, None, "col"),
            P(),
            P(),
        ),
        out_specs=(
            P(("tok", "row"), "col"),
            P(("tok", "row"), "col"),
            P(None, None, "col", None),
            P(None, None, None, "row"),
            P(None, "row", None),
            P(None, None, "col"),
            P(None, None, "col", None),
            P(None, None, None, "row"),
            P(None, "row", None),
            P(None, None, "col"),
        ),
        check_vma=False,
    )
```

```python
import functools
import math

import jax
import jax.numpy as jnp
from jax import lax
from jax.experimental import pallas as pl
from jax.experimental.pallas import tpu as pltpu
from jax.sharding import PartitionSpec as P

D = 2048
HEAD_DIM = 128
RANK = 16
ADAPTERS = 8
PROMPT = 1024
CONT_LEN = 128
SLAB = 1152

adapter_scale = 2.0
norm_eps = 1e-06
rope_base = 500000.0
very_low = -1e30
bf16 = jnp.bfloat16
f32 = jnp.float32
log2_scale = math.log2(math.e) / math.sqrt(HEAD_DIM)
score_scale = 1.0 / math.sqrt(HEAD_DIM)
BLOCK = 384
TILE = 512
MESH = pl.DeviceIdType.MESH


def mm(left, right):
    return jnp.dot(left, right, preferred_element_type=f32)


def mm_nt(left, right):
    return lax.dot_general(left, right, (((1,), (1,)), ((), ())), preferred_element_type=f32)


class Links:
    def __init__(self, send_sem, recv_sem, local_sem):
        self.tok = lax.axis_index("tok")
        self.row, self.col = lax.axis_index("row"), lax.axis_index("col")
        self.xn, self.yn, self.dg = self.row ^ 1, self.row ^ 2, self.row ^ 3
        self.send_sem, self.recv_sem, self.local_sem = send_sem, recv_sem, local_sem
        self.used, self.local_used = 0, 0

    def take(self, count):
        self.used += count
        return self.used - count

    def copy(self, source, target, index, recv_index, row, col=None, tok=None):
        return pltpu.make_async_remote_copy(
            src_ref=source,
            dst_ref=target,
            send_sem=self.send_sem.at[index],
            recv_sem=self.recv_sem.at[recv_index],
            device_id={
                "tok": self.tok if tok is None else tok,
                "row": row,
                "col": self.col if col is None else col,
            },
            device_id_type=MESH,
        )

    def local(self, source, target):
        self.local_used += 1
        return pltpu.make_async_copy(source, target, self.local_sem.at[self.local_used - 1])

    def plan(self, *pairs):
        return [self.local(source, target) for source, target in pairs]

    def fetch(self, *pairs):
        return start_all(self.plan(*pairs))

    def greet(self, rows=2, columns=False, twin=False):
        barrier = pltpu.get_barrier_semaphore()
        places = [(self.tok, self.row ^ step, self.col) for step in range(1, rows + 1)]
        if columns:
            places += [(self.tok, self.row, self.col ^ step) for step in range(1, 4)]
        if twin:
            places += [(self.tok ^ 1, self.row, self.col)]
        for tok, row, col in places:
            pl.semaphore_signal(
                barrier,
                inc=1,
                device_id={"tok": tok, "row": row, "col": col},
                device_id_type=MESH,
            )
        pl.semaphore_wait(barrier, len(places))


def start_all(copies):
    for copy in copies:
        copy.start()
    return copies


def wait_all(copies):
    for copy in copies:
        copy.wait()


class Exchange:
    def __init__(self, links, axis, piece_at, slot_at):
        self.links, self.axis = links, axis
        self.me = links.row if axis == "row" else links.col
        self.piece_at, self.slot_at = piece_at, slot_at
        self.base = links.take(3)
        self.own = links.local(piece_at(self.me), slot_at(self.me))

    def copy(self, source, target, step):
        links, other, index = self.links, self.me ^ step, self.base + step - 1
        row, col = (other, links.col) if self.axis == "row" else (links.row, other)
        return links.copy(source, target, index, index, row, col)

    def start(self):
        for step in range(1, 4):
            self.copy(self.piece_at(self.me ^ step), self.slot_at(self.me), step).start()
        self.own.start()

    def arrived(self):
        for step in range(1, 4):
            landed = self.slot_at(self.me ^ step)
            self.copy(landed, landed, step).wait_recv()
        self.own.wait()

    def sent(self):
        for step in range(1, 4):
            self.copy(self.piece_at(self.me ^ step), self.slot_at(self.me), step).wait_send()


def features(ref, width):
    return lambda col: ref.at[:, pl.ds(pl.multiple_of(col * width, width), width)]


def slot(ref):
    return lambda key: ref.at[key]


def token_rows(ref, count):
    return lambda row: ref.at[pl.ds(pl.multiple_of(row * count, 16), count)]


def gather(links, all_ref, work, before=None, after=None):
    me, xn, yn, dg = links.row, links.xn, links.yn, links.dg
    half = all_ref.shape[1] // 2
    top, low = pl.ds(0, half), pl.ds(half, half)
    base = links.take(6)

    def move(owner, part, index, other):
        place = all_ref.at[owner, part, pl.ds(0, D)]
        return links.copy(place, place, base + index, base + index, other)

    sends = [move(me, top, 0, xn), move(me, low, 1, yn), move(me, low, 2, xn), move(me, top, 3, yn)]
    for copy in sends:
        copy.start()
    if before:
        before()
    if work:
        work(me)
    move(xn, top, 0, xn).wait_recv()
    sends.append(move(xn, top, 4, yn))
    sends[-1].start()
    move(yn, low, 1, yn).wait_recv()
    sends.append(move(yn, low, 5, xn))
    sends[-1].start()
    if after:
        after()
    move(xn, low, 2, xn).wait_recv()
    if work:
        work(xn)
    move(yn, top, 3, yn).wait_recv()
    if work:
        work(yn)
    move(dg, top, 4, yn).wait_recv()
    move(dg, low, 5, xn).wait_recv()
    if work:
        work(dg)
    for copy in sends:
        copy.wait_send()


SLICES = 4


def scatter(links, product, o_ref, out_buf, relay_buf, final_buf, block=None, ready=None, hooks=None):
    me, xn, yn, dg = links.row, links.xn, links.yn, links.dg
    count, width = o_ref.shape[0], o_ref.shape[1] // SLICES
    half = count // 2
    top, low = pl.ds(0, half), pl.ds(half, half)
    base = links.take(6 * SLICES)
    all_copies = []

    def columns(k):
        at = block(k) * width if block else k * width
        return pl.ds(pl.multiple_of(at, width), width)

    def add(place, k, rows, relay):
        out_buf[place, k, rows] = (
            out_buf[place, k, rows].astype(f32) + relay_buf[relay, k].astype(f32)
        ).astype(bf16)

    def relay(k):
        copies = all_copies[k]
        copies[0].wait_recv()
        add(2, k, top, 0)
        copies[4].start()
        copies[1].wait_recv()
        add(1, k, low, 1)
        copies[5].start()

    def finish(k):
        for copy in all_copies[k][2:]:
            copy.wait_recv()

    for k in range(SLICES):
        cols = columns(k)

        def move(source, target, index, other, k=k):
            at = base + 6 * k + index
            return links.copy(source, target, at, at, other)

        copies = [
            move(out_buf.at[0, k, top], relay_buf.at[0, k], 0, xn),
            move(out_buf.at[0, k, low], relay_buf.at[1, k], 1, yn),
            move(out_buf.at[1, k, top], final_buf.at[0, k, top], 2, xn),
            move(out_buf.at[2, k, low], final_buf.at[1, k, low], 3, yn),
            move(out_buf.at[2, k, top], final_buf.at[1, k, top], 4, yn),
            move(out_buf.at[1, k, low], final_buf.at[0, k, low], 5, xn),
        ]
        all_copies.append(copies)
        if ready:
            ready(k)
        for place, (owner, first) in enumerate(((dg, (0, 1)), (xn, (2,)), (yn, (3,)))):
            out_buf[place, k] = product(owner, k, cols).astype(bf16)
            for index in first:
                copies[index].start()
        if k:
            relay(k - 1)
        if hooks:
            o_ref[:, cols] = product(me, k, cols)
            hooks[k](columns, finish)
    for k in range(SLICES):
        if k == (0 if hooks else SLICES // 2):
            relay(SLICES - 1)
        if not hooks:
            o_ref[:, columns(k)] = product(me, k, columns(k))

    def sent():
        for copies in all_copies:
            for copy in copies:
                copy.wait_send()

    return columns, finish, sent


def finish_all(result):
    _, finish, sent = result
    for k in range(SLICES):
        finish(k)
    sent()


def each_tile(width, step, body):
    @pl.loop(0, width // step)
    def _(tile):
        body(pl.multiple_of(tile * step, step))


def lower(rows, factor):
    step = rows.shape[1] // 4
    parts = [
        mm_nt(rows[:, at : at + step], factor[:, at : at + step])
        for at in range(0, rows.shape[1], step)
    ]
    return (adapter_scale * functools.reduce(jnp.add, parts)).astype(bf16)


def leave_product(y_ref, weight, f1_ref, low_ref, loads):
    depth = f1_ref.shape[1]
    used = []

    def product(owner, k, cols):
        if k == 0:
            if loads:
                loads[len(used)].wait()
            used.append(True)
            lowered = lower(y_ref[owner, :, :depth], f1_ref[...])
            low_ref[owner] = lowered
            y_ref[owner, :, depth:] = lowered
        return weight(y_ref[owner], cols)

    return product


class Streams:
    def __init__(self, links, rows, blocks, late=()):
        order = (links.dg, links.xn, links.yn, links.row)
        self.rows = []
        if rows:
            cols = pl.ds(0, rows[0].shape[2])
            self.rows = links.plan(*[(rows[0].at[k], rows[1].at[k, :, cols]) for k in order])
        self.blocks = blocks
        self.late = links.plan(*late)
        start_all(self.rows[:1])
        start_all(blocks[0])

    def ready(self, k):
        wait_all(self.blocks[k])
        if k == 0:
            start_all(self.rows[1:])
        if k < SLICES - 1:
            start_all(self.blocks[k + 1])
        if k == 1:
            start_all(self.late)


def load_qkv(links, w_hbm, w_ref, blocks):
    half, width = w_hbm.shape[1] // 4, w_hbm.shape[2]
    return [
        links.plan(
            *[
                (
                    w_hbm.at[2 * c + t, pl.ds(p * half, half)],
                    w_ref.at[
                        pl.ds(pl.multiple_of((2 * c + t) * half, half), half),
                        pl.ds(p * width, width),
                    ],
                )
                for t in range(2)
                for p in range(3)
            ]
        )
        for c in blocks
    ]


def load_out(links, w_hbm, w_ref):
    half, width = w_hbm.shape[1] // 4, w_hbm.shape[2]
    return [
        links.plan(
            *[
                (
                    w_hbm.at[2 * c + t, pl.ds(3 * half, half)],
                    w_ref.at[pl.ds(t * half, half), pl.ds(c * width, width)],
                )
                for t in range(2)
            ]
        )
        for c in range(4)
    ]


def load_down(links, w_hbm, w_ref):
    half, width = w_hbm.shape[1:]
    return [
        links.plan(
            *[
                (
                    w_hbm.at[2 * c + t],
                    w_ref.at[pl.ds(t * half, half), pl.ds(c * width, width)],
                )
                for t in range(2)
            ]
        )
        for c in range(4)
    ]


def load_ffn(links, w_hbm, w_ref):
    half, width = w_hbm.shape[2:]
    return [
        links.plan(
            *[
                (
                    w_hbm.at[2 * c + t, g],
                    w_ref.at[pl.ds((2 * c + t) * half, half), pl.ds(g * width, width)],
                )
                for t in range(2)
                for g in range(2)
            ]
        )
        for c in range(4)
    ]


def inverse_of(values):
    return lax.rsqrt(jnp.mean(values * values, axis=1, keepdims=True) + norm_eps)


def norm_back(values, weighted):
    inverse = inverse_of(values)
    inner = jnp.mean(values * weighted, axis=1, keepdims=True)
    return inverse * weighted - values * (inverse**3 * inner)


def gated(gate, up):
    return gate * jax.nn.sigmoid(gate) * up


def gated_back(grad, gate, up):
    sig = jax.nn.sigmoid(gate)
    act = gate * sig
    return (grad * up * (sig + act * (1.0 - sig)), grad * act)


QKV_A, OUT_B, FFN_A, DOWN_B = slice(0, 48), slice(48, 64), slice(64, 96), slice(96, 112)
GAIN0, GAIN1 = slice(112, 113), slice(113, 114)


def share_stats(links, stat_ref, first, second):
    blank = jnp.zeros((6, first.shape[0]), f32)
    sums = [jnp.sum(value.T, axis=0, keepdims=True) for value in (first, second)]
    stat_ref[links.row] = jnp.concatenate(sums + [blank], axis=0)
    base = links.take(3)
    mine = stat_ref.at[links.row]
    copies = []
    for index, other in enumerate((links.xn, links.yn, links.dg)):
        copies.append(links.copy(mine, mine, base + index, base + index, other))
        copies[-1].start()
    for index, other in enumerate((links.xn, links.yn, links.dg)):
        theirs = stat_ref.at[other]
        links.copy(theirs, theirs, base + index, base + index, other).wait_recv()
    for copy in copies:
        copy.wait_send()
    return stat_ref[0] + stat_ref[1] + stat_ref[2] + stat_ref[3]


def lane_sums(values):
    return functools.reduce(
        jnp.add, [values[:, at : at + 128] for at in range(0, values.shape[1], 128)]
    )


def intake_kernel(
    x_hbm, cot_hbm, ids_ref, gain_ref, qkv_lower_ref, out_raise_ref, ffn_lower_ref, down_raise_ref,
    qkv_raise_ref, out_lower_ref, ffn_raise_ref, down_lower_ref,
    own_ref, cot_ref, factors_ref, factors_t_ref, qkv_b_ref, out_a_ref, out_at_ref, ffn_b_ref,
    down_a_ref, down_at_ref,
    middle_ref, pieces_ref, send_sem, recv_sem, local_sem,
):
    links = Links(send_sem, recv_sem, local_sem)
    links.greet(rows=3, columns=True)
    width = pieces_ref.shape[2]
    first = Exchange(links, "row", slot(x_hbm), slot(middle_ref))
    second = Exchange(links, "col", slot(middle_ref), features(own_ref, width))
    turned = Exchange(links, "row", slot(cot_hbm), slot(cot_ref))
    spread = Exchange(links, "col", slot(pieces_ref), features(factors_ref, width))
    first.start()
    base = 4 * links.tok
    for place in range(4):
        for p in range(7):
            chosen = ids_ref[base + place, p]
            if p < 3:
                value = qkv_lower_ref[p, chosen]
            elif p == 3:
                value = out_raise_ref[chosen]
            elif p < 6:
                value = ffn_lower_ref[p - 4, chosen]
            else:
                value = down_raise_ref[chosen]
            pieces_ref[place, p * RANK : (p + 1) * RANK] = value
        pieces_ref[place, 7 * RANK :] = gain_ref[...]
    spread.start()
    first.arrived()
    second.start()
    turned.start()
    own = base + links.col
    for ref in (qkv_b_ref, out_a_ref, ffn_b_ref, down_a_ref):
        ref[...] = jnp.zeros_like(ref)
    for p in range(3):
        cols = slice(p * qkv_raise_ref.shape[3], (p + 1) * qkv_raise_ref.shape[3])
        qkv_b_ref[p * RANK : (p + 1) * RANK, cols] = qkv_raise_ref[p, ids_ref[own, p]]
    for p in range(2):
        cols = slice(p * ffn_raise_ref.shape[3], (p + 1) * ffn_raise_ref.shape[3])
        rows = slice((4 + p) * RANK, (5 + p) * RANK)
        ffn_b_ref[rows, cols] = ffn_raise_ref[p, ids_ref[own, 4 + p]]
    out_a_ref[OUT_B] = out_lower_ref[ids_ref[own, 3]]
    down_a_ref[DOWN_B] = down_lower_ref[ids_ref[own, 6]]
    spread.arrived()
    for source, target in (
        (out_a_ref, out_at_ref), (down_a_ref, down_at_ref), (factors_ref, factors_t_ref)
    ):
        target[...] = source[...].astype(f32).T.astype(bf16)
    for exchange in (second, turned):
        exchange.arrived()
    for exchange in (first, spread, second, turned):
        exchange.sent()


def enter_qkv_kernel(
    x_ref, w_hbm, factors_ref, f2_ref,
    all_hbm, low_ref, lin_hbm, inv_ref,
    all_ref, lin_ref, w_ref, sq_ref, stat_ref, send_sem, recv_sem, local_sem,
):
    links = Links(send_sem, recv_sem, local_sem)
    width = w_ref.shape[1]
    loads = start_all(sum(load_qkv(links, w_hbm, w_ref, range(4)), []))
    loads += links.fetch((f2_ref, w_ref.at[pl.ds(D, 128)]))
    all_ref[links.row, :, :D] = x_ref[...]
    links.greet(rows=3)
    count = x_ref.shape[0]
    stores = []

    def work(owner):
        lowered = lower(all_ref[owner, :, :D], factors_ref[...])
        low_ref[owner] = lowered
        all_ref[owner, :, D:] = lowered
        rows = all_ref[owner]
        third = width // 3
        for index in range(3):
            cols = slice(index * third, (index + 1) * third)
            value = mm(rows, w_ref[:, cols])
            lin_ref[owner, :, cols] = value
            if index < 2:
                place = pl.ds(pl.multiple_of(owner * count, 8), count)
                sq_ref[index, place] = lane_sums(value * value)
        stores.extend(
            links.fetch(
                (lin_ref.at[owner], lin_hbm.at[owner]),
                (all_ref.at[owner, :, pl.ds(0, D)], all_hbm.at[owner]),
            )
        )

    gather(links, all_ref, work, lambda: wait_all(loads))
    total = share_stats(links, stat_ref, sq_ref[0], sq_ref[1])
    inv_ref[...] = lax.rsqrt(total / D + norm_eps).T
    wait_all(stores)


def summed(o_ref, final_buf, rows):
    return o_ref[rows] + jnp.concatenate(
        [
            final_buf[0, k, rows].astype(f32) + final_buf[1, k, rows].astype(f32)
            for k in range(SLICES)
        ],
        axis=1,
    )


def leave_out_kernel(
    y_hbm, w_hbm, f1_ref, factors_ref, x_ref,
    lin_ref, low_ref, hidden_ref, all_ref,
    y_ref, w_ref, out_buf, relay_buf, final_buf, send_sem, recv_sem, local_sem,
):
    links = Links(send_sem, recv_sem, local_sem)
    streams = Streams(links, (y_hbm, y_ref), load_out(links, w_hbm, w_ref))
    w_ref[f1_ref.shape[1] :] = factors_ref[...]
    links.greet()
    product = leave_product(
        y_ref, lambda rows, cols: mm(rows, w_ref[:, cols]), f1_ref, low_ref, streams.rows
    )
    finish_all(
        scatter(links, product, lin_ref, out_buf, relay_buf, final_buf, ready=streams.ready)
    )
    gain = factors_ref[GAIN0].astype(f32)

    @pl.loop(0, lin_ref.shape[0] // 32)
    def _(tile):
        rows = pl.ds(pl.multiple_of(tile * 32, 32), 32)
        value = summed(lin_ref, final_buf, rows)
        lin_ref[rows] = value
        hidden = x_ref[rows].astype(f32) + value * inverse_of(value) * gain
        hidden_ref[rows] = hidden
        all_ref[links.row, rows] = hidden.astype(bf16)

    gather(links, all_ref, None)


def flat_weight(ref):
    return ref[...].reshape(D, ref.shape[3])


def ffn_kernel(h_ref, wg_ref, wu_ref, factors_ref, fg_ref, fu_ref, low_ref, gate_ref, up_ref, act_ref):
    @pl.when(pl.program_id(0) == 0)
    def _():
        low_ref[...] = lower(h_ref[...], factors_ref[...])

    lowered = low_ref[...]
    rank = lowered.shape[1] // 2
    for at in range(0, SLAB, BLOCK):
        rows = slice(at, at + BLOCK)
        gate = mm(h_ref[rows], flat_weight(wg_ref)) + mm(lowered[rows], fg_ref[...])
        up = mm(h_ref[rows], flat_weight(wu_ref)) + mm(lowered[rows], fu_ref[...])
        gate_ref[rows] = gate.astype(bf16)
        up_ref[rows] = up.astype(bf16)
        act_ref[rows] = gated(gate, up).astype(bf16)


def ffn(h_all, w, factors, f2):
    width = f2.shape[1] // 2
    step = 256
    tiles = width // step
    low = jax.ShapeDtypeStruct((SLAB, f2.shape[0]), bf16)
    wide = jax.ShapeDtypeStruct((SLAB, width), bf16)
    whole = lambda value: pl.BlockSpec(value.shape, lambda t: (0, 0))
    cols = lambda rows, base: pl.BlockSpec((rows, step), lambda t: (0, base * tiles + t))
    block = (w.shape[0], 1, w.shape[2], step)
    part = lambda which: pl.BlockSpec(block, lambda t: (0, which, 0, t))
    return pl.pallas_call(
        ffn_kernel,
        grid=(tiles,),
        in_specs=[whole(h_all), part(0), part(1), whole(factors)]
        + [cols(f2.shape[0], 0), cols(f2.shape[0], 1)],
        out_specs=[whole(low)] + [cols(SLAB, 0)] * 3,
        out_shape=[low, wide, wide, wide],
        compiler_params=pltpu.CompilerParams(vmem_limit_bytes=48 << 20),
        cost_estimate=pl.CostEstimate(
            flops=4 * SLAB * D * width, bytes_accessed=4 * D * width + 10 * SLAB * width,
            transcendentals=SLAB * width,
        ),
        name="ffn",
    )(h_all, w, w, factors, f2, f2)


def leave_down_kernel(
    y_hbm, w_hbm, f1_ref, factors_ref, hidden_hbm, cot_ref,
    low_ref, out_ref, dm_ref, own_cot_ref,
    y_ref, w_ref, hidden_ref, lin_ref, out_buf, relay_buf, final_buf,
    send_sem, recv_sem, local_sem,
):
    links = Links(send_sem, recv_sem, local_sem)
    streams = Streams(
        links, (y_hbm, y_ref), load_down(links, w_hbm, w_ref), [(hidden_hbm, hidden_ref)]
    )
    links.greet(columns=True)
    turned = Exchange(links, "col", slot(cot_ref), features(own_cot_ref, cot_ref.shape[2]))
    w_ref[f1_ref.shape[1] :] = factors_ref[...]
    product = leave_product(
        y_ref, lambda rows, cols: mm(rows, w_ref[:, cols]), f1_ref, low_ref, streams.rows
    )
    def ready(k):
        if k == 2:
            turned.start()
        streams.ready(k)

    finish_all(
        scatter(
            links, product, lin_ref, out_buf, relay_buf, final_buf,
            ready=ready,
        )
    )
    turned.arrived()
    wait_all(streams.late)
    gain = factors_ref[GAIN1].astype(f32)

    @pl.loop(0, lin_ref.shape[0] // 32)
    def _(tile):
        rows = pl.ds(pl.multiple_of(tile * 32, 32), 32)
        value = summed(lin_ref, final_buf, rows)
        out_ref[rows] = (hidden_ref[rows] + value * inverse_of(value) * gain).astype(bf16)
        dm_ref[rows] = norm_back(value, own_cot_ref[rows].astype(f32) * gain).astype(bf16)

    turned.sent()


def widen(source_ref, target_ref):
    @pl.loop(0, source_ref.shape[0] // 64)
    def _(tile):
        rows = pl.ds(pl.multiple_of(tile * 64, 64), 64)
        target_ref[rows] = source_ref[rows].astype(f32)


def finish_kernel(
    chosen_ref, out_ref, grad_ref, parts_ref, every_ref,
    out32_ref, grad32_ref, qkv_lower_ref, out_raise_ref, ffn_lower_ref, down_raise_ref,
    qkv_raise_ref, out_lower_ref, ffn_raise_ref, down_lower_ref,
):
    widen(out_ref, out32_ref)
    widen(grad_ref, grad32_ref)
    targets = [qkv_lower_ref.at[p] for p in range(3)]
    targets += [out_raise_ref, ffn_lower_ref.at[0], ffn_lower_ref.at[1], down_raise_ref]
    for p, target in enumerate(targets):
        rows = slice(p % 2 * RANK, (p % 2 + 1) * RANK)
        for adapter in range(ADAPTERS):
            target[adapter] = parts_ref[p // 2, adapter, rows].astype(f32)
    targets = [qkv_raise_ref.at[p] for p in range(3)]
    targets += [out_lower_ref, ffn_raise_ref.at[0], ffn_raise_ref.at[1], down_lower_ref]
    base = 0
    for p, target in enumerate(targets):
        step = 256
        weights = [chosen_ref[p, at] for at in range(64)]

        @pl.loop(0, target.shape[2] // step)
        def _(tile, p=p, target=target, base=base, weights=weights):
            cols = pl.ds(pl.multiple_of(base + tile * step, step), step)
            here = pl.ds(pl.multiple_of(tile * step, step), step)
            values = [every_ref[g, :, cols].astype(f32) for g in range(8)]
            for adapter in range(ADAPTERS):
                terms = [weights[adapter * 8 + g] * values[g] for g in range(8)]
                target[adapter, :, here] = functools.reduce(jnp.add, terms)

        base += target.shape[2]


def finish(chosen, layer_out, grad_in, col_parts, every, head_width, ff_width):
    piece = col_parts.shape[3]

    def out(*shape):
        return jax.ShapeDtypeStruct(shape, f32)

    return pl.pallas_call(
        finish_kernel,
        in_specs=[SMEM] + [VMEM] * 4,
        out_specs=[VMEM] * 10,
        out_shape=[
            out(*layer_out.shape), out(*grad_in.shape),
            out(3, ADAPTERS, RANK, piece), out(ADAPTERS, RANK, piece),
            out(2, ADAPTERS, RANK, piece), out(ADAPTERS, RANK, piece),
            out(3, ADAPTERS, RANK, head_width), out(ADAPTERS, RANK, head_width),
            out(2, ADAPTERS, RANK, ff_width), out(ADAPTERS, RANK, ff_width),
        ],
        compiler_params=pltpu.CompilerParams(vmem_limit_bytes=48 << 20),
        cost_estimate=pl.CostEstimate(flops=10**8, bytes_accessed=16 << 20, transcendentals=0),
        name="finish",
    )(chosen, layer_out, grad_in, col_parts, every)


def back_down_kernel(
    dm_ref, w_hbm, factors_ref, f2_ref, gate_hbm, up_hbm, out_ref,
    all_hbm, low_ref, grad_hbm, out_mid_ref,
    all_ref, w_ref, gate_ref, up_ref, grad_ref, send_sem, recv_sem, local_sem,
):
    links = Links(send_sem, recv_sem, local_sem)
    loads = start_all(sum(load_down(links, w_hbm, w_ref), []))
    order = (links.row, links.xn, links.yn, links.dg)
    gates = [
        links.plan((gate_hbm.at[k], gate_ref.at[k]), (up_hbm.at[k], up_ref.at[k])) for k in order
    ]
    start_all(gates[0])
    all_ref[links.row, :, :D] = dm_ref[...]
    w_ref[:, D:] = f2_ref[...]
    links.greet(columns=True)
    width = w_ref.shape[0]
    turned = Exchange(links, "col", features(out_ref, out_mid_ref.shape[2]), slot(out_mid_ref))
    stores = []

    def before():
        wait_all(loads)
        for gate in gates[1:]:
            start_all(gate)

    def work(owner):
        wait_all(gates[len(stores) // 2])
        lowered = lower(all_ref[owner, :, :D], factors_ref[...])
        low_ref[owner] = lowered
        all_ref[owner, :, D:] = lowered

        def body(at):
            cols, far = pl.ds(at, TILE), pl.ds(pl.multiple_of(width + at, TILE), TILE)
            grad = mm_nt(all_ref[owner], w_ref[cols, :])
            gate, up = gate_ref[owner, :, cols].astype(f32), up_ref[owner, :, cols].astype(f32)
            grad_gate, grad_up = gated_back(grad, gate, up)
            grad_ref[owner, :, cols] = grad_gate.astype(bf16)
            grad_ref[owner, :, far] = grad_up.astype(bf16)

        each_tile(width, TILE, body)
        stores.extend(
            links.fetch(
                (grad_ref.at[owner], grad_hbm.at[owner]),
                (all_ref.at[owner, :, pl.ds(0, D)], all_hbm.at[owner]),
            )
        )

    gather(links, all_ref, work, before, turned.start)
    turned.arrived()
    turned.sent()
    wait_all(stores)


def back_ffn_kernel(
    y_hbm, w_hbm, f1_ref, factors_ref, factors_t_ref, cot_hbm, attn_hbm,
    low_ref, hidden_ref, da_ref,
    y_ref, w_ref, cot_ref, attn_ref, lin_ref, out_buf, relay_buf, final_buf,
    send_sem, recv_sem, local_sem,
):
    links = Links(send_sem, recv_sem, local_sem)
    streams = Streams(
        links,
        (y_hbm, y_ref),
        load_ffn(links, w_hbm, w_ref),
        [(cot_hbm, cot_ref), (attn_hbm, attn_ref)],
    )
    links.greet()
    w_ref[:, f1_ref.shape[1] :] = factors_t_ref[...]
    product = leave_product(
        y_ref, lambda rows, cols: mm_nt(rows, w_ref[cols, :]), f1_ref, low_ref, streams.rows
    )
    finish_all(
        scatter(
            links, product, lin_ref, out_buf, relay_buf, final_buf,
            ready=streams.ready,
        )
    )
    wait_all(streams.late)
    gain = factors_ref[GAIN0].astype(f32)

    @pl.loop(0, lin_ref.shape[0] // 32)
    def _(tile):
        rows = pl.ds(pl.multiple_of(tile * 32, 32), 32)
        value = summed(lin_ref, final_buf, rows) + cot_ref[rows].astype(f32)
        hidden_ref[rows] = value
        da_ref[rows] = norm_back(attn_ref[rows], value * gain).astype(bf16)


def mm_tn(left, right):
    return lax.dot_general(left, right, (((0,), (0,)), ((), ())), preferred_element_type=f32)


def back_out_kernel(
    da_ref, w_hbm, factors_ref, f2_ref, out_low_ref, attn_ref, down_low_ref, down_dlow_ref,
    ffn_low_ref, ffn_dlow_ref, dm_hbm, act_hbm, grad_hbm, h_hbm,
    heads_ref, cols_ref, rows_ref,
    all_ref, w_ref, dm_ref, act_ref, grad_ref, h_ref, raise_ref, lower_ref, send_sem, recv_sem, local_sem,
):
    links = Links(send_sem, recv_sem, local_sem)
    load = start_all(sum(load_out(links, w_hbm, w_ref), []))
    all_ref[links.row, :, :D] = da_ref[...]
    w_ref[:, D:] = f2_ref[...]
    links.greet()
    loads = []

    def before():
        loads.extend(
            links.fetch((dm_hbm, dm_ref), (act_hbm, act_ref), (grad_hbm, grad_ref), (h_hbm, h_ref))
        )
        wait_all(load)

    heads, half = heads_ref.shape[2], grad_ref.shape[1] // 2

    def after():
        wait_all(loads)
        down_raise = mm_tn(down_low_ref[:, DOWN_B], dm_ref[...])
        cols_ref[3 * RANK : 4 * RANK] = down_raise.astype(bf16)
        cols_ref[RANK : 3 * RANK] = mm_tn(ffn_dlow_ref[:, FFN_A], h_ref[...]).astype(bf16)
        for p in range(2):
            low = ffn_low_ref[:, (4 + p) * RANK : (5 + p) * RANK]
            raised = mm_tn(low, grad_ref[:, p * half : (p + 1) * half])
            rows_ref[:, heads + p * half : heads + (p + 1) * half] = raised.astype(bf16)
        rows_ref[:, heads + 2 * half :] = mm_tn(down_dlow_ref[:, DOWN_B], act_ref[...]).astype(bf16)

    def work(owner):
        lowered = lower(all_ref[owner, :, :D], factors_ref[...])
        all_ref[owner, :, D:] = lowered
        heads_ref[owner] = mm_nt(all_ref[owner], w_ref[...]).astype(bf16)
        raise_ref[...] += mm_tn(out_low_ref[owner, :, OUT_B], all_ref[owner, :, :D])
        lower_ref[...] += mm_tn(lowered[:, OUT_B], attn_ref[owner])

    raise_ref[...] = jnp.zeros_like(raise_ref)
    lower_ref[...] = jnp.zeros_like(lower_ref)
    gather(links, all_ref, work, before, after)
    cols_ref[0:RANK] = raise_ref[...].astype(bf16)
    rows_ref[:, :heads] = lower_ref[...].astype(bf16)


def prepare_kernel(
    wq_hbm, wk_hbm, dv_ref, lin_hbm, inv_ref, inner_ref, f1_ref, low_ref, early_ref,
    grad_ref, rows_ref,
    wq_ref, wk_ref, lin_ref, total_ref, stat_ref, send_sem, recv_sem, local_sem,
):
    links = Links(send_sem, recv_sem, local_sem)
    third = wq_ref.shape[1]
    loads = links.fetch(
        (wq_hbm, wq_ref),
        (wk_hbm, wk_ref),
        (lin_hbm.at[:, pl.ds(0, 2 * third)], lin_ref),
    )
    links.greet(rows=3)
    total = share_stats(links, stat_ref, inner_ref[0], inner_ref[1])
    total_ref[...] = total.T / D
    wait_all(loads)

    @pl.loop(0, SLAB // 96)
    def _(tile):
        rows = pl.ds(pl.multiple_of(tile * 96, 96), 96)
        inverse = inv_ref[rows]
        factor = inverse**3 * total_ref[rows]
        for index, source in enumerate((wq_ref, wk_ref)):
            cols = slice(index * third, (index + 1) * third)
            one = slice(index, index + 1)
            value = inverse[:, one] * source[rows] - lin_ref[rows, cols] * factor[:, one]
            grad_ref[rows, cols] = value.astype(bf16)
        grad_ref[rows, 2 * third : 3 * third] = dv_ref[rows]

    grad_ref[:, 3 * third :] = lower(grad_ref[:, : 3 * third], f1_ref[...])
    for index in range(3):
        cols = slice(index * third, (index + 1) * third)
        low = low_ref[:, index * RANK : (index + 1) * RANK]
        rows_ref[:, cols] = mm_tn(low, grad_ref[:, cols]).astype(bf16)
    rows_ref[:, 3 * third :] = early_ref[...]


def back_qkv_kernel(
    grad_ref, w_hbm, factors_t_ref, hidden_hbm, x_hbm, early_ref, chosen_ref,
    turn_buf, sums_ref,
    w_ref, hidden_ref, x_ref, sum_ref, own_ref, middle_ref, parts_ref, got_ref, total_ref, groups_ref,
    placed_ref, out_buf, relay_buf, final_buf, send_sem, recv_sem, local_sem,
):
    links = Links(send_sem, recv_sem, local_sem)
    steps = (2, 3, 1, 0)
    streams = Streams(
        links,
        None,
        load_qkv(links, w_hbm, w_ref, [links.col ^ step for step in steps]),
        [(hidden_hbm, hidden_ref)],
    )
    x_load = links.plan((x_hbm, x_ref))
    depth = w_ref.shape[1] - 128
    w_ref[:, depth:] = factors_t_ref[...]
    links.greet(rows=3, columns=True, twin=True)
    width = own_ref.shape[2]
    count = grad_ref.shape[1]
    by_row = Exchange(links, "row", slot(parts_ref), slot(got_ref))
    base = 4 * links.tok
    by_col = Exchange(
        links, "col", slot(total_ref), lambda key: groups_ref.at[base + key]
    )
    index = links.take(1)
    mine, theirs = groups_ref.at[pl.ds(base, 4)], groups_ref.at[pl.ds(4 - base, 4)]
    to_twin = links.copy(mine, mine, index, index, links.row, tok=links.tok ^ 1)
    from_twin = links.copy(theirs, theirs, index, index, links.row, tok=links.tok ^ 1)
    mine_half, their_half = (pl.ds(tok * RANK, RANK) for tok in (links.tok, 1 - links.tok))
    spread = Exchange(
        links,
        "row",
        lambda key: placed_ref.at[:, mine_half],
        lambda key: sums_ref.at[key, :, mine_half],
    )
    index = links.take(1)
    sent_half, got_half = sums_ref.at[:, :, mine_half], sums_ref.at[:, :, their_half]
    half_out = links.copy(sent_half, sent_half, index, index, links.row, tok=links.tok ^ 1)
    half_in = links.copy(got_half, got_half, index, index, links.row, tok=links.tok ^ 1)

    def lower_grad():
        wait_all(x_load)
        late = 0.0
        for owner in range(4):
            late = late + mm_tn(grad_ref[owner, :, depth : depth + 3 * RANK], x_ref[owner])
        late = late.astype(bf16)
        parts_ref[0] = late[0 : 2 * RANK]
        parts_ref[1, :RANK] = late[2 * RANK :]
        parts_ref[1, RANK:] = early_ref[:RANK]
        parts_ref[2] = early_ref[RANK : 3 * RANK]
        parts_ref[3, :RANK] = early_ref[3 * RANK :]
        parts_ref[3, RANK:] = jnp.zeros((RANK, D), bf16)
        by_row.start()

    def add_rows():
        by_row.arrived()
        for f in range(4):
            cols = slice(f * width, (f + 1) * width)
            value = got_ref[0, :, cols].astype(f32)
            for q in range(1, 4):
                value = value + got_ref[q, :, cols].astype(f32)
            total_ref[f] = value.astype(bf16)
        by_col.start()

    def share():
        by_col.arrived()
        to_twin.start()

    def place_groups():
        from_twin.wait_recv()
        for half in range(2):
            rows = slice(half * RANK, (half + 1) * RANK)
            values = [groups_ref[g, rows].astype(f32) for g in range(8)]
            for adapter in range(ADAPTERS):
                value = 0.0
                for g in range(8):
                    value = value + chosen_ref[2 * links.row + half, adapter * 8 + g] * values[g]
                placed_ref[adapter, rows] = value.astype(bf16)
        spread.start()

    def product(owner, k, cols):
        return mm_nt(grad_ref[owner], w_ref[cols, :])

    z_base, row_base = links.take(3), links.take(4)
    near = links.local(middle_ref.at[links.row], token_rows(turn_buf, count)(links.row))
    z_copies = []

    def leave_col(k, columns, finish):
        finish(k)
        cols, step = columns(k), steps[k]
        value = (
            sum_ref[:, cols]
            + final_buf[0, k].astype(f32)
            + final_buf[1, k].astype(f32)
            + hidden_ref[:, cols]
        ).astype(bf16)
        if step == 0:
            middle_ref[links.col] = value
            return
        own_ref[k] = value
        at = z_base + k
        copy = links.copy(
            own_ref.at[k], middle_ref.at[links.col], at, at, links.row, links.col ^ step
        )
        copy.start()
        z_copies.append(copy)

    def to_row(step):
        other = links.row ^ step
        return links.copy(
            middle_ref.at[other],
            token_rows(turn_buf, count)(links.row),
            row_base + step,
            row_base + step,
            other,
        )

    def leave_row(k):
        source = links.col ^ steps[k]
        if steps[k]:
            at = z_base + k
            landed = middle_ref.at[source]
            links.copy(landed, landed, at, at, links.row, source).wait_recv()
        step = links.row ^ source

        @pl.when(step == 0)
        def _():
            near.start()

        @pl.when(step != 0)
        def _():
            to_row(step).start()

    def first(columns, finish):
        start_all(x_load)

    def second(columns, finish):
        lower_grad()

    def third(columns, finish):
        wait_all(streams.late)
        leave_col(0, columns, finish)

    def fourth(columns, finish):
        add_rows()
        leave_col(1, columns, finish)

    columns, finish, sent = scatter(
        links, product, sum_ref, out_buf, relay_buf, final_buf,
        block=lambda k: links.col ^ steps[k],
        ready=streams.ready,
        hooks=[first, second, third, fourth],
    )
    leave_row(0)
    share()
    leave_col(2, columns, finish)
    leave_col(3, columns, finish)
    leave_row(3)
    place_groups()
    leave_row(2)
    leave_row(1)
    spread.arrived()
    half_out.start()
    near.wait()
    for step in range(1, 4):
        landed = token_rows(turn_buf, count)(links.row ^ step)
        at = row_base + step
        links.copy(landed, landed, at, at, links.row ^ step).wait_recv()
    half_in.wait_recv()
    for step in range(1, 4):
        to_row(step).wait_send()
    half_out.wait_send()
    for copy in z_copies:
        copy.wait_send()
    to_twin.wait_send()
    for exchange in (by_row, by_col, spread):
        exchange.sent()
    sent()


VMEM = pl.BlockSpec(memory_space=pltpu.VMEM)
ANY = pl.BlockSpec(memory_space=pl.ANY)
SMEM = pl.BlockSpec(memory_space=pltpu.SMEM)


def linked(kernel, number, operands, outs, scratch, flops):
    specs = [ANY if isinstance(value, tuple) else VMEM for value in operands]
    values = [value[0] if isinstance(value, tuple) else value for value in operands]
    specs = [
        SMEM if value.ndim == 2 and value.shape[0] == 8 and value.dtype != bf16 else spec
        for spec, value in zip(specs, values)
    ]
    return pl.pallas_call(
        kernel,
        in_specs=specs,
        out_specs=[ANY if len(out) == 3 else VMEM for out in outs],
        out_shape=[jax.ShapeDtypeStruct(out[0], out[1]) for out in outs],
        scratch_shapes=[pltpu.VMEM(shape, kind) for shape, kind in scratch]
        + [
            pltpu.SemaphoreType.DMA((48,)),
            pltpu.SemaphoreType.DMA((48,)),
            pltpu.SemaphoreType.DMA((48,)),
        ],
        compiler_params=pltpu.CompilerParams(
            collective_id=number, has_side_effects=True, vmem_limit_bytes=60 << 20
        ),
        cost_estimate=pl.CostEstimate(
            flops=flops, bytes_accessed=flops // 400, transcendentals=0
        ),
        name=kernel.__name__,
    )(*values)


def scatter_buffers(count):
    part = D // SLICES
    return [
        ((3, SLICES, count, part), bf16),
        ((2, SLICES, count // 2, part), bf16),
        ((2, SLICES, count, part), bf16),
    ]


def score_blocks(k_ref, q_block, bias_ref, start, stop):
    parts = []
    if start:
        parts.append(mm_nt(k_ref[0:start], q_block) + bias_ref[0:start])
    own = mm_nt(k_ref[start:stop], q_block) + bias_ref[start:stop]
    keys = lax.broadcasted_iota(jnp.int32, own.shape, 0)
    queries = lax.broadcasted_iota(jnp.int32, own.shape, 1)
    parts.append(jnp.where(keys <= queries, own, very_low))
    return parts

def attend_kernel(q_ref, k_ref, v_ref, inv_ref, gain_ref, cos_ref, sin_ref, bias_ref,
                  ql_ref, kl_ref, vl_ref, o_ref, lse_ref):
    for source, target, index in ((q_ref, ql_ref, 0), (k_ref, kl_ref, 1)):
        normed = source[...] * inv_ref[:, index:index+1] * gain_ref[index:index+1, :]
        target[...] = (normed * cos_ref[...] + pltpu.roll(normed, HEAD_DIM // 2, 1) * sin_ref[...]).astype(bf16)
    values = v_ref[...].astype(bf16)
    vl_ref[...] = values
    values_t = v_ref[...].T.astype(bf16)
    for start in range(0, SLAB, BLOCK):
        stop = start + BLOCK
        parts = score_blocks(kl_ref, ql_ref[start:stop], bias_ref, start, stop)
        top = functools.reduce(jnp.maximum, [jnp.max(p, axis=0, keepdims=True) for p in parts]) * log2_scale
        total, out, at = 0.0, 0.0, 0
        for part in parts:
            shifted = jnp.exp2(part * log2_scale - top)
            total = total + jnp.sum(shifted, axis=0, keepdims=True)
            out = out + mm(values_t[:, at:at+part.shape[0]], shifted.astype(bf16))
            at += part.shape[0]
        o_ref[start:stop] = (out / total).T.astype(bf16)
        lse_ref[0, :, start:stop] = top + jnp.log2(total)

def attend_back_kernel(ql_ref, kl_ref, vl_ref, o_ref, do_ref, lse_ref, q_ref, k_ref, gain_ref, cos_ref, sin_ref, bias_ref, *refs):
    mid_ref, wq_ref, wk_ref, dv_ref, sum_ref, turn_ref, dk_sum, dv_sum, *sems = refs if len(refs) > 8 else (None, *refs[:4], None, *refs[4:])
    if sems:
        links = Links(*sems)
        turned = Exchange(links, "row", slot(mid_ref), token_rows(turn_ref, mid_ref.shape[1]))

        @pl.when(pl.program_id(0) == 0)
        def _():
            links.greet(rows=3)
            turned.start()

    keys_t = kl_ref[...].astype(f32).T.astype(bf16)
    delta_all = jnp.sum((do_ref[...].astype(f32) * o_ref[...].astype(f32)).T, axis=0, keepdims=True)
    dk_sum[...] = jnp.zeros_like(dk_sum)
    dv_sum[...] = jnp.zeros_like(dv_sum)
    def unrotate(values):
        return values * cos_ref[...] - pltpu.roll(values, HEAD_DIM // 2, 1) * sin_ref[...]
    dq_parts = []
    for start in range(0, SLAB, BLOCK):
        stop = start + BLOCK
        queries, grads = ql_ref[start:stop], do_ref[start:stop]
        parts = score_blocks(kl_ref, queries, bias_ref, start, stop)
        lse, delta = lse_ref[0, :, start:stop], delta_all[:, start:stop]
        at, dq = 0, 0.0
        for part in parts:
            span = slice(at, at + part.shape[0])
            probs = jnp.exp2(part * log2_scale - lse)
            dv_sum[span] += mm(probs.astype(bf16), grads)
            dscore = (probs * (mm_nt(vl_ref[span], grads) - delta)).astype(bf16)
            dk_sum[span] += mm(dscore, queries)
            dq = dq + mm(keys_t[:, span], dscore)
            at += part.shape[0]
        dq_parts.append(dq.T)
    dq_all = jnp.concatenate(dq_parts, axis=0) * score_scale
    dv_ref[...] = dv_sum[...].astype(bf16)
    wq = unrotate(dq_all) * gain_ref[0:1, :]
    wk = unrotate(dk_sum[...] * score_scale) * gain_ref[1:2, :]
    wq_ref[...] = wq.astype(wq_ref.dtype)
    wk_ref[...] = wk.astype(wk_ref.dtype)
    first = pl.program_id(0) == 0
    for index, (weighted, source) in enumerate(((wq, q_ref), (wk, k_ref))):
        product = weighted * source[...]

        @pl.when(first)
        def _():
            sum_ref[index] = product

        @pl.when(jnp.logical_not(first))
        def _():
            sum_ref[index] += product

    if sems:

        @pl.when(pl.program_id(0) == pl.num_programs(0) - 1)
        def _():
            turned.arrived()
            turned.sent()


def attend_specs(heads):
    col = lambda base: pl.BlockSpec((SLAB, HEAD_DIM), lambda h: (0, base * heads + h))
    whole = lambda shape: pl.BlockSpec(shape, lambda h: (0,) * len(shape))
    return col, whole

def attend(qkv_lin, inverses, gains, cosine, sine, bias):
    heads = qkv_lin.shape[1] // (3 * HEAD_DIM)
    col, whole = attend_specs(heads)
    low = jax.ShapeDtypeStruct((SLAB, heads * HEAD_DIM), bf16)
    return pl.pallas_call(
        attend_kernel, grid=(heads,),
        in_specs=[col(0), col(1), col(2), whole((SLAB, 8)), pl.BlockSpec((2, HEAD_DIM), lambda h: (0, h)),
                  whole((SLAB, HEAD_DIM)), whole((SLAB, HEAD_DIM)), whole((SLAB, 1))],
        out_specs=[col(0)] * 4 + [pl.BlockSpec((1, 1, SLAB), lambda h: (h, 0, 0))],
        out_shape=[low] * 4 + [jax.ShapeDtypeStruct((heads, 1, SLAB), f32)],
        compiler_params=pltpu.CompilerParams(vmem_limit_bytes=48 << 20),
        cost_estimate=pl.CostEstimate(flops=heads*4*SLAB*SLAB*HEAD_DIM, bytes_accessed=heads*SLAB*HEAD_DIM*20, transcendentals=heads*SLAB*SLAB),
        name="attend",
    )(qkv_lin, qkv_lin, qkv_lin, inverses, gains, cosine, sine, bias)

def attend_back(ql, kl, vl, o, do, lse, qkv_lin, gains, cosine, sine, bias, middle=None):
    heads = ql.shape[1] // HEAD_DIM
    col, whole = attend_specs(heads)
    wide = jax.ShapeDtypeStruct(ql.shape, f32)
    outs = [wide, wide, jax.ShapeDtypeStruct(ql.shape, bf16)]
    outs.append(jax.ShapeDtypeStruct((2, SLAB, HEAD_DIM), f32))
    moved, turned, params, sems = [], [], dict(vmem_limit_bytes=48 << 20), []
    if middle is not None:
        moved, turned = [middle], [jax.ShapeDtypeStruct((SLAB, middle.shape[2]), bf16)]
        params.update(collective_id=10, has_side_effects=True)
        sems = [pltpu.SemaphoreType.DMA((4,))] * 3
    hbm = pl.BlockSpec(memory_space=pl.ANY)
    return pl.pallas_call(
        attend_back_kernel,
        grid=(heads,),
        in_specs=[col(0)] * 5
        + [pl.BlockSpec((1, 1, SLAB), lambda h: (h, 0, 0)), col(0), col(1)]
        + [pl.BlockSpec((2, HEAD_DIM), lambda h: (0, h))]
        + [whole((SLAB, HEAD_DIM)), whole((SLAB, HEAD_DIM)), whole((SLAB, 1))]
        + [hbm] * len(moved),
        out_specs=[col(0)] * 3 + [whole((2, SLAB, HEAD_DIM))] + [hbm] * len(turned),
        out_shape=outs + turned,
        scratch_shapes=[pltpu.VMEM((SLAB, HEAD_DIM), f32)] * 2 + sems,
        compiler_params=pltpu.CompilerParams(**params),
        cost_estimate=pl.CostEstimate(
            flops=heads * 10 * SLAB * SLAB * HEAD_DIM,
            bytes_accessed=heads * SLAB * HEAD_DIM * 30,
            transcendentals=heads * SLAB * SLAB,
        ),
        name="attend_back",
    )(ql, kl, vl, o, do, lse, qkv_lin, qkv_lin, gains, cosine, sine, bias, *moved)


def dot(left, right):
    return jnp.dot(left, right, preferred_element_type=f32)


def dot_nt(left, right):
    return lax.dot_general(left, right, (((1,), (1,)), ((), ())), preferred_element_type=f32)


def dot_tn(left, right):
    return lax.dot_general(left, right, (((0,), (0,)), ((), ())), preferred_element_type=f32)


def gather_weight(local):
    half = local.shape[0] // lax.axis_size("tok")
    part = lax.dynamic_slice_in_dim(local, lax.axis_index("tok") * half, half, 0)
    return lax.all_gather(part, ("col", "tok"), axis=0, tiled=True)


def to_tokens(values):
    rows, cols = lax.axis_size("row"), lax.axis_size("col")
    width = values.shape[1]
    mixed = lax.all_to_all(values, "row", 0, 0, tiled=True)
    mixed = lax.all_to_all(mixed, "col", 0, 0, tiled=True)
    return mixed.reshape(cols, SLAB // rows, width).transpose(1, 0, 2).reshape(SLAB // rows, -1)


def from_tokens(values):
    rows, cols = lax.axis_size("row"), lax.axis_size("col")
    count = values.shape[0]
    mixed = values.reshape(count, cols, -1).transpose(1, 0, 2).reshape(cols * count, -1)
    mixed = lax.all_to_all(mixed, "col", 0, 0, tiled=True)
    return lax.all_to_all(mixed, "row", 0, 0, tiled=True)


def reorder(values, outer, inner):
    if outer == 1 or inner == 1:
        return values
    rest = values.shape[0] // (outer * inner)
    shape = (outer, inner, rest) + values.shape[1:]
    return values.reshape(shape).swapaxes(0, 1).reshape(values.shape)


def gather_tokens(values):
    rows, per_slab = lax.axis_size("row"), lax.axis_size("row") // lax.axis_size("col")
    return reorder(lax.all_gather(values, "row", axis=0, tiled=True), rows, per_slab)


def scatter_tokens(values):
    rows, per_slab = lax.axis_size("row"), lax.axis_size("row") // lax.axis_size("col")
    values = reorder(values.astype(bf16), per_slab, rows)
    return lax.psum_scatter(values, "row", scatter_dimension=0, tiled=True).astype(f32)


def token_places(length):
    slot_ids = jnp.arange(SLAB, dtype=jnp.int32)
    return jnp.where(slot_ids < PROMPT, slot_ids, length + (slot_ids - PROMPT) % CONT_LEN)


def rotation(places, head_size):
    half_dim = head_size // 2
    frequency = jnp.exp(
        -(2.0 * jnp.arange(half_dim, dtype=f32) / head_size) * math.log(rope_base)
    )
    angles = places.astype(f32)[:, None] * frequency[None, :]
    return (jnp.cos(angles), jnp.sin(angles))


def pick(adapters, ids):
    onehot = (ids[:, None] == jnp.arange(adapters.shape[0], dtype=jnp.int32)).astype(adapters.dtype)
    return jnp.tensordot(onehot, adapters, axes=1)


def place(ids, gradients):
    onehot = (jnp.arange(ADAPTERS, dtype=jnp.int32)[:, None] == ids[None, :]).astype(f32)
    total = 0.0
    for index in range(gradients.shape[0]):
        weight = onehot[:, index].reshape((ADAPTERS,) + (1,) * (gradients.ndim - 1))
        total = total + weight * gradients[index][None].astype(f32)
    return total


def block_diagonal(factors):
    count = len(factors)
    lines = []
    for index, factor in enumerate(factors):
        blank = jnp.zeros_like(factor)
        lines.append(
            jnp.concatenate([factor if k == index else blank for k in range(count)], axis=1)
        )
    return jnp.concatenate(lines, axis=0)


def enter(x, w, f1, f2):
    everything = gather_tokens(x)
    lowered = (adapter_scale * dot_nt(everything, f1)).astype(bf16)
    return everything, lowered, dot(everything, w) + dot(lowered, f2)


def leave(y, w, f1, f2):
    lowered = (adapter_scale * dot_nt(y, f1)).astype(bf16)
    return scatter_tokens(dot_nt(y, w) + dot(lowered, f2)), lowered


def split_layer(
    layer_in, cotangent, qkv_weight, out_weight, ffn_weight, down_weight, head_gain, post_gain,
    adapters, adapter_ids, tables,
):
    qkv_lower, out_raise, ffn_lower, down_raise, qkv_raise, out_lower, ffn_raise, down_lower = (
        adapters
    )
    col_count = lax.axis_size("col")
    group_base = lax.axis_index("tok") * col_count
    group = group_base + lax.axis_index("col")
    slab_ids = lax.dynamic_slice_in_dim(adapter_ids, group_base, col_count, 0)
    own_ids = lax.dynamic_index_in_dim(adapter_ids, group, 0, keepdims=False)
    size = layer_in.shape[1]
    local = jnp.concatenate([qkv_weight.transpose(1, 0, 2).reshape(size, -1), out_weight.T], axis=1)
    attn_full = gather_weight(local)
    ffn_full = gather_weight(ffn_weight.transpose(1, 0, 2).reshape(size, -1))
    down_full = gather_weight(down_weight.T)
    pieces = jnp.concatenate(
        [pick(qkv_lower[p], slab_ids[:, p]) for p in range(3)]
        + [pick(out_raise, slab_ids[:, 3])]
        + [pick(ffn_lower[p], slab_ids[:, 4 + p]) for p in range(2)]
        + [pick(down_raise, slab_ids[:, 6])]
        + [jnp.broadcast_to(jnp.pad(post_gain, ((0, 14), (0, 0))), (col_count, RANK, size))],
        axis=1,
    )
    qkv_b = block_diagonal([pick(qkv_raise[p], own_ids[p : p + 1])[0] for p in range(3)])
    out_a = pick(out_lower, own_ids[3:4])[0]
    ffn_b = block_diagonal([pick(ffn_raise[p], own_ids[4 + p : 5 + p])[0] for p in range(2)])
    down_a = pick(down_lower, own_ids[6:7])[0]
    factors = lax.all_to_all(pieces, "col", 0, 0, tiled=True)
    factors = factors.transpose(1, 0, 2).reshape(-1, D)
    qkv_a, out_b, ffn_a, down_b = (factors[part] for part in (QKV_A, OUT_B, FFN_A, DOWN_B))
    gains = factors[GAIN0.start : GAIN1.stop].astype(f32)
    width = qkv_b.shape[1]
    head_width, ff_width = width // 3, ffn_b.shape[1] // 2
    x_own = to_tokens(layer_in)
    x_all, qkv_low, qkv_lin = enter(x_own, attn_full[:, :width], qkv_a, qkv_b)
    q_lin, k_lin = qkv_lin[:, :head_width], qkv_lin[:, head_width : 2 * head_width]
    squares = jnp.stack([jnp.sum(q_lin * q_lin, axis=1), jnp.sum(k_lin * k_lin, axis=1)], axis=1)
    inverses = lax.rsqrt(lax.psum(squares, "row") / D + norm_eps)
    inverses = jnp.concatenate([inverses] * 4, axis=1)
    q_low, k_low, v_low, attn_low, log_sums = attend(qkv_lin, inverses, head_gain, *tables)
    attn_lin, out_low = leave(attn_low, attn_full[:, width:], out_a, out_b)
    hidden = x_own.astype(f32) + attn_lin * inverse_of(attn_lin) * gains[0]
    h_all, ffn_low, ffn_lin = enter(hidden.astype(bf16), ffn_full, ffn_a, ffn_b)
    gate_lin, up_lin = ffn_lin[:, :ff_width], ffn_lin[:, ff_width:]
    act_low = gated(gate_lin, up_lin).astype(bf16)
    mlp_lin, down_low = leave(act_low, down_full, down_a, down_b)
    layer_out = hidden + mlp_lin * inverse_of(mlp_lin) * gains[1]
    layer_out = from_tokens(layer_out.astype(bf16)).astype(f32)
    grad_out = to_tokens(cotangent).astype(f32)
    grad_mlp = norm_back(mlp_lin, grad_out * gains[1]).astype(bf16)
    dm_all, down_dlow, grad_act = enter(grad_mlp, down_full, down_b, down_a)
    grad_ffn = jnp.concatenate(gated_back(grad_act, gate_lin, up_lin), axis=1).astype(bf16)
    grad_ffn_in, ffn_dlow = leave(grad_ffn, ffn_full, ffn_b, ffn_a)
    grad_hidden = grad_out + grad_ffn_in
    grad_attn = norm_back(attn_lin, grad_hidden * gains[0]).astype(bf16)
    da_all, out_dlow, grad_heads = enter(grad_attn, attn_full[:, width:], out_b, out_a)
    weighted_q, weighted_k, grad_v, inner = attend_back(
        q_low, k_low, v_low, attn_low, grad_heads.astype(bf16), log_sums, qkv_lin, head_gain, *tables
    )
    inner = lax.psum(jnp.sum(inner, axis=2).T, "row")
    factor = inverses[:, :2] ** 3 * inner / D
    grad_qkv = jnp.concatenate(
        [
            (inverses[:, 0:1] * weighted_q - q_lin * factor[:, 0:1]).astype(bf16),
            (inverses[:, 1:2] * weighted_k - k_lin * factor[:, 1:2]).astype(bf16),
            grad_v,
        ],
        axis=1,
    )
    grad_qkv_in, qkv_dlow = leave(grad_qkv, attn_full[:, :width], qkv_b, qkv_a)
    grad_in = from_tokens((grad_hidden + grad_qkv_in).astype(bf16)).astype(f32)
    parts = jnp.concatenate(
        [dot_tn(qkv_dlow, x_all), dot_tn(out_low, da_all), dot_tn(ffn_dlow, h_all)]
        + [dot_tn(down_low, dm_all)]
    )
    parts = parts.astype(bf16).reshape(7, RANK, col_count, size).transpose(2, 0, 1, 3)
    parts = lax.all_to_all(parts, "col", 0, 0, tiled=True)
    placed = [place(slab_ids[:, p], parts[:, p]) for p in range(7)]
    col_grads = list(lax.psum(jnp.stack(placed).astype(bf16), ("tok", "row")).astype(f32))
    own_rows = jnp.concatenate(
        [diagonal(dot_tn(qkv_low, grad_qkv), 3), dot_tn(out_dlow, attn_low)]
        + [diagonal(dot_tn(ffn_low, grad_ffn), 2), dot_tn(down_dlow, act_low)],
        axis=1,
    )
    every = lax.all_gather(own_rows.astype(bf16), ("tok", "col"), axis=0)
    row_grads, at = [], 0
    for p in range(7):
        part = ff_width if p > 3 else head_width
        row_grads.append(place(adapter_ids[:, p], every[:, :, at : at + part]))
        at += part
    return (
        layer_out, grad_in,
        jnp.stack(col_grads[0:3]), col_grads[3], jnp.stack(col_grads[4:6]), col_grads[6],
        jnp.stack(row_grads[0:3]), row_grads[3], jnp.stack(row_grads[4:6]), row_grads[6],
    )


def flat(values):
    return values.reshape((SLAB,) + values.shape[2:])


def cube(values):
    return values.reshape((4, SLAB // 4) + values.shape[1:])


def linked_layer(
    layer_in, cotangent, qkv_weight, out_weight, ffn_weight, down_weight, head_gain, post_gain,
    adapters, adapter_ids, tables,
):
    count = SLAB // 4
    piece = (4, count, layer_in.shape[1])
    head_width, ff_width = qkv_weight.shape[2], ffn_weight.shape[2]
    width = 3 * head_width
    buffers = scatter_buffers(count)
    per = 2 * SLAB * D
    tokens = ((4, count, D), bf16)
    own = ((count, D), bf16)
    wide = ((count, D), f32)

    def gather_halves(local, axis):
        half = local.shape[axis] // 2
        return lax.dynamic_slice_in_dim(local, lax.axis_index("tok") * half, half, axis)

    def gathered(local):
        return lax.all_gather(local, ("col", "tok"), axis=0)

    attn_full = gathered(
        jnp.concatenate(
            [gather_halves(qkv_weight, 1).reshape(-1, head_width), gather_halves(out_weight, 0)]
        )
    )
    ffn_full = gathered(gather_halves(ffn_weight, 1))
    down_full = gathered(gather_halves(down_weight, 0))

    (
        x_own, cot_mid, factors, factors_t, qkv_b, out_a, out_at, ffn_b, down_a, down_at
    ) = linked(
        intake_kernel, 1,
        [(cube(layer_in),), (cube(cotangent),), adapter_ids]
        + [jnp.pad(post_gain, ((0, RANK - 2), (0, 0)))]
        + adapters,
        [own, (piece, bf16), ((128, D), bf16), ((D, 128), bf16), ((128, width), bf16)]
        + [((128, head_width), bf16), ((head_width, 128), bf16), ((128, 2 * ff_width), bf16)]
        + [((128, ff_width), bf16), ((ff_width, 128), bf16)],
        [(piece, bf16), ((4, 128, piece[2]), bf16)],
        per * 128,
    )
    low = ((4, count, 128), bf16)
    tall = ((4, count, D + 128), bf16)
    x_all, qkv_low, qkv_lin, inverses = linked(
        enter_qkv_kernel, 2,
        [x_own, (attn_full,), factors, (qkv_b,)],
        [tokens + (ANY,), low, ((4, count, width), f32, ANY), ((SLAB, 8), f32)],
        [tall, ((4, count, width), f32), ((D + 128, width), bf16), ((2, SLAB, 128), f32)]
        + [((4, 8, SLAB), f32)],
        per * width,
    )
    qkv_lin = flat(qkv_lin)
    q_low, k_low, v_low, attn_low, log_sums = attend(qkv_lin, inverses, head_gain, *tables)
    attn_lin, out_low, hidden, h_all = linked(
        leave_out_kernel, 3,
        [(cube(attn_low),), (attn_full,), out_a, factors, x_own],
        [wide, low, wide, tokens],
        [((4, count, head_width + 128), bf16), ((head_width + 128, D), bf16)] + buffers,
        per * head_width,
    )
    h_all = flat(h_all)
    ffn_low, gate_lin, up_lin, act_low = ffn(h_all, ffn_full, factors, ffn_b)
    down_low, own_out, grad_mlp, own_cot = linked(
        leave_down_kernel, 4,
        [(cube(act_low),), (down_full,), down_a, factors, (hidden,), cot_mid],
        [low, own, own, own],
        [((4, count, ff_width + 128), bf16), ((ff_width + 128, D), bf16), wide, wide] + buffers,
        per * ff_width,
    )
    dm_all, down_dlow, grad_ffn, out_mid = linked(
        back_down_kernel, 5,
        [grad_mlp, (down_full,), factors, down_at, (cube(gate_lin),), (cube(up_lin),), own_out],
        [tokens + (ANY,), low, ((4, count, 2 * ff_width), bf16, ANY), (piece, bf16)],
        [tall, ((ff_width, D + 128), bf16)]
        + [((4, count, ff_width), bf16)] * 2
        + [((4, count, 2 * ff_width), bf16)],
        per * ff_width,
    )
    ffn_dlow, grad_hidden, grad_attn = linked(
        back_ffn_kernel, 6,
        [(grad_ffn,), (ffn_full,), ffn_b, factors, factors_t, (own_cot,), (attn_lin,)],
        [low, wide, own],
        [((4, count, 2 * ff_width + 128), bf16), ((D, 2 * ff_width + 128), bf16), own, wide, wide]
        + buffers,
        per * 2 * ff_width,
    )
    grad_heads, early_cols, early_rows = linked(
        back_out_kernel, 7,
        [grad_attn, (attn_full,), factors, out_at, out_low, cube(attn_low), flat(down_low)]
        + [flat(down_dlow), ffn_low, flat(ffn_dlow), (flat(dm_all),), (act_low,)]
        + [(flat(grad_ffn),), (h_all,)],
        [((4, count, head_width), bf16), ((64, D), bf16)]
        + [((16, head_width + 3 * ff_width), bf16)],
        [tall, ((head_width, D + 128), bf16), ((SLAB, D), bf16)]
        + [((SLAB, ff_width), bf16), ((SLAB, 2 * ff_width), bf16), ((SLAB, D), bf16)]
        + [((16, D), f32), ((16, head_width), f32)],
        per * head_width,
    )
    weighted_q, weighted_k, grad_v, inner, layer_out = attend_back(
        q_low, k_low, v_low, attn_low, flat(grad_heads), log_sums, qkv_lin, head_gain, *tables,
        out_mid,
    )
    grad_qkv, own_rows = linked(
        prepare_kernel, 8,
        [(weighted_q,), (weighted_k,), grad_v, (qkv_lin,), inverses, inner, qkv_b, flat(qkv_low)]
        + [early_rows],
        [((SLAB, width + 128), bf16)]
        + [((16, width + head_width + 3 * ff_width), bf16)],
        [((SLAB, head_width), f32)] * 2
        + [((SLAB, 2 * head_width), f32), ((SLAB, 8), f32), ((4, 8, SLAB), f32)],
        per * 128,
    )
    every = lax.all_gather(own_rows, ("tok", "col"), axis=0)
    numbers = jnp.arange(ADAPTERS, dtype=jnp.int32)
    chosen = (adapter_ids.T[:, None, :] == numbers[None, :, None]).astype(f32).reshape(7, -1)
    chosen = jnp.pad(chosen, ((0, 1), (0, 0)))
    grad_in, col_parts = linked(
        back_qkv_kernel, 9,
        [cube(grad_qkv), (attn_full,), factors_t, (grad_hidden,), (x_all,)]
        + [early_cols, chosen],
        [(layer_in.shape, bf16), ((4, ADAPTERS, 32, piece[2]), bf16)],
        [((D, width + 128), bf16), wide, tokens, wide, (piece, bf16), (piece, bf16)]
        + [((4, 32, D), bf16)] * 2
        + [((4, 32, piece[2]), bf16), ((8, 32, piece[2]), bf16)]
        + [((ADAPTERS, 32, piece[2]), bf16)]
        + buffers,
        per * width,
    )
    return finish(chosen, layer_out, grad_in, col_parts, every, head_width, ff_width)


def diagonal(values, count):
    width = values.shape[1] // count
    return jnp.concatenate(
        [
            values[k * RANK : (k + 1) * RANK, k * width : (k + 1) * width]
            for k in range(count)
        ],
        axis=1,
    )


def on_device(
    layer_in,
    cotangent,
    qkv_weight,
    out_weight,
    ffn_weight,
    down_weight,
    qk_gain,
    post_gain,
    qkv_lower,
    qkv_raise,
    out_lower,
    out_raise,
    ffn_lower,
    ffn_raise,
    down_lower,
    down_raise,
    adapter_ids,
    prompt_len,
):
    group = lax.axis_index("tok") * lax.axis_size("col") + lax.axis_index("col")
    length = lax.dynamic_index_in_dim(prompt_len, group, 0, keepdims=False)
    cosine, sine = rotation(token_places(length), HEAD_DIM)
    cosine = jnp.concatenate([cosine, cosine], axis=1)
    sine = jnp.concatenate([-sine, sine], axis=1)
    slots = jnp.arange(SLAB, dtype=jnp.int32)
    bias = jnp.where((slots < length) | (slots >= PROMPT), 0.0, very_low)[:, None].astype(f32)

    plane = (lax.axis_size("tok"), lax.axis_size("row"), lax.axis_size("col"))
    layer = linked_layer if plane == (2, 4, 4) else split_layer
    adapters = [
        qkv_lower.swapaxes(2, 3), out_raise, ffn_lower.swapaxes(2, 3), down_raise,
        qkv_raise, out_lower.swapaxes(1, 2), ffn_raise, down_lower.swapaxes(1, 2),
    ]
    (
        layer_out, grad_in, qkv_lower_grad, out_raise_grad, ffn_lower_grad, down_raise_grad,
        qkv_raise_grad, out_lower_grad, ffn_raise_grad, down_lower_grad,
    ) = layer(
        layer_in, cotangent, qkv_weight, out_weight, ffn_weight, down_weight, qk_gain.astype(f32),
        post_gain, adapters, adapter_ids, (cosine, sine, bias),
    )
    return (
        layer_out,
        grad_in,
        qkv_lower_grad.swapaxes(2, 3),
        qkv_raise_grad,
        out_lower_grad.swapaxes(1, 2),
        out_raise_grad,
        ffn_lower_grad.swapaxes(2, 3),
        ffn_raise_grad,
        down_lower_grad.swapaxes(1, 2),
        down_raise_grad,
    )


def solution(mesh):
    return jax.shard_map(
        on_device,
        mesh=mesh,
        in_specs=(
            P(("tok", "row"), "col"),
            P(("tok", "row"), "col"),
            P(None, "col", "row"),
            P("row", "col"),
            P(None, "col", "row"),
            P("row", "col"),
            P(None, "row"),
            P(None, "col"),
            P(None, None, "col", None),
            P(None, None, None, "row"),
            P(None, "row", None),
            P(None, None, "col"),
            P(None, None, "col", None),
            P(None, None, None, "row"),
            P(None, "row", None),
            P(None, None, "col"),
            P(),
            P(),
        ),
        out_specs=(
            P(("tok", "row"), "col"),
            P(("tok", "row"), "col"),
            P(None, None, "col", None),
            P(None, None, None, "row"),
            P(None, "row", None),
            P(None, None, "col"),
            P(None, None, "col", None),
            P(None, None, None, "row"),
            P(None, "row", None),
            P(None, None, "col"),
        ),
        check_vma=False,
    )
```
